32 devices in a mesh: grp: 2 (over y), row: 4 (over x, core), col: 4 (over z).
Axes of the slice: x: 2, y: 2, z: 4, core: 2. Of those that a mesh axis runs over, the one named last changes fastest.
Arguments:
- pair_map: float32 [256, 128, 128], P(('grp', 'row'), 'col'), parts along dimension 0, may hold values from -6 to 6
- pair_mask: int32 [256, 128], P(('grp', 'row'), 'col'), parts along dimension 0, may hold values from 0 to 1, as said below
- gain_in: float32 [2, 128], replicated, may hold values from 0.5 to 1.5
- proj_weight: bfloat16 [2, 128, 512], replicated, may hold values from -0.5 to 0.5
- gate_weight: bfloat16 [2, 128, 128], replicated, may hold values from -0.5 to 0.5
- gain_out: float32 [2, 128], replicated, may hold values from 0.5 to 1.5
- out_weight: bfloat16 [2, 128, 128], replicated, may hold values from -0.5 to 0.5
- trans_gain: float32 [128], replicated, may hold values from 0.5 to 1.5
- trans_up: bfloat16 [128, 1024], replicated, may hold values from -0.5 to 0.5
- trans_down: bfloat16 [512, 128], replicated, may hold values from -0.25 to 0.25
Outputs:
- pair_out: float32 [256, 128, 128], P(('grp', 'row'), 'col'), parts along dimension 0
The draws below stay inside these ranges and needn't reach their ends.
There are 2 independent parts, one for each index of `grp`. The reference program is written for one: setup_inputs(seed, part) draws one part's arguments, and reference() takes and returns one part's arrays. A program takes and returns all parts, laid end to end along the dimension named above; an argument that names none is the same for every part. Nothing has to cross between parts.
Inputs may be any that keep to these rules, and one draw needn't show every extreme that they name: pair_mask[i, j] is 1 exactly when both i and j are below one valid length of the complex, which is at least 64.
All inputs are finite; a program needn't handle non-finite values.
Results may differ from the reference program's by a relative error of at most 0.0053.
Values may be sent and summed in bfloat16 or wider, within the bound.
No kernel may reach another device: no remote copies, remote signals or barrier semaphores. Data moves between devices by JAX's collectives and lax.ppermute only.
A program may use at most 128 MiB of HBM per device.

```python
import jax
import jax.numpy as jnp
from jax import lax

C = 128
HID = 128
FFN = 512
N = 128


def draw_pair_mask(key, part):
    key = jax.random.fold_in(key, 7)
    length = jax.random.randint(key, (), N // 2, N + 1)
    valid = (jnp.arange(N) < length).astype(jnp.int32)
    return valid[:, None] * valid[None, :]


def block_levels(own_key, extent, cuts, least, high):
    level, own = 1.0, jax.random.fold_in(own_key, 6)
    for position, shards_of in cuts:
        steps = jnp.exp(jax.random.uniform(jax.random.fold_in(own, position), (shards_of,), jnp.float32, least / len(cuts), high / len(cuts)))
        level = level * jnp.repeat(steps, extent[position] // shards_of).reshape([-1 if axis == position else 1 for axis in range(len(extent))])
    return level


def gaussian(key, dims, scale, limit, shards=(), held_as=jnp.bfloat16):
    array = scale * jax.random.normal(key, dims, jnp.float32)
    if shards:
        array = array * block_levels(key, dims, shards, -0.22, 0.18)
    return jnp.clip(array, -limit, limit).astype(held_as)


def setup_inputs(seed: int = 0, part: int = 0) -> dict:
    key_of = jax.random.split(jax.random.key(seed), 11)
    own_keys = jax.random.split(jax.random.fold_in(key_of[10], part), 11)
    return {
        "pair_map": gaussian(own_keys[0], (N, N, C), 1.0, 6.0, ((0, 4), (1, 4)), jnp.float32),
        "pair_mask": draw_pair_mask(jax.random.fold_in(jax.random.fold_in(key_of[10], part), 71), part),
        "gain_in": jnp.clip(1.0 + 0.1 * jax.random.normal(key_of[2], (2, C), jnp.float32), 0.5, 1.5),
        "proj_weight": gaussian(key_of[3], (2, C, 4 * HID), C ** -0.5, 0.5),
        "gate_weight": gaussian(key_of[4], (2, C, C), C ** -0.5, 0.5),
        "gain_out": jnp.clip(1.0 + 0.1 * jax.random.normal(key_of[5], (2, HID), jnp.float32), 0.5, 1.5),
        "out_weight": gaussian(key_of[6], (2, HID, C), HID ** -0.5, 0.5),
        "trans_gain": jnp.clip(1.0 + 0.1 * jax.random.normal(key_of[7], (C,), jnp.float32), 0.5, 1.5),
        "trans_up": gaussian(key_of[8], (C, 2 * FFN), C ** -0.5, 0.5),
        "trans_down": gaussian(key_of[9], (FFN, C), FFN ** -0.5, 0.25),
    }


def layer_norm(values, gain):
    row_mean = lax.optimization_barrier(jnp.mean(values, axis=-1, keepdims=True))
    centred = values - row_mean
    spread = lax.optimization_barrier(jnp.mean(centred * centred, axis=-1, keepdims=True))
    return centred * lax.rsqrt(spread + 1e-05) * gain

def linear_map(values, weight):
    shape = values.shape
    flat = values.reshape(-1, shape[-1])
    result = jnp.dot(flat, weight, preferred_element_type=jnp.float32)
    return result.reshape(shape[:-1] + (weight.shape[1],))

def project(pair_map, pair_mask, gain, proj_weight, gate_weight):
    normed = layer_norm(pair_map, gain).astype(jnp.bfloat16)
    projected = linear_map(normed, proj_weight)
    width = proj_weight.shape[1] // 4
    keep_mask = pair_mask[..., None].astype(jnp.float32)
    left_act = (jax.nn.sigmoid(projected[..., :width]) * projected[..., width:2 * width] * keep_mask).astype(jnp.bfloat16)
    right_act = (jax.nn.sigmoid(projected[..., 2 * width:3 * width]) * projected[..., 3 * width:] * keep_mask).astype(jnp.bfloat16)
    gate_act = jax.nn.sigmoid(linear_map(normed, gate_weight))
    return (left_act, right_act, gate_act)

def finish(pair_map, combined, gate_act, gain, out_weight):
    hidden = layer_norm(combined, gain).astype(jnp.bfloat16)
    return pair_map + gate_act * linear_map(hidden, out_weight)

def reference(pair_map, pair_mask, gain_in, proj_weight, gate_weight, gain_out, out_weight, trans_gain, trans_up, trans_down):
    current = pair_map
    for update in range(2):
        left_act, right_act, gate_act = project(current, pair_mask, gain_in[update], proj_weight[update], gate_weight[update])
        left_full = left_act.astype(jnp.float32).transpose(2, 0, 1)
        right_full = right_act.astype(jnp.float32).transpose(2, 0, 1)
        if update == 0:
            combined = jnp.einsum('cik,cjk->cij', left_full, right_full, precision=lax.Precision.HIGHEST)
        else:
            combined = jnp.einsum('cki,ckj->cij', left_full, right_full, precision=lax.Precision.HIGHEST)
        combined = combined.transpose(1, 2, 0)
        current = finish(current, combined, gate_act, gain_out[update], out_weight[update])
    trans_in = layer_norm(current, trans_gain).astype(jnp.bfloat16)
    up_part = linear_map(trans_in, trans_up)
    trans_hidden = (jax.nn.silu(up_part[..., :FFN]) * up_part[..., FFN:]).astype(jnp.bfloat16)
    return current + linear_map(trans_hidden, trans_down)
```

```python
import jax
import jax.numpy as jnp
from jax import lax
from jax.sharding import PartitionSpec as P

AXES = ("row", "col")


def channel_norm(values, gain):
    mean = jnp.mean(values, axis=0, keepdims=True)
    centred = values - mean
    spread = jnp.mean(centred * centred, axis=0, keepdims=True)
    return centred * lax.rsqrt(spread + 1e-05) * gain[:, None]


def apply_weight(weight, values):
    return lax.dot_general(
        weight, values, (((0,), (0,)), ((), ())), preferred_element_type=jnp.float32
    )


def project(current, keep_mask, gain, proj_weight, gate_weight, devices):
    normed = channel_norm(current, gain).astype(jnp.bfloat16)
    projected = apply_weight(proj_weight, normed)
    width = proj_weight.shape[1] // 4
    tokens = current.shape[1]
    left_act = (jax.nn.sigmoid(projected[:width]) * projected[width : 2 * width] * keep_mask).astype(jnp.bfloat16)
    right_act = (
        jax.nn.sigmoid(projected[2 * width : 3 * width]) * projected[3 * width :] * keep_mask
    ).astype(jnp.bfloat16)
    share = width // devices
    both = jnp.stack(
        [left_act.reshape(devices, share, tokens), right_act.reshape(devices, share, tokens)], axis=1
    )
    return both, jax.nn.sigmoid(apply_weight(gate_weight, normed))


def combine(both, rows, cols, height, breadth, outgoing):
    share = both.shape[2]

    def whole(part):
        blocks = part.reshape(rows, cols, share, height, breadth)
        return blocks.transpose(2, 0, 3, 1, 4).reshape(share, rows * height, cols * breadth)

    left, right = whole(both[:, 0]), whole(both[:, 1])
    spec = "cik,cjk->cij" if outgoing else "cki,ckj->cij"
    combined = jnp.einsum(spec, left, right, preferred_element_type=jnp.float32).astype(jnp.bfloat16)
    combined = combined.reshape(share, rows, height, cols, breadth).transpose(1, 3, 0, 2, 4)
    return combined.reshape(rows * cols, share, height * breadth)


def exchange(values):
    return lax.all_to_all(values, AXES, split_axis=0, concat_axis=0, tiled=True)


def per_device(
    rows,
    cols,
    pair_map,
    pair_mask,
    gain_in,
    proj_weight,
    gate_weight,
    gain_out,
    out_weight,
    trans_gain,
    trans_up,
    trans_down,
):
    height, breadth, channels = pair_map.shape
    current = pair_map.reshape(height * breadth, channels).T
    keep_mask = pair_mask.reshape(1, height * breadth).astype(jnp.float32)
    for update in range(2):
        both, gate_act = project(
            current, keep_mask, gain_in[update], proj_weight[update], gate_weight[update], rows * cols
        )
        combined = exchange(combine(exchange(both), rows, cols, height, breadth, update == 0))
        combined = combined.reshape(-1, height * breadth).astype(jnp.float32)
        hidden = channel_norm(combined, gain_out[update]).astype(jnp.bfloat16)
        current = current + gate_act * apply_weight(out_weight[update], hidden)
    trans_in = channel_norm(current, trans_gain).astype(jnp.bfloat16)
    up_part = apply_weight(trans_up, trans_in)
    half = trans_down.shape[0]
    trans_hidden = (jax.nn.silu(up_part[:half]) * up_part[half:]).astype(jnp.bfloat16)
    result = current + apply_weight(trans_down, trans_hidden)
    return result.T.reshape(height, breadth, channels)


def solution(mesh):
    rows, cols = mesh.shape["row"], mesh.shape["col"]
    spread = P(("grp", "row"), "col", None)
    in_specs = (spread, P(("grp", "row"), "col")) + (P(),) * 8

    def body(*args):
        return per_device(rows, cols, *args)

    return jax.shard_map(body, mesh=mesh, in_specs=in_specs, out_specs=spread, check_vma=False)
```

```python
import functools

import jax
import jax.numpy as jnp
from jax import lax
from jax.experimental import pallas as pl
from jax.experimental.pallas import tpu as pltpu
from jax.sharding import PartitionSpec as P

AXES = ("row", "col")
LANES = 128
VMEM_BYTES = 48 * 1024 * 1024
F32, BF16 = jnp.float32, jnp.bfloat16


def dot(left, right, contract=(1, 0)):
    return lax.dot_general(
        left, right, (((contract[0],), (contract[1],)), ((), ())), preferred_element_type=F32
    )


def sigmoid(values):
    return 0.5 * jnp.tanh(0.5 * values) + 0.5


def spread_gain(row, lanes):
    tile = jnp.broadcast_to(row, (LANES, row.shape[1])).T
    return jnp.concatenate([tile] * (lanes // LANES), axis=1)


def channel_norm(values, gain):
    centred = values - jnp.mean(values, axis=0, keepdims=True)
    spread = jnp.mean(centred * centred, axis=0, keepdims=True)
    return (centred * lax.rsqrt(spread + 1e-05) * gain).astype(BF16)


def token_mask(mask, lines, slots):
    height, breadth = mask.shape
    wide = jnp.concatenate([mask.astype(F32)] * slots, axis=1)
    row = lax.broadcasted_iota(jnp.int32, wide.shape, 0)
    lane = lax.broadcasted_iota(jnp.int32, wide.shape, 1)
    wide = jnp.where(row % slots == lane // breadth, wide, 0.0).astype(BF16)
    line = lax.broadcasted_iota(jnp.int32, (lines, height), 0)
    source = lax.broadcasted_iota(jnp.int32, (lines, height), 1)
    return dot((source // slots == line).astype(BF16), wide)


def emit_message(normed, weight_t, mask, line, message_ref, stage_ref, share):
    projected = dot(weight_t, normed)
    hid = weight_t.shape[0] // 4
    owners = hid // share
    for part in range(normed.shape[1] // LANES):
        here = projected[:, part * LANES : (part + 1) * LANES]
        keep = mask[line + part : line + part + 1]
        left = sigmoid(here[:hid]) * here[hid : 2 * hid] * keep
        right = sigmoid(here[2 * hid : 3 * hid]) * here[3 * hid :] * keep
        at = line + part
        if share % 8 == 0:
            for owner in range(owners):
                rows = slice(owner * share, (owner + 1) * share)
                both = jnp.concatenate([left[rows], right[rows]], axis=0).astype(BF16)
                message_ref[owner, 2 * share * at : 2 * share * (at + 1), :] = both
        else:
            lines = message_ref.shape[1] // 2
            stage_ref[pl.ds(2 * at, owners, stride=2 * lines), :] = left
            stage_ref[pl.ds(2 * at + 1, owners, stride=2 * lines), :] = right
    if share % 8 and line + normed.shape[1] // LANES == mask.shape[0]:
        message_ref[...] = stage_ref[...].astype(BF16).reshape(message_ref.shape)


def project_kernel(update, share, chunk, x_ref, mask_ref, gain_ref, weight_ref, message_ref, normed_ref, stage_ref):
    tokens = x_ref.shape[0]
    lines = tokens // LANES
    mask = token_mask(mask_ref[...], lines, LANES // mask_ref.shape[1])
    gain = spread_gain(gain_ref[update : update + 1, :], chunk)
    weight_t = weight_ref[...].T
    for start in range(0, tokens, chunk):
        current = x_ref[start : start + chunk, :].T
        normed = channel_norm(current, gain)
        normed_ref[:, start : start + chunk] = normed
        emit_message(normed, weight_t, mask, start // LANES, message_ref, stage_ref, share)


def gate_kernel(normed_ref, weight_ref, gate_ref):
    gate_ref[...] = sigmoid(dot(weight_ref[...].T, normed_ref[...]))


def gate_turn_kernel(normed_ref, weight_ref, x_ref, gate_ref, turned_ref):
    gate_ref[...] = sigmoid(dot(weight_ref[...].T, normed_ref[...]))
    turned_ref[...] = x_ref[...].T


def swap_slots(parts, breadth):
    parts = list(parts)
    slot = lax.broadcasted_iota(jnp.int32, parts[0].shape, 1) // breadth
    step = 1
    while step < len(parts):
        low = (slot // step) % 2 == 0
        for first in range(len(parts)):
            if first & step:
                continue
            a, b = parts[first], parts[first | step]
            parts[first] = jnp.where(low, a, pltpu.roll(b, step * breadth, 1))
            parts[first | step] = jnp.where(low, pltpu.roll(a, LANES - step * breadth, 1), b)
        step *= 2
    return parts


def combine_kernel(rows, cols, breadth, share, outgoing, both_ref, combined_ref, stage_ref, result_ref):
    slots = LANES // breadth
    span = both_ref.shape[1]
    lines = span // (2 * share)
    height = lines * slots
    tokens = rows * height
    group = rows * lines
    stage_ref[...] = both_ref[...].astype(F32).reshape(stage_ref.shape)

    natural = lax.broadcasted_iota(jnp.int32, (tokens, tokens), 0)
    held = lax.broadcasted_iota(jnp.int32, (tokens, tokens), 1)
    if not outgoing:
        natural, held = held, natural
    inner = held % group
    target = inner // lines * height + inner % lines * slots + held // group
    order = (natural == target).astype(BF16)

    def whole(side, channel):
        columns = [[] for _ in range(slots)]
        for high in range(cols // slots):
            parts = []
            for low in range(slots):
                col = high * slots + low
                parts.append(
                    jnp.concatenate(
                        [
                            stage_ref[
                                pl.ds((row * cols + col) * span + side * share + channel, lines, stride=2 * share), :
                            ]
                            for row in range(rows)
                        ],
                        axis=0,
                    )
                )
            for slot, part in enumerate(swap_slots(parts, breadth)):
                columns[slot].append(part)
        return jnp.concatenate([jnp.concatenate(column, axis=1) for column in columns], axis=0).astype(BF16)

    for channel in range(share):
        left, right = whole(0, channel), whole(1, channel)
        if outgoing:
            combined = dot(left, dot(order, right).astype(BF16), (1, 1))
        else:
            combined = dot(dot(order, left, (1, 1)).astype(BF16), right)
        for high in range(cols // slots):
            parts = [
                combined[slot * group : (slot + 1) * group, high * LANES : (high + 1) * LANES]
                for slot in range(slots)
            ]
            for low, part in enumerate(swap_slots(parts, breadth)):
                for row in range(rows):
                    base = (row * cols + high * slots + low) * lines * share + channel
                    result_ref[pl.ds(base, lines, stride=share), :] = part[row * lines : (row + 1) * lines]
    combined_ref[...] = result_ref[...].astype(BF16).reshape(combined_ref.shape)


def read_combined(stage_ref, owners, lines, share, first, count):
    columns = []
    for line in range(first, first + count):
        if share % 8 == 0:
            columns.append(
                jnp.concatenate(
                    [
                        stage_ref[(owner * lines + line) * share : (owner * lines + line + 1) * share, :]
                        for owner in range(owners)
                    ],
                    axis=0,
                )
            )
        else:
            columns.append(stage_ref[pl.ds(line, owners, stride=lines), :])
    return jnp.concatenate(columns, axis=1)


def middle_kernel(
    share,
    chunk,
    combined_ref,
    x_ref,
    gate_ref,
    gain_out_ref,
    out_weight_ref,
    mask_ref,
    gain_ref,
    weight_ref,
    message_ref,
    normed_ref,
    next_ref,
    stage_ref,
    message_stage_ref,
):
    tokens = x_ref.shape[1]
    lines = tokens // LANES
    owners = combined_ref.shape[0]
    stage_ref[...] = combined_ref[...].astype(F32).reshape(stage_ref.shape)
    mask = token_mask(mask_ref[...], lines, LANES // mask_ref.shape[1])
    gain_out = spread_gain(gain_out_ref[0:1, :], chunk)
    gain = spread_gain(gain_ref[1:2, :], chunk)
    out_t, weight_t = out_weight_ref[...].T, weight_ref[...].T
    for start in range(0, tokens, chunk):
        here = slice(start, start + chunk)
        combined = read_combined(stage_ref, owners, lines, share, start // LANES, chunk // LANES)
        hidden = channel_norm(combined, gain_out)
        current = x_ref[:, here] + gate_ref[:, here] * dot(out_t, hidden)
        next_ref[:, here] = current
        normed = channel_norm(current, gain)
        normed_ref[:, here] = normed
        emit_message(normed, weight_t, mask, start // LANES, message_ref, message_stage_ref, share)


def last_kernel(
    share,
    chunk,
    combined_ref,
    x_ref,
    gate_ref,
    gain_out_ref,
    out_weight_ref,
    gain_ref,
    up_ref,
    down_ref,
    result_ref,
    stage_ref,
):
    tokens = x_ref.shape[1]
    lines = tokens // LANES
    owners = combined_ref.shape[0]
    stage_ref[...] = combined_ref[...].astype(F32).reshape(stage_ref.shape)
    gain_out = spread_gain(gain_out_ref[1:2, :], chunk)
    gain = spread_gain(gain_ref[...], chunk)
    out_t, up_t, down_t = out_weight_ref[...].T, up_ref[...].T, down_ref[...].T
    half = down_t.shape[1]
    for start in range(0, tokens, chunk):
        here = slice(start, start + chunk)
        combined = read_combined(stage_ref, owners, lines, share, start // LANES, chunk // LANES)
        hidden = channel_norm(combined, gain_out)
        current = x_ref[:, here] + gate_ref[:, here] * dot(out_t, hidden)
        up_part = dot(up_t, channel_norm(current, gain))
        first = up_part[:half]
        trans_hidden = (first * sigmoid(first) * up_part[half:]).astype(BF16)
        result_ref[here, :] = (current + dot(down_t, trans_hidden)).T


def whole_spec(array):
    return pl.BlockSpec(array.shape, lambda step, dims=array.ndim: (0,) * dims)


def picked_spec(array, index):
    return pl.BlockSpec((None,) + array.shape[1:], lambda step: (index,) + (0,) * (array.ndim - 1))


def call(kernel, operands, picks, outs, scratch=()):
    specs = [
        picked_spec(array, picks[n]) if n in picks else whole_spec(array) for n, array in enumerate(operands)
    ]
    shapes = [jax.ShapeDtypeStruct(shape, dtype) for shape, dtype in outs]
    return pl.pallas_call(
        kernel,
        grid=(1,),
        in_specs=specs,
        out_specs=[whole_spec(shape) for shape in shapes],
        out_shape=shapes,
        scratch_shapes=[pltpu.VMEM(shape, F32) for shape in scratch],
        compiler_params=pltpu.CompilerParams(vmem_limit_bytes=VMEM_BYTES),
    )(*operands)


def exchange(values):
    return lax.all_to_all(values, AXES, split_axis=0, concat_axis=0, tiled=True)


def per_device(
    rows,
    cols,
    pair_map,
    pair_mask,
    gain_in,
    proj_weight,
    gate_weight,
    gain_out,
    out_weight,
    trans_gain,
    trans_up,
    trans_down,
):
    height, breadth, channels = pair_map.shape
    tokens = height * breadth
    lines = tokens // LANES
    hid = gain_out.shape[1]
    owners = rows * cols
    share = hid // owners
    chunk = min(2 * LANES, tokens)
    message = ((owners, 2 * share * lines, LANES), BF16)
    answer = ((owners, share * lines, LANES), BF16)
    staged = (owners * 2 * share * lines, LANES)
    result = (owners * share * lines, LANES)
    spare = (8, LANES) if share % 8 == 0 else staged
    flat = pair_map.reshape(tokens, channels)

    def combine(both, outgoing):
        (combined,) = call(
            functools.partial(combine_kernel, rows, cols, breadth, share, outgoing),
            (both,),
            {},
            [answer],
            (staged, result),
        )
        return combined

    both, normed = call(
        functools.partial(project_kernel, 0, share, chunk),
        (flat, pair_mask, gain_in, proj_weight),
        {3: 0},
        [message, ((channels, tokens), BF16)],
        (spare,),
    )
    both = exchange(both)
    gate, current = call(
        gate_turn_kernel,
        (normed, gate_weight, flat),
        {1: 0},
        [((channels, tokens), F32), ((channels, tokens), F32)],
    )
    combined = exchange(combine(both, True))
    both, normed, current = call(
        functools.partial(middle_kernel, share, chunk),
        (combined, current, gate, gain_out, out_weight, pair_mask, gain_in, proj_weight),
        {4: 0, 7: 1},
        [message, ((channels, tokens), BF16), ((channels, tokens), F32)],
        (result, spare),
    )
    both = exchange(both)
    (gate,) = call(gate_kernel, (normed, gate_weight), {1: 1}, [((channels, tokens), F32)])
    combined = exchange(combine(both, False))
    (pair_out,) = call(
        functools.partial(last_kernel, share, chunk),
        (combined, current, gate, gain_out, out_weight, trans_gain.reshape(1, -1), trans_up, trans_down),
        {4: 1},
        [((tokens, channels), F32)],
        (result,),
    )
    return pair_out.reshape(height, breadth, channels)


def solution(mesh):
    rows, cols = mesh.shape["row"], mesh.shape["col"]
    spread = P(("grp", "row"), "col", None)
    in_specs = (spread, P(("grp", "row"), "col")) + (P(),) * 8

    def body(*args):
        return per_device(rows, cols, *args)

    return jax.shard_map(body, mesh=mesh, in_specs=in_specs, out_specs=spread, check_vma=False)
```

```python
import functools

import jax
import jax.numpy as jnp
from jax import lax
from jax.experimental import pallas as pl
from jax.experimental.pallas import tpu as pltpu
from jax.sharding import PartitionSpec as P

AXES = ("row", "col")
LANES = 128
VMEM_BYTES = 48 * 1024 * 1024
F32, BF16 = jnp.float32, jnp.bfloat16


def dot(left, right, contract=(1, 0)):
    return lax.dot_general(
        left, right, (((contract[0],), (contract[1],)), ((), ())), preferred_element_type=F32
    )


def sigmoid(values):
    return 0.5 * jnp.tanh(0.5 * values) + 0.5


def spread_gain(row, lanes):
    tile = jnp.broadcast_to(row, (LANES, row.shape[1])).T
    return jnp.concatenate([tile] * (lanes // LANES), axis=1)


def channel_norm(values, gain):
    centred = values - jnp.mean(values, axis=0, keepdims=True)
    spread = jnp.mean(centred * centred, axis=0, keepdims=True)
    return (centred * lax.rsqrt(spread + 1e-05) * gain).astype(BF16)


def token_mask(mask, lines, slots):
    height, breadth = mask.shape
    wide = jnp.concatenate([mask.astype(F32)] * slots, axis=1)
    row = lax.broadcasted_iota(jnp.int32, wide.shape, 0)
    lane = lax.broadcasted_iota(jnp.int32, wide.shape, 1)
    wide = jnp.where(row % slots == lane // breadth, wide, 0.0).astype(BF16)
    line = lax.broadcasted_iota(jnp.int32, (lines, height), 0)
    source = lax.broadcasted_iota(jnp.int32, (lines, height), 1)
    return dot((source // slots == line).astype(BF16), wide)


def pairwise(rows, cols, share):
    owners = rows * cols
    return owners <= 16 and owners & (owners - 1) == 0 and share % 8 == 0


def partners(cols, refs, owners):
    if len(refs) == 1:
        return [(refs[0].at[n], n) for n in range(owners)]
    own = lax.axis_index("row") * cols + lax.axis_index("col")
    return [(ref, jnp.bitwise_xor(own, n)) for n, ref in enumerate(refs)]


def project_act(normed, weight_t, mask, line, act_ref):
    projected = dot(weight_t, normed)
    hid = weight_t.shape[0] // 4
    for part in range(normed.shape[1] // LANES):
        here = projected[:, part * LANES : (part + 1) * LANES]
        keep = mask[line + part : line + part + 1]
        lanes = slice((line + part) * LANES, (line + part + 1) * LANES)
        act_ref[:hid, lanes] = sigmoid(here[:hid]) * here[hid : 2 * hid] * keep
        act_ref[hid:, lanes] = sigmoid(here[2 * hid : 3 * hid]) * here[3 * hid :] * keep


def emit_messages(cols, share, act_ref, message_refs):
    hid = act_ref.shape[0] // 2
    lines = act_ref.shape[1] // LANES
    for block_ref, owner in partners(cols, message_refs, hid // share):
        slabs = [
            act_ref[pl.ds(side * hid + owner * share, share), line * LANES : (line + 1) * LANES]
            for line in range(lines)
            for side in range(2)
        ]
        block_ref[...] = jnp.concatenate(slabs, axis=0).astype(BF16)


def gather_blocks(cols, refs, owners, stage_ref):
    for block_ref, owner in partners(cols, refs, owners):
        span = block_ref.shape[0]
        stage_ref[pl.ds(pl.multiple_of(owner * span, span), span), :] = block_ref[...].astype(F32)


def project_kernel(update, cols, share, chunk, ins, outs, act_ref):
    x_ref, mask_ref, gain_ref, weight_ref = ins
    normed_ref, *message_refs = outs
    tokens = x_ref.shape[0]
    mask = token_mask(mask_ref[...], tokens // LANES, LANES // mask_ref.shape[1])
    gain = spread_gain(gain_ref[update : update + 1, :], chunk)
    weight_t = weight_ref[...].T
    for start in range(0, tokens, chunk):
        normed = channel_norm(x_ref[start : start + chunk, :].T, gain)
        normed_ref[:, start : start + chunk] = normed
        project_act(normed, weight_t, mask, start // LANES, act_ref)
    emit_messages(cols, share, act_ref, message_refs)


def gate_kernel(ins, outs):
    normed_ref, weight_ref = ins
    outs[0][...] = sigmoid(dot(weight_ref[...].T, normed_ref[...]))


def gate_turn_kernel(ins, outs):
    normed_ref, weight_ref, x_ref = ins
    gate_ref, turned_ref = outs
    gate_ref[...] = sigmoid(dot(weight_ref[...].T, normed_ref[...]))
    turned_ref[...] = x_ref[...].T


def swap_slots(parts, breadth):
    parts = list(parts)
    slot = lax.broadcasted_iota(jnp.int32, parts[0].shape, 1) // breadth
    step = 1
    while step < len(parts):
        low = (slot // step) % 2 == 0
        for first in range(len(parts)):
            if first & step:
                continue
            a, b = parts[first], parts[first | step]
            parts[first] = jnp.where(low, a, pltpu.roll(b, step * breadth, 1))
            parts[first | step] = jnp.where(low, pltpu.roll(a, LANES - step * breadth, 1), b)
        step *= 2
    return parts


def combine_kernel(rows, cols, breadth, share, outgoing, ins, outs, stage_ref, result_ref):
    slots = LANES // breadth
    span = stage_ref.shape[0] // (rows * cols)
    lines = span // (2 * share)
    height = lines * slots
    tokens = rows * height
    group = rows * lines
    gather_blocks(cols, ins, rows * cols, stage_ref)

    natural = lax.broadcasted_iota(jnp.int32, (tokens, tokens), 0)
    held = lax.broadcasted_iota(jnp.int32, (tokens, tokens), 1)
    if not outgoing:
        natural, held = held, natural
    inner = held % group
    target = inner // lines * height + inner % lines * slots + held // group
    order = (natural == target).astype(BF16)

    def whole(side, channel):
        columns = [[] for _ in range(slots)]
        for high in range(cols // slots):
            parts = []
            for low in range(slots):
                col = high * slots + low
                parts.append(
                    jnp.concatenate(
                        [
                            stage_ref[
                                pl.ds((row * cols + col) * span + side * share + channel, lines, stride=2 * share), :
                            ]
                            for row in range(rows)
                        ],
                        axis=0,
                    )
                )
            for slot, part in enumerate(swap_slots(parts, breadth)):
                columns[slot].append(part)
        return jnp.concatenate([jnp.concatenate(column, axis=1) for column in columns], axis=0).astype(BF16)

    for channel in range(share):
        left, right = whole(0, channel), whole(1, channel)
        if outgoing:
            combined = dot(left, dot(order, right).astype(BF16), (1, 1))
        else:
            combined = dot(dot(order, left, (1, 1)).astype(BF16), right)
        for high in range(cols // slots):
            parts = [
                combined[slot * group : (slot + 1) * group, high * LANES : (high + 1) * LANES]
                for slot in range(slots)
            ]
            for low, part in enumerate(swap_slots(parts, breadth)):
                for row in range(rows):
                    base = (row * cols + high * slots + low) * lines * share + channel
                    result_ref[pl.ds(base, lines, stride=share), :] = part[row * lines : (row + 1) * lines]
    for block_ref, owner in partners(cols, outs, rows * cols):
        span = block_ref.shape[0]
        block_ref[...] = result_ref[pl.ds(pl.multiple_of(owner * span, span), span), :].astype(BF16)


def read_combined(stage_ref, owners, lines, share, first, count):
    columns = []
    for line in range(first, first + count):
        if share % 8 == 0:
            columns.append(
                jnp.concatenate(
                    [
                        stage_ref[(owner * lines + line) * share : (owner * lines + line + 1) * share, :]
                        for owner in range(owners)
                    ],
                    axis=0,
                )
            )
        else:
            columns.append(stage_ref[pl.ds(line, owners, stride=lines), :])
    return jnp.concatenate(columns, axis=1)


def middle_kernel(cols, share, chunk, ins, outs, stage_ref, act_ref):
    x_ref, gate_ref, gain_out_ref, out_weight_ref, mask_ref, gain_ref, weight_ref, *combined_refs = ins
    normed_ref, next_ref, *message_refs = outs
    tokens = x_ref.shape[1]
    lines = tokens // LANES
    owners = x_ref.shape[0] // share
    gather_blocks(cols, combined_refs, owners, stage_ref)
    mask = token_mask(mask_ref[...], lines, LANES // mask_ref.shape[1])
    gain_out = spread_gain(gain_out_ref[0:1, :], chunk)
    gain = spread_gain(gain_ref[1:2, :], chunk)
    out_t, weight_t = out_weight_ref[...].T, weight_ref[...].T
    for start in range(0, tokens, chunk):
        here = slice(start, start + chunk)
        combined = read_combined(stage_ref, owners, lines, share, start // LANES, chunk // LANES)
        hidden = channel_norm(combined, gain_out)
        current = x_ref[:, here] + gate_ref[:, here] * dot(out_t, hidden)
        next_ref[:, here] = current
        normed = channel_norm(current, gain)
        normed_ref[:, here] = normed
        project_act(normed, weight_t, mask, start // LANES, act_ref)
    emit_messages(cols, share, act_ref, message_refs)


def last_kernel(cols, share, chunk, ins, outs, stage_ref):
    x_ref, gate_ref, gain_out_ref, out_weight_ref, gain_ref, up_ref, down_ref, *combined_refs = ins
    (result_ref,) = outs
    tokens = x_ref.shape[1]
    lines = tokens // LANES
    owners = x_ref.shape[0] // share
    gather_blocks(cols, combined_refs, owners, stage_ref)
    gain_out = spread_gain(gain_out_ref[1:2, :], chunk)
    gain = spread_gain(gain_ref[...], chunk)
    out_t, up_t, down_t = out_weight_ref[...].T, up_ref[...].T, down_ref[...].T
    half = down_t.shape[1]
    for start in range(0, tokens, chunk):
        here = slice(start, start + chunk)
        combined = read_combined(stage_ref, owners, lines, share, start // LANES, chunk // LANES)
        hidden = channel_norm(combined, gain_out)
        current = x_ref[:, here] + gate_ref[:, here] * dot(out_t, hidden)
        up_part = dot(up_t, channel_norm(current, gain))
        first = up_part[:half]
        trans_hidden = (first * sigmoid(first) * up_part[half:]).astype(BF16)
        result_ref[here, :] = (current + dot(down_t, trans_hidden)).T


def whole_spec(array):
    return pl.BlockSpec(array.shape, lambda step, dims=array.ndim: (0,) * dims)


def picked_spec(array, index):
    return pl.BlockSpec((None,) + array.shape[1:], lambda step: (index,) + (0,) * (array.ndim - 1))


def call(kernel, operands, picks, outs, scratch=()):
    specs = [
        picked_spec(array, picks[n]) if n in picks else whole_spec(array) for n, array in enumerate(operands)
    ]
    shapes = [jax.ShapeDtypeStruct(shape, dtype) for shape, dtype in outs]
    count = len(operands)

    def body(*refs):
        kernel(refs[:count], refs[count : count + len(outs)], *refs[count + len(outs) :])

    return pl.pallas_call(
        body,
        grid=(1,),
        in_specs=specs,
        out_specs=[whole_spec(shape) for shape in shapes],
        out_shape=shapes,
        scratch_shapes=[pltpu.VMEM(shape, F32) for shape in scratch],
        compiler_params=pltpu.CompilerParams(vmem_limit_bytes=VMEM_BYTES),
    )(*operands)


def exchange(cols, blocks):
    if len(blocks) == 1:
        return [lax.all_to_all(blocks[0], AXES, split_axis=0, concat_axis=0, tiled=True)]
    owners = len(blocks)
    received = list(blocks)
    for n in sorted(range(1, owners), key=lambda n: (-(n % cols), n)):
        received[n] = lax.ppermute(blocks[n], AXES, [(device, device ^ n) for device in range(owners)])
    return received


def per_device(
    rows,
    cols,
    pair_map,
    pair_mask,
    gain_in,
    proj_weight,
    gate_weight,
    gain_out,
    out_weight,
    trans_gain,
    trans_up,
    trans_down,
):
    height, breadth, channels = pair_map.shape
    tokens = height * breadth
    lines = tokens // LANES
    hid = gain_out.shape[1]
    owners = rows * cols
    share = hid // owners
    chunk = min(2 * LANES, tokens)
    flat = pair_map.reshape(tokens, channels)
    act = (2 * hid, tokens)
    staged = (owners * 2 * share * lines, LANES)
    result = (owners * share * lines, LANES)
    narrow, wide = ((channels, tokens), BF16), ((channels, tokens), F32)

    def blocks(span):
        if pairwise(rows, cols, share):
            return [((span, LANES), BF16)] * owners
        return [((owners, span, LANES), BF16)]

    messages, answers = blocks(2 * share * lines), blocks(share * lines)

    def combine(both, outgoing):
        kernel = functools.partial(combine_kernel, rows, cols, breadth, share, outgoing)
        return exchange(cols, call(kernel, both, {}, answers, (staged, result)))

    normed, *both = call(
        functools.partial(project_kernel, 0, cols, share, chunk),
        (flat, pair_mask, gain_in, proj_weight),
        {3: 0},
        [narrow] + messages,
        (act,),
    )
    both = exchange(cols, both)
    gate, current = call(gate_turn_kernel, (normed, gate_weight, flat), {1: 0}, [wide, wide])
    combined = combine(both, True)
    normed, current, *both = call(
        functools.partial(middle_kernel, cols, share, chunk),
        (current, gate, gain_out, out_weight, pair_mask, gain_in, proj_weight, *combined),
        {3: 0, 6: 1},
        [narrow, wide] + messages,
        (result, act),
    )
    both = exchange(cols, both)
    (gate,) = call(gate_kernel, (normed, gate_weight), {1: 1}, [wide])
    combined = combine(both, False)
    (pair_out,) = call(
        functools.partial(last_kernel, cols, share, chunk),
        (current, gate, gain_out, out_weight, trans_gain.reshape(1, -1), trans_up, trans_down, *combined),
        {3: 1},
        [((tokens, channels), F32)],
        (result,),
    )
    return pair_out.reshape(height, breadth, channels)


def solution(mesh):
    rows, cols = mesh.shape["row"], mesh.shape["col"]
    spread = P(("grp", "row"), "col", None)
    in_specs = (spread, P(("grp", "row"), "col")) + (P(),) * 8

    def body(*args):
        return per_device(rows, cols, *args)

    return jax.shard_map(body, mesh=mesh, in_specs=in_specs, out_specs=spread, check_vma=False)
```

```python
import functools

import jax
import jax.numpy as jnp
from jax import lax
from jax.experimental import pallas as pl
from jax.experimental.pallas import tpu as pltpu
from jax.sharding import PartitionSpec as P

AXES = ("row", "col")
LANES = 128
VMEM_BYTES = 48 * 1024 * 1024
FULL_VMEM_BYTES = 60 * 1024 * 1024
F32, BF16 = jnp.float32, jnp.bfloat16


def dot(left, right, contract=(1, 0)):
    return lax.dot_general(
        left, right, (((contract[0],), (contract[1],)), ((), ())), preferred_element_type=F32
    )


def sigmoid(values):
    return 0.5 * jnp.tanh(0.5 * values) + 0.5


def channel_norm(values, gain):
    wide = jnp.concatenate([gain] * (values.shape[1] // LANES), axis=1)
    centred = values - jnp.mean(values, axis=0, keepdims=True)
    spread = jnp.mean(centred * centred, axis=0, keepdims=True)
    return (centred * lax.rsqrt(spread + 1e-05) * wide).astype(BF16)


def spread_gain(row):
    return jnp.broadcast_to(row, (LANES, row.shape[1])).T


def token_mask(mask, lines):
    height, breadth = mask.shape
    wide = jnp.concatenate([mask.astype(F32)] * (LANES // breadth), axis=1)
    row = lax.broadcasted_iota(jnp.int32, wide.shape, 0)
    lane = lax.broadcasted_iota(jnp.int32, wide.shape, 1)
    wide = jnp.where(row // lines == lane // breadth, wide, 0.0).astype(BF16)
    line = lax.broadcasted_iota(jnp.int32, (lines, height), 0)
    source = lax.broadcasted_iota(jnp.int32, (lines, height), 1)
    return dot((source % lines == line).astype(BF16), wide)


def emit_message(normed, weight_t, mask, line, message_ref, stage_ref, share):
    projected = dot(weight_t, normed)
    hid = weight_t.shape[0] // 4
    owners = hid // share
    for part in range(normed.shape[1] // LANES):
        here = projected[:, part * LANES : (part + 1) * LANES]
        at = line + part
        keep = mask[at : at + 1]
        left = sigmoid(here[:hid]) * here[hid : 2 * hid] * keep
        right = sigmoid(here[2 * hid : 3 * hid]) * here[3 * hid :] * keep
        if share % 8 == 0:
            for owner in range(owners):
                rows = slice(owner * share, (owner + 1) * share)
                both = jnp.concatenate([left[rows], right[rows]], axis=0).astype(BF16)
                message_ref[owner, 2 * share * at : 2 * share * (at + 1), :] = both
        else:
            lines = message_ref.shape[1] // 2
            stage_ref[pl.ds(2 * at, owners, stride=2 * lines), :] = left
            stage_ref[pl.ds(2 * at + 1, owners, stride=2 * lines), :] = right
    if share % 8 and line + normed.shape[1] // LANES == mask.shape[0]:
        message_ref[...] = stage_ref[...].astype(BF16).reshape(message_ref.shape)


def project_kernel(share, chunk, ins, outs, stage_ref, x_ref, mask_ref, gain_ref, weight_ref, sems):
    message_ref, normed_ref, turned_ref, lines_ref = outs
    x_in, mask_in, gain_in, weight_in = ins
    pairs = [(gain_in, gain_ref), (mask_in, mask_ref), (weight_in.at[0], weight_ref), (x_in, x_ref)]
    copies = [pltpu.make_async_copy(src, dst, sems.at[n]) for n, (src, dst) in enumerate(pairs)]
    for copy in copies:
        copy.start()
    height, breadth, channels = x_ref.shape
    tokens = height * breadth
    lines = tokens // LANES
    copies[0].wait()
    copies[1].wait()
    mask = token_mask(mask_ref[...], lines)
    lines_ref[...] = mask
    gain = spread_gain(gain_ref[0:1, :])
    copies[2].wait()
    weight_t = weight_ref[...].T
    copies[3].wait()
    for start in range(0, tokens, chunk):
        first = start // LANES
        held = [
            x_ref[slot * lines + line]
            for line in range(first, first + chunk // LANES)
            for slot in range(LANES // breadth)
        ]
        current = jnp.concatenate(held, axis=0).T
        turned_ref[:, start : start + chunk] = current
        normed = channel_norm(current, gain)
        normed_ref[:, start : start + chunk] = normed
        emit_message(normed, weight_t, mask, first, message_ref, stage_ref, share)


def prepare_kernel(ins, outs):
    normed_ref, gate_ref, proj_ref, out_ref, up_ref, down_ref, gain_in_ref, gain_out_ref, trans_gain_ref = ins
    gate_out, proj_out, out_out, up_out, down_out, gains_out = outs
    gate_out[...] = sigmoid(dot(gate_ref[...].T, normed_ref[...]))
    proj_out[...] = proj_ref[...].T
    for update in range(2):
        out_out[update] = out_ref[update].T
    up_out[...] = up_ref[...].T
    down_out[...] = down_ref[...].T
    rows = [gain_out_ref[0:1, :], gain_in_ref[1:2, :], gain_out_ref[1:2, :], trans_gain_ref[...]]
    for n, row in enumerate(rows):
        gains_out[n] = spread_gain(row)


def gate_kernel(ins, outs):
    normed_ref, weight_ref = ins
    outs[0][...] = sigmoid(dot(weight_ref[...].T, normed_ref[...]))


def swap_slots(parts, breadth):
    parts = list(parts)
    slot = lax.broadcasted_iota(jnp.int32, parts[0].shape, 1) // breadth
    step = 1
    while step < len(parts):
        low = (slot // step) % 2 == 0
        for first in range(len(parts)):
            if first & step:
                continue
            a, b = parts[first], parts[first | step]
            parts[first] = jnp.where(low, a, pltpu.roll(b, step * breadth, 1))
            parts[first | step] = jnp.where(low, pltpu.roll(a, LANES - step * breadth, 1), b)
        step *= 2
    return parts


def combine_kernel(rows, cols, breadth, share, outgoing, ins, outs, stage_ref, result_ref):
    (both_ref,), (combined_ref,) = ins, outs
    slots = LANES // breadth
    span = both_ref.shape[1]
    lines = span // (2 * share)
    stage_ref[...] = both_ref[...].astype(F32).reshape(stage_ref.shape)

    def whole(side, channel):
        columns = []
        for high in range(cols // slots):
            parts = []
            for low in range(slots):
                base = (high * slots + low) * span + side * share + channel
                held = [
                    stage_ref[pl.ds(row * cols * span + base, lines, stride=2 * share), :] for row in range(rows)
                ]
                parts.append(jnp.concatenate(held, axis=0))
            parts = swap_slots(parts, breadth)
            columns.append(
                jnp.concatenate(
                    [part[row * lines : (row + 1) * lines] for row in range(rows) for part in parts], axis=0
                )
            )
        return jnp.concatenate(columns, axis=1).astype(BF16)

    for channel in range(share):
        left, right = whole(0, channel), whole(1, channel)
        combined = dot(left, right, (1, 1) if outgoing else (0, 0))
        for high in range(cols // slots):
            lanes = slice(high * LANES, (high + 1) * LANES)
            parts = [
                jnp.concatenate(
                    [
                        combined[(row * slots + slot) * lines : (row * slots + slot + 1) * lines, lanes]
                        for row in range(rows)
                    ],
                    axis=0,
                )
                for slot in range(slots)
            ]
            for low, part in enumerate(swap_slots(parts, breadth)):
                for row in range(rows):
                    base = (row * cols + high * slots + low) * lines * share + channel
                    result_ref[pl.ds(base, lines, stride=share), :] = part[row * lines : (row + 1) * lines]
    combined_ref[...] = result_ref[...].astype(BF16).reshape(combined_ref.shape)


def read_combined(stage_ref, owners, lines, share, first, count):
    columns = []
    for line in range(first, first + count):
        if share % 8 == 0:
            held = [
                stage_ref[(owner * lines + line) * share : (owner * lines + line + 1) * share, :]
                for owner in range(owners)
            ]
            columns.append(jnp.concatenate(held, axis=0))
        else:
            columns.append(stage_ref[pl.ds(line, owners, stride=lines), :])
    return jnp.concatenate(columns, axis=1)


def middle_kernel(share, chunk, ins, outs, stage_ref, message_stage_ref):
    combined_ref, x_ref, gate_ref, gains_ref, out_ref, mask_ref, weight_ref = ins
    message_ref, normed_ref, next_ref = outs
    tokens = x_ref.shape[1]
    lines = tokens // LANES
    owners = combined_ref.shape[0]
    stage_ref[...] = combined_ref[...].astype(F32).reshape(stage_ref.shape)
    mask = mask_ref[...]
    for start in range(0, tokens, chunk):
        here = slice(start, start + chunk)
        combined = read_combined(stage_ref, owners, lines, share, start // LANES, chunk // LANES)
        hidden = channel_norm(combined, gains_ref[0])
        current = x_ref[:, here] + gate_ref[:, here] * dot(out_ref[0], hidden)
        next_ref[:, here] = current
        normed = channel_norm(current, gains_ref[1])
        normed_ref[:, here] = normed
        emit_message(normed, weight_ref[...], mask, start // LANES, message_ref, message_stage_ref, share)


def last_kernel(share, chunk, ins, outs, stage_ref):
    combined_ref, x_ref, gate_ref, gains_ref, out_ref, up_ref, down_ref = ins
    (result_ref,) = outs
    height, breadth, channels = result_ref.shape
    tokens = x_ref.shape[1]
    lines = tokens // LANES
    owners = combined_ref.shape[0]
    half = down_ref.shape[1]
    stage_ref[...] = combined_ref[...].astype(F32).reshape(stage_ref.shape)
    for start in range(0, tokens, chunk):
        here = slice(start, start + chunk)
        combined = read_combined(stage_ref, owners, lines, share, start // LANES, chunk // LANES)
        hidden = channel_norm(combined, gains_ref[2])
        current = x_ref[:, here] + gate_ref[:, here] * dot(out_ref[1], hidden)
        up_part = dot(up_ref[...], channel_norm(current, gains_ref[3]))
        first = up_part[:half]
        trans_hidden = (first * sigmoid(first) * up_part[half:]).astype(BF16)
        result = (current + dot(down_ref[...], trans_hidden)).T
        for part in range(chunk // LANES):
            for slot in range(LANES // breadth):
                base = part * LANES + slot * breadth
                result_ref[slot * lines + start // LANES + part] = result[base : base + breadth]


def whole_spec(array):
    return pl.BlockSpec(array.shape, lambda step, dims=array.ndim: (0,) * dims)


def picked_spec(array, index):
    return pl.BlockSpec((None,) + array.shape[1:], lambda step: (index,) + (0,) * (array.ndim - 1))


def call(kernel, operands, picks, outs, scratch=(), in_place=False):
    limit = FULL_VMEM_BYTES if in_place else VMEM_BYTES
    specs = [
        picked_spec(array, picks[n]) if n in picks else whole_spec(array) for n, array in enumerate(operands)
    ]
    if in_place:
        specs = [pl.BlockSpec(memory_space=pltpu.HBM)] * len(operands)
    shapes = [jax.ShapeDtypeStruct(shape, dtype) for shape, dtype in outs]
    count = len(operands)

    def body(*refs):
        kernel(refs[:count], refs[count : count + len(outs)], *refs[count + len(outs) :])

    return pl.pallas_call(
        body,
        grid=(1,),
        in_specs=specs,
        out_specs=[whole_spec(shape) for shape in shapes],
        out_shape=shapes,
        scratch_shapes=list(scratch),
        compiler_params=pltpu.CompilerParams(vmem_limit_bytes=limit),
    )(*operands)


def exchange(values):
    return lax.all_to_all(values, AXES, split_axis=0, concat_axis=0, tiled=True)


def per_device(
    rows,
    cols,
    pair_map,
    pair_mask,
    gain_in,
    proj_weight,
    gate_weight,
    gain_out,
    out_weight,
    trans_gain,
    trans_up,
    trans_down,
):
    height, breadth, channels = pair_map.shape
    tokens = height * breadth
    lines = tokens // LANES
    hid = gain_out.shape[1]
    owners = rows * cols
    share = hid // owners
    chunk = min(2 * LANES, tokens)
    message = ((owners, 2 * share * lines, LANES), BF16)
    answer = ((owners, share * lines, LANES), BF16)
    staged = pltpu.VMEM((owners * 2 * share * lines, LANES), F32)
    result = pltpu.VMEM((owners * share * lines, LANES), F32)
    spare = pltpu.VMEM((8, LANES), F32) if share % 8 == 0 else staged
    narrow, wide = ((channels, tokens), BF16), ((channels, tokens), F32)

    def combine(both, outgoing):
        kernel = functools.partial(combine_kernel, rows, cols, breadth, share, outgoing)
        (combined,) = call(kernel, (both,), {}, [answer], (staged, result))
        return combined

    both, normed, current, mask = call(
        functools.partial(project_kernel, share, chunk),
        (pair_map, pair_mask, gain_in, proj_weight),
        {},
        [message, narrow, wide, ((lines, LANES), F32)],
        (
            spare,
            pltpu.VMEM(pair_map.shape, F32),
            pltpu.VMEM(pair_mask.shape, jnp.int32),
            pltpu.VMEM(gain_in.shape, F32),
            pltpu.VMEM(proj_weight.shape[1:], BF16),
            pltpu.SemaphoreType.DMA((4,)),
        ),
        in_place=True,
    )
    gate, proj_t, out_t, up_t, down_t, gains = call(
        prepare_kernel,
        (
            normed,
            gate_weight,
            proj_weight,
            out_weight,
            trans_up,
            trans_down,
            gain_in,
            gain_out,
            trans_gain.reshape(1, -1),
        ),
        {1: 0, 2: 1},
        [
            wide,
            (proj_weight.shape[:0:-1], BF16),
            ((2, out_weight.shape[2], hid), BF16),
            (trans_up.shape[::-1], BF16),
            (trans_down.shape[::-1], BF16),
            ((4, channels, LANES), F32),
        ],
    )
    combined = exchange(combine(exchange(both), True))
    both, normed, current = call(
        functools.partial(middle_kernel, share, chunk),
        (combined, current, gate, gains, out_t, mask, proj_t),
        {},
        [message, narrow, wide],
        (result, spare),
    )
    (gate,) = call(gate_kernel, (normed, gate_weight), {1: 1}, [wide])
    combined = exchange(combine(exchange(both), False))
    (pair_out,) = call(
        functools.partial(last_kernel, share, chunk),
        (combined, current, gate, gains, out_t, up_t, down_t),
        {},
        [(pair_map.shape, F32)],
        (result,),
    )
    return pair_out


def solution(mesh):
    rows, cols = mesh.shape["row"], mesh.shape["col"]
    spread = P(("grp", "row"), "col", None)
    in_specs = (spread, P(("grp", "row"), "col")) + (P(),) * 8

    def body(*args):
        return per_device(rows, cols, *args)

    return jax.shard_map(body, mesh=mesh, in_specs=in_specs, out_specs=spread, check_vma=False)
```

```python
import functools

import jax
import jax.numpy as jnp
from jax import lax
from jax.experimental import pallas as pl
from jax.experimental.pallas import tpu as pltpu
from jax.sharding import PartitionSpec as P

AXES = ("col", "row")
LANES = 128
VMEM_BYTES = 48 * 1024 * 1024
FULL_VMEM_BYTES = 60 * 1024 * 1024
F32, BF16 = jnp.float32, jnp.bfloat16


def dot(left, right, contract=(1, 0)):
    return lax.dot_general(
        left, right, (((contract[0],), (contract[1],)), ((), ())), preferred_element_type=F32
    )


def sigmoid(values):
    return 0.5 * jnp.tanh(0.5 * values) + 0.5


def channel_norm(values, gain):
    wide = jnp.concatenate([gain] * (values.shape[1] // LANES), axis=1)
    centred = values - jnp.mean(values, axis=0, keepdims=True)
    spread = jnp.mean(centred * centred, axis=0, keepdims=True)
    return (centred * lax.rsqrt(spread + 1e-05) * wide).astype(BF16)


def spread_gain(row):
    return jnp.broadcast_to(row, (LANES, row.shape[1])).T


def token_mask(mask, lines):
    height, breadth = mask.shape
    wide = jnp.concatenate([mask.astype(F32)] * (LANES // breadth), axis=1)
    row = lax.broadcasted_iota(jnp.int32, wide.shape, 0)
    lane = lax.broadcasted_iota(jnp.int32, wide.shape, 1)
    wide = jnp.where(row // lines == lane // breadth, wide, 0.0).astype(BF16)
    line = lax.broadcasted_iota(jnp.int32, (lines, height), 0)
    source = lax.broadcasted_iota(jnp.int32, (lines, height), 1)
    return dot((source % lines == line).astype(BF16), wide)


def emit_message(normed, weight_t, mask, line, message_ref, stage_ref, share):
    projected = dot(weight_t, normed)
    hid = weight_t.shape[0] // 4
    owners = hid // share
    for part in range(normed.shape[1] // LANES):
        here = projected[:, part * LANES : (part + 1) * LANES]
        at = line + part
        keep = mask[at : at + 1]
        left = sigmoid(here[:hid]) * here[hid : 2 * hid] * keep
        right = sigmoid(here[2 * hid : 3 * hid]) * here[3 * hid :] * keep
        if share % 8 == 0:
            for owner in range(owners):
                rows = slice(owner * share, (owner + 1) * share)
                both = jnp.concatenate([left[rows], right[rows]], axis=0).astype(BF16)
                message_ref[owner, 2 * share * at : 2 * share * (at + 1), :] = both
        else:
            lines = message_ref.shape[1] // 2
            stage_ref[pl.ds(2 * at, owners, stride=2 * lines), :] = left
            stage_ref[pl.ds(2 * at + 1, owners, stride=2 * lines), :] = right
    if share % 8 and line + normed.shape[1] // LANES == mask.shape[0]:
        message_ref[...] = stage_ref[...].astype(BF16).reshape(message_ref.shape)


def project_kernel(share, chunk, ins, outs, stage_ref, x_ref, mask_ref, gain_ref, weight_ref, sems):
    message_ref, normed_ref, turned_ref, lines_ref = outs
    x_in, mask_in, gain_in, weight_in = ins
    pairs = [(gain_in, gain_ref), (mask_in, mask_ref), (weight_in.at[0], weight_ref), (x_in, x_ref)]
    copies = [pltpu.make_async_copy(src, dst, sems.at[n]) for n, (src, dst) in enumerate(pairs)]
    for copy in copies:
        copy.start()
    height, breadth, channels = x_ref.shape
    tokens = height * breadth
    lines = tokens // LANES
    copies[0].wait()
    copies[1].wait()
    mask = token_mask(mask_ref[...], lines)
    lines_ref[...] = mask
    gain = spread_gain(gain_ref[0:1, :])
    copies[2].wait()
    weight_t = weight_ref[...].T
    copies[3].wait()
    for start in range(0, tokens, chunk):
        first = start // LANES
        held = [
            x_ref[slot * lines + line]
            for line in range(first, first + chunk // LANES)
            for slot in range(LANES // breadth)
        ]
        current = jnp.concatenate(held, axis=0).T
        turned_ref[:, start : start + chunk] = current
        normed = channel_norm(current, gain)
        normed_ref[:, start : start + chunk] = normed
        emit_message(normed, weight_t, mask, first, message_ref, stage_ref, share)


def prepare_kernel(ins, outs):
    normed_ref, gate_ref, proj_ref, out_ref, up_ref, down_ref, gain_in_ref, gain_out_ref, trans_gain_ref = ins
    gate_out, proj_out, out_out, up_out, down_out, gains_out = outs
    gate_out[...] = sigmoid(dot(gate_ref[...].T, normed_ref[...]))
    proj_out[...] = proj_ref[...].T
    for update in range(2):
        out_out[update] = out_ref[update].T
    up_out[...] = up_ref[...].T
    down_out[...] = down_ref[...].T
    rows = [gain_out_ref[0:1, :], gain_in_ref[1:2, :], gain_out_ref[1:2, :], trans_gain_ref[...]]
    for n, row in enumerate(rows):
        gains_out[n] = spread_gain(row)


def gate_kernel(ins, outs):
    normed_ref, weight_ref = ins
    outs[0][...] = sigmoid(dot(weight_ref[...].T, normed_ref[...]))


def swap_slots(parts, breadth):
    parts = list(parts)
    slot = lax.broadcasted_iota(jnp.int32, parts[0].shape, 1) // breadth
    step = 1
    while step < len(parts):
        low = (slot // step) % 2 == 0
        for first in range(len(parts)):
            if first & step:
                continue
            a, b = parts[first], parts[first | step]
            parts[first] = jnp.where(low, a, pltpu.roll(b, step * breadth, 1))
            parts[first | step] = jnp.where(low, pltpu.roll(a, LANES - step * breadth, 1), b)
        step *= 2
    return parts


def combine_kernel(rows, cols, breadth, share, outgoing, ins, outs, stage_ref, result_ref):
    (both_ref,), (combined_ref,) = ins, outs
    slots = LANES // breadth
    span = both_ref.shape[1]
    lines = span // (2 * share)
    stage_ref[...] = both_ref[...].astype(F32).reshape(stage_ref.shape)

    def whole(side, channel):
        columns = []
        for high in range(cols // slots):
            parts = []
            for low in range(slots):
                base = (high * slots + low) * rows * span + side * share + channel
                held = [
                    stage_ref[pl.ds(row * span + base, lines, stride=2 * share), :] for row in range(rows)
                ]
                parts.append(jnp.concatenate(held, axis=0))
            parts = swap_slots(parts, breadth)
            columns.append(
                jnp.concatenate(
                    [part[row * lines : (row + 1) * lines] for row in range(rows) for part in parts], axis=0
                )
            )
        return jnp.concatenate(columns, axis=1).astype(BF16)

    for channel in range(share):
        left, right = whole(0, channel), whole(1, channel)
        combined = dot(left, right, (1, 1) if outgoing else (0, 0))
        for high in range(cols // slots):
            lanes = slice(high * LANES, (high + 1) * LANES)
            parts = [
                jnp.concatenate(
                    [
                        combined[(row * slots + slot) * lines : (row * slots + slot + 1) * lines, lanes]
                        for row in range(rows)
                    ],
                    axis=0,
                )
                for slot in range(slots)
            ]
            for low, part in enumerate(swap_slots(parts, breadth)):
                for row in range(rows):
                    base = ((high * slots + low) * rows + row) * lines * share + channel
                    result_ref[pl.ds(base, lines, stride=share), :] = part[row * lines : (row + 1) * lines]
    combined_ref[...] = result_ref[...].astype(BF16).reshape(combined_ref.shape)


def read_combined(stage_ref, owners, lines, share, first, count):
    columns = []
    for line in range(first, first + count):
        if share % 8 == 0:
            held = [
                stage_ref[(owner * lines + line) * share : (owner * lines + line + 1) * share, :]
                for owner in range(owners)
            ]
            columns.append(jnp.concatenate(held, axis=0))
        else:
            columns.append(stage_ref[pl.ds(line, owners, stride=lines), :])
    return jnp.concatenate(columns, axis=1)


def middle_kernel(share, chunk, ins, outs, stage_ref, message_stage_ref):
    combined_ref, x_ref, gate_ref, gains_ref, out_ref, mask_ref, weight_ref = ins
    message_ref, normed_ref, next_ref = outs
    tokens = x_ref.shape[1]
    lines = tokens // LANES
    owners = combined_ref.shape[0]
    stage_ref[...] = combined_ref[...].astype(F32).reshape(stage_ref.shape)
    mask = mask_ref[...]
    for start in range(0, tokens, chunk):
        here = slice(start, start + chunk)
        combined = read_combined(stage_ref, owners, lines, share, start // LANES, chunk // LANES)
        hidden = channel_norm(combined, gains_ref[0])
        current = x_ref[:, here] + gate_ref[:, here] * dot(out_ref[0], hidden)
        next_ref[:, here] = current
        normed = channel_norm(current, gains_ref[1])
        normed_ref[:, here] = normed
        emit_message(normed, weight_ref[...], mask, start // LANES, message_ref, message_stage_ref, share)


def last_kernel(share, chunk, ins, outs, stage_ref):
    combined_ref, x_ref, gate_ref, gains_ref, out_ref, up_ref, down_ref = ins
    (result_ref,) = outs
    height, breadth, channels = result_ref.shape
    tokens = x_ref.shape[1]
    lines = tokens // LANES
    owners = combined_ref.shape[0]
    half = down_ref.shape[1]
    stage_ref[...] = combined_ref[...].astype(F32).reshape(stage_ref.shape)
    for start in range(0, tokens, chunk):
        here = slice(start, start + chunk)
        combined = read_combined(stage_ref, owners, lines, share, start // LANES, chunk // LANES)
        hidden = channel_norm(combined, gains_ref[2])
        current = x_ref[:, here] + gate_ref[:, here] * dot(out_ref[1], hidden)
        up_part = dot(up_ref[...], channel_norm(current, gains_ref[3]))
        first = up_part[:half]
        trans_hidden = (first * sigmoid(first) * up_part[half:]).astype(BF16)
        result = (current + dot(down_ref[...], trans_hidden)).T
        for part in range(chunk // LANES):
            for slot in range(LANES // breadth):
                base = part * LANES + slot * breadth
                result_ref[slot * lines + start // LANES + part] = result[base : base + breadth]


def whole_spec(array):
    return pl.BlockSpec(array.shape, lambda step, dims=array.ndim: (0,) * dims)


def picked_spec(array, index):
    return pl.BlockSpec((None,) + array.shape[1:], lambda step: (index,) + (0,) * (array.ndim - 1))


def call(kernel, operands, picks, outs, scratch=(), in_place=False):
    limit = FULL_VMEM_BYTES if in_place else VMEM_BYTES
    specs = [
        picked_spec(array, picks[n]) if n in picks else whole_spec(array) for n, array in enumerate(operands)
    ]
    if in_place:
        specs = [pl.BlockSpec(memory_space=pltpu.HBM)] * len(operands)
    shapes = [jax.ShapeDtypeStruct(shape, dtype) for shape, dtype in outs]
    count = len(operands)

    def body(*refs):
        kernel(refs[:count], refs[count : count + len(outs)], *refs[count + len(outs) :])

    return pl.pallas_call(
        body,
        grid=(1,),
        in_specs=specs,
        out_specs=[whole_spec(shape) for shape in shapes],
        out_shape=shapes,
        scratch_shapes=list(scratch),
        compiler_params=pltpu.CompilerParams(vmem_limit_bytes=limit),
    )(*operands)


def exchange(values):
    return lax.all_to_all(values, AXES, split_axis=0, concat_axis=0, tiled=True)


def per_device(
    rows,
    cols,
    pair_map,
    pair_mask,
    gain_in,
    proj_weight,
    gate_weight,
    gain_out,
    out_weight,
    trans_gain,
    trans_up,
    trans_down,
):
    height, breadth, channels = pair_map.shape
    tokens = height * breadth
    lines = tokens // LANES
    hid = gain_out.shape[1]
    owners = rows * cols
    share = hid // owners
    chunk = min(2 * LANES, tokens)
    message = ((owners, 2 * share * lines, LANES), BF16)
    answer = ((owners, share * lines, LANES), BF16)
    staged = pltpu.VMEM((owners * 2 * share * lines, LANES), F32)
    result = pltpu.VMEM((owners * share * lines, LANES), F32)
    spare = pltpu.VMEM((8, LANES), F32) if share % 8 == 0 else staged
    narrow, wide = ((channels, tokens), BF16), ((channels, tokens), F32)

    def combine(both, outgoing):
        kernel = functools.partial(combine_kernel, rows, cols, breadth, share, outgoing)
        (combined,) = call(kernel, (both,), {}, [answer], (staged, result))
        return combined

    both, normed, current, mask = call(
        functools.partial(project_kernel, share, chunk),
        (pair_map, pair_mask, gain_in, proj_weight),
        {},
        [message, narrow, wide, ((lines, LANES), F32)],
        (
            spare,
            pltpu.VMEM(pair_map.shape, F32),
            pltpu.VMEM(pair_mask.shape, jnp.int32),
            pltpu.VMEM(gain_in.shape, F32),
            pltpu.VMEM(proj_weight.shape[1:], BF16),
            pltpu.SemaphoreType.DMA((4,)),
        ),
        in_place=True,
    )
    gate, proj_t, out_t, up_t, down_t, gains = call(
        prepare_kernel,
        (
            normed,
            gate_weight,
            proj_weight,
            out_weight,
            trans_up,
            trans_down,
            gain_in,
            gain_out,
            trans_gain.reshape(1, -1),
        ),
        {1: 0, 2: 1},
        [
            wide,
            (proj_weight.shape[:0:-1], BF16),
            ((2, out_weight.shape[2], hid), BF16),
            (trans_up.shape[::-1], BF16),
            (trans_down.shape[::-1], BF16),
            ((4, channels, LANES), F32),
        ],
    )
    combined = exchange(combine(exchange(both), True))
    both, normed, current = call(
        functools.partial(middle_kernel, share, chunk),
        (combined, current, gate, gains, out_t, mask, proj_t),
        {},
        [message, narrow, wide],
        (result, spare),
    )
    (gate,) = call(gate_kernel, (normed, gate_weight), {1: 1}, [wide])
    combined = exchange(combine(exchange(both), False))
    (pair_out,) = call(
        functools.partial(last_kernel, share, chunk),
        (combined, current, gate, gains, out_t, up_t, down_t),
        {},
        [(pair_map.shape, F32)],
        (result,),
    )
    return pair_out


def solution(mesh):
    rows, cols = mesh.shape["row"], mesh.shape["col"]
    spread = P(("grp", "row"), "col", None)
    in_specs = (spread, P(("grp", "row"), "col")) + (P(),) * 8

    def body(*args):
        return per_device(rows, cols, *args)

    return jax.shard_map(body, mesh=mesh, in_specs=in_specs, out_specs=spread, check_vma=False)
```

```python
import functools

import jax
import jax.numpy as jnp
from jax import lax
from jax.experimental import pallas as pl
from jax.experimental.pallas import tpu as pltpu
from jax.sharding import PartitionSpec as P

AXES = ("col", "row")
LANES = 128
VMEM_BYTES = 48 * 1024 * 1024
FULL_VMEM_BYTES = 60 * 1024 * 1024
F32, BF16 = jnp.float32, jnp.bfloat16


def dot(left, right, contract=(1, 0)):
    return lax.dot_general(
        left, right, (((contract[0],), (contract[1],)), ((), ())), preferred_element_type=F32
    )


def sigmoid(values):
    return 0.5 * jnp.tanh(0.5 * values) + 0.5


def channel_norm(values, gain):
    wide = jnp.concatenate([gain] * (values.shape[1] // LANES), axis=1)
    centred = values - jnp.mean(values, axis=0, keepdims=True)
    spread = jnp.mean(centred * centred, axis=0, keepdims=True)
    return (centred * lax.rsqrt(spread + 1e-05) * wide).astype(BF16)


def spread_gain(row):
    return jnp.broadcast_to(row, (LANES, row.shape[1])).T


def token_mask(mask, lines):
    height, breadth = mask.shape
    wide = jnp.concatenate([mask.astype(F32)] * (LANES // breadth), axis=1)
    row = lax.broadcasted_iota(jnp.int32, wide.shape, 0)
    lane = lax.broadcasted_iota(jnp.int32, wide.shape, 1)
    wide = jnp.where(row // lines == lane // breadth, wide, 0.0).astype(BF16)
    line = lax.broadcasted_iota(jnp.int32, (lines, height), 0)
    source = lax.broadcasted_iota(jnp.int32, (lines, height), 1)
    return dot((source % lines == line).astype(BF16), wide)


def emit_message(normed, weight_t, mask, line, message_ref, stage_ref, share):
    projected = dot(weight_t, normed)
    hid = weight_t.shape[0] // 4
    owners = hid // share
    for part in range(normed.shape[1] // LANES):
        here = projected[:, part * LANES : (part + 1) * LANES]
        at = line + part
        keep = mask[at : at + 1]
        left = sigmoid(here[:hid]) * here[hid : 2 * hid] * keep
        right = sigmoid(here[2 * hid : 3 * hid]) * here[3 * hid :] * keep
        if share % 8 == 0:
            for owner in range(owners):
                rows = slice(owner * share, (owner + 1) * share)
                both = jnp.concatenate([left[rows], right[rows]], axis=0).astype(BF16)
                message_ref[owner, 2 * share * at : 2 * share * (at + 1), :] = both
        else:
            lines = message_ref.shape[1] // 2
            stage_ref[pl.ds(2 * at, owners, stride=2 * lines), :] = left
            stage_ref[pl.ds(2 * at + 1, owners, stride=2 * lines), :] = right
    if share % 8 and line + normed.shape[1] // LANES == mask.shape[0]:
        message_ref[...] = stage_ref[...].astype(BF16).reshape(message_ref.shape)


def start_all(pairs, sems, first=0):
    copies = [pltpu.make_async_copy(src, dst, sems.at[first + n]) for n, (src, dst) in enumerate(pairs)]
    for copy in copies:
        copy.start()
    return copies


def line_tokens(x_ref, line):
    return jnp.concatenate([x_ref[slot, line] for slot in range(x_ref.shape[0])], axis=0)


def project_kernel(
    share, chunk, ins, outs, stage_ref, x_ref, mask_ref, gain_ref, weight_ref, held_ref, in_sems, out_sems
):
    (message_out,) = outs
    x_in, mask_in, gain_in, weight_in = ins
    slots, lines, breadth, channels = x_ref.shape
    count = chunk // LANES
    steps = lines // count
    pieces = [slice(n * count, (n + 1) * count) for n in range(steps)]
    small = start_all([(gain_in, gain_ref), (mask_in, mask_ref), (weight_in.at[0], weight_ref)], in_sems)
    large = start_all([(x_in.at[:, piece], x_ref.at[:, piece]) for piece in pieces], in_sems, 3)
    small[0].wait()
    small[1].wait()
    mask = token_mask(mask_ref[...], lines)
    gain = spread_gain(gain_ref[0:1, :])
    small[2].wait()
    weight_t = weight_ref[...].T
    writes = []
    for n, piece in enumerate(pieces):
        large[n].wait()
        current = jnp.concatenate([line_tokens(x_ref, line) for line in range(piece.start, piece.stop)], axis=0).T
        emit_message(channel_norm(current, gain), weight_t, mask, piece.start, held_ref, stage_ref, share)
        if share % 8 == 0:
            rows = slice(2 * share * piece.start, 2 * share * piece.stop)
            writes += start_all([(held_ref.at[:, rows], message_out.at[:, rows])], out_sems, n)
        elif n == steps - 1:
            writes += start_all([(held_ref, message_out)], out_sems)
    for write in writes:
        write.wait()


def prepare(ins, outs):
    x_ref, mask_ref, gate_ref, proj_ref, out_ref, up_ref, down_ref, gain_in_ref, gain_out_ref, trans_gain_ref = ins
    gate_out, x_out, mask_out, gate_t_out, proj_out, out_out, up_out, down_out, gains_out = outs
    lines = x_ref.shape[1]
    gain, gate_t = spread_gain(gain_in_ref[0:1, :]), gate_ref[0].T
    for line in range(lines):
        lanes = slice(line * LANES, (line + 1) * LANES)
        current = line_tokens(x_ref, line).T
        x_out[:, lanes] = current
        gate_out[:, lanes] = sigmoid(dot(gate_t, channel_norm(current, gain)))
    mask_out[...] = token_mask(mask_ref[...], lines)
    gate_t_out[...] = gate_ref[1].T
    proj_out[...] = proj_ref[...].T
    for update in range(2):
        out_out[update] = out_ref[update].T
    up_out[...] = up_ref[...].T
    down_out[...] = down_ref[...].T
    rows = [gain_out_ref[0:1, :], gain_in_ref[1:2, :], gain_out_ref[1:2, :], trans_gain_ref[...]]
    for n, row in enumerate(rows):
        gains_out[n] = spread_gain(row)


def swap_slots(parts, breadth):
    parts = list(parts)
    slot = lax.broadcasted_iota(jnp.int32, parts[0].shape, 1) // breadth
    step = 1
    while step < len(parts):
        low = (slot // step) % 2 == 0
        for first in range(len(parts)):
            if first & step:
                continue
            a, b = parts[first], parts[first | step]
            parts[first] = jnp.where(low, a, pltpu.roll(b, step * breadth, 1))
            parts[first | step] = jnp.where(low, pltpu.roll(a, LANES - step * breadth, 1), b)
        step *= 2
    return parts


def pitch_of(share):
    return share + 1 if share % 8 == 0 else share


def combine_kernel(rows, cols, breadth, share, outgoing, ins, outs, stage_ref, result_ref):
    both_ref, combined_ref = ins[0], outs[0]
    if len(ins) > 1:
        prepare(ins[1:], outs[1:])
    slots = LANES // breadth
    owners, span = both_ref.shape[:2]
    lines = span // (2 * share)
    pitch = pitch_of(share)
    padded = pitch != share
    if padded:
        for owner in range(owners):
            for line in range(lines):
                both = both_ref[owner, 2 * share * line : 2 * share * (line + 1), :].astype(F32)
                for side in range(2):
                    base = ((2 * owner + side) * lines + line) * pitch
                    stage_ref[base : base + share, :] = both[side * share : (side + 1) * share]
    else:
        stage_ref[...] = both_ref[...].astype(F32).reshape(stage_ref.shape)

    def line_rows(owner, side, channel):
        if padded:
            return pl.ds((2 * owner + side) * lines * pitch + channel, lines, stride=pitch)
        return pl.ds(owner * span + side * share + channel, lines, stride=2 * share)

    def whole(side, channel):
        columns = []
        for high in range(cols // slots):
            parts = []
            for low in range(slots):
                col = high * slots + low
                held = [stage_ref[line_rows(col * rows + row, side, channel), :] for row in range(rows)]
                parts.append(jnp.concatenate(held, axis=0))
            parts = swap_slots(parts, breadth)
            columns.append(
                jnp.concatenate(
                    [part[row * lines : (row + 1) * lines] for row in range(rows) for part in parts], axis=0
                )
            )
        return jnp.concatenate(columns, axis=1).astype(BF16)

    for channel in range(share):
        left, right = whole(0, channel), whole(1, channel)
        combined = dot(left, right, (1, 1) if outgoing else (0, 0))
        for high in range(cols // slots):
            lanes = slice(high * LANES, (high + 1) * LANES)
            parts = [
                jnp.concatenate(
                    [
                        combined[(row * slots + slot) * lines : (row * slots + slot + 1) * lines, lanes]
                        for row in range(rows)
                    ],
                    axis=0,
                )
                for slot in range(slots)
            ]
            for low, part in enumerate(swap_slots(parts, breadth)):
                for row in range(rows):
                    base = ((high * slots + low) * rows + row) * lines * pitch + channel
                    result_ref[pl.ds(base, lines, stride=pitch), :] = part[row * lines : (row + 1) * lines]
    if padded:
        for owner in range(owners):
            held = [
                result_ref[(owner * lines + line) * pitch : (owner * lines + line) * pitch + share, :]
                for line in range(lines)
            ]
            combined_ref[owner] = jnp.concatenate(held, axis=0).astype(BF16)
    else:
        combined_ref[...] = result_ref[...].astype(BF16).reshape(combined_ref.shape)


def read_combined(stage_ref, owners, lines, share, first, count):
    columns = []
    for line in range(first, first + count):
        if share % 8 == 0:
            held = [
                stage_ref[(owner * lines + line) * share : (owner * lines + line + 1) * share, :]
                for owner in range(owners)
            ]
            columns.append(jnp.concatenate(held, axis=0))
        else:
            columns.append(stage_ref[pl.ds(line, owners, stride=lines), :])
    return jnp.concatenate(columns, axis=1)


def middle_kernel(share, chunk, ins, outs, stage_ref, message_stage_ref):
    combined_ref, x_ref, gate_ref, mask_ref, gate_t_ref, weight_ref, out_ref, gains_ref = ins
    message_ref, gate_out, next_ref = outs
    tokens = x_ref.shape[1]
    lines = tokens // LANES
    owners = combined_ref.shape[0]
    stage_ref[...] = combined_ref[...].astype(F32).reshape(stage_ref.shape)
    mask = mask_ref[...]
    for start in range(0, tokens, chunk):
        here = slice(start, start + chunk)
        combined = read_combined(stage_ref, owners, lines, share, start // LANES, chunk // LANES)
        hidden = channel_norm(combined, gains_ref[0])
        current = x_ref[:, here] + gate_ref[:, here] * dot(out_ref[0], hidden)
        next_ref[:, here] = current
        normed = channel_norm(current, gains_ref[1])
        emit_message(normed, weight_ref[...], mask, start // LANES, message_ref, message_stage_ref, share)
        gate_out[:, here] = sigmoid(dot(gate_t_ref[...], normed))


def last_kernel(share, chunk, ins, outs, stage_ref, result_ref, sems):
    combined_ref, x_ref, gate_ref, out_ref, up_ref, down_ref, gains_ref = ins
    (result_out,) = outs
    slots, lines, breadth, channels = result_ref.shape
    owners = combined_ref.shape[0]
    half = down_ref.shape[1]
    count = chunk // LANES
    stage_ref[...] = combined_ref[...].astype(F32).reshape(stage_ref.shape)
    writes = []
    for first in range(0, lines, count):
        here = slice(first * LANES, (first + count) * LANES)
        combined = read_combined(stage_ref, owners, lines, share, first, count)
        hidden = channel_norm(combined, gains_ref[2])
        current = x_ref[:, here] + gate_ref[:, here] * dot(out_ref[1], hidden)
        trans_in = channel_norm(current, gains_ref[3])
        block = min(256, half)
        for base in range(0, half, block):
            gate_part = dot(up_ref[base : base + block, :], trans_in)
            up_part = dot(up_ref[half + base : half + base + block, :], trans_in)
            trans_hidden = (gate_part * sigmoid(gate_part) * up_part).astype(BF16)
            current = current + dot(down_ref[:, base : base + block], trans_hidden)
        result = current.T
        for part in range(count):
            for slot in range(slots):
                base = part * LANES + slot * breadth
                result_ref[slot, first + part] = result[base : base + breadth]
        piece = slice(first, first + count)
        writes += start_all([(result_ref.at[:, piece], result_out.at[:, piece])], sems, first // count)
    for write in writes:
        write.wait()


def whole_spec(array):
    return pl.BlockSpec(array.shape, lambda step, dims=array.ndim: (0,) * dims)


def picked_spec(array, index):
    return pl.BlockSpec((None,) + array.shape[1:], lambda step: (index,) + (0,) * (array.ndim - 1))


def call(kernel, operands, outs, scratch=(), picks=None, in_hbm=False, out_hbm=False):
    in_place = pl.BlockSpec(memory_space=pltpu.HBM)
    specs = [
        picked_spec(array, picks[n]) if picks and n in picks else whole_spec(array)
        for n, array in enumerate(operands)
    ]
    shapes = [jax.ShapeDtypeStruct(shape, dtype) for shape, dtype in outs]
    count = len(operands)

    def body(*refs):
        kernel(refs[:count], refs[count : count + len(outs)], *refs[count + len(outs) :])

    return pl.pallas_call(
        body,
        grid=(1,),
        in_specs=[in_place] * count if in_hbm else specs,
        out_specs=[in_place if out_hbm else whole_spec(shape) for shape in shapes],
        out_shape=shapes,
        scratch_shapes=list(scratch),
        compiler_params=pltpu.CompilerParams(vmem_limit_bytes=FULL_VMEM_BYTES if in_hbm else VMEM_BYTES),
    )(*operands)


def exchange(values):
    return lax.all_to_all(values, AXES, split_axis=0, concat_axis=0, tiled=True)


def per_device(
    rows,
    cols,
    pair_map,
    pair_mask,
    gain_in,
    proj_weight,
    gate_weight,
    gain_out,
    out_weight,
    trans_gain,
    trans_up,
    trans_down,
):
    height, breadth, channels = pair_map.shape
    tokens = height * breadth
    lines = tokens // LANES
    hid = gain_out.shape[1]
    owners = rows * cols
    share = hid // owners
    chunk = min(2 * LANES, tokens)
    steps = tokens // chunk
    message = ((owners, 2 * share * lines, LANES), BF16)
    answer = ((owners, share * lines, LANES), BF16)
    result = pltpu.VMEM((owners * share * lines, LANES), F32)
    spare = pltpu.VMEM((8, LANES) if share % 8 == 0 else (owners * 2 * share * lines, LANES), F32)
    wide = ((channels, tokens), F32)
    held = ((LANES // breadth, lines, breadth, channels), F32)
    grouped = pair_map.reshape(held[0])

    def combine(operands, outs, outgoing):
        kernel = functools.partial(combine_kernel, rows, cols, breadth, share, outgoing)
        pitch = pitch_of(share)
        scratch = [pltpu.VMEM((sides * owners * lines * pitch, LANES), F32) for sides in (2, 1)]
        return call(kernel, operands, [answer] + outs, scratch, {4: 1})

    (both,) = call(
        functools.partial(project_kernel, share, chunk),
        (grouped, pair_mask, gain_in, proj_weight),
        [message],
        (
            spare,
            pltpu.VMEM(*held),
            pltpu.VMEM(pair_mask.shape, jnp.int32),
            pltpu.VMEM(gain_in.shape, F32),
            pltpu.VMEM(proj_weight.shape[1:], BF16),
            pltpu.VMEM(*message),
            pltpu.SemaphoreType.DMA((3 + steps,)),
            pltpu.SemaphoreType.DMA((steps,)),
        ),
        in_hbm=True,
        out_hbm=True,
    )
    combined, gate, current, mask, gate_t, proj_t, out_t, up_t, down_t, gains = combine(
        (
            exchange(both),
            grouped,
            pair_mask,
            gate_weight,
            proj_weight,
            out_weight,
            trans_up,
            trans_down,
            gain_in,
            gain_out,
            trans_gain.reshape(1, -1),
        ),
        [
            wide,
            wide,
            ((lines, LANES), F32),
            ((channels, channels), BF16),
            (proj_weight.shape[:0:-1], BF16),
            ((2, channels, hid), BF16),
            (trans_up.shape[::-1], BF16),
            (trans_down.shape[::-1], BF16),
            ((4, channels, LANES), F32),
        ],
        True,
    )
    both, gate, current = call(
        functools.partial(middle_kernel, share, chunk),
        (exchange(combined), current, gate, mask, gate_t, proj_t, out_t, gains),
        [message, wide, wide],
        (result, spare),
    )
    (combined,) = combine((exchange(both),), [], False)
    (pair_out,) = call(
        functools.partial(last_kernel, share, chunk),
        (exchange(combined), current, gate, out_t, up_t, down_t, gains),
        [held],
        (result, pltpu.VMEM(*held), pltpu.SemaphoreType.DMA((steps,))),
        out_hbm=True,
    )
    return pair_out.reshape(pair_map.shape)


def solution(mesh):
    rows, cols = mesh.shape["row"], mesh.shape["col"]
    spread = P(("grp", "row"), "col", None)
    in_specs = (spread, P(("grp", "row"), "col")) + (P(),) * 8

    def body(*args):
        return per_device(rows, cols, *args)

    return jax.shard_map(body, mesh=mesh, in_specs=in_specs, out_specs=spread, check_vma=False)
```

```python
import functools

import jax
import jax.numpy as jnp
from jax import lax
from jax.experimental import pallas as pl
from jax.experimental.pallas import tpu as pltpu
from jax.sharding import PartitionSpec as P

AXES = ("col", "row")
LANES = 128
VMEM_BYTES = 48 * 1024 * 1024
FULL_VMEM_BYTES = 60 * 1024 * 1024
F32, BF16 = jnp.float32, jnp.bfloat16


def dot(left, right, contract=(1, 0)):
    return lax.dot_general(
        left, right, (((contract[0],), (contract[1],)), ((), ())), preferred_element_type=F32
    )


def sigmoid(values):
    return 0.5 * jnp.tanh(0.5 * values) + 0.5


def channel_norm(values, gain):
    wide = jnp.concatenate([gain] * (values.shape[1] // LANES), axis=1)
    centred = values - jnp.mean(values, axis=0, keepdims=True)
    spread = jnp.mean(centred * centred, axis=0, keepdims=True)
    return (centred * lax.rsqrt(spread + 1e-05) * wide).astype(BF16)


def spread_gain(row):
    return jnp.broadcast_to(row, (LANES, row.shape[1])).T


def token_mask(mask, lines):
    height, breadth = mask.shape
    wide = jnp.concatenate([mask.astype(F32)] * (LANES // breadth), axis=1)
    row = lax.broadcasted_iota(jnp.int32, wide.shape, 0)
    lane = lax.broadcasted_iota(jnp.int32, wide.shape, 1)
    wide = jnp.where(row // lines == lane // breadth, wide, 0.0).astype(BF16)
    line = lax.broadcasted_iota(jnp.int32, (lines, height), 0)
    source = lax.broadcasted_iota(jnp.int32, (lines, height), 1)
    return dot((source % lines == line).astype(BF16), wide)


def emit_message(normed, weight_t, mask, line, message_ref, stage_ref, share):
    projected = dot(weight_t, normed)
    hid = weight_t.shape[0] // 4
    owners = hid // share
    for part in range(normed.shape[1] // LANES):
        here = projected[:, part * LANES : (part + 1) * LANES]
        at = line + part
        keep = mask[at : at + 1]
        left = sigmoid(here[:hid]) * here[hid : 2 * hid] * keep
        right = sigmoid(here[2 * hid : 3 * hid]) * here[3 * hid :] * keep
        if share % 8 == 0:
            for owner in range(owners):
                rows = slice(owner * share, (owner + 1) * share)
                both = jnp.concatenate([left[rows], right[rows]], axis=0).astype(BF16)
                message_ref[owner, 2 * share * at : 2 * share * (at + 1), :] = both
        else:
            lines = message_ref.shape[1] // 2
            stage_ref[pl.ds(2 * at, owners, stride=2 * lines), :] = left
            stage_ref[pl.ds(2 * at + 1, owners, stride=2 * lines), :] = right
    if share % 8 and line + normed.shape[1] // LANES == mask.shape[0]:
        message_ref[...] = stage_ref[...].astype(BF16).reshape(message_ref.shape)


def start_all(pairs, sems, first=0):
    copies = [pltpu.make_async_copy(src, dst, sems.at[first + n]) for n, (src, dst) in enumerate(pairs)]
    for copy in copies:
        copy.start()
    return copies


def line_tokens(x_ref, line):
    return jnp.concatenate([x_ref[slot, line] for slot in range(x_ref.shape[0])], axis=0)


def project_kernel(share, ins, outs, stage_ref, x_ref, mask_ref, gain_ref, weight_ref, sems):
    message_ref, normed_ref = outs
    x_in, mask_in, gain_in, weight_in = ins
    lines = x_ref.shape[1]
    pairs = [(weight_in.at[0], weight_ref), (x_in, x_ref), (gain_in, gain_ref), (mask_in, mask_ref)]
    for copy in start_all(pairs, sems):
        copy.wait()
    mask = token_mask(mask_ref[...], lines)
    current = jnp.concatenate([line_tokens(x_ref, line).T for line in range(lines)], axis=1)
    normed = channel_norm(current, spread_gain(gain_ref[0:1, :]))
    emit_message(normed, weight_ref[...].T, mask, 0, message_ref, stage_ref, share)
    normed_ref[...] = normed


def prepare_kernel(ins, outs):
    normed_ref, x_ref, mask_ref, gate_ref, proj_ref, out_ref, up_ref, down_ref, gain_in_ref, gain_out_ref, trans_gain_ref = ins
    gate_out, x_out, mask_out, proj_out, out_out, up_out, down_out, gains_out = outs
    lines = x_ref.shape[1]
    gate_out[...] = sigmoid(dot(gate_ref[...].T, normed_ref[...]))
    for line in range(lines):
        x_out[:, line * LANES : (line + 1) * LANES] = line_tokens(x_ref, line).T
    mask_out[...] = token_mask(mask_ref[...], lines)
    proj_out[...] = proj_ref[...].T
    for update in range(2):
        out_out[update] = out_ref[update].T
    up_out[...] = up_ref[...].T
    down_out[...] = down_ref[...].T
    rows = [gain_out_ref[0:1, :], gain_in_ref[1:2, :], gain_out_ref[1:2, :], trans_gain_ref[...]]
    for n, row in enumerate(rows):
        gains_out[n] = spread_gain(row)


def gate_kernel(ins, outs):
    normed_ref, weight_ref = ins
    outs[0][...] = sigmoid(dot(weight_ref[...].T, normed_ref[...]))


def swap_slots(parts, breadth):
    parts = list(parts)
    slot = lax.broadcasted_iota(jnp.int32, parts[0].shape, 1) // breadth
    step = 1
    while step < len(parts):
        low = (slot // step) % 2 == 0
        for first in range(len(parts)):
            if first & step:
                continue
            a, b = parts[first], parts[first | step]
            parts[first] = jnp.where(low, a, pltpu.roll(b, step * breadth, 1))
            parts[first | step] = jnp.where(low, pltpu.roll(a, LANES - step * breadth, 1), b)
        step *= 2
    return parts


def pitch_of(share):
    return share + 1 if share % 8 == 0 else share


def combine_kernel(rows, cols, breadth, share, outgoing, ins, outs, stage_ref, result_ref):
    (both_ref,), (combined_ref,) = ins, outs
    slots = LANES // breadth
    owners, span = both_ref.shape[:2]
    lines = span // (2 * share)
    pitch = pitch_of(share)
    padded = pitch != share
    if padded:
        for owner in range(owners):
            for line in range(lines):
                both = both_ref[owner, 2 * share * line : 2 * share * (line + 1), :].astype(F32)
                for side in range(2):
                    base = ((2 * owner + side) * lines + line) * pitch
                    stage_ref[base : base + share, :] = both[side * share : (side + 1) * share]
    else:
        stage_ref[...] = both_ref[...].astype(F32).reshape(stage_ref.shape)

    def line_rows(owner, side, channel):
        if padded:
            return pl.ds((2 * owner + side) * lines * pitch + channel, lines, stride=pitch)
        return pl.ds(owner * span + side * share + channel, lines, stride=2 * share)

    def whole(side, channel):
        columns = []
        for high in range(cols // slots):
            parts = []
            for low in range(slots):
                col = high * slots + low
                held = [stage_ref[line_rows(col * rows + row, side, channel), :] for row in range(rows)]
                parts.append(jnp.concatenate(held, axis=0))
            parts = swap_slots(parts, breadth)
            columns.append(
                jnp.concatenate(
                    [part[row * lines : (row + 1) * lines] for row in range(rows) for part in parts], axis=0
                )
            )
        return jnp.concatenate(columns, axis=1).astype(BF16)

    for channel in range(share):
        left, right = whole(0, channel), whole(1, channel)
        combined = dot(left, right, (1, 1) if outgoing else (0, 0))
        for high in range(cols // slots):
            lanes = slice(high * LANES, (high + 1) * LANES)
            parts = [
                jnp.concatenate(
                    [
                        combined[(row * slots + slot) * lines : (row * slots + slot + 1) * lines, lanes]
                        for row in range(rows)
                    ],
                    axis=0,
                )
                for slot in range(slots)
            ]
            for low, part in enumerate(swap_slots(parts, breadth)):
                for row in range(rows):
                    base = ((high * slots + low) * rows + row) * lines * pitch + channel
                    result_ref[pl.ds(base, lines, stride=pitch), :] = part[row * lines : (row + 1) * lines]
    if padded:
        for owner in range(owners):
            held = [
                result_ref[(owner * lines + line) * pitch : (owner * lines + line) * pitch + share, :]
                for line in range(lines)
            ]
            combined_ref[owner] = jnp.concatenate(held, axis=0).astype(BF16)
    else:
        combined_ref[...] = result_ref[...].astype(BF16).reshape(combined_ref.shape)


def read_combined(stage_ref, owners, lines, share, first, count):
    columns = []
    for line in range(first, first + count):
        if share % 8 == 0:
            held = [
                stage_ref[(owner * lines + line) * share : (owner * lines + line + 1) * share, :]
                for owner in range(owners)
            ]
            columns.append(jnp.concatenate(held, axis=0))
        else:
            columns.append(stage_ref[pl.ds(line, owners, stride=lines), :])
    return jnp.concatenate(columns, axis=1)


def middle_kernel(share, chunk, ins, outs, stage_ref, message_stage_ref):
    combined_ref, x_ref, gate_ref, mask_ref, weight_ref, out_ref, gains_ref = ins
    message_ref, normed_ref, next_ref = outs
    tokens = x_ref.shape[1]
    lines = tokens // LANES
    owners = combined_ref.shape[0]
    stage_ref[...] = combined_ref[...].astype(F32).reshape(stage_ref.shape)
    mask = mask_ref[...]
    for start in range(0, tokens, chunk):
        here = slice(start, start + chunk)
        combined = read_combined(stage_ref, owners, lines, share, start // LANES, chunk // LANES)
        hidden = channel_norm(combined, gains_ref[0])
        current = x_ref[:, here] + gate_ref[:, here] * dot(out_ref[0], hidden)
        next_ref[:, here] = current
        normed = channel_norm(current, gains_ref[1])
        emit_message(normed, weight_ref[...], mask, start // LANES, message_ref, message_stage_ref, share)
        normed_ref[:, here] = normed


def last_kernel(share, chunk, ins, outs, stage_ref, result_ref, sems):
    combined_ref, x_ref, gate_ref, out_ref, up_ref, down_ref, gains_ref = ins
    (result_out,) = outs
    slots, lines, breadth, channels = result_ref.shape
    owners = combined_ref.shape[0]
    half = down_ref.shape[1]
    count = chunk // LANES
    stage_ref[...] = combined_ref[...].astype(F32).reshape(stage_ref.shape)
    writes = []
    for first in range(0, lines, count):
        here = slice(first * LANES, (first + count) * LANES)
        combined = read_combined(stage_ref, owners, lines, share, first, count)
        hidden = channel_norm(combined, gains_ref[2])
        current = x_ref[:, here] + gate_ref[:, here] * dot(out_ref[1], hidden)
        trans_in = channel_norm(current, gains_ref[3])
        block = min(256, half)
        for base in range(0, half, block):
            gate_part = dot(up_ref[base : base + block, :], trans_in)
            up_part = dot(up_ref[half + base : half + base + block, :], trans_in)
            trans_hidden = (gate_part * sigmoid(gate_part) * up_part).astype(BF16)
            current = current + dot(down_ref[:, base : base + block], trans_hidden)
        result = current.T
        for part in range(count):
            for slot in range(slots):
                base = part * LANES + slot * breadth
                result_ref[slot, first + part] = result[base : base + breadth]
        piece = slice(first, first + count)
        writes += start_all([(result_ref.at[:, piece], result_out.at[:, piece])], sems, first // count)
    for write in writes:
        write.wait()


def whole_spec(array):
    return pl.BlockSpec(array.shape, lambda step, dims=array.ndim: (0,) * dims)


def picked_spec(array, index):
    return pl.BlockSpec((None,) + array.shape[1:], lambda step: (index,) + (0,) * (array.ndim - 1))


def call(kernel, operands, outs, scratch=(), picks=None, in_hbm=False, out_hbm=False):
    in_place = pl.BlockSpec(memory_space=pltpu.HBM)
    specs = [
        picked_spec(array, picks[n]) if picks and n in picks else whole_spec(array)
        for n, array in enumerate(operands)
    ]
    shapes = [jax.ShapeDtypeStruct(shape, dtype) for shape, dtype in outs]
    count = len(operands)

    def body(*refs):
        kernel(refs[:count], refs[count : count + len(outs)], *refs[count + len(outs) :])

    return pl.pallas_call(
        body,
        grid=(1,),
        in_specs=[in_place] * count if in_hbm else specs,
        out_specs=[in_place if out_hbm else whole_spec(shape) for shape in shapes],
        out_shape=shapes,
        scratch_shapes=list(scratch),
        compiler_params=pltpu.CompilerParams(vmem_limit_bytes=FULL_VMEM_BYTES if in_hbm else VMEM_BYTES),
    )(*operands)


def exchange(values):
    return lax.all_to_all(values, AXES, split_axis=0, concat_axis=0, tiled=True)


def per_device(
    rows,
    cols,
    pair_map,
    pair_mask,
    gain_in,
    proj_weight,
    gate_weight,
    gain_out,
    out_weight,
    trans_gain,
    trans_up,
    trans_down,
):
    height, breadth, channels = pair_map.shape
    tokens = height * breadth
    lines = tokens // LANES
    hid = gain_out.shape[1]
    owners = rows * cols
    share = hid // owners
    chunk = min(4 * LANES, tokens)
    message = ((owners, 2 * share * lines, LANES), BF16)
    answer = ((owners, share * lines, LANES), BF16)
    result = pltpu.VMEM((owners * share * lines, LANES), F32)
    spare = pltpu.VMEM((8, LANES) if share % 8 == 0 else (owners * 2 * share * lines, LANES), F32)
    narrow, wide = ((channels, tokens), BF16), ((channels, tokens), F32)
    held = ((LANES // breadth, lines, breadth, channels), F32)
    grouped = pair_map.reshape(held[0])

    def combine(both, outgoing):
        kernel = functools.partial(combine_kernel, rows, cols, breadth, share, outgoing)
        scratch = [pltpu.VMEM((sides * owners * lines * pitch_of(share), LANES), F32) for sides in (2, 1)]
        return call(kernel, (both,), [answer], scratch)[0]

    both, normed = call(
        functools.partial(project_kernel, share),
        (grouped, pair_mask, gain_in, proj_weight),
        [message, narrow],
        (
            spare,
            pltpu.VMEM(*held),
            pltpu.VMEM(pair_mask.shape, jnp.int32),
            pltpu.VMEM(gain_in.shape, F32),
            pltpu.VMEM(proj_weight.shape[1:], BF16),
            pltpu.SemaphoreType.DMA((4,)),
        ),
        in_hbm=True,
    )
    gate, current, mask, proj_t, out_t, up_t, down_t, gains = call(
        prepare_kernel,
        (
            normed,
            grouped,
            pair_mask,
            gate_weight,
            proj_weight,
            out_weight,
            trans_up,
            trans_down,
            gain_in,
            gain_out,
            trans_gain.reshape(1, -1),
        ),
        [
            wide,
            wide,
            ((lines, LANES), F32),
            (proj_weight.shape[:0:-1], BF16),
            ((2, channels, hid), BF16),
            (trans_up.shape[::-1], BF16),
            (trans_down.shape[::-1], BF16),
            ((4, channels, LANES), F32),
        ],
        picks={3: 0, 4: 1},
    )
    combined = exchange(combine(exchange(both), True))
    both, normed, current = call(
        functools.partial(middle_kernel, share, chunk),
        (combined, current, gate, mask, proj_t, out_t, gains),
        [message, narrow, wide],
        (result, spare),
    )
    (gate,) = call(gate_kernel, (normed, gate_weight), [wide], picks={1: 1})
    combined = exchange(combine(exchange(both), False))
    (pair_out,) = call(
        functools.partial(last_kernel, share, chunk),
        (combined, current, gate, out_t, up_t, down_t, gains),
        [held],
        (result, pltpu.VMEM(*held), pltpu.SemaphoreType.DMA((tokens // chunk,))),
        out_hbm=True,
    )
    return pair_out.reshape(pair_map.shape)


def solution(mesh):
    rows, cols = mesh.shape["row"], mesh.shape["col"]
    spread = P(("grp", "row"), "col", None)
    in_specs = (spread, P(("grp", "row"), "col")) + (P(),) * 8

    def body(*args):
        return per_device(rows, cols, *args)

    return jax.shard_map(body, mesh=mesh, in_specs=in_specs, out_specs=spread, check_vma=False)
```

```python
import functools

import jax
import jax.numpy as jnp
from jax import lax
from jax.experimental import pallas as pl
from jax.experimental.pallas import tpu as pltpu
from jax.sharding import PartitionSpec as P

AXES = ("col", "row")
LANES = 128
VMEM_BYTES = 24 * 1024 * 1024
FULL_VMEM_BYTES = 60 * 1024 * 1024
F32, BF16 = jnp.float32, jnp.bfloat16


def dot(left, right, contract=(1, 0)):
    return lax.dot_general(
        left, right, (((contract[0],), (contract[1],)), ((), ())), preferred_element_type=F32
    )


def sigmoid(values):
    return 0.5 * jnp.tanh(0.5 * values) + 0.5


def channel_norm(values, gain):
    wide = jnp.concatenate([gain] * (values.shape[1] // LANES), axis=1)
    centred = values - jnp.mean(values, axis=0, keepdims=True)
    spread = jnp.mean(centred * centred, axis=0, keepdims=True)
    return (centred * lax.rsqrt(spread + 1e-05) * wide).astype(BF16)


def spread_gain(row):
    return jnp.broadcast_to(row, (LANES, row.shape[1])).T


def token_mask(mask, lines):
    height, breadth = mask.shape
    wide = jnp.concatenate([mask.astype(F32)] * (LANES // breadth), axis=1)
    row = lax.broadcasted_iota(jnp.int32, wide.shape, 0)
    lane = lax.broadcasted_iota(jnp.int32, wide.shape, 1)
    wide = jnp.where(row // lines == lane // breadth, wide, 0.0).astype(BF16)
    line = lax.broadcasted_iota(jnp.int32, (lines, height), 0)
    source = lax.broadcasted_iota(jnp.int32, (lines, height), 1)
    return dot((source % lines == line).astype(BF16), wide)


def arrange(weight, parts, take):
    width = weight.shape[1]
    hid = width // 4
    row = lax.broadcasted_iota(jnp.int32, (width, width), 0)
    source = lax.broadcasted_iota(jnp.int32, (width, width), 1)
    block = 2 * hid // parts
    owners = hid // (parts * take)
    inner = row % block
    channel = (row // (2 * block) * take + inner % take) * owners + inner // (2 * take)
    wanted = inner // take % 2 * (2 * hid) + row // block % 2 * hid + channel
    return dot((source == wanted).astype(BF16), weight, (1, 1)).astype(BF16)


def emit_messages(normed, weight_t, mask, line, message_refs, take):
    block = weight_t.shape[0] // (2 * len(message_refs))
    size = 2 * take
    count = normed.shape[1] // LANES
    group = max(1, 16 // size)
    for part, message_ref in enumerate(message_refs):
        projected = dot(weight_t[2 * part * block : 2 * (part + 1) * block], normed)
        act = sigmoid(projected[:block]) * projected[block:]
        acts = [act[:, n * LANES : (n + 1) * LANES] * mask[line + n : line + n + 1] for n in range(count)]
        for owner in range(block // size):
            rows = slice(owner * size, (owner + 1) * size)
            for first in range(0, count, group):
                held = jnp.concatenate([act[rows] for act in acts[first : first + group]], axis=0).astype(BF16)
                message_ref[owner, size * (line + first) : size * (line + first + group), :] = held


def start_all(pairs, sems, first=0):
    copies = [pltpu.make_async_copy(src, dst, sems.at[first + n]) for n, (src, dst) in enumerate(pairs)]
    for copy in copies:
        copy.start()
    return copies


def line_tokens(x_ref, line):
    return jnp.concatenate([x_ref[slot, line] for slot in range(x_ref.shape[0])], axis=0)


def project_kernel(parts, take, ins, outs, x_ref, mask_ref, gain_ref, weight_ref, sems):
    normed_ref, *message_refs = outs
    x_in, mask_in, gain_in, weight_in = ins
    lines = x_ref.shape[1]
    pairs = [(weight_in.at[0], weight_ref), (x_in, x_ref), (gain_in, gain_ref), (mask_in, mask_ref)]
    for copy in start_all(pairs, sems):
        copy.wait()
    mask = token_mask(mask_ref[...], lines)
    current = jnp.concatenate([line_tokens(x_ref, line).T for line in range(lines)], axis=1)
    normed = channel_norm(current, spread_gain(gain_ref[0:1, :]))
    emit_messages(normed, arrange(weight_ref[...], parts, take), mask, 0, message_refs, take)
    normed_ref[...] = normed


def prepare_kernel(parts, take, ins, outs):
    normed_ref, x_ref, mask_ref, gate_ref, proj_ref, out_ref, up_ref, down_ref, gain_in_ref, gain_out_ref, trans_gain_ref = ins
    gate_out, x_out, mask_out, proj_out, out_out, up_out, down_out, gains_out = outs
    lines = x_ref.shape[1]
    gate_out[...] = sigmoid(dot(gate_ref[...].T, normed_ref[...]))
    for line in range(lines):
        x_out[:, line * LANES : (line + 1) * LANES] = line_tokens(x_ref, line).T
    mask_out[...] = token_mask(mask_ref[...], lines)
    proj_out[...] = arrange(proj_ref[...], parts, take)
    for update in range(2):
        out_out[update] = out_ref[update].T
    up_out[...] = up_ref[...].T
    down_out[...] = down_ref[...].T
    rows = [gain_out_ref[0:1, :], gain_in_ref[1:2, :], gain_out_ref[1:2, :], trans_gain_ref[...]]
    for n, row in enumerate(rows):
        gains_out[n] = spread_gain(row)


def gate_kernel(ins, outs):
    normed_ref, weight_ref = ins
    outs[0][...] = sigmoid(dot(weight_ref[...].T, normed_ref[...]))


def swap_slots(parts, breadth):
    parts = list(parts)
    slot = lax.broadcasted_iota(jnp.int32, parts[0].shape, 1) // breadth
    step = 1
    while step < len(parts):
        low = (slot // step) % 2 == 0
        for first in range(len(parts)):
            if first & step:
                continue
            a, b = parts[first], parts[first | step]
            parts[first] = jnp.where(low, a, pltpu.roll(b, step * breadth, 1))
            parts[first | step] = jnp.where(low, pltpu.roll(a, LANES - step * breadth, 1), b)
        step *= 2
    return parts


def combine_kernel(rows, cols, breadth, take, outgoing, ins, outs, stage_ref):
    (both_ref,), (combined_ref,) = ins, outs
    slots = LANES // breadth
    owners, span = both_ref.shape[:2]
    size = 2 * take
    lines = span // size
    pitch = size + 1
    for owner in range(owners):
        both = both_ref[owner].astype(F32)
        for line in range(lines):
            base = (owner * lines + line) * pitch
            stage_ref[base : base + size, :] = both[line * size : (line + 1) * size]

    def whole(side, channel):
        columns = []
        for high in range(cols // slots):
            parts = []
            for low in range(slots):
                first = (high * slots + low) * rows
                held = [
                    stage_ref[pl.ds((first + row) * lines * pitch + side * take + channel, lines, stride=pitch), :]
                    for row in range(rows)
                ]
                parts.append(jnp.concatenate(held, axis=0))
            parts = swap_slots(parts, breadth)
            columns.append(
                jnp.concatenate(
                    [part[row * lines : (row + 1) * lines] for row in range(rows) for part in parts], axis=0
                )
            )
        return jnp.concatenate(columns, axis=1).astype(BF16)

    group = min(take, max(1, 16 // lines))
    for channel in range(0, take, group):
        answers = [[] for _ in range(owners)]
        for n in range(channel, channel + group):
            left, right = whole(0, n), whole(1, n)
            combined = dot(left, right, (1, 1) if outgoing else (0, 0))
            for high in range(cols // slots):
                lanes = slice(high * LANES, (high + 1) * LANES)
                parts = [
                    jnp.concatenate(
                        [
                            combined[(row * slots + slot) * lines : (row * slots + slot + 1) * lines, lanes]
                            for row in range(rows)
                        ],
                        axis=0,
                    )
                    for slot in range(slots)
                ]
                for low, part in enumerate(swap_slots(parts, breadth)):
                    for row in range(rows):
                        owner = (high * slots + low) * rows + row
                        answers[owner].append(part[row * lines : (row + 1) * lines])
        for owner, held in enumerate(answers):
            at = slice(channel * lines, (channel + group) * lines)
            combined_ref[owner, at, :] = jnp.concatenate(held, axis=0).astype(BF16)


def hold_answers(combined_refs, stage_ref):
    for part, combined_ref in enumerate(combined_refs):
        owners, span = combined_ref.shape[:2]
        for owner in range(owners):
            base = (part * owners + owner) * (span + 1)
            stage_ref[base : base + span, :] = combined_ref[owner].astype(F32)


def read_combined(stage_ref, parts, owners, take, lines, first, count):
    span = take * lines
    columns = []
    for line in range(first, first + count):
        held = [
            stage_ref[pl.ds(part * owners * (span + 1) + n * lines + line, owners, stride=span + 1), :]
            for part in range(parts)
            for n in range(take)
        ]
        columns.append(jnp.concatenate(held, axis=0))
    return jnp.concatenate(columns, axis=1)


def middle_kernel(parts, take, chunk, ins, outs, stage_ref):
    x_ref, gate_ref, mask_ref, weight_ref, out_ref, gains_ref, *combined_refs = ins
    normed_ref, next_ref, *message_refs = outs
    tokens = x_ref.shape[1]
    lines = tokens // LANES
    owners = combined_refs[0].shape[0]
    hold_answers(combined_refs, stage_ref)
    mask, weight_t = mask_ref[...], weight_ref[...]
    for start in range(0, tokens, chunk):
        here = slice(start, start + chunk)
        combined = read_combined(stage_ref, parts, owners, take, lines, start // LANES, chunk // LANES)
        hidden = channel_norm(combined, gains_ref[0])
        current = x_ref[:, here] + gate_ref[:, here] * dot(out_ref[0], hidden)
        next_ref[:, here] = current
        normed = channel_norm(current, gains_ref[1])
        normed_ref[:, here] = normed
        emit_messages(normed, weight_t, mask, start // LANES, message_refs, take)


def last_kernel(parts, take, chunk, ins, outs, stage_ref, result_ref, sems):
    x_ref, gate_ref, out_ref, up_ref, down_ref, gains_ref, *combined_refs = ins
    (result_out,) = outs
    slots, lines, breadth, channels = result_ref.shape
    owners = combined_refs[0].shape[0]
    half = down_ref.shape[1]
    count = chunk // LANES
    hold_answers(combined_refs, stage_ref)
    writes = []
    for first in range(0, lines, count):
        here = slice(first * LANES, (first + count) * LANES)
        combined = read_combined(stage_ref, parts, owners, take, lines, first, count)
        hidden = channel_norm(combined, gains_ref[2])
        current = x_ref[:, here] + gate_ref[:, here] * dot(out_ref[1], hidden)
        trans_in = channel_norm(current, gains_ref[3])
        block = min(256, half)
        for base in range(0, half, block):
            gate_part = dot(up_ref[base : base + block, :], trans_in)
            up_part = dot(up_ref[half + base : half + base + block, :], trans_in)
            trans_hidden = (gate_part * sigmoid(gate_part) * up_part).astype(BF16)
            current = current + dot(down_ref[:, base : base + block], trans_hidden)
        result = current.T
        for part in range(count):
            for slot in range(slots):
                base = part * LANES + slot * breadth
                result_ref[slot, first + part] = result[base : base + breadth]
        piece = slice(first, first + count)
        writes += start_all([(result_ref.at[:, piece], result_out.at[:, piece])], sems, first // count)
    for write in writes:
        write.wait()


def whole_spec(array):
    return pl.BlockSpec(array.shape, lambda step, dims=array.ndim: (0,) * dims)


def picked_spec(array, index):
    return pl.BlockSpec((None,) + array.shape[1:], lambda step: (index,) + (0,) * (array.ndim - 1))


def call(kernel, operands, outs, scratch=(), picks=None, in_hbm=False, out_hbm=False):
    in_place = pl.BlockSpec(memory_space=pltpu.HBM)
    specs = [
        picked_spec(array, picks[n]) if picks and n in picks else whole_spec(array)
        for n, array in enumerate(operands)
    ]
    shapes = [jax.ShapeDtypeStruct(shape, dtype) for shape, dtype in outs]
    count = len(operands)

    def body(*refs):
        kernel(refs[:count], refs[count : count + len(outs)], *refs[count + len(outs) :])

    return pl.pallas_call(
        body,
        grid=(1,),
        in_specs=[in_place] * count if in_hbm else specs,
        out_specs=[in_place if out_hbm else whole_spec(shape) for shape in shapes],
        out_shape=shapes,
        scratch_shapes=list(scratch),
        compiler_params=pltpu.CompilerParams(vmem_limit_bytes=FULL_VMEM_BYTES if in_hbm else VMEM_BYTES),
    )(*operands)


def exchange(values):
    return lax.all_to_all(values, AXES, split_axis=0, concat_axis=0, tiled=True)


def per_device(
    rows,
    cols,
    pair_map,
    pair_mask,
    gain_in,
    proj_weight,
    gate_weight,
    gain_out,
    out_weight,
    trans_gain,
    trans_up,
    trans_down,
):
    height, breadth, channels = pair_map.shape
    tokens = height * breadth
    lines = tokens // LANES
    hid = gain_out.shape[1]
    owners = rows * cols
    share = hid // owners
    parts = 2 if share % 8 == 0 else 1
    take = share // parts
    chunk = min(max(4, 8 // take) * LANES, tokens)
    messages = [((owners, 2 * take * lines, LANES), BF16)] * parts
    answer = ((owners, take * lines, LANES), BF16)
    answers = pltpu.VMEM((parts * owners * (take * lines + 1), LANES), F32)
    narrow, wide = ((channels, tokens), BF16), ((channels, tokens), F32)
    held = ((LANES // breadth, lines, breadth, channels), F32)
    grouped = pair_map.reshape(held[0])

    def combine(messages, outgoing):
        kernel = functools.partial(combine_kernel, rows, cols, breadth, take, outgoing)
        scratch = [pltpu.VMEM((owners * lines * (2 * take + 1), LANES), F32)]
        received = [exchange(both) for both in messages]
        return [exchange(call(kernel, (both,), [answer], scratch)[0]) for both in received]

    normed, *both = call(
        functools.partial(project_kernel, parts, take),
        (grouped, pair_mask, gain_in, proj_weight),
        [narrow] + messages,
        (
            pltpu.VMEM(*held),
            pltpu.VMEM(pair_mask.shape, jnp.int32),
            pltpu.VMEM(gain_in.shape, F32),
            pltpu.VMEM(proj_weight.shape[1:], BF16),
            pltpu.SemaphoreType.DMA((4,)),
        ),
        in_hbm=True,
    )
    gate, current, mask, proj_t, out_t, up_t, down_t, gains = call(
        functools.partial(prepare_kernel, parts, take),
        (
            normed,
            grouped,
            pair_mask,
            gate_weight,
            proj_weight,
            out_weight,
            trans_up,
            trans_down,
            gain_in,
            gain_out,
            trans_gain.reshape(1, -1),
        ),
        [
            wide,
            wide,
            ((lines, LANES), F32),
            (proj_weight.shape[:0:-1], BF16),
            ((2, channels, hid), BF16),
            (trans_up.shape[::-1], BF16),
            (trans_down.shape[::-1], BF16),
            ((4, channels, LANES), F32),
        ],
        picks={3: 0, 4: 1},
    )
    combined = combine(both, True)
    normed, current, *both = call(
        functools.partial(middle_kernel, parts, take, chunk),
        (current, gate, mask, proj_t, out_t, gains, *combined),
        [narrow, wide] + messages,
        (answers,),
    )
    (gate,) = call(gate_kernel, (normed, gate_weight), [wide], picks={1: 1})
    combined = combine(both, False)
    (pair_out,) = call(
        functools.partial(last_kernel, parts, take, chunk),
        (current, gate, out_t, up_t, down_t, gains, *combined),
        [held],
        (answers, pltpu.VMEM(*held), pltpu.SemaphoreType.DMA((tokens // chunk,))),
        out_hbm=True,
    )
    return pair_out.reshape(pair_map.shape)


def solution(mesh):
    rows, cols = mesh.shape["row"], mesh.shape["col"]
    spread = P(("grp", "row"), "col", None)
    in_specs = (spread, P(("grp", "row"), "col")) + (P(),) * 8

    def body(*args):
        return per_device(rows, cols, *args)

    return jax.shard_map(body, mesh=mesh, in_specs=in_specs, out_specs=spread, check_vma=False)
```

```python
import functools

import jax
import jax.numpy as jnp
from jax import lax
from jax.experimental import pallas as pl
from jax.experimental.pallas import tpu as pltpu
from jax.sharding import PartitionSpec as P

AXES = ("col", "row")
LANES = 128
VMEM_BYTES = 24 * 1024 * 1024
FULL_VMEM_BYTES = 60 * 1024 * 1024
F32, BF16 = jnp.float32, jnp.bfloat16


def dot(left, right, contract=(1, 0)):
    return lax.dot_general(
        left, right, (((contract[0],), (contract[1],)), ((), ())), preferred_element_type=F32
    )


def sigmoid(values):
    return 0.5 * jnp.tanh(0.5 * values) + 0.5


def channel_norm(values, gain):
    wide = jnp.concatenate([gain] * (values.shape[1] // LANES), axis=1)
    centred = values - jnp.mean(values, axis=0, keepdims=True)
    spread = jnp.mean(centred * centred, axis=0, keepdims=True)
    return (centred * lax.rsqrt(spread + 1e-05) * wide).astype(BF16)


def spread_gain(row):
    return jnp.broadcast_to(row, (LANES, row.shape[1])).T


def token_mask(mask, lines):
    height, breadth = mask.shape
    wide = jnp.concatenate([mask.astype(F32)] * (LANES // breadth), axis=1)
    row = lax.broadcasted_iota(jnp.int32, wide.shape, 0)
    lane = lax.broadcasted_iota(jnp.int32, wide.shape, 1)
    wide = jnp.where(row // lines == lane // breadth, wide, 0.0).astype(BF16)
    line = lax.broadcasted_iota(jnp.int32, (lines, height), 0)
    source = lax.broadcasted_iota(jnp.int32, (lines, height), 1)
    return dot((source % lines == line).astype(BF16), wide)


def emit_message(normed, weight_t, mask, line, message_ref, stage_ref, share):
    projected = dot(weight_t, normed)
    hid = weight_t.shape[0] // 4
    owners = hid // share
    for part in range(normed.shape[1] // LANES):
        here = projected[:, part * LANES : (part + 1) * LANES]
        at = line + part
        keep = mask[at : at + 1]
        left = sigmoid(here[:hid]) * here[hid : 2 * hid] * keep
        right = sigmoid(here[2 * hid : 3 * hid]) * here[3 * hid :] * keep
        if share % 8 == 0:
            for owner in range(owners):
                rows = slice(owner * share, (owner + 1) * share)
                both = jnp.concatenate([left[rows], right[rows]], axis=0).astype(BF16)
                message_ref[owner, 2 * share * at : 2 * share * (at + 1), :] = both
        else:
            lines = message_ref.shape[1] // 2
            stage_ref[pl.ds(2 * at, owners, stride=2 * lines), :] = left
            stage_ref[pl.ds(2 * at + 1, owners, stride=2 * lines), :] = right
    if share % 8 and line + normed.shape[1] // LANES == mask.shape[0]:
        message_ref[...] = stage_ref[...].astype(BF16).reshape(message_ref.shape)


def start_all(pairs, sems, first=0):
    copies = [pltpu.make_async_copy(src, dst, sems.at[first + n]) for n, (src, dst) in enumerate(pairs)]
    for copy in copies:
        copy.start()
    return copies


def line_tokens(x_ref, line):
    return jnp.concatenate([x_ref[slot, line] for slot in range(x_ref.shape[0])], axis=0)


def project_kernel(share, ins, outs, stage_ref, x_ref, mask_ref, gain_ref, weight_ref, sems):
    message_ref, normed_ref = outs
    x_in, mask_in, gain_in, weight_in = ins
    lines = x_ref.shape[1]
    pairs = [(weight_in.at[0], weight_ref), (x_in, x_ref), (gain_in, gain_ref), (mask_in, mask_ref)]
    for copy in start_all(pairs, sems):
        copy.wait()
    mask = token_mask(mask_ref[...], lines)
    current = jnp.concatenate([line_tokens(x_ref, line).T for line in range(lines)], axis=1)
    normed = channel_norm(current, spread_gain(gain_ref[0:1, :]))
    emit_message(normed, weight_ref[...].T, mask, 0, message_ref, stage_ref, share)
    normed_ref[...] = normed


def prepare_kernel(ins, outs):
    normed_ref, x_ref, mask_ref, gate_ref, gain_in_ref, gain_out_ref, trans_gain_ref = ins
    gate_out, x_out, mask_out, gains_out = outs
    lines = x_ref.shape[1]
    gate_out[...] = sigmoid(dot(gate_ref[...].T, normed_ref[...]))
    for line in range(lines):
        x_out[:, line * LANES : (line + 1) * LANES] = line_tokens(x_ref, line).T
    mask_out[...] = token_mask(mask_ref[...], lines)
    rows = [gain_out_ref[0:1, :], gain_in_ref[1:2, :], gain_out_ref[1:2, :], trans_gain_ref[...]]
    gains_out[...] = jnp.concatenate(rows + rows, axis=0)


def swap_slots(parts, breadth):
    parts = list(parts)
    slot = lax.broadcasted_iota(jnp.int32, parts[0].shape, 1) // breadth
    step = 1
    while step < len(parts):
        low = (slot // step) % 2 == 0
        for first in range(len(parts)):
            if first & step:
                continue
            a, b = parts[first], parts[first | step]
            parts[first] = jnp.where(low, a, pltpu.roll(b, step * breadth, 1))
            parts[first | step] = jnp.where(low, pltpu.roll(a, LANES - step * breadth, 1), b)
        step *= 2
    return parts


def pitch_of(share):
    return share + 1 if share % 8 == 0 else share


def combine_kernel(rows, cols, breadth, share, outgoing, ins, outs, stage_ref, result_ref):
    both_ref, combined_ref = ins[0], outs[0]
    slots = LANES // breadth
    owners, span = both_ref.shape[:2]
    lines = span // (2 * share)
    pitch = pitch_of(share)
    padded = pitch != share
    if padded:
        for owner in range(owners):
            for line in range(lines):
                both = both_ref[owner, 2 * share * line : 2 * share * (line + 1), :].astype(F32)
                for side in range(2):
                    base = ((2 * owner + side) * lines + line) * pitch
                    stage_ref[base : base + share, :] = both[side * share : (side + 1) * share]
    else:
        stage_ref[...] = both_ref[...].astype(F32).reshape(stage_ref.shape)

    def line_rows(owner, side, channel):
        if padded:
            return pl.ds((2 * owner + side) * lines * pitch + channel, lines, stride=pitch)
        return pl.ds(owner * span + side * share + channel, lines, stride=2 * share)

    def whole(side, channel):
        columns = []
        for high in range(cols // slots):
            parts = []
            for low in range(slots):
                col = high * slots + low
                held = [stage_ref[line_rows(col * rows + row, side, channel), :] for row in range(rows)]
                parts.append(jnp.concatenate(held, axis=0))
            parts = swap_slots(parts, breadth)
            columns.append(
                jnp.concatenate(
                    [part[row * lines : (row + 1) * lines] for row in range(rows) for part in parts], axis=0
                )
            )
        return jnp.concatenate(columns, axis=1).astype(BF16)

    for channel in range(share):
        left, right = whole(0, channel), whole(1, channel)
        combined = dot(left, right, (1, 1) if outgoing else (0, 0))
        for high in range(cols // slots):
            lanes = slice(high * LANES, (high + 1) * LANES)
            parts = [
                jnp.concatenate(
                    [
                        combined[(row * slots + slot) * lines : (row * slots + slot + 1) * lines, lanes]
                        for row in range(rows)
                    ],
                    axis=0,
                )
                for slot in range(slots)
            ]
            for low, part in enumerate(swap_slots(parts, breadth)):
                for row in range(rows):
                    base = ((high * slots + low) * rows + row) * lines * pitch + channel
                    result_ref[pl.ds(base, lines, stride=pitch), :] = part[row * lines : (row + 1) * lines]
    if padded:
        for owner in range(owners):
            held = [
                result_ref[(owner * lines + line) * pitch : (owner * lines + line) * pitch + share, :]
                for line in range(lines)
            ]
            combined_ref[owner] = jnp.concatenate(held, axis=0).astype(BF16)
    else:
        combined_ref[...] = result_ref[...].astype(BF16).reshape(combined_ref.shape)


def read_combined(stage_ref, owners, lines, share, first, count):
    columns = []
    for line in range(first, first + count):
        if share % 8 == 0:
            held = [
                stage_ref[(owner * lines + line) * share : (owner * lines + line + 1) * share, :]
                for owner in range(owners)
            ]
            columns.append(jnp.concatenate(held, axis=0))
        else:
            columns.append(stage_ref[pl.ds(line, owners, stride=lines), :])
    return jnp.concatenate(columns, axis=1)


def middle_kernel(share, chunk, ins, outs, stage_ref, message_stage_ref):
    combined_ref, x_ref, gate_ref, mask_ref, gains_ref, proj_ref, gate_weight_ref, out_ref = ins
    message_ref, gate_out, next_ref = outs
    tokens = x_ref.shape[1]
    lines = tokens // LANES
    owners = combined_ref.shape[0]
    stage_ref[...] = combined_ref[...].astype(F32).reshape(stage_ref.shape)
    mask = mask_ref[...]
    gain_out, gain = [spread_gain(gains_ref[n : n + 1, :]) for n in (0, 1)]
    out_t, proj_t, gate_t = out_ref[...].T, proj_ref[...].T, gate_weight_ref[...].T
    for start in range(0, tokens, chunk):
        here = slice(start, start + chunk)
        combined = read_combined(stage_ref, owners, lines, share, start // LANES, chunk // LANES)
        hidden = channel_norm(combined, gain_out)
        current = x_ref[:, here] + gate_ref[:, here] * dot(out_t, hidden)
        next_ref[:, here] = current
        normed = channel_norm(current, gain)
        emit_message(normed, proj_t, mask, start // LANES, message_ref, message_stage_ref, share)
        gate_out[:, here] = sigmoid(dot(gate_t, normed))


def last_kernel(share, chunk, ins, outs, stage_ref, result_ref, sems):
    combined_ref, x_ref, gate_ref, gains_ref, out_ref, up_ref, down_ref = ins
    (result_out,) = outs
    slots, lines, breadth, channels = result_ref.shape
    owners = combined_ref.shape[0]
    half = down_ref.shape[0]
    count = chunk // LANES
    gain_out, gain = [spread_gain(gains_ref[n : n + 1, :]) for n in (2, 3)]
    out_t, up_t, down_t = out_ref[...].T, up_ref[...].T, down_ref[...].T
    stage_ref[...] = combined_ref[...].astype(F32).reshape(stage_ref.shape)
    writes = []
    for first in range(0, lines, count):
        here = slice(first * LANES, (first + count) * LANES)
        combined = read_combined(stage_ref, owners, lines, share, first, count)
        hidden = channel_norm(combined, gain_out)
        current = x_ref[:, here] + gate_ref[:, here] * dot(out_t, hidden)
        trans_in = channel_norm(current, gain)
        block = min(256, half)
        for base in range(0, half, block):
            gate_part = dot(up_t[base : base + block], trans_in)
            up_part = dot(up_t[half + base : half + base + block], trans_in)
            trans_hidden = (gate_part * sigmoid(gate_part) * up_part).astype(BF16)
            current = current + dot(down_t[:, base : base + block], trans_hidden)
        result = current.T
        for part in range(count):
            for slot in range(slots):
                base = part * LANES + slot * breadth
                result_ref[slot, first + part] = result[base : base + breadth]
        piece = slice(first, first + count)
        writes += start_all([(result_ref.at[:, piece], result_out.at[:, piece])], sems, first // count)
    for write in writes:
        write.wait()


def whole_spec(array):
    return pl.BlockSpec(array.shape, lambda step, dims=array.ndim: (0,) * dims)


def picked_spec(array, index):
    return pl.BlockSpec((None,) + array.shape[1:], lambda step: (index,) + (0,) * (array.ndim - 1))


def call(kernel, operands, outs, scratch=(), picks=None, in_hbm=False, out_hbm=False):
    in_place = pl.BlockSpec(memory_space=pltpu.HBM)
    specs = [
        picked_spec(array, picks[n]) if picks and n in picks else whole_spec(array)
        for n, array in enumerate(operands)
    ]
    shapes = [jax.ShapeDtypeStruct(shape, dtype) for shape, dtype in outs]
    count = len(operands)

    def body(*refs):
        kernel(refs[:count], refs[count : count + len(outs)], *refs[count + len(outs) :])

    return pl.pallas_call(
        body,
        grid=(1,),
        in_specs=[in_place] * count if in_hbm else specs,
        out_specs=[in_place if out_hbm else whole_spec(shape) for shape in shapes],
        out_shape=shapes,
        scratch_shapes=list(scratch),
        compiler_params=pltpu.CompilerParams(vmem_limit_bytes=FULL_VMEM_BYTES if in_hbm else VMEM_BYTES),
    )(*operands)


def exchange(values):
    return lax.all_to_all(values, AXES, split_axis=0, concat_axis=0, tiled=True)


def per_device(
    rows,
    cols,
    pair_map,
    pair_mask,
    gain_in,
    proj_weight,
    gate_weight,
    gain_out,
    out_weight,
    trans_gain,
    trans_up,
    trans_down,
):
    height, breadth, channels = pair_map.shape
    tokens = height * breadth
    lines = tokens // LANES
    hid = gain_out.shape[1]
    owners = rows * cols
    share = hid // owners
    chunk = min(4 * LANES, tokens)
    message = ((owners, 2 * share * lines, LANES), BF16)
    answer = ((owners, share * lines, LANES), BF16)
    result = pltpu.VMEM((owners * share * lines, LANES), F32)
    spare = pltpu.VMEM((8, LANES) if share % 8 == 0 else (owners * 2 * share * lines, LANES), F32)
    narrow, wide = ((channels, tokens), BF16), ((channels, tokens), F32)
    held = ((LANES // breadth, lines, breadth, channels), F32)
    grouped = pair_map.reshape(held[0])

    def combine(operands, outgoing):
        kernel = functools.partial(combine_kernel, rows, cols, breadth, share, outgoing)
        scratch = [pltpu.VMEM((sides * owners * lines * pitch_of(share), LANES), F32) for sides in (2, 1)]
        return call(kernel, operands, [answer], scratch)[0]

    both, normed = call(
        functools.partial(project_kernel, share),
        (grouped, pair_mask, gain_in, proj_weight),
        [message, narrow],
        (
            spare,
            pltpu.VMEM(*held),
            pltpu.VMEM(pair_mask.shape, jnp.int32),
            pltpu.VMEM(gain_in.shape, F32),
            pltpu.VMEM(proj_weight.shape[1:], BF16),
            pltpu.SemaphoreType.DMA((4,)),
        ),
        in_hbm=True,
    )
    gate, current, mask, gains = call(
        prepare_kernel,
        (normed, grouped, pair_mask, gate_weight, gain_in, gain_out, trans_gain.reshape(1, -1)),
        [wide, wide, ((lines, LANES), F32), ((8, channels), F32)],
        picks={3: 0},
    )
    combined = exchange(combine((exchange(both), mask), True))
    both, gate, current = call(
        functools.partial(middle_kernel, share, chunk),
        (combined, current, gate, mask, gains, proj_weight, gate_weight, out_weight),
        [message, wide, wide],
        (result, spare),
        picks={5: 1, 6: 1, 7: 0},
    )
    combined = exchange(combine((exchange(both),), False))
    (pair_out,) = call(
        functools.partial(last_kernel, share, chunk),
        (combined, current, gate, gains, out_weight, trans_up, trans_down),
        [held],
        (result, pltpu.VMEM(*held), pltpu.SemaphoreType.DMA((tokens // chunk,))),
        picks={4: 1},
        out_hbm=True,
    )
    return pair_out.reshape(pair_map.shape)


def solution(mesh):
    rows, cols = mesh.shape["row"], mesh.shape["col"]
    spread = P(("grp", "row"), "col", None)
    in_specs = (spread, P(("grp", "row"), "col")) + (P(),) * 8

    def body(*args):
        return per_device(rows, cols, *args)

    return jax.shard_map(body, mesh=mesh, in_specs=in_specs, out_specs=spread, check_vma=False)
```

```python
import functools

import jax
import jax.numpy as jnp
from jax import lax
from jax.experimental import pallas as pl
from jax.experimental.pallas import tpu as pltpu
from jax.sharding import Mesh
from jax.sharding import PartitionSpec as P

NEAR_AXES = ("near", "row")
ALL_AXES = ("half", "near", "row")
LANES = 128
VMEM_BYTES = 24 * 1024 * 1024
FULL_VMEM_BYTES = 60 * 1024 * 1024
F32, BF16 = jnp.float32, jnp.bfloat16


def dot(left, right, contract=(1, 0)):
    return lax.dot_general(
        left, right, (((contract[0],), (contract[1],)), ((), ())), preferred_element_type=F32
    )


def sigmoid(values):
    return 0.5 * jnp.tanh(0.5 * values) + 0.5


def channel_norm(values, gain):
    wide = jnp.concatenate([gain] * (values.shape[1] // LANES), axis=1)
    centred = values - jnp.mean(values, axis=0, keepdims=True)
    spread = jnp.mean(centred * centred, axis=0, keepdims=True)
    return (centred * lax.rsqrt(spread + 1e-05) * wide).astype(BF16)


def spread_gain(row):
    return jnp.broadcast_to(row, (LANES, row.shape[1])).T


def token_mask(mask, lines):
    height, breadth = mask.shape
    wide = jnp.concatenate([mask.astype(F32)] * (LANES // breadth), axis=1)
    row = lax.broadcasted_iota(jnp.int32, wide.shape, 0)
    lane = lax.broadcasted_iota(jnp.int32, wide.shape, 1)
    wide = jnp.where(row // lines == lane // breadth, wide, 0.0).astype(BF16)
    line = lax.broadcasted_iota(jnp.int32, (lines, height), 0)
    source = lax.broadcasted_iota(jnp.int32, (lines, height), 1)
    return dot((source % lines == line).astype(BF16), wide)


def emit_message(normed, weight_t, mask, line, message_ref, stage_ref, share):
    projected = dot(weight_t, normed)
    hid = weight_t.shape[0] // 4
    owners = hid // share
    for part in range(normed.shape[1] // LANES):
        here = projected[:, part * LANES : (part + 1) * LANES]
        at = line + part
        keep = mask[at : at + 1]
        left = sigmoid(here[:hid]) * here[hid : 2 * hid] * keep
        right = sigmoid(here[2 * hid : 3 * hid]) * here[3 * hid :] * keep
        if share % 8 == 0:
            for owner in range(owners):
                rows = slice(owner * share, (owner + 1) * share)
                both = jnp.concatenate([left[rows], right[rows]], axis=0).astype(BF16)
                message_ref[owner, 2 * share * at : 2 * share * (at + 1), :] = both
        else:
            lines = message_ref.shape[1] // 2
            stage_ref[pl.ds(2 * at, owners, stride=2 * lines), :] = left
            stage_ref[pl.ds(2 * at + 1, owners, stride=2 * lines), :] = right
    if share % 8 and line + normed.shape[1] // LANES == mask.shape[0]:
        message_ref[...] = stage_ref[...].astype(BF16).reshape(message_ref.shape)


def start_all(pairs, sems, first=0):
    copies = [pltpu.make_async_copy(src, dst, sems.at[first + n]) for n, (src, dst) in enumerate(pairs)]
    for copy in copies:
        copy.start()
    return copies


def line_tokens(x_ref, line):
    return jnp.concatenate([x_ref[slot, line] for slot in range(x_ref.shape[0])], axis=0)


def project_kernel(share, ins, outs, stage_ref, x_ref, mask_ref, gain_ref, weight_ref, sems):
    message_ref, normed_ref = outs
    x_in, mask_in, gain_in, weight_in = ins
    lines = x_ref.shape[1]
    pairs = [(weight_in.at[0], weight_ref), (x_in, x_ref), (gain_in, gain_ref), (mask_in, mask_ref)]
    for copy in start_all(pairs, sems):
        copy.wait()
    mask = token_mask(mask_ref[...], lines)
    current = jnp.concatenate([line_tokens(x_ref, line).T for line in range(lines)], axis=1)
    normed = channel_norm(current, spread_gain(gain_ref[0:1, :]))
    emit_message(normed, weight_ref[...].T, mask, 0, message_ref, stage_ref, share)
    normed_ref[...] = normed


def prepare_kernel(ins, outs):
    normed_ref, x_ref, mask_ref, gate_ref, gain_in_ref, gain_out_ref, trans_gain_ref = ins
    gate_out, x_out, mask_out, gains_out = outs
    lines = x_ref.shape[1]
    gate_out[...] = sigmoid(dot(gate_ref[...].T, normed_ref[...]))
    for line in range(lines):
        x_out[:, line * LANES : (line + 1) * LANES] = line_tokens(x_ref, line).T
    mask_out[...] = token_mask(mask_ref[...], lines)
    rows = [gain_out_ref[0:1, :], gain_in_ref[1:2, :], gain_out_ref[1:2, :], trans_gain_ref[...]]
    gains_out[...] = jnp.concatenate(rows + rows, axis=0)


def swap_slots(parts, breadth):
    parts = list(parts)
    slot = lax.broadcasted_iota(jnp.int32, parts[0].shape, 1) // breadth
    step = 1
    while step < len(parts):
        low = (slot // step) % 2 == 0
        for first in range(len(parts)):
            if first & step:
                continue
            a, b = parts[first], parts[first | step]
            parts[first] = jnp.where(low, a, pltpu.roll(b, step * breadth, 1))
            parts[first | step] = jnp.where(low, pltpu.roll(a, LANES - step * breadth, 1), b)
        step *= 2
    return parts


def pitch_of(share):
    return share + 1 if share % 8 == 0 else share


def combine_kernel(rows, cols, near, breadth, share, outgoing, ins, outs, stage_ref, result_ref):
    both_ref, combined_ref = ins[0], outs[0]
    slots = LANES // breadth
    owners, span = both_ref.shape[:2]
    lines = span // (2 * share)
    pitch = pitch_of(share)
    padded = pitch != share
    if padded:
        for owner in range(owners):
            for line in range(lines):
                both = both_ref[owner, 2 * share * line : 2 * share * (line + 1), :].astype(F32)
                for side in range(2):
                    base = ((2 * owner + side) * lines + line) * pitch
                    stage_ref[base : base + share, :] = both[side * share : (side + 1) * share]
    else:
        stage_ref[...] = both_ref[...].astype(F32).reshape(stage_ref.shape)

    def line_rows(owner, side, channel):
        if padded:
            return pl.ds((2 * owner + side) * lines * pitch + channel, lines, stride=pitch)
        return pl.ds(owner * span + side * share + channel, lines, stride=2 * share)

    def whole(side, wanted):
        places = [(channel, col) for channel in wanted for col in range(near)]
        columns = []
        for first in range(0, len(places), slots):
            parts = []
            for channel, col in places[first : first + slots]:
                held = [stage_ref[line_rows(col * rows + row, side, channel), :] for row in range(rows)]
                parts.append(jnp.concatenate(held, axis=0))
            parts = swap_slots(parts, breadth)
            columns.append(
                jnp.concatenate(
                    [part[row * lines : (row + 1) * lines] for row in range(rows) for part in parts], axis=0
                )
            )
        return jnp.concatenate(columns, axis=1).astype(BF16)

    group = max(1, slots // near)
    for base in range(0, share, group):
        wanted = range(base, base + group)
        left, right = whole(0, wanted), whole(1, wanted)
        for place, channel in enumerate(wanted):
            mine = left
            if group > 1:
                lane = lax.broadcasted_iota(jnp.int32, left.shape, 1)
                mine = jnp.where(lane // (near * breadth) == place, left, jnp.zeros_like(left))
            combined = dot(mine, right, (1, 1) if outgoing else (0, 0))
            for high in range(cols // slots):
                lanes = slice(high * LANES, (high + 1) * LANES)
                parts = [
                    jnp.concatenate(
                        [
                            combined[(row * slots + slot) * lines : (row * slots + slot + 1) * lines, lanes]
                            for row in range(rows)
                        ],
                        axis=0,
                    )
                    for slot in range(slots)
                ]
                for low, part in enumerate(swap_slots(parts, breadth)):
                    for row in range(rows):
                        at = ((high * slots + low) * rows + row) * lines * pitch + channel
                        result_ref[pl.ds(at, lines, stride=pitch), :] = part[row * lines : (row + 1) * lines]
    if padded:
        for owner in range(rows * cols):
            held = [
                result_ref[(owner * lines + line) * pitch : (owner * lines + line) * pitch + share, :]
                for line in range(lines)
            ]
            combined_ref[owner] = jnp.concatenate(held, axis=0).astype(BF16)
    else:
        combined_ref[...] = result_ref[...].astype(BF16).reshape(combined_ref.shape)


def hold_combined(combined_ref, stage_ref):
    owners = stage_ref.shape[0] // combined_ref.shape[1]
    total = combined_ref[:owners].astype(F32)
    for first in range(owners, combined_ref.shape[0], owners):
        total = total + combined_ref[first : first + owners].astype(F32)
    stage_ref[...] = total.reshape(stage_ref.shape)


def read_combined(stage_ref, owners, lines, share, first, count):
    columns = []
    for line in range(first, first + count):
        if share % 8 == 0:
            held = [
                stage_ref[(owner * lines + line) * share : (owner * lines + line + 1) * share, :]
                for owner in range(owners)
            ]
            columns.append(jnp.concatenate(held, axis=0))
        else:
            columns.append(stage_ref[pl.ds(line, owners, stride=lines), :])
    return jnp.concatenate(columns, axis=1)


def middle_kernel(share, next_share, chunk, ins, outs, stage_ref, message_stage_ref):
    combined_ref, x_ref, gate_ref, mask_ref, gains_ref, proj_ref, gate_weight_ref, out_ref = ins
    message_ref, gate_out, next_ref = outs
    tokens = x_ref.shape[1]
    lines = tokens // LANES
    owners = x_ref.shape[0] // share
    hold_combined(combined_ref, stage_ref)
    mask = mask_ref[...]
    gain_out, gain = [spread_gain(gains_ref[n : n + 1, :]) for n in (0, 1)]
    out_t, proj_t, gate_t = out_ref[...].T, proj_ref[...].T, gate_weight_ref[...].T
    for start in range(0, tokens, chunk):
        here = slice(start, start + chunk)
        combined = read_combined(stage_ref, owners, lines, share, start // LANES, chunk // LANES)
        hidden = channel_norm(combined, gain_out)
        current = x_ref[:, here] + gate_ref[:, here] * dot(out_t, hidden)
        next_ref[:, here] = current
        normed = channel_norm(current, gain)
        emit_message(normed, proj_t, mask, start // LANES, message_ref, message_stage_ref, next_share)
        gate_out[:, here] = sigmoid(dot(gate_t, normed))


def last_kernel(share, chunk, ins, outs, stage_ref, result_ref, sems):
    combined_ref, x_ref, gate_ref, gains_ref, out_ref, up_ref, down_ref = ins
    (result_out,) = outs
    slots, lines, breadth, channels = result_ref.shape
    owners = x_ref.shape[0] // share
    half = down_ref.shape[0]
    count = chunk // LANES
    gain_out, gain = [spread_gain(gains_ref[n : n + 1, :]) for n in (2, 3)]
    out_t, up_t, down_t = out_ref[...].T, up_ref[...].T, down_ref[...].T
    hold_combined(combined_ref, stage_ref)
    writes = []
    for first in range(0, lines, count):
        here = slice(first * LANES, (first + count) * LANES)
        combined = read_combined(stage_ref, owners, lines, share, first, count)
        hidden = channel_norm(combined, gain_out)
        current = x_ref[:, here] + gate_ref[:, here] * dot(out_t, hidden)
        trans_in = channel_norm(current, gain)
        block = min(256, half)
        for base in range(0, half, block):
            gate_part = dot(up_t[base : base + block], trans_in)
            up_part = dot(up_t[half + base : half + base + block], trans_in)
            trans_hidden = (gate_part * sigmoid(gate_part) * up_part).astype(BF16)
            current = current + dot(down_t[:, base : base + block], trans_hidden)
        result = current.T
        for part in range(count):
            for slot in range(slots):
                base = part * LANES + slot * breadth
                result_ref[slot, first + part] = result[base : base + breadth]
        piece = slice(first, first + count)
        writes += start_all([(result_ref.at[:, piece], result_out.at[:, piece])], sems, first // count)
    for write in writes:
        write.wait()


def whole_spec(array):
    return pl.BlockSpec(array.shape, lambda step, dims=array.ndim: (0,) * dims)


def picked_spec(array, index):
    return pl.BlockSpec((None,) + array.shape[1:], lambda step: (index,) + (0,) * (array.ndim - 1))


def call(kernel, operands, outs, scratch=(), picks=None, in_hbm=False, out_hbm=False):
    in_place = pl.BlockSpec(memory_space=pltpu.HBM)
    specs = [
        picked_spec(array, picks[n]) if picks and n in picks else whole_spec(array)
        for n, array in enumerate(operands)
    ]
    shapes = [jax.ShapeDtypeStruct(shape, dtype) for shape, dtype in outs]
    count = len(operands)

    def body(*refs):
        kernel(refs[:count], refs[count : count + len(outs)], *refs[count + len(outs) :])

    return pl.pallas_call(
        body,
        grid=(1,),
        in_specs=[in_place] * count if in_hbm else specs,
        out_specs=[in_place if out_hbm else whole_spec(shape) for shape in shapes],
        out_shape=shapes,
        scratch_shapes=list(scratch),
        compiler_params=pltpu.CompilerParams(vmem_limit_bytes=FULL_VMEM_BYTES if in_hbm else VMEM_BYTES),
    )(*operands)


def exchange(values, axes):
    return lax.all_to_all(values, axes, split_axis=0, concat_axis=0, tiled=True)


def per_device(
    rows,
    halves,
    nears,
    pair_map,
    pair_mask,
    gain_in,
    proj_weight,
    gate_weight,
    gain_out,
    out_weight,
    trans_gain,
    trans_up,
    trans_down,
):
    height, breadth, channels = pair_map.shape
    tokens = height * breadth
    lines = tokens // LANES
    hid = gain_out.shape[1]
    cols = halves * nears
    owners = rows * cols
    share = hid // owners
    chunk = min(4 * LANES, tokens)
    split = halves if share % 8 == 0 else 1
    first_share = split * share
    held = ((LANES // breadth, lines, breadth, channels), F32)
    grouped = pair_map.reshape(held[0])
    wide, narrow = ((channels, tokens), F32), ((channels, tokens), BF16)
    result = pltpu.VMEM((owners * share * lines, LANES), F32)
    spare = pltpu.VMEM((8, LANES) if share % 8 == 0 else (owners * 2 * share * lines, LANES), F32)

    def message(own):
        return ((hid // own, 2 * own * lines, LANES), BF16)

    def combine(operands, own, outgoing):
        near = cols * share // own
        kernel = functools.partial(combine_kernel, rows, cols, near, breadth, own, outgoing)
        block = lines * pitch_of(own)
        scratch = [pltpu.VMEM((count * block, LANES), F32) for count in (2 * rows * near, owners)]
        answer = ((owners, own * lines, LANES), BF16)
        return exchange(call(kernel, operands, [answer], scratch)[0], ALL_AXES)

    both, normed = call(
        functools.partial(project_kernel, first_share),
        (grouped, pair_mask, gain_in, proj_weight),
        [message(first_share), narrow],
        (
            spare,
            pltpu.VMEM(*held),
            pltpu.VMEM(pair_mask.shape, jnp.int32),
            pltpu.VMEM(gain_in.shape, F32),
            pltpu.VMEM(proj_weight.shape[1:], BF16),
            pltpu.SemaphoreType.DMA((4,)),
        ),
        in_hbm=True,
    )
    gate, current, mask, gains = call(
        prepare_kernel,
        (normed, grouped, pair_mask, gate_weight, gain_in, gain_out, trans_gain.reshape(1, -1)),
        [wide, wide, ((lines, LANES), F32), ((8, channels), F32)],
        picks={3: 0},
    )
    both = exchange(both, NEAR_AXES if split > 1 else ALL_AXES)
    combined = combine((both, mask), first_share, True)
    both, gate, current = call(
        functools.partial(middle_kernel, first_share, share, chunk),
        (combined, current, gate, mask, gains, proj_weight, gate_weight, out_weight),
        [message(share), wide, wide],
        (result, spare),
        picks={5: 1, 6: 1, 7: 0},
    )
    combined = combine((exchange(both, ALL_AXES),), share, False)
    (pair_out,) = call(
        functools.partial(last_kernel, share, chunk),
        (combined, current, gate, gains, out_weight, trans_up, trans_down),
        [held],
        (result, pltpu.VMEM(*held), pltpu.SemaphoreType.DMA((tokens // chunk,))),
        picks={4: 1},
        out_hbm=True,
    )
    return pair_out.reshape(pair_map.shape)


def solution(mesh):
    groups, rows, cols = (mesh.shape[name] for name in ("grp", "row", "col"))
    halves = 2 if cols % 2 == 0 else 1
    nears = cols // halves
    folded = Mesh(mesh.devices.reshape(groups, rows, halves, nears), ("grp", "row", "half", "near"))
    tokens = (("grp", "row"), ("half", "near"))
    in_specs = (P(*tokens, None), P(*tokens)) + (P(),) * 8

    def body(*args):
        return per_device(rows, halves, nears, *args)

    return jax.shard_map(body, mesh=folded, in_specs=in_specs, out_specs=P(*tokens, None), check_vma=False)
```

```python
import functools

import jax
import jax.numpy as jnp
from jax import lax
from jax.experimental import pallas as pl
from jax.experimental.pallas import tpu as pltpu
from jax.sharding import Mesh
from jax.sharding import PartitionSpec as P

NEAR_AXES = ("near", "row")
ALL_AXES = ("half", "near", "row")
LANES = 128
VMEM_BYTES = 24 * 1024 * 1024
FULL_VMEM_BYTES = 60 * 1024 * 1024
F32, BF16 = jnp.float32, jnp.bfloat16


def dot(left, right, contract=(1, 0)):
    return lax.dot_general(
        left, right, (((contract[0],), (contract[1],)), ((), ())), preferred_element_type=F32
    )


def sigmoid(values):
    return 0.5 * jnp.tanh(0.5 * values) + 0.5


def channel_norm(values, gain):
    wide = jnp.concatenate([gain] * (values.shape[1] // LANES), axis=1)
    centred = values - jnp.mean(values, axis=0, keepdims=True)
    spread = jnp.mean(centred * centred, axis=0, keepdims=True)
    return (centred * lax.rsqrt(spread + 1e-05) * wide).astype(BF16)


def spread_gain(row):
    return jnp.broadcast_to(row, (LANES, row.shape[1])).T


def token_mask(mask, lines):
    height, breadth = mask.shape
    wide = jnp.concatenate([mask.astype(F32)] * (LANES // breadth), axis=1)
    row = lax.broadcasted_iota(jnp.int32, wide.shape, 0)
    lane = lax.broadcasted_iota(jnp.int32, wide.shape, 1)
    wide = jnp.where(row // lines == lane // breadth, wide, 0.0).astype(BF16)
    line = lax.broadcasted_iota(jnp.int32, (lines, height), 0)
    source = lax.broadcasted_iota(jnp.int32, (lines, height), 1)
    return dot((source % lines == line).astype(BF16), wide)


def emit_message(normed, weight_t, mask, line, message_ref, stage_ref, share):
    projected = dot(weight_t, normed)
    hid = weight_t.shape[0] // 4
    owners = hid // share
    for part in range(normed.shape[1] // LANES):
        here = projected[:, part * LANES : (part + 1) * LANES]
        at = line + part
        keep = mask[at : at + 1]
        left = sigmoid(here[:hid]) * here[hid : 2 * hid] * keep
        right = sigmoid(here[2 * hid : 3 * hid]) * here[3 * hid :] * keep
        if share % 8 == 0:
            for owner in range(owners):
                rows = slice(owner * share, (owner + 1) * share)
                both = jnp.concatenate([left[rows], right[rows]], axis=0).astype(BF16)
                message_ref[owner, 2 * share * at : 2 * share * (at + 1), :] = both
        else:
            lines = message_ref.shape[1] // 2
            stage_ref[pl.ds(2 * at, owners, stride=2 * lines), :] = left
            stage_ref[pl.ds(2 * at + 1, owners, stride=2 * lines), :] = right
    if share % 8 and line + normed.shape[1] // LANES == mask.shape[0]:
        message_ref[...] = stage_ref[...].astype(BF16).reshape(message_ref.shape)


def start_all(pairs, sems, first=0):
    copies = [pltpu.make_async_copy(src, dst, sems.at[first + n]) for n, (src, dst) in enumerate(pairs)]
    for copy in copies:
        copy.start()
    return copies


def line_tokens(x_ref, line):
    return jnp.concatenate([x_ref[slot, line] for slot in range(x_ref.shape[0])], axis=0)


def project_kernel(share, ins, outs, stage_ref, x_ref, mask_ref, gain_ref, weight_ref, sems):
    message_ref, normed_ref = outs
    x_in, mask_in, gain_in, weight_in = ins
    lines = x_ref.shape[1]
    pairs = [(weight_in.at[0], weight_ref), (x_in, x_ref), (gain_in, gain_ref), (mask_in, mask_ref)]
    for copy in start_all(pairs, sems):
        copy.wait()
    mask = token_mask(mask_ref[...], lines)
    current = jnp.concatenate([line_tokens(x_ref, line).T for line in range(lines)], axis=1)
    normed = channel_norm(current, spread_gain(gain_ref[0:1, :]))
    emit_message(normed, weight_ref[...].T, mask, 0, message_ref, stage_ref, share)
    normed_ref[...] = normed


def prepare_kernel(ins, outs):
    normed_ref, x_ref, mask_ref, gate_ref, gain_in_ref, gain_out_ref, trans_gain_ref = ins
    gate_out, x_out, mask_out, gains_out = outs
    lines = x_ref.shape[1]
    gate_out[...] = sigmoid(dot(gate_ref[...].T, normed_ref[...]))
    for line in range(lines):
        x_out[:, line * LANES : (line + 1) * LANES] = line_tokens(x_ref, line).T
    mask_out[...] = token_mask(mask_ref[...], lines)
    rows = [gain_out_ref[0:1, :], gain_in_ref[1:2, :], gain_out_ref[1:2, :], trans_gain_ref[...]]
    gains_out[...] = jnp.concatenate(rows + rows, axis=0)


def one_hot(rows, columns, wanted):
    row = lax.broadcasted_iota(jnp.int32, (rows, columns), 0)
    column = lax.broadcasted_iota(jnp.int32, (rows, columns), 1)
    return (wanted(row) == column).astype(BF16)


def swap_matrix(slots, breadth):
    size = slots * LANES
    return one_hot(
        size, size, lambda lane: lane // breadth % slots * LANES + lane // LANES * breadth + lane % breadth
    )


def combine_kernel(rows, cols, near, breadth, share, outgoing, ins, outs):
    both_ref, combined_ref = ins[0], outs[0]
    slots = LANES // breadth
    span = both_ref.shape[1]
    lines = span // (2 * share)
    pack = max(1, slots // near)
    groups = share // pack
    size = span // pack
    swap = swap_matrix(slots, breadth)

    def source(row):
        channel = row // size * groups + row // lines % groups
        return row % lines * (2 * share) + row // (groups * lines) % 2 * share + channel

    order = one_hot(span, span, source)
    wide = []
    for row in range(rows):
        here = jnp.concatenate([both_ref[col * rows + row] for col in range(near)], axis=1)
        here = dot(order, here).astype(BF16)
        wide.append(jnp.concatenate([here[n * size : (n + 1) * size] for n in range(pack)], axis=1))
    wide = jnp.concatenate(wide, axis=0)
    block = slots * LANES
    swapped = [dot(wide[:, first : first + block], swap) for first in range(0, wide.shape[1], block)]

    def whole(side, group):
        columns = []
        for part in swapped:
            held = []
            for row in range(rows):
                first = row * size + (side * groups + group) * lines
                held += [part[first : first + lines, slot * LANES : (slot + 1) * LANES] for slot in range(slots)]
            columns.append(jnp.concatenate(held, axis=0))
        return jnp.concatenate(columns, axis=1).astype(BF16)

    products = [None] * share
    for group in range(groups):
        left, right = whole(0, group), whole(1, group)
        for place in range(pack):
            mine = left
            if pack > 1:
                lane = lax.broadcasted_iota(jnp.int32, left.shape, 1)
                mine = jnp.where(lane // (near * breadth) == place, left, jnp.zeros_like(left))
            products[place * groups + group] = dot(mine, right, (1, 1) if outgoing else (0, 0))

    for high in range(cols // slots):
        lanes = slice(high * LANES, (high + 1) * LANES)
        held = []
        for row in range(rows):
            for product in products:
                parts = [
                    product[(row * slots + slot) * lines : (row * slots + slot + 1) * lines, lanes]
                    for slot in range(slots)
                ]
                held.append(jnp.concatenate(parts, axis=1))
        back = dot(jnp.concatenate(held, axis=0).astype(BF16), swap).astype(BF16)
        for low in range(slots):
            for row in range(rows):
                first = row * share * lines
                combined_ref[(high * slots + low) * rows + row] = back[
                    first : first + share * lines, low * LANES : (low + 1) * LANES
                ]


def hold_combined(combined_ref, stage_ref, share):
    span = combined_ref.shape[1]
    lines = span // share
    owners = stage_ref.shape[0] // span
    halves = combined_ref.shape[0] // owners
    order = one_hot(span, span, lambda row: row % share * lines + row // share)
    order = jnp.concatenate([order] * halves, axis=1)
    for first in range(0, owners, 2):
        blocks = [
            jnp.concatenate([combined_ref[half * owners + owner] for half in range(halves)], axis=0)
            for owner in (first, first + 1)
        ]
        ordered = dot(order, jnp.concatenate(blocks, axis=1))
        for n in range(2):
            stage_ref[(first + n) * span : (first + n + 1) * span, :] = ordered[:, n * LANES : (n + 1) * LANES]


def read_combined(stage_ref, owners, lines, share, first, count):
    columns = []
    for line in range(first, first + count):
        if share % 8 == 0:
            held = [
                stage_ref[(owner * lines + line) * share : (owner * lines + line + 1) * share, :]
                for owner in range(owners)
            ]
            columns.append(jnp.concatenate(held, axis=0))
        else:
            columns.append(stage_ref[pl.ds(line, owners, stride=lines), :])
    return jnp.concatenate(columns, axis=1)


def middle_kernel(share, next_share, chunk, ins, outs, stage_ref, message_stage_ref):
    combined_ref, x_ref, gate_ref, mask_ref, gains_ref, proj_ref, gate_weight_ref, out_ref = ins
    message_ref, gate_out, next_ref = outs
    tokens = x_ref.shape[1]
    lines = tokens // LANES
    owners = x_ref.shape[0] // share
    hold_combined(combined_ref, stage_ref, share)
    mask = mask_ref[...]
    gain_out, gain = [spread_gain(gains_ref[n : n + 1, :]) for n in (0, 1)]
    out_t, proj_t, gate_t = out_ref[...].T, proj_ref[...].T, gate_weight_ref[...].T
    for start in range(0, tokens, chunk):
        here = slice(start, start + chunk)
        combined = read_combined(stage_ref, owners, lines, share, start // LANES, chunk // LANES)
        hidden = channel_norm(combined, gain_out)
        current = x_ref[:, here] + gate_ref[:, here] * dot(out_t, hidden)
        next_ref[:, here] = current
        normed = channel_norm(current, gain)
        emit_message(normed, proj_t, mask, start // LANES, message_ref, message_stage_ref, next_share)
        gate_out[:, here] = sigmoid(dot(gate_t, normed))


def last_kernel(share, chunk, ins, outs, stage_ref, result_ref, sems):
    combined_ref, x_ref, gate_ref, gains_ref, out_ref, up_ref, down_ref = ins
    (result_out,) = outs
    slots, lines, breadth, channels = result_ref.shape
    owners = x_ref.shape[0] // share
    half = down_ref.shape[0]
    count = chunk // LANES
    gain_out, gain = [spread_gain(gains_ref[n : n + 1, :]) for n in (2, 3)]
    out_t, up_t, down_t = out_ref[...].T, up_ref[...].T, down_ref[...].T
    hold_combined(combined_ref, stage_ref, share)
    writes = []
    for first in range(0, lines, count):
        here = slice(first * LANES, (first + count) * LANES)
        combined = read_combined(stage_ref, owners, lines, share, first, count)
        hidden = channel_norm(combined, gain_out)
        current = x_ref[:, here] + gate_ref[:, here] * dot(out_t, hidden)
        trans_in = channel_norm(current, gain)
        block = min(256, half)
        for base in range(0, half, block):
            gate_part = dot(up_t[base : base + block], trans_in)
            up_part = dot(up_t[half + base : half + base + block], trans_in)
            trans_hidden = (gate_part * sigmoid(gate_part) * up_part).astype(BF16)
            current = current + dot(down_t[:, base : base + block], trans_hidden)
        result = current.T
        for part in range(count):
            for slot in range(slots):
                base = part * LANES + slot * breadth
                result_ref[slot, first + part] = result[base : base + breadth]
        piece = slice(first, first + count)
        writes += start_all([(result_ref.at[:, piece], result_out.at[:, piece])], sems, first // count)
    for write in writes:
        write.wait()


def whole_spec(array):
    return pl.BlockSpec(array.shape, lambda step, dims=array.ndim: (0,) * dims)


def picked_spec(array, index):
    return pl.BlockSpec((None,) + array.shape[1:], lambda step: (index,) + (0,) * (array.ndim - 1))


def call(kernel, operands, outs, scratch=(), picks=None, in_hbm=False, out_hbm=False):
    in_place = pl.BlockSpec(memory_space=pltpu.HBM)
    specs = [
        picked_spec(array, picks[n]) if picks and n in picks else whole_spec(array)
        for n, array in enumerate(operands)
    ]
    shapes = [jax.ShapeDtypeStruct(shape, dtype) for shape, dtype in outs]
    count = len(operands)

    def body(*refs):
        kernel(refs[:count], refs[count : count + len(outs)], *refs[count + len(outs) :])

    return pl.pallas_call(
        body,
        grid=(1,),
        in_specs=[in_place] * count if in_hbm else specs,
        out_specs=[in_place if out_hbm else whole_spec(shape) for shape in shapes],
        out_shape=shapes,
        scratch_shapes=list(scratch),
        compiler_params=pltpu.CompilerParams(vmem_limit_bytes=FULL_VMEM_BYTES if in_hbm else VMEM_BYTES),
    )(*operands)


def exchange(values, axes):
    return lax.all_to_all(values, axes, split_axis=0, concat_axis=0, tiled=True)


def per_device(
    rows,
    halves,
    nears,
    pair_map,
    pair_mask,
    gain_in,
    proj_weight,
    gate_weight,
    gain_out,
    out_weight,
    trans_gain,
    trans_up,
    trans_down,
):
    height, breadth, channels = pair_map.shape
    tokens = height * breadth
    lines = tokens // LANES
    hid = gain_out.shape[1]
    cols = halves * nears
    owners = rows * cols
    share = hid // owners
    chunk = min(4 * LANES, tokens)
    split = halves if share % 8 == 0 else 1
    first_share = split * share
    held = ((LANES // breadth, lines, breadth, channels), F32)
    grouped = pair_map.reshape(held[0])
    wide, narrow = ((channels, tokens), F32), ((channels, tokens), BF16)
    result = pltpu.VMEM((owners * share * lines, LANES), F32)
    spare = pltpu.VMEM((8, LANES) if share % 8 == 0 else (owners * 2 * share * lines, LANES), F32)

    def message(own):
        return ((hid // own, 2 * own * lines, LANES), BF16)

    def combine(operands, own, outgoing):
        near = cols * share // own
        kernel = functools.partial(combine_kernel, rows, cols, near, breadth, own, outgoing)
        answer = ((owners, own * lines, LANES), BF16)
        return exchange(call(kernel, operands, [answer])[0], ALL_AXES)

    both, normed = call(
        functools.partial(project_kernel, first_share),
        (grouped, pair_mask, gain_in, proj_weight),
        [message(first_share), narrow],
        (
            spare,
            pltpu.VMEM(*held),
            pltpu.VMEM(pair_mask.shape, jnp.int32),
            pltpu.VMEM(gain_in.shape, F32),
            pltpu.VMEM(proj_weight.shape[1:], BF16),
            pltpu.SemaphoreType.DMA((4,)),
        ),
        in_hbm=True,
    )
    gate, current, mask, gains = call(
        prepare_kernel,
        (normed, grouped, pair_mask, gate_weight, gain_in, gain_out, trans_gain.reshape(1, -1)),
        [wide, wide, ((lines, LANES), F32), ((8, channels), F32)],
        picks={3: 0},
    )
    both = exchange(both, NEAR_AXES if split > 1 else ALL_AXES)
    combined = combine((both, mask), first_share, True)
    both, gate, current = call(
        functools.partial(middle_kernel, first_share, share, chunk),
        (combined, current, gate, mask, gains, proj_weight, gate_weight, out_weight),
        [message(share), wide, wide],
        (result, spare),
        picks={5: 1, 6: 1, 7: 0},
    )
    combined = combine((exchange(both, ALL_AXES),), share, False)
    (pair_out,) = call(
        functools.partial(last_kernel, share, chunk),
        (combined, current, gate, gains, out_weight, trans_up, trans_down),
        [held],
        (result, pltpu.VMEM(*held), pltpu.SemaphoreType.DMA((tokens // chunk,))),
        picks={4: 1},
        out_hbm=True,
    )
    return pair_out.reshape(pair_map.shape)


def solution(mesh):
    groups, rows, cols = (mesh.shape[name] for name in ("grp", "row", "col"))
    halves = 2 if cols % 2 == 0 else 1
    nears = cols // halves
    folded = Mesh(mesh.devices.reshape(groups, rows, halves, nears), ("grp", "row", "half", "near"))
    tokens = (("grp", "row"), ("half", "near"))
    in_specs = (P(*tokens, None), P(*tokens)) + (P(),) * 8

    def body(*args):
        return per_device(rows, halves, nears, *args)

    return jax.shard_map(body, mesh=folded, in_specs=in_specs, out_specs=P(*tokens, None), check_vma=False)
```

```python
import functools

import jax
import jax.numpy as jnp
from jax import lax
from jax.experimental import pallas as pl
from jax.experimental.pallas import tpu as pltpu
from jax.sharding import Mesh
from jax.sharding import PartitionSpec as P

NEAR_AXES = ("near", "row")
ALL_AXES = ("half", "near", "row")
LANES = 128
VMEM_BYTES = 24 * 1024 * 1024
FULL_VMEM_BYTES = 60 * 1024 * 1024
F32, BF16 = jnp.float32, jnp.bfloat16


def dot(left, right, contract=(1, 0)):
    return lax.dot_general(
        left, right, (((contract[0],), (contract[1],)), ((), ())), preferred_element_type=F32
    )


def halved(weight):
    return weight.T * 0.5


def twice_sigmoid(half):
    return jnp.tanh(half) + 1.0


def channel_norm(values, gain):
    wide = jnp.concatenate([gain] * (values.shape[1] // LANES), axis=1)
    centred = values - jnp.mean(values, axis=0, keepdims=True)
    spread = jnp.mean(centred * centred, axis=0, keepdims=True)
    return (centred * lax.rsqrt(spread + 1e-05) * wide).astype(BF16)


def spread_gain(row):
    return jnp.broadcast_to(row, (LANES, row.shape[1])).T


def token_mask(mask, lines):
    height, breadth = mask.shape
    wide = jnp.concatenate([mask.astype(F32)] * (LANES // breadth), axis=1)
    row = lax.broadcasted_iota(jnp.int32, wide.shape, 0)
    lane = lax.broadcasted_iota(jnp.int32, wide.shape, 1)
    wide = jnp.where(row // lines == lane // breadth, wide, 0.0).astype(BF16)
    line = lax.broadcasted_iota(jnp.int32, (lines, height), 0)
    source = lax.broadcasted_iota(jnp.int32, (lines, height), 1)
    return dot((source % lines == line).astype(BF16), wide)


def emit_message(normed, weight_t, mask, line, message_ref, stage_ref, share):
    projected = dot(weight_t, normed)
    hid = weight_t.shape[0] // 4
    owners = hid // share
    for part in range(normed.shape[1] // LANES):
        here = projected[:, part * LANES : (part + 1) * LANES]
        at = line + part
        keep = mask[at : at + 1]
        left = twice_sigmoid(here[:hid]) * here[hid : 2 * hid] * keep
        right = twice_sigmoid(here[2 * hid : 3 * hid]) * here[3 * hid :] * keep
        if share % 8 == 0:
            for owner in range(owners):
                rows = slice(owner * share, (owner + 1) * share)
                both = jnp.concatenate([left[rows], right[rows]], axis=0).astype(BF16)
                message_ref[owner, 2 * share * at : 2 * share * (at + 1), :] = both
        else:
            lines = message_ref.shape[1] // 2
            stage_ref[pl.ds(2 * at, owners, stride=2 * lines), :] = left
            stage_ref[pl.ds(2 * at + 1, owners, stride=2 * lines), :] = right
    if share % 8 and line + normed.shape[1] // LANES == mask.shape[0]:
        message_ref[...] = stage_ref[...].astype(BF16).reshape(message_ref.shape)


def start_all(pairs, sems, first=0):
    copies = [pltpu.make_async_copy(src, dst, sems.at[first + n]) for n, (src, dst) in enumerate(pairs)]
    for copy in copies:
        copy.start()
    return copies


def line_tokens(x_ref, line):
    return jnp.concatenate([x_ref[slot, line] for slot in range(x_ref.shape[0])], axis=0)


def project_kernel(share, ins, outs, stage_ref, x_ref, mask_ref, gain_ref, weight_ref, sems):
    (message_ref,) = outs
    x_in, mask_in, gain_in, weight_in = ins
    lines = x_ref.shape[1]
    pairs = [(weight_in.at[0], weight_ref), (x_in, x_ref), (gain_in, gain_ref), (mask_in, mask_ref)]
    for copy in start_all(pairs, sems):
        copy.wait()
    mask = token_mask(mask_ref[...], lines)
    current = jnp.concatenate([line_tokens(x_ref, line).T for line in range(lines)], axis=1)
    normed = channel_norm(current, spread_gain(gain_ref[0:1, :]))
    emit_message(normed, halved(weight_ref[...]), mask, 0, message_ref, stage_ref, share)


def prepare_kernel(ins, outs):
    x_ref, mask_ref, gate_ref, gain_in_ref, gain_out_ref, trans_gain_ref = ins
    gate_out, x_out, mask_out, gains_out = outs
    lines = x_ref.shape[1]
    current = jnp.concatenate([line_tokens(x_ref, line).T for line in range(lines)], axis=1)
    x_out[...] = current
    normed = channel_norm(current, spread_gain(gain_in_ref[0:1, :]))
    gate_out[...] = twice_sigmoid(dot(halved(gate_ref[0]), normed))
    mask_out[...] = token_mask(mask_ref[...], lines)
    rows = [gain_out_ref[0:1, :], gain_in_ref[1:2, :], gain_out_ref[1:2, :], trans_gain_ref[...]]
    gains_out[...] = jnp.concatenate(rows + rows, axis=0)


def one_hot(rows, columns, wanted):
    row = lax.broadcasted_iota(jnp.int32, (rows, columns), 0)
    column = lax.broadcasted_iota(jnp.int32, (rows, columns), 1)
    return (wanted(row) == column).astype(BF16)


def swap_matrix(slots, breadth):
    size = slots * LANES
    return one_hot(
        size, size, lambda lane: lane // breadth % slots * LANES + lane // LANES * breadth + lane % breadth
    )


def combine_kernel(rows, cols, near, breadth, share, outgoing, ins, outs):
    both_ref, combined_ref = ins[0], outs[0]
    slots = LANES // breadth
    span = both_ref.shape[1]
    lines = span // (2 * share)
    pack = max(1, slots // near)
    groups = share // pack
    size = span // pack
    swap = swap_matrix(slots, breadth)

    def source(row):
        channel = row // size * groups + row // lines % groups
        return row % lines * (2 * share) + row // (groups * lines) % 2 * share + channel

    order = one_hot(span, span, source)
    wide = []
    for row in range(rows):
        here = jnp.concatenate([both_ref[col * rows + row] for col in range(near)], axis=1)
        here = dot(order, here).astype(BF16)
        wide.append(jnp.concatenate([here[n * size : (n + 1) * size] for n in range(pack)], axis=1))
    wide = jnp.concatenate(wide, axis=0)
    block = slots * LANES
    swapped = [dot(wide[:, first : first + block], swap) for first in range(0, wide.shape[1], block)]

    def whole(side, group):
        columns = []
        for part in swapped:
            held = []
            for row in range(rows):
                first = row * size + (side * groups + group) * lines
                held += [part[first : first + lines, slot * LANES : (slot + 1) * LANES] for slot in range(slots)]
            columns.append(jnp.concatenate(held, axis=0))
        return jnp.concatenate(columns, axis=1).astype(BF16)

    products = [None] * share
    for group in range(groups):
        left, right = whole(0, group), whole(1, group)
        for place in range(pack):
            mine = left
            if pack > 1:
                lane = lax.broadcasted_iota(jnp.int32, left.shape, 1)
                mine = jnp.where(lane // (near * breadth) == place, left, jnp.zeros_like(left))
            products[place * groups + group] = dot(mine, right, (1, 1) if outgoing else (0, 0))

    for high in range(cols // slots):
        lanes = slice(high * LANES, (high + 1) * LANES)
        held = []
        for row in range(rows):
            for product in products:
                parts = [
                    product[(row * slots + slot) * lines : (row * slots + slot + 1) * lines, lanes]
                    for slot in range(slots)
                ]
                held.append(jnp.concatenate(parts, axis=1))
        back = dot(jnp.concatenate(held, axis=0).astype(BF16), swap).astype(BF16)
        for low in range(slots):
            for row in range(rows):
                first = row * share * lines
                combined_ref[(high * slots + low) * rows + row] = back[
                    first : first + share * lines, low * LANES : (low + 1) * LANES
                ]


def hold_combined(combined_ref, stage_ref, share):
    span = combined_ref.shape[1]
    lines = span // share
    owners = stage_ref.shape[0] // span
    halves = combined_ref.shape[0] // owners
    order = one_hot(span, span, lambda row: row % share * lines + row // share)
    order = jnp.concatenate([order] * halves, axis=1)
    for first in range(0, owners, 2):
        blocks = [
            jnp.concatenate([combined_ref[half * owners + owner] for half in range(halves)], axis=0)
            for owner in (first, first + 1)
        ]
        ordered = dot(order, jnp.concatenate(blocks, axis=1))
        for n in range(2):
            stage_ref[(first + n) * span : (first + n + 1) * span, :] = ordered[:, n * LANES : (n + 1) * LANES]


def read_combined(stage_ref, owners, lines, share, first, count):
    columns = []
    for line in range(first, first + count):
        if share % 8 == 0:
            held = [
                stage_ref[(owner * lines + line) * share : (owner * lines + line + 1) * share, :]
                for owner in range(owners)
            ]
            columns.append(jnp.concatenate(held, axis=0))
        else:
            columns.append(stage_ref[pl.ds(line, owners, stride=lines), :])
    return jnp.concatenate(columns, axis=1)


def middle_kernel(share, next_share, chunk, ins, outs, stage_ref, message_stage_ref):
    combined_ref, x_ref, gate_ref, mask_ref, gains_ref, proj_ref, gate_weight_ref, out_ref = ins
    message_ref, gate_out, next_ref = outs
    tokens = x_ref.shape[1]
    lines = tokens // LANES
    owners = x_ref.shape[0] // share
    hold_combined(combined_ref, stage_ref, share)
    mask = mask_ref[...]
    gain_out, gain = [spread_gain(gains_ref[n : n + 1, :]) for n in (0, 1)]
    out_t, proj_t, gate_t = halved(out_ref[0]), halved(proj_ref[1]), halved(gate_weight_ref[1])
    for start in range(0, tokens, chunk):
        here = slice(start, start + chunk)
        combined = read_combined(stage_ref, owners, lines, share, start // LANES, chunk // LANES)
        hidden = channel_norm(combined, gain_out)
        current = x_ref[:, here] + gate_ref[:, here] * dot(out_t, hidden)
        next_ref[:, here] = current
        normed = channel_norm(current, gain)
        emit_message(normed, proj_t, mask, start // LANES, message_ref, message_stage_ref, next_share)
        gate_out[:, here] = twice_sigmoid(dot(gate_t, normed))


def last_kernel(share, chunk, ins, outs, stage_ref, result_ref, sems):
    combined_ref, x_ref, gate_ref, gains_ref, out_ref, up_ref, down_ref = ins
    (result_out,) = outs
    slots, lines, breadth, channels = result_ref.shape
    owners = x_ref.shape[0] // share
    half = down_ref.shape[0]
    count = chunk // LANES
    gain_out, gain = [spread_gain(gains_ref[n : n + 1, :]) for n in (2, 3)]
    out_t, down_t = halved(out_ref[1]), down_ref[...].T
    gate_t, up_t = halved(up_ref[:, :half]), up_ref[:, half:].T
    hold_combined(combined_ref, stage_ref, share)
    writes = []
    for first in range(0, lines, count):
        here = slice(first * LANES, (first + count) * LANES)
        combined = read_combined(stage_ref, owners, lines, share, first, count)
        hidden = channel_norm(combined, gain_out)
        current = x_ref[:, here] + gate_ref[:, here] * dot(out_t, hidden)
        trans_in = channel_norm(current, gain)
        block = min(256, half)
        for base in range(0, half, block):
            gate_part = dot(gate_t[base : base + block], trans_in)
            up_part = dot(up_t[base : base + block], trans_in)
            trans_hidden = (gate_part * twice_sigmoid(gate_part) * up_part).astype(BF16)
            current = current + dot(down_t[:, base : base + block], trans_hidden)
        result = current.T
        for part in range(count):
            for slot in range(slots):
                base = part * LANES + slot * breadth
                result_ref[slot, first + part] = result[base : base + breadth]
        piece = slice(first, first + count)
        writes += start_all([(result_ref.at[:, piece], result_out.at[:, piece])], sems, first // count)
    for write in writes:
        write.wait()


def call(kernel, operands, outs, scratch=(), in_hbm=False, out_hbm=False):
    in_place, held = pl.BlockSpec(memory_space=pltpu.HBM), pl.BlockSpec(memory_space=pltpu.VMEM)
    count = len(operands)

    def body(*refs):
        kernel(refs[:count], refs[count : count + len(outs)], *refs[count + len(outs) :])

    return pl.pallas_call(
        body,
        in_specs=[in_place if in_hbm else held] * count,
        out_specs=[in_place if out_hbm else held] * len(outs),
        out_shape=[jax.ShapeDtypeStruct(shape, dtype) for shape, dtype in outs],
        scratch_shapes=list(scratch),
        compiler_params=pltpu.CompilerParams(vmem_limit_bytes=FULL_VMEM_BYTES if in_hbm else VMEM_BYTES),
    )(*operands)


def exchange(values, axes):
    return lax.all_to_all(values, axes, split_axis=0, concat_axis=0, tiled=True)


def per_device(
    rows,
    halves,
    nears,
    pair_map,
    pair_mask,
    gain_in,
    proj_weight,
    gate_weight,
    gain_out,
    out_weight,
    trans_gain,
    trans_up,
    trans_down,
):
    height, breadth, channels = pair_map.shape
    tokens = height * breadth
    lines = tokens // LANES
    hid = gain_out.shape[1]
    cols = halves * nears
    owners = rows * cols
    share = hid // owners
    chunk = min(4 * LANES, tokens)
    split = halves if share % 8 == 0 else 1
    first_share = split * share
    held = ((LANES // breadth, lines, breadth, channels), F32)
    grouped = pair_map.reshape(held[0])
    wide = ((channels, tokens), F32)
    result = pltpu.VMEM((owners * share * lines, LANES), F32)
    spare = pltpu.VMEM((8, LANES) if share % 8 == 0 else (owners * 2 * share * lines, LANES), F32)

    def message(own):
        return ((hid // own, 2 * own * lines, LANES), BF16)

    def combine(operands, own, outgoing):
        near = cols * share // own
        kernel = functools.partial(combine_kernel, rows, cols, near, breadth, own, outgoing)
        answer = ((owners, own * lines, LANES), BF16)
        return exchange(call(kernel, operands, [answer])[0], ALL_AXES)

    (both,) = call(
        functools.partial(project_kernel, first_share),
        (grouped, pair_mask, gain_in, proj_weight),
        [message(first_share)],
        (
            spare,
            pltpu.VMEM(*held),
            pltpu.VMEM(pair_mask.shape, jnp.int32),
            pltpu.VMEM(gain_in.shape, F32),
            pltpu.VMEM(proj_weight.shape[1:], BF16),
            pltpu.SemaphoreType.DMA((4,)),
        ),
        in_hbm=True,
    )
    gate, current, mask, gains = call(
        prepare_kernel,
        (grouped, pair_mask, gate_weight, gain_in, gain_out, trans_gain.reshape(1, -1)),
        [wide, wide, ((lines, LANES), F32), ((8, channels), F32)],
    )
    both = exchange(both, NEAR_AXES if split > 1 else ALL_AXES)
    combined = combine((both, mask), first_share, True)
    both, gate, current = call(
        functools.partial(middle_kernel, first_share, share, chunk),
        (combined, current, gate, mask, gains, proj_weight, gate_weight, out_weight),
        [message(share), wide, wide],
        (result, spare),
    )
    combined = combine((exchange(both, ALL_AXES),), share, False)
    (pair_out,) = call(
        functools.partial(last_kernel, share, chunk),
        (combined, current, gate, gains, out_weight, trans_up, trans_down),
        [held],
        (result, pltpu.VMEM(*held), pltpu.SemaphoreType.DMA((tokens // chunk,))),
        out_hbm=True,
    )
    return pair_out.reshape(pair_map.shape)


def solution(mesh):
    groups, rows, cols = (mesh.shape[name] for name in ("grp", "row", "col"))
    halves = 2 if cols % 2 == 0 else 1
    nears = cols // halves
    folded = Mesh(mesh.devices.reshape(groups, rows, halves, nears), ("grp", "row", "half", "near"))
    tokens = (("grp", "row"), ("half", "near"))
    in_specs = (P(*tokens, None), P(*tokens)) + (P(),) * 8

    def body(*args):
        return per_device(rows, halves, nears, *args)

    return jax.shard_map(body, mesh=folded, in_specs=in_specs, out_specs=P(*tokens, None), check_vma=False)
```

```python
import functools

import jax
import jax.numpy as jnp
from jax import lax
from jax.experimental import pallas as pl
from jax.experimental.pallas import tpu as pltpu
from jax.sharding import Mesh
from jax.sharding import PartitionSpec as P

NEAR_AXES = ("near", "row")
ALL_AXES = ("near", "row", "half")
LANES = 128
VMEM_BYTES = 24 * 1024 * 1024
FULL_VMEM_BYTES = 60 * 1024 * 1024
F32, BF16 = jnp.float32, jnp.bfloat16


def count_devices(axes, sizes):
    found = {}
    for half in range(sizes["half"]):
        for near in range(sizes["near"]):
            for row in range(sizes["row"]):
                index, at = 0, {"half": half, "near": near, "row": row}
                for axis in axes:
                    index = index * sizes[axis] + at[axis]
                found[half, near, row] = index
    return found


def dot(left, right, contract=(1, 0)):
    return lax.dot_general(
        left, right, (((contract[0],), (contract[1],)), ((), ())), preferred_element_type=F32
    )


def halved(weight):
    return weight.T * 0.5


def twice_sigmoid(half):
    return jnp.tanh(half) + 1.0


def channel_norm(values, gain):
    wide = jnp.concatenate([gain] * (values.shape[1] // LANES), axis=1)
    centred = values - jnp.mean(values, axis=0, keepdims=True)
    spread = jnp.mean(centred * centred, axis=0, keepdims=True)
    return (centred * lax.rsqrt(spread + 1e-05) * wide).astype(BF16)


def spread_gain(row):
    return jnp.broadcast_to(row, (LANES, row.shape[1])).T


def token_mask(mask, lines):
    height, breadth = mask.shape
    wide = jnp.concatenate([mask.astype(F32)] * (LANES // breadth), axis=1)
    row = lax.broadcasted_iota(jnp.int32, wide.shape, 0)
    lane = lax.broadcasted_iota(jnp.int32, wide.shape, 1)
    wide = jnp.where(row // lines == lane // breadth, wide, 0.0).astype(BF16)
    line = lax.broadcasted_iota(jnp.int32, (lines, height), 0)
    source = lax.broadcasted_iota(jnp.int32, (lines, height), 1)
    return dot((source % lines == line).astype(BF16), wide)


def emit_message(normed, weight_t, mask, line, message_ref, stage_ref, share):
    projected = dot(weight_t, normed)
    hid = weight_t.shape[0] // 4
    owners = hid // share
    for part in range(normed.shape[1] // LANES):
        here = projected[:, part * LANES : (part + 1) * LANES]
        at = line + part
        keep = mask[at : at + 1]
        left = twice_sigmoid(here[:hid]) * here[hid : 2 * hid] * keep
        right = twice_sigmoid(here[2 * hid : 3 * hid]) * here[3 * hid :] * keep
        if share % 8 == 0:
            for owner in range(owners):
                rows = slice(owner * share, (owner + 1) * share)
                both = jnp.concatenate([left[rows], right[rows]], axis=0).astype(BF16)
                message_ref[owner, 2 * share * at : 2 * share * (at + 1), :] = both
        else:
            lines = message_ref.shape[1] // 2
            stage_ref[pl.ds(2 * at, owners, stride=2 * lines), :] = left
            stage_ref[pl.ds(2 * at + 1, owners, stride=2 * lines), :] = right
    if share % 8 and line + normed.shape[1] // LANES == mask.shape[0]:
        message_ref[...] = stage_ref[...].astype(BF16).reshape(message_ref.shape)


def start_all(pairs, sems, first=0):
    copies = [pltpu.make_async_copy(src, dst, sems.at[first + n]) for n, (src, dst) in enumerate(pairs)]
    for copy in copies:
        copy.start()
    return copies


def line_tokens(x_ref, line):
    return jnp.concatenate([x_ref[slot, line] for slot in range(x_ref.shape[0])], axis=0)


def project_kernel(share, ins, outs, stage_ref, x_ref, mask_ref, gain_ref, weight_ref, message_ref, sems, out_sems):
    (message_out,) = outs
    x_in, mask_in, gain_in, weight_in = ins
    lines = x_ref.shape[1]
    pairs = [(gain_in, gain_ref), (mask_in, mask_ref), (weight_in.at[0], weight_ref)]
    pairs += [(x_in.at[slot], x_ref.at[slot]) for slot in range(x_ref.shape[0])]
    for copy in start_all(pairs, sems):
        copy.wait()
    mask = token_mask(mask_ref[...], lines)
    current = jnp.concatenate([line_tokens(x_ref, line).T for line in range(lines)], axis=1)
    normed = channel_norm(current, spread_gain(gain_ref[0:1, :]))
    emit_message(normed, halved(weight_ref[...]), mask, 0, message_ref, stage_ref, share)
    size = message_ref.shape[0] // out_sems.shape[0]
    blocks = [pl.ds(first, size) for first in range(0, message_ref.shape[0], size)]
    for copy in start_all([(message_ref.at[block], message_out.at[block]) for block in blocks], out_sems):
        copy.wait()


def prepare_kernel(ins, outs):
    x_ref, mask_ref, gate_ref, gain_in_ref, gain_out_ref, trans_gain_ref = ins
    gate_out, x_out, mask_out, gains_out = outs
    lines = x_ref.shape[1]
    current = jnp.concatenate([line_tokens(x_ref, line).T for line in range(lines)], axis=1)
    x_out[...] = current
    normed = channel_norm(current, spread_gain(gain_in_ref[0:1, :]))
    gate_out[...] = twice_sigmoid(dot(halved(gate_ref[0]), normed))
    mask_out[...] = token_mask(mask_ref[...], lines)
    rows = [gain_out_ref[0:1, :], gain_in_ref[1:2, :], gain_out_ref[1:2, :], trans_gain_ref[...]]
    gains_out[...] = jnp.concatenate(rows + rows, axis=0)


def one_hot(rows, columns, wanted):
    row = lax.broadcasted_iota(jnp.int32, (rows, columns), 0)
    column = lax.broadcasted_iota(jnp.int32, (rows, columns), 1)
    return (wanted(row) == column).astype(BF16)


def swap_matrix(slots, breadth):
    size = slots * LANES
    return one_hot(
        size, size, lambda lane: lane // breadth % slots * LANES + lane // LANES * breadth + lane % breadth
    )


def combine_kernel(sizes, sources, owners, breadth, share, outgoing, ins, outs):
    rows, cols = sizes["row"], sizes["half"] * sizes["near"]
    near = len(sources) // rows
    both_ref, combined_ref = ins[0], outs[0]
    slots = LANES // breadth
    span = both_ref.shape[1]
    lines = span // (2 * share)
    pack = max(1, slots // near)
    groups = share // pack
    size = span // pack
    swap = swap_matrix(slots, breadth)

    def source(row):
        channel = row // size * groups + row // lines % groups
        return row % lines * (2 * share) + row // (groups * lines) % 2 * share + channel

    order = one_hot(span, span, source)
    wide = []
    for row in range(rows):
        here = jnp.concatenate([both_ref[sources[col, row]] for col in range(near)], axis=1)
        here = dot(order, here).astype(BF16)
        wide.append(jnp.concatenate([here[n * size : (n + 1) * size] for n in range(pack)], axis=1))
    wide = jnp.concatenate(wide, axis=0)
    block = slots * LANES
    swapped = [dot(wide[:, first : first + block], swap) for first in range(0, wide.shape[1], block)]

    def whole(side, group):
        columns = []
        for part in swapped:
            held = []
            for row in range(rows):
                first = row * size + (side * groups + group) * lines
                held += [part[first : first + lines, slot * LANES : (slot + 1) * LANES] for slot in range(slots)]
            columns.append(jnp.concatenate(held, axis=0))
        return jnp.concatenate(columns, axis=1).astype(BF16)

    products = [None] * share
    for group in range(groups):
        left, right = whole(0, group), whole(1, group)
        for place in range(pack):
            mine = left
            if pack > 1:
                lane = lax.broadcasted_iota(jnp.int32, left.shape, 1)
                mine = jnp.where(lane // (near * breadth) == place, left, jnp.zeros_like(left))
            products[place * groups + group] = dot(mine, right, (1, 1) if outgoing else (0, 0))

    for high in range(cols // slots):
        lanes = slice(high * LANES, (high + 1) * LANES)
        held = []
        for row in range(rows):
            for product in products:
                parts = [
                    product[(row * slots + slot) * lines : (row * slots + slot + 1) * lines, lanes]
                    for slot in range(slots)
                ]
                held.append(jnp.concatenate(parts, axis=1))
        back = dot(jnp.concatenate(held, axis=0).astype(BF16), swap).astype(BF16)
        for low in range(slots):
            for row in range(rows):
                first = row * share * lines
                combined_ref[owners[high * slots + low, row]] = back[
                    first : first + share * lines, low * LANES : (low + 1) * LANES
                ]


def hold_combined(combined_ref, stage_ref, share, sources):
    span = combined_ref.shape[1]
    lines = span // share
    order = one_hot(span, span, lambda row: row % share * lines + row // share)
    order = jnp.concatenate([order] * len(sources[0]), axis=1)
    for first in range(0, len(sources), 2):
        blocks = [
            jnp.concatenate([combined_ref[source] for source in sources[owner]], axis=0)
            for owner in (first, first + 1)
        ]
        ordered = dot(order, jnp.concatenate(blocks, axis=1))
        for n in range(2):
            stage_ref[(first + n) * span : (first + n + 1) * span, :] = ordered[:, n * LANES : (n + 1) * LANES]


def read_combined(stage_ref, owners, lines, share, first, count):
    columns = []
    for line in range(first, first + count):
        if share % 8 == 0:
            held = [
                stage_ref[(owner * lines + line) * share : (owner * lines + line + 1) * share, :]
                for owner in range(owners)
            ]
            columns.append(jnp.concatenate(held, axis=0))
        else:
            columns.append(stage_ref[pl.ds(line, owners, stride=lines), :])
    return jnp.concatenate(columns, axis=1)


def middle_kernel(share, sources, next_share, chunk, ins, outs, stage_ref, message_stage_ref):
    combined_ref, x_ref, gate_ref, mask_ref, gains_ref, proj_ref, gate_weight_ref, out_ref = ins
    message_ref, gate_out, next_ref = outs
    tokens = x_ref.shape[1]
    lines = tokens // LANES
    owners = x_ref.shape[0] // share
    hold_combined(combined_ref, stage_ref, share, sources)
    mask = mask_ref[...]
    gain_out, gain = [spread_gain(gains_ref[n : n + 1, :]) for n in (0, 1)]
    out_t, proj_t, gate_t = halved(out_ref[0]), halved(proj_ref[1]), halved(gate_weight_ref[1])
    for start in range(0, tokens, chunk):
        here = slice(start, start + chunk)
        combined = read_combined(stage_ref, owners, lines, share, start // LANES, chunk // LANES)
        hidden = channel_norm(combined, gain_out)
        current = x_ref[:, here] + gate_ref[:, here] * dot(out_t, hidden)
        next_ref[:, here] = current
        normed = channel_norm(current, gain)
        emit_message(normed, proj_t, mask, start // LANES, message_ref, message_stage_ref, next_share)
        gate_out[:, here] = twice_sigmoid(dot(gate_t, normed))


def last_kernel(share, sources, chunk, ins, outs, stage_ref, result_ref, sems):
    combined_ref, x_ref, gate_ref, gains_ref, out_ref, up_ref, down_ref = ins
    (result_out,) = outs
    slots, lines, breadth, channels = result_ref.shape
    owners = x_ref.shape[0] // share
    half = down_ref.shape[0]
    count = chunk // LANES
    gain_out, gain = [spread_gain(gains_ref[n : n + 1, :]) for n in (2, 3)]
    out_t, down_t = halved(out_ref[1]), down_ref[...].T
    gate_t, up_t = halved(up_ref[:, :half]), up_ref[:, half:].T
    hold_combined(combined_ref, stage_ref, share, sources)
    writes = []
    for first in range(0, lines, count):
        here = slice(first * LANES, (first + count) * LANES)
        combined = read_combined(stage_ref, owners, lines, share, first, count)
        hidden = channel_norm(combined, gain_out)
        current = x_ref[:, here] + gate_ref[:, here] * dot(out_t, hidden)
        trans_in = channel_norm(current, gain)
        block = min(256, half)
        for base in range(0, half, block):
            gate_part = dot(gate_t[base : base + block], trans_in)
            up_part = dot(up_t[base : base + block], trans_in)
            trans_hidden = (gate_part * twice_sigmoid(gate_part) * up_part).astype(BF16)
            current = current + dot(down_t[:, base : base + block], trans_hidden)
        result = current.T
        for part in range(count):
            for slot in range(slots):
                base = part * LANES + slot * breadth
                result_ref[slot, first + part] = result[base : base + breadth]
        piece = slice(first, first + count)
        pairs = [(result_ref.at[slot, piece], result_out.at[slot, piece]) for slot in range(slots)]
        writes += start_all(pairs, sems, first // count * slots)
    for write in writes:
        write.wait()


def call(kernel, operands, outs, scratch=(), in_hbm=False, out_hbm=False):
    in_place, held = pl.BlockSpec(memory_space=pltpu.HBM), pl.BlockSpec(memory_space=pltpu.VMEM)
    count = len(operands)

    def body(*refs):
        kernel(refs[:count], refs[count : count + len(outs)], *refs[count + len(outs) :])

    return pl.pallas_call(
        body,
        in_specs=[in_place if in_hbm else held] * count,
        out_specs=[in_place if out_hbm else held] * len(outs),
        out_shape=[jax.ShapeDtypeStruct(shape, dtype) for shape, dtype in outs],
        scratch_shapes=list(scratch),
        compiler_params=pltpu.CompilerParams(vmem_limit_bytes=FULL_VMEM_BYTES if in_hbm else VMEM_BYTES),
    )(*operands)


def exchange(values, axes):
    return lax.all_to_all(values, axes, split_axis=0, concat_axis=0, tiled=True)


def per_device(
    sizes,
    pair_map,
    pair_mask,
    gain_in,
    proj_weight,
    gate_weight,
    gain_out,
    out_weight,
    trans_gain,
    trans_up,
    trans_down,
):
    height, breadth, channels = pair_map.shape
    tokens = height * breadth
    lines = tokens // LANES
    hid = gain_out.shape[1]
    rows, cols = sizes["row"], sizes["half"] * sizes["near"]
    owners = rows * cols
    share = hid // owners
    chunk = min(4 * LANES, tokens)
    split = sizes["half"] if share % 8 == 0 else 1
    first_share = split * share
    held = ((LANES // breadth, lines, breadth, channels), F32)
    grouped = pair_map.reshape(held[0])
    wide = ((channels, tokens), F32)
    result = pltpu.VMEM((owners * share * lines, LANES), F32)
    spare = pltpu.VMEM((8, LANES) if share % 8 == 0 else (owners * 2 * share * lines, LANES), F32)

    def message(own):
        return ((hid // own, 2 * own * lines, LANES), BF16)

    nears = sizes["near"]
    by_all, by_near = count_devices(ALL_AXES, sizes), count_devices(NEAR_AXES, sizes)
    everyone = {(half * nears + near, row): n for (half, near, row), n in by_all.items()}
    beside = {(near, row): n for (half, near, row), n in by_near.items()} if split > 1 else everyone
    single = [[n] for n in range(owners)]
    paired = [[] for _ in range(owners // split)]
    for at, n in by_all.items():
        paired[by_near[at] if split > 1 else n].append(n)

    def combine(operands, own, sources, outgoing):
        kernel = functools.partial(combine_kernel, sizes, sources, everyone, breadth, own, outgoing)
        answer = ((owners, own * lines, LANES), BF16)
        return exchange(call(kernel, operands, [answer])[0], ALL_AXES)

    (both,) = call(
        functools.partial(project_kernel, first_share),
        (grouped, pair_mask, gain_in, proj_weight),
        [message(first_share)],
        (
            spare,
            pltpu.VMEM(*held),
            pltpu.VMEM(pair_mask.shape, jnp.int32),
            pltpu.VMEM(gain_in.shape, F32),
            pltpu.VMEM(proj_weight.shape[1:], BF16),
            pltpu.VMEM(*message(first_share)),
            pltpu.SemaphoreType.DMA((3 + LANES // breadth,)),
            pltpu.SemaphoreType.DMA((8,)),
        ),
        in_hbm=True,
        out_hbm=True,
    )
    gate, current, mask, gains = call(
        prepare_kernel,
        (grouped, pair_mask, gate_weight, gain_in, gain_out, trans_gain.reshape(1, -1)),
        [wide, wide, ((lines, LANES), F32), ((8, channels), F32)],
    )
    both = exchange(both, NEAR_AXES if split > 1 else ALL_AXES)
    combined = combine((both, mask), first_share, beside, True)
    both, gate, current = call(
        functools.partial(middle_kernel, first_share, paired, share, chunk),
        (combined, current, gate, mask, gains, proj_weight, gate_weight, out_weight),
        [message(share), wide, wide],
        (result, spare),
    )
    combined = combine((exchange(both, ALL_AXES),), share, everyone, False)
    (pair_out,) = call(
        functools.partial(last_kernel, share, single, chunk),
        (combined, current, gate, gains, out_weight, trans_up, trans_down),
        [held],
        (result, pltpu.VMEM(*held), pltpu.SemaphoreType.DMA((tokens // chunk * (LANES // breadth),))),
        out_hbm=True,
    )
    return pair_out.reshape(pair_map.shape)


def solution(mesh):
    groups, rows, cols = (mesh.shape[name] for name in ("grp", "row", "col"))
    halves = 2 if cols % 2 == 0 else 1
    sizes = {"half": halves, "near": cols // halves, "row": rows}
    folded = Mesh(mesh.devices.reshape(groups, rows, halves, cols // halves), ("grp", "row", "half", "near"))
    tokens = (("grp", "row"), ("half", "near"))
    in_specs = (P(*tokens, None), P(*tokens)) + (P(),) * 8

    def body(*args):
        return per_device(sizes, *args)

    return jax.shard_map(body, mesh=folded, in_specs=in_specs, out_specs=P(*tokens, None), check_vma=False)
```

```python
import functools

import jax
import jax.numpy as jnp
from jax import lax
from jax.experimental import pallas as pl
from jax.experimental.pallas import tpu as pltpu
from jax.sharding import Mesh
from jax.sharding import PartitionSpec as P

NEAR_AXES = ("near", "row")
ALL_AXES = ("half", "near", "row")
LANES = 128
VMEM_BYTES = 24 * 1024 * 1024
F32, BF16 = jnp.float32, jnp.bfloat16


def dot(left, right, contract=(1, 0)):
    return lax.dot_general(
        left, right, (((contract[0],), (contract[1],)), ((), ())), preferred_element_type=F32
    )


def halved(weight):
    return weight.T * 0.5


def twice_sigmoid(half):
    return jnp.tanh(half) + 1.0


def channel_norm(values, gain):
    wide = jnp.concatenate([gain] * (values.shape[1] // LANES), axis=1)
    centred = values - jnp.mean(values, axis=0, keepdims=True)
    spread = jnp.mean(centred * centred, axis=0, keepdims=True)
    return (centred * lax.rsqrt(spread + 1e-05) * wide).astype(BF16)


def spread_gain(row):
    return jnp.broadcast_to(row, (LANES, row.shape[1])).T


def token_mask(mask, lines):
    height, breadth = mask.shape
    wide = jnp.concatenate([mask.astype(F32)] * (LANES // breadth), axis=1)
    row = lax.broadcasted_iota(jnp.int32, wide.shape, 0)
    lane = lax.broadcasted_iota(jnp.int32, wide.shape, 1)
    wide = jnp.where(row // lines == lane // breadth, wide, 0.0).astype(BF16)
    line = lax.broadcasted_iota(jnp.int32, (lines, height), 0)
    source = lax.broadcasted_iota(jnp.int32, (lines, height), 1)
    return dot((source % lines == line).astype(BF16), wide)


def emit_message(normed, weight_t, mask, line, message_ref, stage_ref, share):
    projected = dot(weight_t, normed)
    hid = weight_t.shape[0] // 4
    owners = hid // share
    for part in range(normed.shape[1] // LANES):
        here = projected[:, part * LANES : (part + 1) * LANES]
        at = line + part
        keep = mask[at : at + 1]
        left = twice_sigmoid(here[:hid]) * here[hid : 2 * hid] * keep
        right = twice_sigmoid(here[2 * hid : 3 * hid]) * here[3 * hid :] * keep
        if share % 8 == 0:
            for owner in range(owners):
                rows = slice(owner * share, (owner + 1) * share)
                both = jnp.concatenate([left[rows], right[rows]], axis=0).astype(BF16)
                message_ref[owner, 2 * share * at : 2 * share * (at + 1), :] = both
        else:
            lines = message_ref.shape[1] // 2
            stage_ref[pl.ds(2 * at, owners, stride=2 * lines), :] = left
            stage_ref[pl.ds(2 * at + 1, owners, stride=2 * lines), :] = right
    if share % 8 and line + normed.shape[1] // LANES == mask.shape[0]:
        message_ref[...] = stage_ref[...].astype(BF16).reshape(message_ref.shape)


def start_all(pairs, sems, first=0):
    copies = [pltpu.make_async_copy(src, dst, sems.at[first + n]) for n, (src, dst) in enumerate(pairs)]
    for copy in copies:
        copy.start()
    return copies


def line_tokens(x_ref, line):
    return jnp.concatenate([x_ref[slot, line] for slot in range(x_ref.shape[0])], axis=0)


def project_kernel(share, ins, outs, stage_ref, x_ref, mask_ref, weight_ref, gate_ref, gain_in_ref, gain_out_ref, trans_gain_ref, sems):
    message_ref, gate_out, turned_out, mask_out, gains_out = outs
    x_in, mask_in, weight_in, gate_in, gain_in, gain_out, trans_gain = ins
    lines = x_ref.shape[1]
    pairs = [
        (weight_in.at[0], weight_ref),
        (x_in, x_ref),
        (gain_in, gain_in_ref),
        (mask_in, mask_ref),
        (gate_in.at[0], gate_ref),
        (gain_out, gain_out_ref),
        (trans_gain, trans_gain_ref),
    ]
    for copy in start_all(pairs, sems):
        copy.wait()
    mask = token_mask(mask_ref[...], lines)
    current = jnp.concatenate([line_tokens(x_ref, line).T for line in range(lines)], axis=1)
    normed = channel_norm(current, spread_gain(gain_in_ref[0:1, :]))
    emit_message(normed, halved(weight_ref[...]), mask, 0, message_ref, stage_ref, share)
    gate_out[...] = twice_sigmoid(dot(halved(gate_ref[...]), normed))
    turned_out[...] = current
    mask_out[...] = mask
    rows = [gain_out_ref[0:1, :], gain_in_ref[1:2, :], gain_out_ref[1:2, :], trans_gain_ref[...]]
    gains_out[...] = jnp.concatenate(rows + rows, axis=0)


def one_hot(rows, columns, wanted):
    row = lax.broadcasted_iota(jnp.int32, (rows, columns), 0)
    column = lax.broadcasted_iota(jnp.int32, (rows, columns), 1)
    return (wanted(row) == column).astype(BF16)


def swap_matrix(slots, breadth):
    size = slots * LANES
    return one_hot(
        size, size, lambda lane: lane // breadth % slots * LANES + lane // LANES * breadth + lane % breadth
    )


def combine_kernel(rows, cols, near, breadth, share, outgoing, ins, outs):
    (both_ref,), (combined_ref,) = ins, outs
    slots = LANES // breadth
    span = both_ref.shape[1]
    lines = span // (2 * share)
    pack = max(1, slots // near)
    groups = share // pack
    size = span // pack
    swap = swap_matrix(slots, breadth)

    def source(row):
        channel = row // size * groups + row // lines % groups
        return row % lines * (2 * share) + row // (groups * lines) % 2 * share + channel

    order = one_hot(span, span, source)
    wide = []
    for row in range(rows):
        here = jnp.concatenate([both_ref[col * rows + row] for col in range(near)], axis=1)
        here = dot(order, here).astype(BF16)
        wide.append(jnp.concatenate([here[n * size : (n + 1) * size] for n in range(pack)], axis=1))
    wide = jnp.concatenate(wide, axis=0)
    block = slots * LANES
    swapped = [dot(wide[:, first : first + block], swap) for first in range(0, wide.shape[1], block)]

    def whole(side, group):
        columns = []
        for part in swapped:
            held = []
            for row in range(rows):
                first = row * size + (side * groups + group) * lines
                held += [part[first : first + lines, slot * LANES : (slot + 1) * LANES] for slot in range(slots)]
            columns.append(jnp.concatenate(held, axis=0))
        return jnp.concatenate(columns, axis=1).astype(BF16)

    products = [None] * share
    for group in range(groups):
        left, right = whole(0, group), whole(1, group)
        for place in range(pack):
            mine = left
            if pack > 1:
                lane = lax.broadcasted_iota(jnp.int32, left.shape, 1)
                mine = jnp.where(lane // (near * breadth) == place, left, jnp.zeros_like(left))
            products[place * groups + group] = dot(mine, right, (1, 1) if outgoing else (0, 0))

    for high in range(cols // slots):
        lanes = slice(high * LANES, (high + 1) * LANES)
        held = []
        for row in range(rows):
            for product in products:
                parts = [
                    product[(row * slots + slot) * lines : (row * slots + slot + 1) * lines, lanes]
                    for slot in range(slots)
                ]
                held.append(jnp.concatenate(parts, axis=1))
        back = dot(jnp.concatenate(held, axis=0).astype(BF16), swap).astype(BF16)
        for low in range(slots):
            for row in range(rows):
                first = row * share * lines
                combined_ref[(high * slots + low) * rows + row] = back[
                    first : first + share * lines, low * LANES : (low + 1) * LANES
                ]


def hold_combined(combined_ref, stage_ref, share):
    span = combined_ref.shape[1]
    lines = span // share
    owners = stage_ref.shape[0] // span
    halves = combined_ref.shape[0] // owners
    order = one_hot(span, span, lambda row: row % share * lines + row // share)
    order = jnp.concatenate([order] * halves, axis=1)
    for first in range(0, owners, 2):
        blocks = [
            jnp.concatenate([combined_ref[half * owners + owner] for half in range(halves)], axis=0)
            for owner in (first, first + 1)
        ]
        ordered = dot(order, jnp.concatenate(blocks, axis=1))
        for n in range(2):
            stage_ref[(first + n) * span : (first + n + 1) * span, :] = ordered[:, n * LANES : (n + 1) * LANES]


def read_combined(stage_ref, owners, lines, share, first, count):
    columns = []
    for line in range(first, first + count):
        if share % 8 == 0:
            held = [
                stage_ref[(owner * lines + line) * share : (owner * lines + line + 1) * share, :]
                for owner in range(owners)
            ]
            columns.append(jnp.concatenate(held, axis=0))
        else:
            columns.append(stage_ref[pl.ds(line, owners, stride=lines), :])
    return jnp.concatenate(columns, axis=1)


def middle_kernel(share, next_share, chunk, ins, outs, stage_ref, message_stage_ref):
    combined_ref, x_ref, gate_ref, mask_ref, gains_ref, proj_ref, gate_weight_ref, out_ref = ins
    message_ref, gate_out, next_ref = outs
    tokens = x_ref.shape[1]
    lines = tokens // LANES
    owners = x_ref.shape[0] // share
    hold_combined(combined_ref, stage_ref, share)
    mask = mask_ref[...]
    gain_out, gain = [spread_gain(gains_ref[n : n + 1, :]) for n in (0, 1)]
    out_t, proj_t, gate_t = halved(out_ref[0]), halved(proj_ref[1]), halved(gate_weight_ref[1])
    for start in range(0, tokens, chunk):
        here = slice(start, start + chunk)
        combined = read_combined(stage_ref, owners, lines, share, start // LANES, chunk // LANES)
        hidden = channel_norm(combined, gain_out)
        current = x_ref[:, here] + gate_ref[:, here] * dot(out_t, hidden)
        next_ref[:, here] = current
        normed = channel_norm(current, gain)
        emit_message(normed, proj_t, mask, start // LANES, message_ref, message_stage_ref, next_share)
        gate_out[:, here] = twice_sigmoid(dot(gate_t, normed))


def last_kernel(share, chunk, ins, outs, stage_ref, result_ref, sems):
    combined_ref, x_ref, gate_ref, gains_ref, out_ref, up_ref, down_ref = ins
    (result_out,) = outs
    slots, lines, breadth, channels = result_ref.shape
    owners = x_ref.shape[0] // share
    half = down_ref.shape[0]
    count = chunk // LANES
    gain_out, gain = [spread_gain(gains_ref[n : n + 1, :]) for n in (2, 3)]
    out_t, down_t = halved(out_ref[1]), down_ref[...].T
    gate_t, up_t = halved(up_ref[:, :half]), up_ref[:, half:].T
    hold_combined(combined_ref, stage_ref, share)
    writes = []
    for first in range(0, lines, count):
        here = slice(first * LANES, (first + count) * LANES)
        combined = read_combined(stage_ref, owners, lines, share, first, count)
        hidden = channel_norm(combined, gain_out)
        current = x_ref[:, here] + gate_ref[:, here] * dot(out_t, hidden)
        trans_in = channel_norm(current, gain)
        block = min(256, half)
        for base in range(0, half, block):
            gate_part = dot(gate_t[base : base + block], trans_in)
            up_part = dot(up_t[base : base + block], trans_in)
            trans_hidden = (gate_part * twice_sigmoid(gate_part) * up_part).astype(BF16)
            current = current + dot(down_t[:, base : base + block], trans_hidden)
        result = current.T
        for part in range(count):
            for slot in range(slots):
                base = part * LANES + slot * breadth
                result_ref[slot, first + part] = result[base : base + breadth]
        piece = slice(first, first + count)
        writes += start_all([(result_ref.at[:, piece], result_out.at[:, piece])], sems, first // count)
    for write in writes:
        write.wait()


def call(kernel, operands, outs, scratch=(), in_hbm=False, out_hbm=False):
    in_place, held = pl.BlockSpec(memory_space=pltpu.HBM), pl.BlockSpec(memory_space=pltpu.VMEM)
    count = len(operands)

    def body(*refs):
        kernel(refs[:count], refs[count : count + len(outs)], *refs[count + len(outs) :])

    return pl.pallas_call(
        body,
        in_specs=[in_place if in_hbm else held] * count,
        out_specs=[in_place if out_hbm else held] * len(outs),
        out_shape=[jax.ShapeDtypeStruct(shape, dtype) for shape, dtype in outs],
        scratch_shapes=list(scratch),
        compiler_params=pltpu.CompilerParams(vmem_limit_bytes=VMEM_BYTES),
    )(*[pltpu.with_memory_space_constraint(array, pltpu.HBM) if in_hbm else array for array in operands])


def exchange(values, axes):
    return lax.all_to_all(values, axes, split_axis=0, concat_axis=0, tiled=True)


def per_device(
    rows,
    halves,
    nears,
    pair_map,
    pair_mask,
    gain_in,
    proj_weight,
    gate_weight,
    gain_out,
    out_weight,
    trans_gain,
    trans_up,
    trans_down,
):
    height, breadth, channels = pair_map.shape
    tokens = height * breadth
    lines = tokens // LANES
    hid = gain_out.shape[1]
    cols = halves * nears
    owners = rows * cols
    share = hid // owners
    chunk = min(4 * LANES, tokens)
    split = halves if share % 8 == 0 else 1
    first_share = split * share
    held = ((LANES // breadth, lines, breadth, channels), F32)
    grouped = pair_map.reshape(held[0])
    wide = ((channels, tokens), F32)
    result = pltpu.VMEM((owners * share * lines, LANES), F32)
    spare = pltpu.VMEM((8, LANES) if share % 8 == 0 else (owners * 2 * share * lines, LANES), F32)

    def message(own):
        return ((hid // own, 2 * own * lines, LANES), BF16)

    def combine(both, own, outgoing):
        near = cols * share // own
        kernel = functools.partial(combine_kernel, rows, cols, near, breadth, own, outgoing)
        answer = ((owners, own * lines, LANES), BF16)
        return exchange(call(kernel, (both,), [answer])[0], ALL_AXES)

    operands = (grouped, pair_mask, proj_weight, gate_weight, gain_in, gain_out, trans_gain.reshape(1, -1))
    both, gate, current, mask, gains = call(
        functools.partial(project_kernel, first_share),
        operands,
        [message(first_share), wide, wide, ((lines, LANES), F32), ((8, channels), F32)],
        (
            spare,
            *[
                pltpu.VMEM(array.shape[1:] if array.ndim == 3 else array.shape, array.dtype)
                for array in operands
            ],
            pltpu.SemaphoreType.DMA((len(operands),)),
        ),
        in_hbm=True,
    )
    both = exchange(both, NEAR_AXES if split > 1 else ALL_AXES)
    combined = combine(both, first_share, True)
    both, gate, current = call(
        functools.partial(middle_kernel, first_share, share, chunk),
        (combined, current, gate, mask, gains, proj_weight, gate_weight, out_weight),
        [message(share), wide, wide],
        (result, spare),
    )
    combined = combine(exchange(both, ALL_AXES), share, False)
    (pair_out,) = call(
        functools.partial(last_kernel, share, chunk),
        (combined, current, gate, gains, out_weight, trans_up, trans_down),
        [held],
        (result, pltpu.VMEM(*held), pltpu.SemaphoreType.DMA((tokens // chunk,))),
        out_hbm=True,
    )
    return pair_out.reshape(pair_map.shape)


def solution(mesh):
    groups, rows, cols = (mesh.shape[name] for name in ("grp", "row", "col"))
    halves = 2 if cols % 2 == 0 else 1
    nears = cols // halves
    folded = Mesh(mesh.devices.reshape(groups, rows, halves, nears), ("grp", "row", "half", "near"))
    tokens = (("grp", "row"), ("half", "near"))
    in_specs = (P(*tokens, None), P(*tokens)) + (P(),) * 8

    def body(*args):
        return per_device(rows, halves, nears, *args)

    return jax.shard_map(body, mesh=folded, in_specs=in_specs, out_specs=P(*tokens, None), check_vma=False)
```

```python
import functools

import jax
import jax.numpy as jnp
from jax import lax
from jax.experimental import pallas as pl
from jax.experimental.pallas import tpu as pltpu
from jax.sharding import Mesh
from jax.sharding import PartitionSpec as P

NEAR_AXES = ("near", "row")
ALL_AXES = ("half", "near", "row")
LANES = 128
VMEM_BYTES = 24 * 1024 * 1024
F32, BF16 = jnp.float32, jnp.bfloat16


def dot(left, right, contract=(1, 0)):
    return lax.dot_general(
        left, right, (((contract[0],), (contract[1],)), ((), ())), preferred_element_type=F32
    )


def halved(weight):
    return weight.T * 0.5


def twice_sigmoid(half):
    return jnp.tanh(half) + 1.0


def channel_norm(values, gain):
    wide = jnp.concatenate([gain] * (values.shape[1] // LANES), axis=1)
    centred = values - jnp.mean(values, axis=0, keepdims=True)
    spread = jnp.mean(centred * centred, axis=0, keepdims=True)
    return (centred * lax.rsqrt(spread + 1e-05) * wide).astype(BF16)


def spread_gain(row):
    return jnp.broadcast_to(row, (LANES, row.shape[1])).T


def token_mask(mask, lines):
    height, breadth = mask.shape
    wide = jnp.concatenate([mask.astype(F32)] * (LANES // breadth), axis=1)
    row = lax.broadcasted_iota(jnp.int32, wide.shape, 0)
    lane = lax.broadcasted_iota(jnp.int32, wide.shape, 1)
    wide = jnp.where(row // lines == lane // breadth, wide, 0.0).astype(BF16)
    line = lax.broadcasted_iota(jnp.int32, (lines, height), 0)
    source = lax.broadcasted_iota(jnp.int32, (lines, height), 1)
    return dot((source % lines == line).astype(BF16), wide)


def emit_message(normed, weight_t, mask, line, message_ref, stage_ref, share):
    projected = dot(weight_t, normed)
    hid = weight_t.shape[0] // 4
    owners = hid // share
    for part in range(normed.shape[1] // LANES):
        here = projected[:, part * LANES : (part + 1) * LANES]
        at = line + part
        keep = mask[at : at + 1]
        left = twice_sigmoid(here[:hid]) * here[hid : 2 * hid] * keep
        right = twice_sigmoid(here[2 * hid : 3 * hid]) * here[3 * hid :] * keep
        if share % 8 == 0:
            for owner in range(owners):
                rows = slice(owner * share, (owner + 1) * share)
                both = jnp.concatenate([left[rows], right[rows]], axis=0).astype(BF16)
                message_ref[owner, 2 * share * at : 2 * share * (at + 1), :] = both
        else:
            lines = message_ref.shape[1] // 2
            stage_ref[pl.ds(2 * at, owners, stride=2 * lines), :] = left
            stage_ref[pl.ds(2 * at + 1, owners, stride=2 * lines), :] = right
    if share % 8 and line + normed.shape[1] // LANES == mask.shape[0]:
        message_ref[...] = stage_ref[...].astype(BF16).reshape(message_ref.shape)


def start_all(pairs, sems, first=0):
    copies = [pltpu.make_async_copy(src, dst, sems.at[first + n]) for n, (src, dst) in enumerate(pairs)]
    for copy in copies:
        copy.start()
    return copies


def line_tokens(x_ref, line):
    return jnp.concatenate([x_ref[slot, line] for slot in range(x_ref.shape[0])], axis=0)


def project_kernel(share, ins, outs, stage_ref, x_ref, mask_ref, weight_ref, gate_ref, gain_in_ref, gain_out_ref, trans_gain_ref, sems):
    message_ref, gate_out, turned_out, mask_out, gains_out = outs
    x_in, mask_in, weight_in, gate_in, gain_in, gain_out, trans_gain = ins
    lines = x_ref.shape[1]
    pairs = [
        (weight_in.at[0], weight_ref),
        (x_in, x_ref),
        (gain_in, gain_in_ref),
        (mask_in, mask_ref),
        (gate_in.at[0], gate_ref),
        (gain_out, gain_out_ref),
        (trans_gain, trans_gain_ref),
    ]
    for copy in start_all(pairs, sems):
        copy.wait()
    mask = token_mask(mask_ref[...], lines)
    current = jnp.concatenate([line_tokens(x_ref, line).T for line in range(lines)], axis=1)
    normed = channel_norm(current, spread_gain(gain_in_ref[0:1, :]))
    emit_message(normed, halved(weight_ref[...]), mask, 0, message_ref, stage_ref, share)
    gate_out[...] = twice_sigmoid(dot(halved(gate_ref[...]), normed))
    turned_out[...] = current
    mask_out[...] = mask
    rows = [gain_out_ref[0:1, :], gain_in_ref[1:2, :], gain_out_ref[1:2, :], trans_gain_ref[...]]
    gains_out[...] = jnp.concatenate(rows + rows, axis=0)


def one_hot(rows, columns, wanted):
    row = lax.broadcasted_iota(jnp.int32, (rows, columns), 0)
    column = lax.broadcasted_iota(jnp.int32, (rows, columns), 1)
    return (wanted(row) == column).astype(BF16)


def swap_matrix(slots, breadth):
    size = slots * LANES
    return one_hot(
        size, size, lambda lane: lane // breadth % slots * LANES + lane // LANES * breadth + lane % breadth
    )


def combine_kernel(rows, cols, near, breadth, share, outgoing, ins, outs):
    (both_ref,), (combined_ref,) = ins, outs
    slots = LANES // breadth
    span = both_ref.shape[1]
    lines = span // (2 * share)
    pack = max(1, slots // near)
    groups = share // pack
    size = span // pack
    swap = swap_matrix(slots, breadth)

    def source(row):
        channel = row // size * groups + row // lines % groups
        return row % lines * (2 * share) + row // (groups * lines) % 2 * share + channel

    order = one_hot(span, span, source)
    wide = []
    for row in range(rows):
        here = jnp.concatenate([both_ref[col * rows + row] for col in range(near)], axis=1)
        here = dot(order, here).astype(BF16)
        wide.append(jnp.concatenate([here[n * size : (n + 1) * size] for n in range(pack)], axis=1))
    wide = jnp.concatenate(wide, axis=0)
    block = slots * LANES
    swapped = [dot(wide[:, first : first + block], swap) for first in range(0, wide.shape[1], block)]

    def whole(side, group):
        columns = []
        for part in swapped:
            held = []
            for row in range(rows):
                first = row * size + (side * groups + group) * lines
                held += [part[first : first + lines, slot * LANES : (slot + 1) * LANES] for slot in range(slots)]
            columns.append(jnp.concatenate(held, axis=0))
        return jnp.concatenate(columns, axis=1).astype(BF16)

    products = [None] * share
    for group in range(groups):
        left, right = whole(0, group), whole(1, group)
        for place in range(pack):
            mine = left
            if pack > 1:
                lane = lax.broadcasted_iota(jnp.int32, left.shape, 1)
                mine = jnp.where(lane // (near * breadth) == place, left, jnp.zeros_like(left))
            products[place * groups + group] = dot(mine, right, (1, 1) if outgoing else (0, 0))

    for high in range(cols // slots):
        lanes = slice(high * LANES, (high + 1) * LANES)
        held = []
        for row in range(rows):
            for product in products:
                parts = [
                    product[(row * slots + slot) * lines : (row * slots + slot + 1) * lines, lanes]
                    for slot in range(slots)
                ]
                held.append(jnp.concatenate(parts, axis=1))
        back = dot(jnp.concatenate(held, axis=0).astype(BF16), swap).astype(BF16)
        for low in range(slots):
            for row in range(rows):
                first = row * share * lines
                combined_ref[(high * slots + low) * rows + row] = back[
                    first : first + share * lines, low * LANES : (low + 1) * LANES
                ]


def hold_combined(combined_ref, stage_ref, share):
    span = combined_ref.shape[1]
    lines = span // share
    owners = stage_ref.shape[0] // span
    halves = combined_ref.shape[0] // owners
    order = one_hot(span, span, lambda row: row % share * lines + row // share)
    order = jnp.concatenate([order] * halves, axis=1)
    for first in range(0, owners, 2):
        blocks = [
            jnp.concatenate([combined_ref[half * owners + owner] for half in range(halves)], axis=0)
            for owner in (first, first + 1)
        ]
        ordered = dot(order, jnp.concatenate(blocks, axis=1))
        for n in range(2):
            stage_ref[(first + n) * span : (first + n + 1) * span, :] = ordered[:, n * LANES : (n + 1) * LANES]


def read_combined(stage_ref, owners, lines, share, first, count):
    columns = []
    for line in range(first, first + count):
        if share % 8 == 0:
            held = [
                stage_ref[(owner * lines + line) * share : (owner * lines + line + 1) * share, :]
                for owner in range(owners)
            ]
            columns.append(jnp.concatenate(held, axis=0))
        else:
            columns.append(stage_ref[pl.ds(line, owners, stride=lines), :])
    return jnp.concatenate(columns, axis=1)


def middle_kernel(share, next_share, chunk, ins, outs, stage_ref, message_stage_ref):
    combined_ref, x_ref, gate_ref, mask_ref, gains_ref, proj_ref, gate_weight_ref, out_ref = ins
    message_ref, gate_out, next_ref = outs
    tokens = x_ref.shape[1]
    lines = tokens // LANES
    owners = x_ref.shape[0] // share
    hold_combined(combined_ref, stage_ref, share)
    mask = mask_ref[...]
    gain_out, gain = [spread_gain(gains_ref[n : n + 1, :]) for n in (0, 1)]
    out_t, proj_t, gate_t = halved(out_ref[0]), halved(proj_ref[1]), halved(gate_weight_ref[1])
    for start in range(0, tokens, chunk):
        here = slice(start, start + chunk)
        combined = read_combined(stage_ref, owners, lines, share, start // LANES, chunk // LANES)
        hidden = channel_norm(combined, gain_out)
        current = x_ref[:, here] + gate_ref[:, here] * dot(out_t, hidden)
        next_ref[:, here] = current
        normed = channel_norm(current, gain)
        emit_message(normed, proj_t, mask, start // LANES, message_ref, message_stage_ref, next_share)
        gate_out[:, here] = twice_sigmoid(dot(gate_t, normed))


def last_kernel(share, chunk, ins, outs, stage_ref, result_ref, sems):
    combined_ref, x_ref, gate_ref, gains_ref, out_ref, up_ref, down_ref = ins
    (result_out,) = outs
    slots, lines, breadth, channels = result_ref.shape
    owners = x_ref.shape[0] // share
    half = down_ref.shape[0]
    count = chunk // LANES
    gain_out, gain = [spread_gain(gains_ref[n : n + 1, :]) for n in (2, 3)]
    out_t, down_t = halved(out_ref[1]), down_ref[...].T
    gate_t, up_t = halved(up_ref[:, :half]), up_ref[:, half:].T
    hold_combined(combined_ref, stage_ref, share)
    combined = read_combined(stage_ref, owners, lines, share, 0, lines)
    hidden = channel_norm(combined, gain_out)
    whole = x_ref[...] + gate_ref[...] * dot(out_t, hidden)
    trans_in = channel_norm(whole, gain)
    writes = []
    for first in range(0, lines, count):
        here = slice(first * LANES, (first + count) * LANES)
        current = whole[:, here]
        block = min(256, half)
        for base in range(0, half, block):
            gate_part = dot(gate_t[base : base + block], trans_in[:, here])
            up_part = dot(up_t[base : base + block], trans_in[:, here])
            trans_hidden = (gate_part * twice_sigmoid(gate_part) * up_part).astype(BF16)
            current = current + dot(down_t[:, base : base + block], trans_hidden)
        result = current.T
        for part in range(count):
            for slot in range(slots):
                base = part * LANES + slot * breadth
                result_ref[slot, first + part] = result[base : base + breadth]
        piece = slice(first, first + count)
        writes += start_all([(result_ref.at[:, piece], result_out.at[:, piece])], sems, first // count)
    for write in writes:
        write.wait()


def call(kernel, operands, outs, scratch=(), in_hbm=False, out_hbm=False):
    in_place, held = pl.BlockSpec(memory_space=pltpu.HBM), pl.BlockSpec(memory_space=pltpu.VMEM)
    count = len(operands)

    def body(*refs):
        kernel(refs[:count], refs[count : count + len(outs)], *refs[count + len(outs) :])

    return pl.pallas_call(
        body,
        in_specs=[in_place if in_hbm else held] * count,
        out_specs=[in_place if out_hbm else held] * len(outs),
        out_shape=[jax.ShapeDtypeStruct(shape, dtype) for shape, dtype in outs],
        scratch_shapes=list(scratch),
        compiler_params=pltpu.CompilerParams(vmem_limit_bytes=VMEM_BYTES),
    )(*[pltpu.with_memory_space_constraint(array, pltpu.HBM) if in_hbm else array for array in operands])


def exchange(values, axes):
    return lax.all_to_all(values, axes, split_axis=0, concat_axis=0, tiled=True)


def per_device(
    rows,
    halves,
    nears,
    pair_map,
    pair_mask,
    gain_in,
    proj_weight,
    gate_weight,
    gain_out,
    out_weight,
    trans_gain,
    trans_up,
    trans_down,
):
    height, breadth, channels = pair_map.shape
    tokens = height * breadth
    lines = tokens // LANES
    hid = gain_out.shape[1]
    cols = halves * nears
    owners = rows * cols
    share = hid // owners
    chunk = min(2 * LANES, tokens)
    split = halves if share % 8 == 0 else 1
    first_share = split * share
    held = ((LANES // breadth, lines, breadth, channels), F32)
    grouped = pair_map.reshape(held[0])
    wide = ((channels, tokens), F32)
    result = pltpu.VMEM((owners * share * lines, LANES), F32)
    spare = pltpu.VMEM((8, LANES) if share % 8 == 0 else (owners * 2 * share * lines, LANES), F32)

    def message(own):
        return ((hid // own, 2 * own * lines, LANES), BF16)

    def combine(both, own, outgoing):
        near = cols * share // own
        kernel = functools.partial(combine_kernel, rows, cols, near, breadth, own, outgoing)
        answer = ((owners, own * lines, LANES), BF16)
        return exchange(call(kernel, (both,), [answer])[0], ALL_AXES)

    operands = (grouped, pair_mask, proj_weight, gate_weight, gain_in, gain_out, trans_gain.reshape(1, -1))
    both, gate, current, mask, gains = call(
        functools.partial(project_kernel, first_share),
        operands,
        [message(first_share), wide, wide, ((lines, LANES), F32), ((8, channels), F32)],
        (
            spare,
            *[
                pltpu.VMEM(array.shape[1:] if array.ndim == 3 else array.shape, array.dtype)
                for array in operands
            ],
            pltpu.SemaphoreType.DMA((len(operands),)),
        ),
        in_hbm=True,
    )
    both = exchange(both, NEAR_AXES if split > 1 else ALL_AXES)
    combined = combine(both, first_share, True)
    both, gate, current = call(
        functools.partial(middle_kernel, first_share, share, tokens),
        (combined, current, gate, mask, gains, proj_weight, gate_weight, out_weight),
        [message(share), wide, wide],
        (result, spare),
    )
    combined = combine(exchange(both, ALL_AXES), share, False)
    (pair_out,) = call(
        functools.partial(last_kernel, share, chunk),
        (combined, current, gate, gains, out_weight, trans_up, trans_down),
        [held],
        (result, pltpu.VMEM(*held), pltpu.SemaphoreType.DMA((tokens // chunk,))),
        out_hbm=True,
    )
    return pair_out.reshape(pair_map.shape)


def solution(mesh):
    groups, rows, cols = (mesh.shape[name] for name in ("grp", "row", "col"))
    halves = 2 if cols % 2 == 0 else 1
    nears = cols // halves
    folded = Mesh(mesh.devices.reshape(groups, rows, halves, nears), ("grp", "row", "half", "near"))
    tokens = (("grp", "row"), ("half", "near"))
    in_specs = (P(*tokens, None), P(*tokens)) + (P(),) * 8

    def body(*args):
        return per_device(rows, halves, nears, *args)

    return jax.shard_map(body, mesh=folded, in_specs=in_specs, out_specs=P(*tokens, None), check_vma=False)
```

```python
import functools

import jax
import jax.numpy as jnp
from jax import lax
from jax.experimental import pallas as pl
from jax.experimental.pallas import tpu as pltpu
from jax.sharding import Mesh
from jax.sharding import PartitionSpec as P

NEAR_AXES = ("near", "row")
ALL_AXES = ("half", "near", "row")
LANES = 128
VMEM_BYTES = 24 * 1024 * 1024
F32, BF16 = jnp.float32, jnp.bfloat16


def dot(left, right, contract=(1, 0)):
    return lax.dot_general(
        left, right, (((contract[0],), (contract[1],)), ((), ())), preferred_element_type=F32
    )


def halved(weight):
    return weight.T * 0.5


def twice_sigmoid(half):
    return jnp.tanh(half) + 1.0


def channel_norm(values, gain):
    wide = jnp.concatenate([gain] * (values.shape[1] // LANES), axis=1)
    centred = values - jnp.mean(values, axis=0, keepdims=True)
    spread = jnp.mean(centred * centred, axis=0, keepdims=True)
    return (centred * lax.rsqrt(spread + 1e-05) * wide).astype(BF16)


def spread_gain(row):
    return jnp.broadcast_to(row, (LANES, row.shape[1])).T


def token_mask(mask, lines):
    height, breadth = mask.shape
    wide = jnp.concatenate([mask.astype(F32)] * (LANES // breadth), axis=1)
    row = lax.broadcasted_iota(jnp.int32, wide.shape, 0)
    lane = lax.broadcasted_iota(jnp.int32, wide.shape, 1)
    wide = jnp.where(row // lines == lane // breadth, wide, 0.0).astype(BF16)
    line = lax.broadcasted_iota(jnp.int32, (lines, height), 0)
    source = lax.broadcasted_iota(jnp.int32, (lines, height), 1)
    return dot((source % lines == line).astype(BF16), wide)


def emit_message(normed, weight_t, mask, line, message_ref, stage_ref, share):
    projected = dot(weight_t, normed)
    hid = weight_t.shape[0] // 4
    owners = hid // share
    for part in range(normed.shape[1] // LANES):
        here = projected[:, part * LANES : (part + 1) * LANES]
        at = line + part
        keep = mask[at : at + 1]
        left = twice_sigmoid(here[:hid]) * here[hid : 2 * hid] * keep
        right = twice_sigmoid(here[2 * hid : 3 * hid]) * here[3 * hid :] * keep
        if share % 8 == 0:
            for owner in range(owners):
                rows = slice(owner * share, (owner + 1) * share)
                both = jnp.concatenate([left[rows], right[rows]], axis=0).astype(BF16)
                message_ref[owner, 2 * share * at : 2 * share * (at + 1), :] = both
        else:
            lines = message_ref.shape[1] // 2
            stage_ref[pl.ds(2 * at, owners, stride=2 * lines), :] = left
            stage_ref[pl.ds(2 * at + 1, owners, stride=2 * lines), :] = right
    if share % 8 and line + normed.shape[1] // LANES == mask.shape[0]:
        message_ref[...] = stage_ref[...].astype(BF16).reshape(message_ref.shape)


def start_all(pairs, sems, first=0):
    copies = [pltpu.make_async_copy(src, dst, sems.at[first + n]) for n, (src, dst) in enumerate(pairs)]
    for copy in copies:
        copy.start()
    return copies


def line_tokens(x_ref, line):
    return jnp.concatenate([x_ref[slot, line] for slot in range(x_ref.shape[0])], axis=0)


def project_kernel(share, ins, outs, stage_ref, x_ref, mask_ref, weight_ref, gate_ref, gain_in_ref, gain_out_ref, trans_gain_ref, sems):
    message_ref, gate_out, turned_out, mask_out, gains_out = outs
    x_in, mask_in, weight_in, gate_in, gain_in, gain_out, trans_gain = ins
    lines = x_ref.shape[1]
    pairs = [
        (weight_in.at[0], weight_ref),
        (x_in, x_ref),
        (gain_in, gain_in_ref),
        (mask_in, mask_ref),
        (gate_in.at[0], gate_ref),
        (gain_out, gain_out_ref),
        (trans_gain, trans_gain_ref),
    ]
    for copy in start_all(pairs, sems):
        copy.wait()
    mask = token_mask(mask_ref[...], lines)
    current = jnp.concatenate([line_tokens(x_ref, line).T for line in range(lines)], axis=1)
    normed = channel_norm(current, spread_gain(gain_in_ref[0:1, :]))
    emit_message(normed, halved(weight_ref[...]), mask, 0, message_ref, stage_ref, share)
    gate_out[...] = twice_sigmoid(dot(halved(gate_ref[...]), normed))
    turned_out[...] = current
    mask_out[...] = mask
    rows = [gain_out_ref[0:1, :], gain_in_ref[1:2, :], gain_out_ref[1:2, :], trans_gain_ref[...]]
    gains_out[...] = jnp.concatenate(rows + rows, axis=0)


def one_hot(rows, columns, wanted):
    row = lax.broadcasted_iota(jnp.int32, (rows, columns), 0)
    column = lax.broadcasted_iota(jnp.int32, (rows, columns), 1)
    return (wanted(row) == column).astype(BF16)


def swap_matrix(slots, breadth):
    size = slots * LANES
    return one_hot(
        size, size, lambda lane: lane // breadth % slots * LANES + lane // LANES * breadth + lane % breadth
    )


def combine_kernel(rows, cols, near, breadth, share, outgoing, ins, outs):
    (both_ref,), (combined_ref,) = ins, outs
    slots = LANES // breadth
    span = both_ref.shape[1]
    lines = span // (2 * share)
    pack = max(1, slots // near)
    groups = share // pack
    size = span // pack
    swap = swap_matrix(slots, breadth)

    def source(row):
        channel = row // size * groups + row // lines % groups
        return row % lines * (2 * share) + row // (groups * lines) % 2 * share + channel

    order = one_hot(span, span, source)
    wide = []
    for row in range(rows):
        here = jnp.concatenate([both_ref[col * rows + row] for col in range(near)], axis=1)
        here = dot(order, here).astype(BF16)
        wide.append(jnp.concatenate([here[n * size : (n + 1) * size] for n in range(pack)], axis=1))
    wide = jnp.concatenate(wide, axis=0)
    block = slots * LANES
    swapped = [dot(wide[:, first : first + block], swap) for first in range(0, wide.shape[1], block)]

    def whole(side, group):
        columns = []
        for part in swapped:
            held = []
            for row in range(rows):
                first = row * size + (side * groups + group) * lines
                held += [part[first : first + lines, slot * LANES : (slot + 1) * LANES] for slot in range(slots)]
            columns.append(jnp.concatenate(held, axis=0))
        return jnp.concatenate(columns, axis=1).astype(BF16)

    products = [None] * share
    for group in range(groups):
        left, right = whole(0, group), whole(1, group)
        for place in range(pack):
            mine = left
            if pack > 1:
                lane = lax.broadcasted_iota(jnp.int32, left.shape, 1)
                mine = jnp.where(lane // (near * breadth) == place, left, jnp.zeros_like(left))
            products[place * groups + group] = dot(mine, right, (1, 1) if outgoing else (0, 0))

    for high in range(cols // slots):
        lanes = slice(high * LANES, (high + 1) * LANES)
        held = []
        for row in range(rows):
            for product in products:
                parts = [
                    product[(row * slots + slot) * lines : (row * slots + slot + 1) * lines, lanes]
                    for slot in range(slots)
                ]
                held.append(jnp.concatenate(parts, axis=1))
        back = dot(jnp.concatenate(held, axis=0).astype(BF16), swap).astype(BF16)
        for low in range(slots):
            for row in range(rows):
                first = row * share * lines
                combined_ref[(high * slots + low) * rows + row] = back[
                    first : first + share * lines, low * LANES : (low + 1) * LANES
                ]


def hold_combined(combined_ref, stage_ref, share):
    span = combined_ref.shape[1]
    lines = span // share
    owners = stage_ref.shape[0] // span
    halves = combined_ref.shape[0] // owners
    order = one_hot(span, span, lambda row: row % share * lines + row // share)
    order = jnp.concatenate([order] * halves, axis=1)
    for first in range(0, owners, 2):
        blocks = [
            jnp.concatenate([combined_ref[half * owners + owner] for half in range(halves)], axis=0)
            for owner in (first, first + 1)
        ]
        ordered = dot(order, jnp.concatenate(blocks, axis=1))
        for n in range(2):
            stage_ref[(first + n) * span : (first + n + 1) * span, :] = ordered[:, n * LANES : (n + 1) * LANES]


def read_combined(stage_ref, owners, lines, share, first, count):
    columns = []
    for line in range(first, first + count):
        if share % 8 == 0:
            held = [
                stage_ref[(owner * lines + line) * share : (owner * lines + line + 1) * share, :]
                for owner in range(owners)
            ]
            columns.append(jnp.concatenate(held, axis=0))
        else:
            columns.append(stage_ref[pl.ds(line, owners, stride=lines), :])
    return jnp.concatenate(columns, axis=1)


def middle_kernel(share, next_share, chunk, ins, outs, stage_ref, message_stage_ref):
    combined_ref, x_ref, gate_ref, mask_ref, gains_ref, proj_ref, gate_weight_ref, out_ref = ins
    message_ref, gate_out, next_ref = outs
    tokens = x_ref.shape[1]
    lines = tokens // LANES
    owners = x_ref.shape[0] // share
    hold_combined(combined_ref, stage_ref, share)
    mask = mask_ref[...]
    gain_out, gain = [spread_gain(gains_ref[n : n + 1, :]) for n in (0, 1)]
    out_t, proj_t, gate_t = halved(out_ref[0]), halved(proj_ref[1]), halved(gate_weight_ref[1])
    for start in range(0, tokens, chunk):
        here = slice(start, start + chunk)
        combined = read_combined(stage_ref, owners, lines, share, start // LANES, chunk // LANES)
        hidden = channel_norm(combined, gain_out)
        current = x_ref[:, here] + gate_ref[:, here] * dot(out_t, hidden)
        next_ref[:, here] = current
        normed = channel_norm(current, gain)
        emit_message(normed, proj_t, mask, start // LANES, message_ref, message_stage_ref, next_share)
        gate_out[:, here] = twice_sigmoid(dot(gate_t, normed))


def last_kernel(share, chunk, ins, outs, stage_ref, result_ref, sems):
    combined_ref, x_ref, gate_ref, gains_ref, out_ref, up_ref, down_ref = ins
    (result_out,) = outs
    slots, lines, breadth, channels = result_ref.shape
    owners = x_ref.shape[0] // share
    half = down_ref.shape[0]
    count = chunk // LANES
    gain_out, gain = [spread_gain(gains_ref[n : n + 1, :]) for n in (2, 3)]
    out_t, down_t = halved(out_ref[1]), down_ref[...].T
    gate_t, up_t = halved(up_ref[:, :half]), up_ref[:, half:].T
    hold_combined(combined_ref, stage_ref, share)
    combined = read_combined(stage_ref, owners, lines, share, 0, lines)
    hidden = channel_norm(combined, gain_out)
    current = x_ref[...] + gate_ref[...] * dot(out_t, hidden)
    trans_in = channel_norm(current, gain)
    block = min(256, half)
    for base in range(0, half, block):
        gate_part = dot(gate_t[base : base + block], trans_in)
        up_part = dot(up_t[base : base + block], trans_in)
        trans_hidden = (gate_part * twice_sigmoid(gate_part) * up_part).astype(BF16)
        current = current + dot(down_t[:, base : base + block], trans_hidden)
    writes = []
    for first in range(0, lines, count):
        for line in range(first, first + count):
            result = current[:, line * LANES : (line + 1) * LANES].T
            for slot in range(slots):
                result_ref[slot, line] = result[slot * breadth : (slot + 1) * breadth]
        piece = slice(first, first + count)
        writes += start_all([(result_ref.at[:, piece], result_out.at[:, piece])], sems, first // count)
    for write in writes:
        write.wait()


def call(kernel, operands, outs, scratch=(), in_hbm=False, out_hbm=False):
    in_place, held = pl.BlockSpec(memory_space=pltpu.HBM), pl.BlockSpec(memory_space=pltpu.VMEM)
    count = len(operands)

    def body(*refs):
        kernel(refs[:count], refs[count : count + len(outs)], *refs[count + len(outs) :])

    return pl.pallas_call(
        body,
        in_specs=[in_place if in_hbm else held] * count,
        out_specs=[in_place if out_hbm else held] * len(outs),
        out_shape=[jax.ShapeDtypeStruct(shape, dtype) for shape, dtype in outs],
        scratch_shapes=list(scratch),
        compiler_params=pltpu.CompilerParams(vmem_limit_bytes=VMEM_BYTES),
    )(*[pltpu.with_memory_space_constraint(array, pltpu.HBM) if in_hbm else array for array in operands])


def exchange(values, axes):
    return lax.all_to_all(values, axes, split_axis=0, concat_axis=0, tiled=True)


def per_device(
    rows,
    halves,
    nears,
    pair_map,
    pair_mask,
    gain_in,
    proj_weight,
    gate_weight,
    gain_out,
    out_weight,
    trans_gain,
    trans_up,
    trans_down,
):
    height, breadth, channels = pair_map.shape
    tokens = height * breadth
    lines = tokens // LANES
    hid = gain_out.shape[1]
    cols = halves * nears
    owners = rows * cols
    share = hid // owners
    chunk = min(4 * LANES, tokens)
    split = halves if share % 8 == 0 else 1
    first_share = split * share
    held = ((LANES // breadth, lines, breadth, channels), F32)
    grouped = pair_map.reshape(held[0])
    wide = ((channels, tokens), F32)
    result = pltpu.VMEM((owners * share * lines, LANES), F32)
    spare = pltpu.VMEM((8, LANES) if share % 8 == 0 else (owners * 2 * share * lines, LANES), F32)

    def message(own):
        return ((hid // own, 2 * own * lines, LANES), BF16)

    def combine(both, own, outgoing):
        near = cols * share // own
        kernel = functools.partial(combine_kernel, rows, cols, near, breadth, own, outgoing)
        answer = ((owners, own * lines, LANES), BF16)
        return exchange(call(kernel, (both,), [answer])[0], ALL_AXES)

    operands = (grouped, pair_mask, proj_weight, gate_weight, gain_in, gain_out, trans_gain.reshape(1, -1))
    both, gate, current, mask, gains = call(
        functools.partial(project_kernel, first_share),
        operands,
        [message(first_share), wide, wide, ((lines, LANES), F32), ((8, channels), F32)],
        (
            spare,
            *[
                pltpu.VMEM(array.shape[1:] if array.ndim == 3 else array.shape, array.dtype)
                for array in operands
            ],
            pltpu.SemaphoreType.DMA((len(operands),)),
        ),
        in_hbm=True,
    )
    both = exchange(both, NEAR_AXES if split > 1 else ALL_AXES)
    combined = combine(both, first_share, True)
    both, gate, current = call(
        functools.partial(middle_kernel, first_share, share, tokens),
        (combined, current, gate, mask, gains, proj_weight, gate_weight, out_weight),
        [message(share), wide, wide],
        (result, spare),
    )
    combined = combine(exchange(both, ALL_AXES), share, False)
    (pair_out,) = call(
        functools.partial(last_kernel, share, chunk),
        (combined, current, gate, gains, out_weight, trans_up, trans_down),
        [held],
        (result, pltpu.VMEM(*held), pltpu.SemaphoreType.DMA((tokens // chunk,))),
        out_hbm=True,
    )
    return pair_out.reshape(pair_map.shape)


def solution(mesh):
    groups, rows, cols = (mesh.shape[name] for name in ("grp", "row", "col"))
    halves = 2 if cols % 2 == 0 else 1
    nears = cols // halves
    folded = Mesh(mesh.devices.reshape(groups, rows, halves, nears), ("grp", "row", "half", "near"))
    tokens = (("grp", "row"), ("half", "near"))
    in_specs = (P(*tokens, None), P(*tokens)) + (P(),) * 8

    def body(*args):
        return per_device(rows, halves, nears, *args)

    return jax.shard_map(body, mesh=folded, in_specs=in_specs, out_specs=P(*tokens, None), check_vma=False)
```

```python
import functools

import jax
import jax.numpy as jnp
from jax import lax
from jax.experimental import pallas as pl
from jax.experimental.pallas import tpu as pltpu
from jax.sharding import Mesh
from jax.sharding import PartitionSpec as P

NEAR_AXES = ("near", "row")
ALL_AXES = ("half", "near", "row")
LANES = 128
VMEM_BYTES = 24 * 1024 * 1024
F32, BF16 = jnp.float32, jnp.bfloat16


def dot(left, right, contract=(1, 0)):
    return lax.dot_general(
        left, right, (((contract[0],), (contract[1],)), ((), ())), preferred_element_type=F32
    )


def halved(weight):
    return weight.T * 0.5


def twice_sigmoid(half):
    return jnp.tanh(half) + 1.0


def channel_norm(values, gain):
    wide = jnp.concatenate([gain] * (values.shape[1] // LANES), axis=1)
    centred = values - jnp.mean(values, axis=0, keepdims=True)
    spread = jnp.mean(centred * centred, axis=0, keepdims=True)
    return (centred * lax.rsqrt(spread + 1e-05) * wide).astype(BF16)


def spread_gain(row):
    return jnp.broadcast_to(row, (LANES, row.shape[1])).T


def token_mask(mask, lines):
    height, breadth = mask.shape
    wide = jnp.concatenate([mask.astype(F32)] * (LANES // breadth), axis=1)
    row = lax.broadcasted_iota(jnp.int32, wide.shape, 0)
    lane = lax.broadcasted_iota(jnp.int32, wide.shape, 1)
    wide = jnp.where(row // lines == lane // breadth, wide, 0.0).astype(BF16)
    line = lax.broadcasted_iota(jnp.int32, (lines, height), 0)
    source = lax.broadcasted_iota(jnp.int32, (lines, height), 1)
    return dot((source % lines == line).astype(BF16), wide)


def emit_message(normed, weight_t, mask, line, message_ref, stage_ref, share):
    projected = dot(weight_t, normed)
    hid = weight_t.shape[0] // 4
    owners = hid // share
    for part in range(normed.shape[1] // LANES):
        here = projected[:, part * LANES : (part + 1) * LANES]
        at = line + part
        keep = mask[at : at + 1]
        left = twice_sigmoid(here[:hid]) * here[hid : 2 * hid] * keep
        right = twice_sigmoid(here[2 * hid : 3 * hid]) * here[3 * hid :] * keep
        if share % 8 == 0:
            for owner in range(owners):
                rows = slice(owner * share, (owner + 1) * share)
                both = jnp.concatenate([left[rows], right[rows]], axis=0).astype(BF16)
                message_ref[owner, 2 * share * at : 2 * share * (at + 1), :] = both
        else:
            lines = message_ref.shape[1] // 2
            stage_ref[pl.ds(2 * at, owners, stride=2 * lines), :] = left
            stage_ref[pl.ds(2 * at + 1, owners, stride=2 * lines), :] = right
    if share % 8 and line + normed.shape[1] // LANES == mask.shape[0]:
        message_ref[...] = stage_ref[...].astype(BF16).reshape(message_ref.shape)


def start_all(pairs, sems, first=0):
    copies = [pltpu.make_async_copy(src, dst, sems.at[first + n]) for n, (src, dst) in enumerate(pairs)]
    for copy in copies:
        copy.start()
    return copies


def line_tokens(x_ref, line):
    return jnp.concatenate([x_ref[slot, line] for slot in range(x_ref.shape[0])], axis=0)


def project_kernel(share, ins, outs, stage_ref, x_ref, mask_ref, weight_ref, gate_ref, gain_in_ref, gain_out_ref, trans_gain_ref, sems):
    message_ref, gate_out, turned_out, mask_out, gains_out = outs
    x_in, mask_in, weight_in, gate_in, gain_in, gain_out, trans_gain = ins
    lines = x_ref.shape[1]
    pairs = [
        (weight_in.at[0], weight_ref),
        (x_in, x_ref),
        (gain_in, gain_in_ref),
        (mask_in, mask_ref),
        (gate_in.at[0], gate_ref),
        (gain_out, gain_out_ref),
        (trans_gain, trans_gain_ref),
    ]
    for copy in start_all(pairs, sems):
        copy.wait()
    mask = token_mask(mask_ref[...], lines)
    current = jnp.concatenate([line_tokens(x_ref, line).T for line in range(lines)], axis=1)
    normed = channel_norm(current, spread_gain(gain_in_ref[0:1, :]))
    emit_message(normed, halved(weight_ref[...]), mask, 0, message_ref, stage_ref, share)
    gate_out[...] = twice_sigmoid(dot(halved(gate_ref[...]), normed))
    turned_out[...] = current
    mask_out[...] = mask
    rows = [gain_out_ref[0:1, :], gain_in_ref[1:2, :], gain_out_ref[1:2, :], trans_gain_ref[...]]
    gains_out[...] = jnp.concatenate(rows + rows, axis=0)


def one_hot(rows, columns, wanted):
    row = lax.broadcasted_iota(jnp.int32, (rows, columns), 0)
    column = lax.broadcasted_iota(jnp.int32, (rows, columns), 1)
    return (wanted(row) == column).astype(BF16)


def swap_matrix(slots, breadth):
    size = slots * LANES
    return one_hot(
        size, size, lambda lane: lane // breadth % slots * LANES + lane // LANES * breadth + lane % breadth
    )


def combine_kernel(sources, owners, breadth, share, outgoing, ins, outs):
    near, cols, rows = len(sources), len(owners), len(owners[0])
    (both_ref,), (combined_ref,) = ins, outs
    slots = LANES // breadth
    span = both_ref.shape[1]
    lines = span // (2 * share)
    pack = max(1, slots // near)
    groups = share // pack
    size = span // pack
    swap = swap_matrix(slots, breadth)

    def source(row):
        channel = row // size * groups + row // lines % groups
        return row % lines * (2 * share) + row // (groups * lines) % 2 * share + channel

    order = one_hot(span, span, source)
    wide = []
    for row in range(rows):
        here = jnp.concatenate([both_ref[sources[col][row]] for col in range(near)], axis=1)
        here = dot(order, here).astype(BF16)
        wide.append(jnp.concatenate([here[n * size : (n + 1) * size] for n in range(pack)], axis=1))
    wide = jnp.concatenate(wide, axis=0)
    block = slots * LANES
    swapped = [dot(wide[:, first : first + block], swap) for first in range(0, wide.shape[1], block)]

    def whole(side, group):
        columns = []
        for part in swapped:
            held = []
            for row in range(rows):
                first = row * size + (side * groups + group) * lines
                held += [part[first : first + lines, slot * LANES : (slot + 1) * LANES] for slot in range(slots)]
            columns.append(jnp.concatenate(held, axis=0))
        return jnp.concatenate(columns, axis=1).astype(BF16)

    products = [None] * share
    for group in range(groups):
        left, right = whole(0, group), whole(1, group)
        for place in range(pack):
            mine = left
            if pack > 1:
                lane = lax.broadcasted_iota(jnp.int32, left.shape, 1)
                mine = jnp.where(lane // (near * breadth) == place, left, jnp.zeros_like(left))
            products[place * groups + group] = dot(mine, right, (1, 1) if outgoing else (0, 0))

    for high in range(cols // slots):
        lanes = slice(high * LANES, (high + 1) * LANES)
        held = []
        for row in range(rows):
            for product in products:
                parts = [
                    product[(row * slots + slot) * lines : (row * slots + slot + 1) * lines, lanes]
                    for slot in range(slots)
                ]
                held.append(jnp.concatenate(parts, axis=1))
        back = dot(jnp.concatenate(held, axis=0).astype(BF16), swap).astype(BF16)
        for low in range(slots):
            for row in range(rows):
                first = row * share * lines
                combined_ref[owners[high * slots + low][row]] = back[
                    first : first + share * lines, low * LANES : (low + 1) * LANES
                ]


def hold_combined(combined_ref, stage_ref, share, sources):
    span = combined_ref.shape[1]
    lines = span // share
    order = one_hot(span, span, lambda row: row % share * lines + row // share)
    order = jnp.concatenate([order] * len(sources[0]), axis=1)
    for first in range(0, len(sources), 2):
        blocks = [
            jnp.concatenate([combined_ref[source] for source in sources[owner]], axis=0)
            for owner in (first, first + 1)
        ]
        ordered = dot(order, jnp.concatenate(blocks, axis=1))
        for n in range(2):
            stage_ref[(first + n) * span : (first + n + 1) * span, :] = ordered[:, n * LANES : (n + 1) * LANES]


def read_combined(stage_ref, owners, lines, share, first, count):
    columns = []
    for line in range(first, first + count):
        if share % 8 == 0:
            held = [
                stage_ref[(owner * lines + line) * share : (owner * lines + line + 1) * share, :]
                for owner in range(owners)
            ]
            columns.append(jnp.concatenate(held, axis=0))
        else:
            columns.append(stage_ref[pl.ds(line, owners, stride=lines), :])
    return jnp.concatenate(columns, axis=1)


def middle_kernel(share, sources, next_share, chunk, ins, outs, stage_ref, message_stage_ref):
    combined_ref, x_ref, gate_ref, mask_ref, gains_ref, proj_ref, gate_weight_ref, out_ref = ins
    message_ref, gate_out, next_ref = outs
    tokens = x_ref.shape[1]
    lines = tokens // LANES
    owners = x_ref.shape[0] // share
    hold_combined(combined_ref, stage_ref, share, sources)
    mask = mask_ref[...]
    gain_out, gain = [spread_gain(gains_ref[n : n + 1, :]) for n in (0, 1)]
    out_t, proj_t, gate_t = halved(out_ref[0]), halved(proj_ref[1]), halved(gate_weight_ref[1])
    for start in range(0, tokens, chunk):
        here = slice(start, start + chunk)
        combined = read_combined(stage_ref, owners, lines, share, start // LANES, chunk // LANES)
        hidden = channel_norm(combined, gain_out)
        current = x_ref[:, here] + gate_ref[:, here] * dot(out_t, hidden)
        next_ref[:, here] = current
        normed = channel_norm(current, gain)
        emit_message(normed, proj_t, mask, start // LANES, message_ref, message_stage_ref, next_share)
        gate_out[:, here] = twice_sigmoid(dot(gate_t, normed))


def last_kernel(share, sources, chunk, ins, outs, stage_ref, result_ref, sems):
    combined_ref, x_ref, gate_ref, gains_ref, out_ref, up_ref, down_ref = ins
    (result_out,) = outs
    slots, lines, breadth, channels = result_ref.shape
    owners = x_ref.shape[0] // share
    half = down_ref.shape[0]
    count = chunk // LANES
    gain_out, gain = [spread_gain(gains_ref[n : n + 1, :]) for n in (2, 3)]
    out_t, down_t = halved(out_ref[1]), down_ref[...].T
    gate_t, up_t = halved(up_ref[:, :half]), up_ref[:, half:].T
    hold_combined(combined_ref, stage_ref, share, sources)
    combined = read_combined(stage_ref, owners, lines, share, 0, lines)
    hidden = channel_norm(combined, gain_out)
    current = x_ref[...] + gate_ref[...] * dot(out_t, hidden)
    trans_in = channel_norm(current, gain)
    block = min(256, half)
    for base in range(0, half, block):
        gate_part = dot(gate_t[base : base + block], trans_in)
        up_part = dot(up_t[base : base + block], trans_in)
        trans_hidden = (gate_part * twice_sigmoid(gate_part) * up_part).astype(BF16)
        current = current + dot(down_t[:, base : base + block], trans_hidden)
    writes = []
    for first in range(0, lines, count):
        for line in range(first, first + count):
            result = current[:, line * LANES : (line + 1) * LANES].T
            for slot in range(slots):
                result_ref[slot, line] = result[slot * breadth : (slot + 1) * breadth]
        piece = slice(first, first + count)
        writes += start_all([(result_ref.at[:, piece], result_out.at[:, piece])], sems, first // count)
    for write in writes:
        write.wait()


def call(kernel, operands, outs, scratch=(), in_hbm=False, out_hbm=False):
    in_place, held = pl.BlockSpec(memory_space=pltpu.HBM), pl.BlockSpec(memory_space=pltpu.VMEM)
    count = len(operands)

    def body(*refs):
        kernel(refs[:count], refs[count : count + len(outs)], *refs[count + len(outs) :])

    return pl.pallas_call(
        body,
        in_specs=[in_place if in_hbm else held] * count,
        out_specs=[in_place if out_hbm else held] * len(outs),
        out_shape=[jax.ShapeDtypeStruct(shape, dtype) for shape, dtype in outs],
        scratch_shapes=list(scratch),
        compiler_params=pltpu.CompilerParams(vmem_limit_bytes=VMEM_BYTES),
    )(*[pltpu.with_memory_space_constraint(array, pltpu.HBM) if in_hbm else array for array in operands])


def exchange(values, axes, order=None):
    groups = [order] if order else None
    return lax.all_to_all(values, axes, split_axis=0, concat_axis=0, axis_index_groups=groups, tiled=True)


def per_device(
    rows,
    halves,
    nears,
    pair_map,
    pair_mask,
    gain_in,
    proj_weight,
    gate_weight,
    gain_out,
    out_weight,
    trans_gain,
    trans_up,
    trans_down,
):
    height, breadth, channels = pair_map.shape
    tokens = height * breadth
    lines = tokens // LANES
    hid = gain_out.shape[1]
    cols = halves * nears
    owners = rows * cols
    share = hid // owners
    chunk = min(4 * LANES, tokens)
    split = halves if share % 8 == 0 else 1
    first_share = split * share
    held = ((LANES // breadth, lines, breadth, channels), F32)
    grouped = pair_map.reshape(held[0])
    wide = ((channels, tokens), F32)
    result = pltpu.VMEM((owners * share * lines, LANES), F32)
    spare = pltpu.VMEM((8, LANES) if share % 8 == 0 else (owners * 2 * share * lines, LANES), F32)

    def message(own):
        return ((hid // own, 2 * own * lines, LANES), BF16)

    blocks = list(range(cols))
    blocks.insert(0, blocks.pop((cols - 1) // 2))
    order = [col * rows + row for col in blocks for row in range(rows)]
    everyone = [[order.index(col * rows + row) for row in range(rows)] for col in range(cols)]
    beside = [[near * rows + row for row in range(rows)] for near in range(nears)] if split > 1 else everyone
    single = [[n] for n in range(owners)]
    paired = single if split == 1 else [
        [everyone[half * nears + near][row] for half in range(halves)] for near in range(nears) for row in range(rows)
    ]

    def combine(both, own, sources, outgoing):
        kernel = functools.partial(combine_kernel, sources, everyone, breadth, own, outgoing)
        answer = ((owners, own * lines, LANES), BF16)
        return exchange(call(kernel, (both,), [answer])[0], ALL_AXES, order)

    operands = (grouped, pair_mask, proj_weight, gate_weight, gain_in, gain_out, trans_gain.reshape(1, -1))
    both, gate, current, mask, gains = call(
        functools.partial(project_kernel, first_share),
        operands,
        [message(first_share), wide, wide, ((lines, LANES), F32), ((8, channels), F32)],
        (
            spare,
            *[
                pltpu.VMEM(array.shape[1:] if array.ndim == 3 else array.shape, array.dtype)
                for array in operands
            ],
            pltpu.SemaphoreType.DMA((len(operands),)),
        ),
        in_hbm=True,
    )
    both = exchange(both, NEAR_AXES) if split > 1 else exchange(both, ALL_AXES, order)
    combined = combine(both, first_share, beside, True)
    both, gate, current = call(
        functools.partial(middle_kernel, first_share, paired, share, tokens),
        (combined, current, gate, mask, gains, proj_weight, gate_weight, out_weight),
        [message(share), wide, wide],
        (result, spare),
    )
    combined = combine(exchange(both, ALL_AXES, order), share, everyone, False)
    (pair_out,) = call(
        functools.partial(last_kernel, share, single, chunk),
        (combined, current, gate, gains, out_weight, trans_up, trans_down),
        [held],
        (result, pltpu.VMEM(*held), pltpu.SemaphoreType.DMA((tokens // chunk,))),
        out_hbm=True,
    )
    return pair_out.reshape(pair_map.shape)


def solution(mesh):
    groups, rows, cols = (mesh.shape[name] for name in ("grp", "row", "col"))
    halves = 2 if cols % 2 == 0 else 1
    nears = cols // halves
    folded = Mesh(mesh.devices.reshape(groups, rows, halves, nears), ("grp", "row", "half", "near"))
    tokens = (("grp", "row"), ("half", "near"))
    in_specs = (P(*tokens, None), P(*tokens)) + (P(),) * 8

    def body(*args):
        return per_device(rows, halves, nears, *args)

    return jax.shard_map(body, mesh=folded, in_specs=in_specs, out_specs=P(*tokens, None), check_vma=False)
```

```python
import functools

import jax
import jax.numpy as jnp
from jax import lax
from jax.experimental import pallas as pl
from jax.experimental.pallas import tpu as pltpu
from jax.sharding import Mesh
from jax.sharding import PartitionSpec as P

NEAR_AXES = ("near", "row")
ALL_AXES = ("half", "near", "row")
LANES = 128
VMEM_BYTES = 24 * 1024 * 1024
F32, BF16 = jnp.float32, jnp.bfloat16


def dot(left, right, contract=(1, 0)):
    return lax.dot_general(
        left, right, (((contract[0],), (contract[1],)), ((), ())), preferred_element_type=F32
    )


def halved(weight):
    return weight.T * 0.5


def twice_sigmoid(half):
    return jnp.tanh(half) + 1.0


def channel_norm(values, gain):
    wide = jnp.concatenate([gain] * (values.shape[1] // LANES), axis=1)
    centred = values - jnp.mean(values, axis=0, keepdims=True)
    spread = jnp.mean(centred * centred, axis=0, keepdims=True)
    return (centred * lax.rsqrt(spread + 1e-05) * wide).astype(BF16)


def spread_gain(row):
    return jnp.broadcast_to(row, (LANES, row.shape[1])).T


def token_mask(mask, lines):
    height, breadth = mask.shape
    wide = jnp.concatenate([mask.astype(F32)] * (LANES // breadth), axis=1)
    row = lax.broadcasted_iota(jnp.int32, wide.shape, 0)
    lane = lax.broadcasted_iota(jnp.int32, wide.shape, 1)
    wide = jnp.where(row // lines == lane // breadth, wide, 0.0).astype(BF16)
    line = lax.broadcasted_iota(jnp.int32, (lines, height), 0)
    source = lax.broadcasted_iota(jnp.int32, (lines, height), 1)
    return dot((source % lines == line).astype(BF16), wide)


def emit_message(normed, weight_t, mask, line, message_ref, stage_ref, share):
    projected = dot(weight_t, normed)
    hid = weight_t.shape[0] // 4
    owners = hid // share
    for part in range(normed.shape[1] // LANES):
        here = projected[:, part * LANES : (part + 1) * LANES]
        at = line + part
        keep = mask[at : at + 1]
        left = twice_sigmoid(here[:hid]) * here[hid : 2 * hid] * keep
        right = twice_sigmoid(here[2 * hid : 3 * hid]) * here[3 * hid :] * keep
        if share % 8 == 0:
            for owner in range(owners):
                rows = slice(owner * share, (owner + 1) * share)
                both = jnp.concatenate([left[rows], right[rows]], axis=0).astype(BF16)
                message_ref[owner, 2 * share * at : 2 * share * (at + 1), :] = both
        else:
            lines = message_ref.shape[1] // 2
            stage_ref[pl.ds(2 * at, owners, stride=2 * lines), :] = left
            stage_ref[pl.ds(2 * at + 1, owners, stride=2 * lines), :] = right
    if share % 8 and line + normed.shape[1] // LANES == mask.shape[0]:
        message_ref[...] = stage_ref[...].astype(BF16).reshape(message_ref.shape)


def start_all(pairs, sems, first=0):
    copies = [pltpu.make_async_copy(src, dst, sems.at[first + n]) for n, (src, dst) in enumerate(pairs)]
    for copy in copies:
        copy.start()
    return copies


def line_tokens(x_ref, line):
    return jnp.concatenate([x_ref[slot, line] for slot in range(x_ref.shape[0])], axis=0)


def project_kernel(share, ins, outs, stage_ref, x_ref, mask_ref, weight_ref, gate_ref, gain_in_ref, gain_out_ref, trans_gain_ref, sems):
    message_ref, gate_out, turned_out, mask_out, gains_out = outs
    x_in, mask_in, weight_in, gate_in, gain_in, gain_out, trans_gain = ins
    lines = x_ref.shape[1]
    pairs = [
        (weight_in.at[0], weight_ref),
        (x_in, x_ref),
        (gain_in, gain_in_ref),
        (mask_in, mask_ref),
        (gate_in.at[0], gate_ref),
        (gain_out, gain_out_ref),
        (trans_gain, trans_gain_ref),
    ]
    for copy in start_all(pairs, sems):
        copy.wait()
    mask = token_mask(mask_ref[...], lines)
    current = jnp.concatenate([line_tokens(x_ref, line).T for line in range(lines)], axis=1)
    normed = channel_norm(current, spread_gain(gain_in_ref[0:1, :]))
    emit_message(normed, halved(weight_ref[...]), mask, 0, message_ref, stage_ref, share)
    gate_out[...] = twice_sigmoid(dot(halved(gate_ref[...]), normed))
    turned_out[...] = current
    mask_out[...] = mask
    rows = [gain_out_ref[0:1, :], gain_in_ref[1:2, :], gain_out_ref[1:2, :], trans_gain_ref[...]]
    gains_out[...] = jnp.concatenate(rows + rows, axis=0)


def one_hot(rows, columns, wanted):
    row = lax.broadcasted_iota(jnp.int32, (rows, columns), 0)
    column = lax.broadcasted_iota(jnp.int32, (rows, columns), 1)
    return (wanted(row) == column).astype(BF16)


def swap_matrix(slots, breadth):
    size = slots * LANES
    return one_hot(
        size, size, lambda lane: lane // breadth % slots * LANES + lane // LANES * breadth + lane % breadth
    )


def combine_kernel(sources, owners, breadth, share, outgoing, ins, outs):
    near, cols, rows = len(sources), len(owners), len(owners[0])
    (both_ref,), (combined_ref,) = ins, outs
    slots = LANES // breadth
    span = both_ref.shape[1]
    lines = span // (2 * share)
    pack = max(1, slots // near)
    groups = share // pack
    size = span // pack
    swap = swap_matrix(slots, breadth)

    def source(row):
        channel = row // size * groups + row // lines % groups
        return row % lines * (2 * share) + row // (groups * lines) % 2 * share + channel

    order = one_hot(span, span, source)
    wide = []
    for row in range(rows):
        here = jnp.concatenate([both_ref[sources[col][row]] for col in range(near)], axis=1)
        here = dot(order, here).astype(BF16)
        wide.append(jnp.concatenate([here[n * size : (n + 1) * size] for n in range(pack)], axis=1))
    wide = jnp.concatenate(wide, axis=0)
    block = slots * LANES
    swapped = [dot(wide[:, first : first + block], swap) for first in range(0, wide.shape[1], block)]

    def whole(side, group):
        columns = []
        for part in swapped:
            held = []
            for row in range(rows):
                first = row * size + (side * groups + group) * lines
                held += [part[first : first + lines, slot * LANES : (slot + 1) * LANES] for slot in range(slots)]
            columns.append(jnp.concatenate(held, axis=0))
        return jnp.concatenate(columns, axis=1).astype(BF16)

    products = [None] * share
    for group in range(groups):
        left, right = whole(0, group), whole(1, group)
        for place in range(pack):
            mine = left
            if pack > 1:
                lane = lax.broadcasted_iota(jnp.int32, left.shape, 1)
                mine = jnp.where(lane // (near * breadth) == place, left, jnp.zeros_like(left))
            products[place * groups + group] = dot(mine, right, (1, 1) if outgoing else (0, 0))

    for high in range(cols // slots):
        lanes = slice(high * LANES, (high + 1) * LANES)
        held = []
        for row in range(rows):
            for product in products:
                parts = [
                    product[(row * slots + slot) * lines : (row * slots + slot + 1) * lines, lanes]
                    for slot in range(slots)
                ]
                held.append(jnp.concatenate(parts, axis=1))
        back = dot(jnp.concatenate(held, axis=0).astype(BF16), swap).astype(BF16)
        for low in range(slots):
            for row in range(rows):
                first = row * share * lines
                combined_ref[owners[high * slots + low][row]] = back[
                    first : first + share * lines, low * LANES : (low + 1) * LANES
                ]


def hold_combined(combined_ref, stage_ref, share, sources):
    span = combined_ref.shape[1]
    lines = span // share
    order = one_hot(span, span, lambda row: row % share * lines + row // share)
    order = jnp.concatenate([order] * len(sources[0]), axis=1)
    for first in range(0, len(sources), 2):
        blocks = [
            jnp.concatenate([combined_ref[source] for source in sources[owner]], axis=0)
            for owner in (first, first + 1)
        ]
        ordered = dot(order, jnp.concatenate(blocks, axis=1))
        for n in range(2):
            stage_ref[(first + n) * span : (first + n + 1) * span, :] = ordered[:, n * LANES : (n + 1) * LANES]


def read_combined(stage_ref, owners, lines, share, first, count):
    columns = []
    for line in range(first, first + count):
        if share % 8 == 0:
            held = [
                stage_ref[(owner * lines + line) * share : (owner * lines + line + 1) * share, :]
                for owner in range(owners)
            ]
            columns.append(jnp.concatenate(held, axis=0))
        else:
            columns.append(stage_ref[pl.ds(line, owners, stride=lines), :])
    return jnp.concatenate(columns, axis=1)


def middle_kernel(share, sources, next_share, chunk, ins, outs, stage_ref, message_stage_ref):
    combined_ref, x_ref, gate_ref, mask_ref, gains_ref, proj_ref, gate_weight_ref, out_ref = ins
    message_ref, gate_out, next_ref = outs
    tokens = x_ref.shape[1]
    lines = tokens // LANES
    owners = x_ref.shape[0] // share
    hold_combined(combined_ref, stage_ref, share, sources)
    mask = mask_ref[...]
    gain_out, gain = [spread_gain(gains_ref[n : n + 1, :]) for n in (0, 1)]
    out_t, proj_t, gate_t = halved(out_ref[0]), halved(proj_ref[1]), halved(gate_weight_ref[1])
    for start in range(0, tokens, chunk):
        here = slice(start, start + chunk)
        combined = read_combined(stage_ref, owners, lines, share, start // LANES, chunk // LANES)
        hidden = channel_norm(combined, gain_out)
        current = x_ref[:, here] + gate_ref[:, here] * dot(out_t, hidden)
        next_ref[:, here] = current
        normed = channel_norm(current, gain)
        emit_message(normed, proj_t, mask, start // LANES, message_ref, message_stage_ref, next_share)
        gate_out[:, here] = twice_sigmoid(dot(gate_t, normed))


def last_kernel(share, sources, chunk, ins, outs, stage_ref, result_ref, sems):
    combined_ref, x_ref, gate_ref, gains_ref, out_ref, up_ref, down_ref = ins
    (result_out,) = outs
    slots, lines, breadth, channels = result_ref.shape
    owners = x_ref.shape[0] // share
    half = down_ref.shape[0]
    count = chunk // LANES
    gain_out, gain = [spread_gain(gains_ref[n : n + 1, :]) for n in (2, 3)]
    out_t, down_t = halved(out_ref[1]), down_ref[...].T
    gate_t, up_t = halved(up_ref[:, :half]), up_ref[:, half:].T
    hold_combined(combined_ref, stage_ref, share, sources)
    combined = read_combined(stage_ref, owners, lines, share, 0, lines)
    hidden = channel_norm(combined, gain_out)
    current = x_ref[...] + gate_ref[...] * dot(out_t, hidden)
    trans_in = channel_norm(current, gain)
    block = min(256, half)
    for base in range(0, half, block):
        gate_part = dot(gate_t[base : base + block], trans_in)
        up_part = dot(up_t[base : base + block], trans_in)
        trans_hidden = (gate_part * twice_sigmoid(gate_part) * up_part).astype(BF16)
        current = current + dot(down_t[:, base : base + block], trans_hidden)
    writes = []
    for first in range(0, lines, count):
        for line in range(first, first + count):
            result = current[:, line * LANES : (line + 1) * LANES].T
            for slot in range(slots):
                result_ref[slot, line] = result[slot * breadth : (slot + 1) * breadth]
        piece = slice(first, first + count)
        writes += start_all([(result_ref.at[:, piece], result_out.at[:, piece])], sems, first // count)
    for write in writes:
        write.wait()


def call(kernel, operands, outs, scratch=(), in_hbm=False, out_hbm=False):
    in_place, held = pl.BlockSpec(memory_space=pltpu.HBM), pl.BlockSpec(memory_space=pltpu.VMEM)
    count = len(operands)

    def body(*refs):
        kernel(refs[:count], refs[count : count + len(outs)], *refs[count + len(outs) :])

    return pl.pallas_call(
        body,
        in_specs=[in_place if in_hbm else held] * count,
        out_specs=[in_place if out_hbm else held] * len(outs),
        out_shape=[jax.ShapeDtypeStruct(shape, dtype) for shape, dtype in outs],
        scratch_shapes=list(scratch),
        compiler_params=pltpu.CompilerParams(vmem_limit_bytes=VMEM_BYTES),
    )(*[pltpu.with_memory_space_constraint(array, pltpu.HBM) if in_hbm else array for array in operands])


def exchange(values, axes, order):
    return lax.all_to_all(values, axes, split_axis=0, concat_axis=0, axis_index_groups=[order], tiled=True)


def per_device(
    rows,
    halves,
    nears,
    pair_map,
    pair_mask,
    gain_in,
    proj_weight,
    gate_weight,
    gain_out,
    out_weight,
    trans_gain,
    trans_up,
    trans_down,
):
    height, breadth, channels = pair_map.shape
    tokens = height * breadth
    lines = tokens // LANES
    hid = gain_out.shape[1]
    cols = halves * nears
    owners = rows * cols
    share = hid // owners
    chunk = min(4 * LANES, tokens)
    split = halves if share % 8 == 0 else 1
    first_share = split * share
    held = ((LANES // breadth, lines, breadth, channels), F32)
    grouped = pair_map.reshape(held[0])
    wide = ((channels, tokens), F32)
    result = pltpu.VMEM((owners * share * lines, LANES), F32)
    spare = pltpu.VMEM((8, LANES) if share % 8 == 0 else (owners * 2 * share * lines, LANES), F32)

    def message(own):
        return ((hid // own, 2 * own * lines, LANES), BF16)

    def listed(count):
        middle = (count - 1) // 2
        places = [(col, row) for col in range(count) for row in range(rows)]
        places.sort(key=lambda at: (at != (middle, 0), -abs(at[0] - middle), -at[1]))
        order = [col * rows + row for col, row in places]
        return order, [[order.index(col * rows + row) for row in range(rows)] for col in range(count)]

    order, everyone = listed(cols)
    near_order, beside = listed(nears) if split > 1 else (order, everyone)
    single = [[n] for n in range(owners)]
    paired = single
    if split > 1:
        paired = [
            [everyone[half * nears + place // rows][place % rows] for half in range(halves)] for place in near_order
        ]

    def combine(both, own, sources, outgoing):
        kernel = functools.partial(combine_kernel, sources, everyone, breadth, own, outgoing)
        answer = ((owners, own * lines, LANES), BF16)
        return exchange(call(kernel, (both,), [answer])[0], ALL_AXES, order)

    operands = (grouped, pair_mask, proj_weight, gate_weight, gain_in, gain_out, trans_gain.reshape(1, -1))
    both, gate, current, mask, gains = call(
        functools.partial(project_kernel, first_share),
        operands,
        [message(first_share), wide, wide, ((lines, LANES), F32), ((8, channels), F32)],
        (
            spare,
            *[
                pltpu.VMEM(array.shape[1:] if array.ndim == 3 else array.shape, array.dtype)
                for array in operands
            ],
            pltpu.SemaphoreType.DMA((len(operands),)),
        ),
        in_hbm=True,
    )
    both = exchange(both, NEAR_AXES if split > 1 else ALL_AXES, near_order)
    combined = combine(both, first_share, beside, True)
    both, gate, current = call(
        functools.partial(middle_kernel, first_share, paired, share, tokens),
        (combined, current, gate, mask, gains, proj_weight, gate_weight, out_weight),
        [message(share), wide, wide],
        (result, spare),
    )
    combined = combine(exchange(both, ALL_AXES, order), share, everyone, False)
    (pair_out,) = call(
        functools.partial(last_kernel, share, single, chunk),
        (combined, current, gate, gains, out_weight, trans_up, trans_down),
        [held],
        (result, pltpu.VMEM(*held), pltpu.SemaphoreType.DMA((tokens // chunk,))),
        out_hbm=True,
    )
    return pair_out.reshape(pair_map.shape)


def solution(mesh):
    groups, rows, cols = (mesh.shape[name] for name in ("grp", "row", "col"))
    halves = 2 if cols % 2 == 0 else 1
    nears = cols // halves
    folded = Mesh(mesh.devices.reshape(groups, rows, halves, nears), ("grp", "row", "half", "near"))
    tokens = (("grp", "row"), ("half", "near"))
    in_specs = (P(*tokens, None), P(*tokens)) + (P(),) * 8

    def body(*args):
        return per_device(rows, halves, nears, *args)

    return jax.shard_map(body, mesh=folded, in_specs=in_specs, out_specs=P(*tokens, None), check_vma=False)
```

```python
import functools

import jax
import jax.numpy as jnp
from jax import lax
from jax.experimental import pallas as pl
from jax.experimental.pallas import tpu as pltpu
from jax.sharding import Mesh
from jax.sharding import PartitionSpec as P

NEAR_AXES = ("near", "row")
ALL_AXES = ("half", "near", "row")
LANES = 128
VMEM_BYTES = 24 * 1024 * 1024
F32, BF16 = jnp.float32, jnp.bfloat16


def dot(left, right, contract=(1, 0)):
    return lax.dot_general(
        left, right, (((contract[0],), (contract[1],)), ((), ())), preferred_element_type=F32
    )


def halved(weight):
    return weight.T * 0.5


def twice_sigmoid(half):
    return jnp.tanh(half) + 1.0


def channel_norm(values, gain):
    wide = jnp.concatenate([gain] * (values.shape[1] // LANES), axis=1)
    centred = values - jnp.mean(values, axis=0, keepdims=True)
    spread = jnp.mean(centred * centred, axis=0, keepdims=True)
    return (centred * lax.rsqrt(spread + 1e-05) * wide).astype(BF16)


def spread_gain(row):
    return jnp.broadcast_to(row, (LANES, row.shape[1])).T


def token_mask(mask, lines):
    height, breadth = mask.shape
    wide = jnp.concatenate([mask.astype(F32)] * (LANES // breadth), axis=1)
    row = lax.broadcasted_iota(jnp.int32, wide.shape, 0)
    lane = lax.broadcasted_iota(jnp.int32, wide.shape, 1)
    wide = jnp.where(row // lines == lane // breadth, wide, 0.0).astype(BF16)
    line = lax.broadcasted_iota(jnp.int32, (lines, height), 0)
    source = lax.broadcasted_iota(jnp.int32, (lines, height), 1)
    return dot((source % lines == line).astype(BF16), wide)


def emit_message(normed, weight_t, mask, line, message_ref, stage_ref, share):
    projected = dot(weight_t, normed)
    hid = weight_t.shape[0] // 4
    owners = hid // share
    for part in range(normed.shape[1] // LANES):
        here = projected[:, part * LANES : (part + 1) * LANES]
        at = line + part
        keep = mask[at : at + 1]
        left = twice_sigmoid(here[:hid]) * here[hid : 2 * hid] * keep
        right = twice_sigmoid(here[2 * hid : 3 * hid]) * here[3 * hid :] * keep
        if share % 8 == 0:
            for owner in range(owners):
                rows = slice(owner * share, (owner + 1) * share)
                both = jnp.concatenate([left[rows], right[rows]], axis=0).astype(BF16)
                message_ref[owner, 2 * share * at : 2 * share * (at + 1), :] = both
        else:
            lines = message_ref.shape[1] // 2
            stage_ref[pl.ds(2 * at, owners, stride=2 * lines), :] = left
            stage_ref[pl.ds(2 * at + 1, owners, stride=2 * lines), :] = right
    if share % 8 and line + normed.shape[1] // LANES == mask.shape[0]:
        message_ref[...] = stage_ref[...].astype(BF16).reshape(message_ref.shape)


def start_all(pairs, sems, first=0):
    copies = [pltpu.make_async_copy(src, dst, sems.at[first + n]) for n, (src, dst) in enumerate(pairs)]
    for copy in copies:
        copy.start()
    return copies


def line_tokens(x_ref, line):
    return jnp.concatenate([x_ref[slot, line] for slot in range(x_ref.shape[0])], axis=0)


def project_kernel(share, ins, outs, stage_ref, x_ref, mask_ref, weight_ref, gate_ref, gain_in_ref, gain_out_ref, trans_gain_ref, sems):
    message_ref, gate_out, turned_out, mask_out, gains_out = outs
    x_in, mask_in, weight_in, gate_in, gain_in, gain_out, trans_gain = ins
    lines = x_ref.shape[1]
    pairs = [
        (weight_in.at[0], weight_ref),
        (x_in, x_ref),
        (gain_in, gain_in_ref),
        (mask_in, mask_ref),
        (gate_in.at[0], gate_ref),
        (gain_out, gain_out_ref),
        (trans_gain, trans_gain_ref),
    ]
    for copy in start_all(pairs, sems):
        copy.wait()
    mask = token_mask(mask_ref[...], lines)
    current = jnp.concatenate([line_tokens(x_ref, line).T for line in range(lines)], axis=1)
    normed = channel_norm(current, spread_gain(gain_in_ref[0:1, :]))
    emit_message(normed, halved(weight_ref[...]), mask, 0, message_ref, stage_ref, share)
    gate_out[...] = twice_sigmoid(dot(halved(gate_ref[...]), normed))
    turned_out[...] = current
    mask_out[...] = mask
    rows = [gain_out_ref[0:1, :], gain_in_ref[1:2, :], gain_out_ref[1:2, :], trans_gain_ref[...]]
    gains_out[...] = jnp.concatenate(rows + rows, axis=0)


def one_hot(rows, columns, wanted):
    row = lax.broadcasted_iota(jnp.int32, (rows, columns), 0)
    column = lax.broadcasted_iota(jnp.int32, (rows, columns), 1)
    return (wanted(row) == column).astype(BF16)


def swap_matrix(slots, breadth):
    size = slots * LANES
    return one_hot(
        size, size, lambda lane: lane // breadth % slots * LANES + lane // LANES * breadth + lane % breadth
    )


def combine_kernel(sources, owners, breadth, share, outgoing, ins, outs):
    near, cols, rows = len(sources), len(owners), len(owners[0])
    (both_ref,), (combined_ref,) = ins, outs
    slots = LANES // breadth
    span = both_ref.shape[1]
    lines = span // (2 * share)
    pack = max(1, slots // near)
    groups = share // pack
    size = span // pack
    swap = swap_matrix(slots, breadth)

    def source(row):
        channel = row // size * groups + row // lines % groups
        return row % lines * (2 * share) + row // (groups * lines) % 2 * share + channel

    order = one_hot(span, span, source)
    wide = []
    for row in range(rows):
        here = jnp.concatenate([both_ref[sources[col][row]] for col in range(near)], axis=1)
        here = dot(order, here).astype(BF16)
        wide.append(jnp.concatenate([here[n * size : (n + 1) * size] for n in range(pack)], axis=1))
    wide = jnp.concatenate(wide, axis=0)
    block = slots * LANES
    swapped = [dot(wide[:, first : first + block], swap) for first in range(0, wide.shape[1], block)]

    def whole(side, group):
        columns = []
        for part in swapped:
            held = []
            for row in range(rows):
                first = row * size + (side * groups + group) * lines
                held += [part[first : first + lines, slot * LANES : (slot + 1) * LANES] for slot in range(slots)]
            columns.append(jnp.concatenate(held, axis=0))
        return jnp.concatenate(columns, axis=1).astype(BF16)

    products = [None] * share
    for group in range(groups):
        left, right = whole(0, group), whole(1, group)
        for place in range(pack):
            mine = left
            if pack > 1:
                lane = lax.broadcasted_iota(jnp.int32, left.shape, 1)
                mine = jnp.where(lane // (near * breadth) == place, left, jnp.zeros_like(left))
            products[place * groups + group] = dot(mine, right, (1, 1) if outgoing else (0, 0))

    for high in range(cols // slots):
        lanes = slice(high * LANES, (high + 1) * LANES)
        held = []
        for row in range(rows):
            for product in products:
                parts = [
                    product[(row * slots + slot) * lines : (row * slots + slot + 1) * lines, lanes]
                    for slot in range(slots)
                ]
                held.append(jnp.concatenate(parts, axis=1))
        back = dot(jnp.concatenate(held, axis=0).astype(BF16), swap).astype(BF16)
        for low in range(slots):
            for row in range(rows):
                first = row * share * lines
                combined_ref[owners[high * slots + low][row]] = back[
                    first : first + share * lines, low * LANES : (low + 1) * LANES
                ]


def hold_combined(combined_ref, stage_ref, share, sources):
    span = combined_ref.shape[1]
    lines = span // share
    order = one_hot(span, span, lambda row: row % share * lines + row // share)
    order = jnp.concatenate([order] * len(sources[0]), axis=1)
    for first in range(0, len(sources), 2):
        blocks = [
            jnp.concatenate([combined_ref[source] for source in sources[owner]], axis=0)
            for owner in (first, first + 1)
        ]
        ordered = dot(order, jnp.concatenate(blocks, axis=1))
        for n in range(2):
            stage_ref[(first + n) * span : (first + n + 1) * span, :] = ordered[:, n * LANES : (n + 1) * LANES]


def read_combined(stage_ref, owners, lines, share, first, count):
    columns = []
    for line in range(first, first + count):
        if share % 8 == 0:
            held = [
                stage_ref[(owner * lines + line) * share : (owner * lines + line + 1) * share, :]
                for owner in range(owners)
            ]
            columns.append(jnp.concatenate(held, axis=0))
        else:
            columns.append(stage_ref[pl.ds(line, owners, stride=lines), :])
    return jnp.concatenate(columns, axis=1)


def middle_kernel(share, sources, next_share, chunk, ins, outs, stage_ref, message_stage_ref):
    combined_ref, x_ref, gate_ref, mask_ref, gains_ref, proj_ref, gate_weight_ref, out_ref = ins
    message_ref, gate_out, next_ref = outs
    tokens = x_ref.shape[1]
    lines = tokens // LANES
    owners = x_ref.shape[0] // share
    hold_combined(combined_ref, stage_ref, share, sources)
    mask = mask_ref[...]
    gain_out, gain = [spread_gain(gains_ref[n : n + 1, :]) for n in (0, 1)]
    out_t, proj_t, gate_t = halved(out_ref[0]), halved(proj_ref[1]), halved(gate_weight_ref[1])
    for start in range(0, tokens, chunk):
        here = slice(start, start + chunk)
        combined = read_combined(stage_ref, owners, lines, share, start // LANES, chunk // LANES)
        hidden = channel_norm(combined, gain_out)
        current = x_ref[:, here] + gate_ref[:, here] * dot(out_t, hidden)
        next_ref[:, here] = current
        normed = channel_norm(current, gain)
        emit_message(normed, proj_t, mask, start // LANES, message_ref, message_stage_ref, next_share)
        gate_out[:, here] = twice_sigmoid(dot(gate_t, normed))


def last_kernel(share, sources, chunk, ins, outs, stage_ref, result_ref, sems):
    combined_ref, x_ref, gate_ref, gains_ref, out_ref, up_ref, down_ref = ins
    (result_out,) = outs
    slots, lines, breadth, channels = result_ref.shape
    owners = x_ref.shape[0] // share
    half = down_ref.shape[0]
    count = chunk // LANES
    gain_out, gain = [spread_gain(gains_ref[n : n + 1, :]) for n in (2, 3)]
    out_t, down_t = halved(out_ref[1]), down_ref[...].T
    gate_t, up_t = halved(up_ref[:, :half]), up_ref[:, half:].T
    hold_combined(combined_ref, stage_ref, share, sources)
    combined = read_combined(stage_ref, owners, lines, share, 0, lines)
    hidden = channel_norm(combined, gain_out)
    current = x_ref[...] + gate_ref[...] * dot(out_t, hidden)
    trans_in = channel_norm(current, gain)
    block = min(256, half)
    for base in range(0, half, block):
        gate_part = dot(gate_t[base : base + block], trans_in)
        up_part = dot(up_t[base : base + block], trans_in)
        trans_hidden = (gate_part * twice_sigmoid(gate_part) * up_part).astype(BF16)
        current = current + dot(down_t[:, base : base + block], trans_hidden)
    writes = []
    for first in range(0, lines, count):
        for line in range(first, first + count):
            result = current[:, line * LANES : (line + 1) * LANES].T
            for slot in range(slots):
                result_ref[slot, line] = result[slot * breadth : (slot + 1) * breadth]
        piece = slice(first, first + count)
        writes += start_all([(result_ref.at[:, piece], result_out.at[:, piece])], sems, first // count)
    for write in writes:
        write.wait()


def call(kernel, operands, outs, scratch=(), in_hbm=False, out_hbm=False):
    in_place, held = pl.BlockSpec(memory_space=pltpu.HBM), pl.BlockSpec(memory_space=pltpu.VMEM)
    count = len(operands)

    def body(*refs):
        kernel(refs[:count], refs[count : count + len(outs)], *refs[count + len(outs) :])

    return pl.pallas_call(
        body,
        in_specs=[in_place if in_hbm else held] * count,
        out_specs=[in_place if out_hbm else held] * len(outs),
        out_shape=[jax.ShapeDtypeStruct(shape, dtype) for shape, dtype in outs],
        scratch_shapes=list(scratch),
        compiler_params=pltpu.CompilerParams(vmem_limit_bytes=VMEM_BYTES),
    )(*[pltpu.with_memory_space_constraint(array, pltpu.HBM) if in_hbm else array for array in operands])


def exchange(values, axes, order):
    return lax.all_to_all(values, axes, split_axis=0, concat_axis=0, axis_index_groups=[order], tiled=True)


def per_device(
    rows,
    halves,
    nears,
    pair_map,
    pair_mask,
    gain_in,
    proj_weight,
    gate_weight,
    gain_out,
    out_weight,
    trans_gain,
    trans_up,
    trans_down,
):
    height, breadth, channels = pair_map.shape
    tokens = height * breadth
    lines = tokens // LANES
    hid = gain_out.shape[1]
    cols = halves * nears
    owners = rows * cols
    share = hid // owners
    chunk = min(4 * LANES, tokens)
    split = halves if share % 8 == 0 else 1
    first_share = split * share
    held = ((LANES // breadth, lines, breadth, channels), F32)
    grouped = pair_map.reshape(held[0])
    wide = ((channels, tokens), F32)
    result = pltpu.VMEM((owners * share * lines, LANES), F32)
    spare = pltpu.VMEM((8, LANES) if share % 8 == 0 else (owners * 2 * share * lines, LANES), F32)

    def message(own):
        return ((hid // own, 2 * own * lines, LANES), BF16)

    def listed(count, rank):
        places = sorted([(col, row) for col in range(count) for row in range(rows)], key=rank)
        order = [col * rows + row for col, row in places]
        return order, [[order.index(col * rows + row) for row in range(rows)] for col in range(count)]

    middle = (cols - 1) // 2
    order, everyone = listed(cols, lambda at: (abs(at[0] - middle), -at[0], at[1]))
    near_order, beside = order, everyone
    if split > 1:
        near_order, beside = listed(nears, lambda at: (at != (0, 0), -at[0], -at[1]))
    single = [[n] for n in range(owners)]
    paired = single
    if split > 1:
        paired = [
            [everyone[half * nears + place // rows][place % rows] for half in range(halves)] for place in near_order
        ]

    def combine(both, own, sources, outgoing):
        kernel = functools.partial(combine_kernel, sources, everyone, breadth, own, outgoing)
        answer = ((owners, own * lines, LANES), BF16)
        return exchange(call(kernel, (both,), [answer])[0], ALL_AXES, order)

    operands = (grouped, pair_mask, proj_weight, gate_weight, gain_in, gain_out, trans_gain.reshape(1, -1))
    both, gate, current, mask, gains = call(
        functools.partial(project_kernel, first_share),
        operands,
        [message(first_share), wide, wide, ((lines, LANES), F32), ((8, channels), F32)],
        (
            spare,
            *[
                pltpu.VMEM(array.shape[1:] if array.ndim == 3 else array.shape, array.dtype)
                for array in operands
            ],
            pltpu.SemaphoreType.DMA((len(operands),)),
        ),
        in_hbm=True,
    )
    both = exchange(both, NEAR_AXES if split > 1 else ALL_AXES, near_order)
    combined = combine(both, first_share, beside, True)
    both, gate, current = call(
        functools.partial(middle_kernel, first_share, paired, share, tokens),
        (combined, current, gate, mask, gains, proj_weight, gate_weight, out_weight),
        [message(share), wide, wide],
        (result, spare),
    )
    combined = combine(exchange(both, ALL_AXES, order), share, everyone, False)
    (pair_out,) = call(
        functools.partial(last_kernel, share, single, chunk),
        (combined, current, gate, gains, out_weight, trans_up, trans_down),
        [held],
        (result, pltpu.VMEM(*held), pltpu.SemaphoreType.DMA((tokens // chunk,))),
        out_hbm=True,
    )
    return pair_out.reshape(pair_map.shape)


def solution(mesh):
    groups, rows, cols = (mesh.shape[name] for name in ("grp", "row", "col"))
    halves = 2 if cols % 2 == 0 else 1
    nears = cols // halves
    folded = Mesh(mesh.devices.reshape(groups, rows, halves, nears), ("grp", "row", "half", "near"))
    tokens = (("grp", "row"), ("half", "near"))
    in_specs = (P(*tokens, None), P(*tokens)) + (P(),) * 8

    def body(*args):
        return per_device(rows, halves, nears, *args)

    return jax.shard_map(body, mesh=folded, in_specs=in_specs, out_specs=P(*tokens, None), check_vma=False)
```

```python
import functools

import jax
import jax.numpy as jnp
from jax import lax
from jax.experimental import pallas as pl
from jax.experimental.pallas import tpu as pltpu
from jax.sharding import Mesh
from jax.sharding import PartitionSpec as P

NEAR_AXES = ("near", "row")
ALL_AXES = ("half", "near", "row")
LANES = 128
VMEM_BYTES = 24 * 1024 * 1024
F32, BF16 = jnp.float32, jnp.bfloat16


def dot(left, right, contract=(1, 0)):
    return lax.dot_general(
        left, right, (((contract[0],), (contract[1],)), ((), ())), preferred_element_type=F32
    )


def halved(weight):
    return weight.T * 0.5


def twice_sigmoid(half):
    return jnp.tanh(half) + 1.0


def channel_norm(values, gain):
    wide = jnp.concatenate([gain] * (values.shape[1] // LANES), axis=1)
    centred = values - jnp.mean(values, axis=0, keepdims=True)
    spread = jnp.mean(centred * centred, axis=0, keepdims=True)
    return (centred * lax.rsqrt(spread + 1e-05) * wide).astype(BF16)


def spread_gain(row):
    return jnp.broadcast_to(row, (LANES, row.shape[1])).T


def token_mask(mask, lines):
    height, breadth = mask.shape
    wide = jnp.concatenate([mask.astype(F32)] * (LANES // breadth), axis=1)
    row = lax.broadcasted_iota(jnp.int32, wide.shape, 0)
    lane = lax.broadcasted_iota(jnp.int32, wide.shape, 1)
    wide = jnp.where(row // lines == lane // breadth, wide, 0.0).astype(BF16)
    line = lax.broadcasted_iota(jnp.int32, (lines, height), 0)
    source = lax.broadcasted_iota(jnp.int32, (lines, height), 1)
    return dot((source % lines == line).astype(BF16), wide)


def emit_message(normed, weight_t, mask, line, message_ref, stage_ref, share):
    projected = dot(weight_t, normed)
    hid = weight_t.shape[0] // 4
    owners = hid // share
    for part in range(normed.shape[1] // LANES):
        here = projected[:, part * LANES : (part + 1) * LANES]
        at = line + part
        keep = mask[at : at + 1]
        left = twice_sigmoid(here[:hid]) * here[hid : 2 * hid] * keep
        right = twice_sigmoid(here[2 * hid : 3 * hid]) * here[3 * hid :] * keep
        if share % 8 == 0:
            for owner in range(owners):
                rows = slice(owner * share, (owner + 1) * share)
                both = jnp.concatenate([left[rows], right[rows]], axis=0).astype(BF16)
                message_ref[owner, 2 * share * at : 2 * share * (at + 1), :] = both
        else:
            lines = message_ref.shape[1] // 2
            stage_ref[pl.ds(2 * at, owners, stride=2 * lines), :] = left
            stage_ref[pl.ds(2 * at + 1, owners, stride=2 * lines), :] = right
    if share % 8 and line + normed.shape[1] // LANES == mask.shape[0]:
        message_ref[...] = stage_ref[...].astype(BF16).reshape(message_ref.shape)


def start_all(pairs, sems, first=0):
    copies = [pltpu.make_async_copy(src, dst, sems.at[first + n]) for n, (src, dst) in enumerate(pairs)]
    for copy in copies:
        copy.start()
    return copies


def line_tokens(x_ref, line):
    return jnp.concatenate([x_ref[slot, line] for slot in range(x_ref.shape[0])], axis=0)


def project_kernel(share, ins, outs, stage_ref, x_ref, mask_ref, weight_ref, gate_ref, gain_in_ref, gain_out_ref, trans_gain_ref, sems):
    message_ref, gate_out, turned_out, mask_out, gains_out = outs
    x_in, mask_in, weight_in, gate_in, gain_in, gain_out, trans_gain = ins
    lines = x_ref.shape[1]
    pairs = [
        (x_in, x_ref),
        (weight_in.at[0], weight_ref),
        (gain_in, gain_in_ref),
        (mask_in, mask_ref),
        (gate_in.at[0], gate_ref),
        (gain_out, gain_out_ref),
        (trans_gain, trans_gain_ref),
    ]
    large, *small = start_all(pairs, sems)
    for copy in small:
        copy.wait()
    mask = token_mask(mask_ref[...], lines)
    gain, weight_t, gate_t = spread_gain(gain_in_ref[0:1, :]), halved(weight_ref[...]), halved(gate_ref[...])
    large.wait()
    current = jnp.concatenate([line_tokens(x_ref, line).T for line in range(lines)], axis=1)
    normed = channel_norm(current, gain)
    emit_message(normed, weight_t, mask, 0, message_ref, stage_ref, share)
    gate_out[...] = twice_sigmoid(dot(gate_t, normed))
    turned_out[...] = current
    mask_out[...] = mask
    rows = [gain_out_ref[0:1, :], gain_in_ref[1:2, :], gain_out_ref[1:2, :], trans_gain_ref[...]]
    gains_out[...] = jnp.concatenate(rows + rows, axis=0)


def one_hot(rows, columns, wanted):
    row = lax.broadcasted_iota(jnp.int32, (rows, columns), 0)
    column = lax.broadcasted_iota(jnp.int32, (rows, columns), 1)
    return (wanted(row) == column).astype(BF16)


def swap_matrix(slots, breadth):
    size = slots * LANES
    return one_hot(
        size, size, lambda lane: lane // breadth % slots * LANES + lane // LANES * breadth + lane % breadth
    )


def combine_kernel(sources, owners, breadth, share, outgoing, ins, outs):
    near, cols, rows = len(sources), len(owners), len(owners[0])
    (both_ref,), (combined_ref,) = ins, outs
    slots = LANES // breadth
    span = both_ref.shape[1]
    lines = span // (2 * share)
    pack = max(1, slots // near)
    groups = share // pack
    size = span // pack
    swap = swap_matrix(slots, breadth)

    def source(row):
        channel = row // size * groups + row // lines % groups
        return row % lines * (2 * share) + row // (groups * lines) % 2 * share + channel

    order = one_hot(span, span, source)
    wide = []
    for row in range(rows):
        here = jnp.concatenate([both_ref[sources[col][row]] for col in range(near)], axis=1)
        here = dot(order, here).astype(BF16)
        wide.append(jnp.concatenate([here[n * size : (n + 1) * size] for n in range(pack)], axis=1))
    wide = jnp.concatenate(wide, axis=0)
    block = slots * LANES
    swapped = [dot(wide[:, first : first + block], swap) for first in range(0, wide.shape[1], block)]

    def whole(side, group):
        columns = []
        for part in swapped:
            held = []
            for row in range(rows):
                first = row * size + (side * groups + group) * lines
                held += [part[first : first + lines, slot * LANES : (slot + 1) * LANES] for slot in range(slots)]
            columns.append(jnp.concatenate(held, axis=0))
        return jnp.concatenate(columns, axis=1).astype(BF16)

    products = [None] * share
    for group in range(groups):
        left, right = whole(0, group), whole(1, group)
        for place in range(pack):
            mine = left
            if pack > 1:
                lane = lax.broadcasted_iota(jnp.int32, left.shape, 1)
                mine = jnp.where(lane // (near * breadth) == place, left, jnp.zeros_like(left))
            products[place * groups + group] = dot(mine, right, (1, 1) if outgoing else (0, 0))

    for high in range(cols // slots):
        lanes = slice(high * LANES, (high + 1) * LANES)
        held = []
        for row in range(rows):
            for product in products:
                parts = [
                    product[(row * slots + slot) * lines : (row * slots + slot + 1) * lines, lanes]
                    for slot in range(slots)
                ]
                held.append(jnp.concatenate(parts, axis=1))
        back = dot(jnp.concatenate(held, axis=0).astype(BF16), swap).astype(BF16)
        for low in range(slots):
            for row in range(rows):
                first = row * share * lines
                combined_ref[owners[high * slots + low][row]] = back[
                    first : first + share * lines, low * LANES : (low + 1) * LANES
                ]


def hold_combined(combined_ref, stage_ref, share, sources):
    span = combined_ref.shape[1]
    lines = span // share
    order = one_hot(span, span, lambda row: row % share * lines + row // share)
    order = jnp.concatenate([order] * len(sources[0]), axis=1)
    for first in range(0, len(sources), 2):
        blocks = [
            jnp.concatenate([combined_ref[source] for source in sources[owner]], axis=0)
            for owner in (first, first + 1)
        ]
        ordered = dot(order, jnp.concatenate(blocks, axis=1))
        for n in range(2):
            stage_ref[(first + n) * span : (first + n + 1) * span, :] = ordered[:, n * LANES : (n + 1) * LANES]


def read_combined(stage_ref, owners, lines, share, first, count):
    columns = []
    for line in range(first, first + count):
        if share % 8 == 0:
            held = [
                stage_ref[(owner * lines + line) * share : (owner * lines + line + 1) * share, :]
                for owner in range(owners)
            ]
            columns.append(jnp.concatenate(held, axis=0))
        else:
            columns.append(stage_ref[pl.ds(line, owners, stride=lines), :])
    return jnp.concatenate(columns, axis=1)


def middle_kernel(share, sources, next_share, chunk, ins, outs, stage_ref, message_stage_ref):
    combined_ref, x_ref, gate_ref, mask_ref, gains_ref, proj_ref, gate_weight_ref, out_ref = ins
    message_ref, gate_out, next_ref = outs
    tokens = x_ref.shape[1]
    lines = tokens // LANES
    owners = x_ref.shape[0] // share
    hold_combined(combined_ref, stage_ref, share, sources)
    mask = mask_ref[...]
    gain_out, gain = [spread_gain(gains_ref[n : n + 1, :]) for n in (0, 1)]
    out_t, proj_t, gate_t = halved(out_ref[0]), halved(proj_ref[1]), halved(gate_weight_ref[1])
    for start in range(0, tokens, chunk):
        here = slice(start, start + chunk)
        combined = read_combined(stage_ref, owners, lines, share, start // LANES, chunk // LANES)
        hidden = channel_norm(combined, gain_out)
        current = x_ref[:, here] + gate_ref[:, here] * dot(out_t, hidden)
        next_ref[:, here] = current
        normed = channel_norm(current, gain)
        emit_message(normed, proj_t, mask, start // LANES, message_ref, message_stage_ref, next_share)
        gate_out[:, here] = twice_sigmoid(dot(gate_t, normed))


def last_kernel(share, sources, chunk, ins, outs, stage_ref, result_ref, sems):
    combined_ref, x_ref, gate_ref, gains_ref, out_ref, up_ref, down_ref = ins
    (result_out,) = outs
    slots, lines, breadth, channels = result_ref.shape
    owners = x_ref.shape[0] // share
    half = down_ref.shape[0]
    count = chunk // LANES
    gain_out, gain = [spread_gain(gains_ref[n : n + 1, :]) for n in (2, 3)]
    out_t, down_t = halved(out_ref[1]), down_ref[...].T
    gate_t, up_t = halved(up_ref[:, :half]), up_ref[:, half:].T
    hold_combined(combined_ref, stage_ref, share, sources)
    combined = read_combined(stage_ref, owners, lines, share, 0, lines)
    hidden = channel_norm(combined, gain_out)
    current = x_ref[...] + gate_ref[...] * dot(out_t, hidden)
    trans_in = channel_norm(current, gain)
    block = min(256, half)
    for base in range(0, half, block):
        gate_part = dot(gate_t[base : base + block], trans_in)
        up_part = dot(up_t[base : base + block], trans_in)
        trans_hidden = (gate_part * twice_sigmoid(gate_part) * up_part).astype(BF16)
        current = current + dot(down_t[:, base : base + block], trans_hidden)
    writes = []
    for first in range(0, lines, count):
        for line in range(first, first + count):
            result = current[:, line * LANES : (line + 1) * LANES].T
            for slot in range(slots):
                result_ref[slot, line] = result[slot * breadth : (slot + 1) * breadth]
        piece = slice(first, first + count)
        writes += start_all([(result_ref.at[:, piece], result_out.at[:, piece])], sems, first // count)
    for write in writes:
        write.wait()


def call(kernel, operands, outs, scratch=(), in_hbm=False, out_hbm=False):
    in_place, held = pl.BlockSpec(memory_space=pltpu.HBM), pl.BlockSpec(memory_space=pltpu.VMEM)
    count = len(operands)

    def body(*refs):
        kernel(refs[:count], refs[count : count + len(outs)], *refs[count + len(outs) :])

    return pl.pallas_call(
        body,
        in_specs=[in_place if in_hbm else held] * count,
        out_specs=[in_place if out_hbm else held] * len(outs),
        out_shape=[jax.ShapeDtypeStruct(shape, dtype) for shape, dtype in outs],
        scratch_shapes=list(scratch),
        compiler_params=pltpu.CompilerParams(vmem_limit_bytes=VMEM_BYTES),
    )(*[pltpu.with_memory_space_constraint(array, pltpu.HBM) if in_hbm else array for array in operands])


def exchange(values, axes, order):
    return lax.all_to_all(values, axes, split_axis=0, concat_axis=0, axis_index_groups=[order], tiled=True)


def per_device(
    rows,
    halves,
    nears,
    pair_map,
    pair_mask,
    gain_in,
    proj_weight,
    gate_weight,
    gain_out,
    out_weight,
    trans_gain,
    trans_up,
    trans_down,
):
    height, breadth, channels = pair_map.shape
    tokens = height * breadth
    lines = tokens // LANES
    hid = gain_out.shape[1]
    cols = halves * nears
    owners = rows * cols
    share = hid // owners
    chunk = min(4 * LANES, tokens)
    split = halves if share % 8 == 0 else 1
    first_share = split * share
    held = ((LANES // breadth, lines, breadth, channels), F32)
    grouped = pair_map.reshape(held[0])
    wide = ((channels, tokens), F32)
    result = pltpu.VMEM((owners * share * lines, LANES), F32)
    spare = pltpu.VMEM((8, LANES) if share % 8 == 0 else (owners * 2 * share * lines, LANES), F32)

    def message(own):
        return ((hid // own, 2 * own * lines, LANES), BF16)

    def listed(count, rank):
        places = sorted([(col, row) for col in range(count) for row in range(rows)], key=rank)
        order = [col * rows + row for col, row in places]
        return order, [[order.index(col * rows + row) for row in range(rows)] for col in range(count)]

    middle = (cols - 1) // 2
    order, everyone = listed(cols, lambda at: (at[0] != middle, at))
    near_order, beside = order, everyone
    if split > 1:
        near_order, beside = listed(nears, lambda at: (at != (0, 0), -at[0], -at[1]))
    single = [[n] for n in range(owners)]
    paired = single
    if split > 1:
        paired = [
            [everyone[half * nears + place // rows][place % rows] for half in range(halves)] for place in near_order
        ]

    def combine(both, own, sources, outgoing):
        kernel = functools.partial(combine_kernel, sources, everyone, breadth, own, outgoing)
        answer = ((owners, own * lines, LANES), BF16)
        return exchange(call(kernel, (both,), [answer])[0], ALL_AXES, order)

    operands = (grouped, pair_mask, proj_weight, gate_weight, gain_in, gain_out, trans_gain.reshape(1, -1))
    both, gate, current, mask, gains = call(
        functools.partial(project_kernel, first_share),
        operands,
        [message(first_share), wide, wide, ((lines, LANES), F32), ((8, channels), F32)],
        (
            spare,
            *[
                pltpu.VMEM(array.shape[1:] if array.ndim == 3 else array.shape, array.dtype)
                for array in operands
            ],
            pltpu.SemaphoreType.DMA((len(operands),)),
        ),
        in_hbm=True,
    )
    both = exchange(both, NEAR_AXES if split > 1 else ALL_AXES, near_order)
    combined = combine(both, first_share, beside, True)
    both, gate, current = call(
        functools.partial(middle_kernel, first_share, paired, share, tokens),
        (combined, current, gate, mask, gains, proj_weight, gate_weight, out_weight),
        [message(share), wide, wide],
        (result, spare),
    )
    combined = combine(exchange(both, ALL_AXES, order), share, everyone, False)
    (pair_out,) = call(
        functools.partial(last_kernel, share, single, chunk),
        (combined, current, gate, gains, out_weight, trans_up, trans_down),
        [held],
        (result, pltpu.VMEM(*held), pltpu.SemaphoreType.DMA((tokens // chunk,))),
        out_hbm=True,
    )
    return pair_out.reshape(pair_map.shape)


def solution(mesh):
    groups, rows, cols = (mesh.shape[name] for name in ("grp", "row", "col"))
    halves = 2 if cols % 2 == 0 else 1
    nears = cols // halves
    folded = Mesh(mesh.devices.reshape(groups, rows, halves, nears), ("grp", "row", "half", "near"))
    tokens = (("grp", "row"), ("half", "near"))
    in_specs = (P(*tokens, None), P(*tokens)) + (P(),) * 8

    def body(*args):
        return per_device(rows, halves, nears, *args)

    return jax.shard_map(body, mesh=folded, in_specs=in_specs, out_specs=P(*tokens, None), check_vma=False)
```

```python
import functools

import jax
import jax.numpy as jnp
from jax import lax
from jax.experimental import pallas as pl
from jax.experimental.pallas import tpu as pltpu
from jax.sharding import Mesh
from jax.sharding import PartitionSpec as P

NEAR_AXES = ("near", "row")
ALL_AXES = ("half", "near", "row")
LANES = 128
VMEM_BYTES = 24 * 1024 * 1024
F32, BF16 = jnp.float32, jnp.bfloat16


def dot(left, right, contract=(1, 0)):
    return lax.dot_general(
        left, right, (((contract[0],), (contract[1],)), ((), ())), preferred_element_type=F32
    )


def halved(weight):
    return weight.T * 0.5


def twice_sigmoid(half):
    return jnp.tanh(half) + 1.0


def channel_norm(values, gain):
    wide = jnp.concatenate([gain] * (values.shape[1] // LANES), axis=1)
    centred = values - jnp.mean(values, axis=0, keepdims=True)
    spread = jnp.mean(centred * centred, axis=0, keepdims=True)
    return (centred * lax.rsqrt(spread + 1e-05) * wide).astype(BF16)


def spread_gain(row):
    return jnp.broadcast_to(row, (LANES, row.shape[1])).T


def token_mask(mask, lines):
    height, breadth = mask.shape
    wide = jnp.concatenate([mask.astype(F32)] * (LANES // breadth), axis=1)
    row = lax.broadcasted_iota(jnp.int32, wide.shape, 0)
    lane = lax.broadcasted_iota(jnp.int32, wide.shape, 1)
    wide = jnp.where(row // lines == lane // breadth, wide, 0.0).astype(BF16)
    line = lax.broadcasted_iota(jnp.int32, (lines, height), 0)
    source = lax.broadcasted_iota(jnp.int32, (lines, height), 1)
    return dot((source % lines == line).astype(BF16), wide)


def emit_message(normed, weight_t, mask, line, message_ref, stage_ref, share):
    projected = dot(weight_t, normed)
    hid = weight_t.shape[0] // 4
    owners = hid // share
    for part in range(normed.shape[1] // LANES):
        here = projected[:, part * LANES : (part + 1) * LANES]
        at = line + part
        keep = mask[at : at + 1]
        left = twice_sigmoid(here[:hid]) * here[hid : 2 * hid] * keep
        right = twice_sigmoid(here[2 * hid : 3 * hid]) * here[3 * hid :] * keep
        if share % 8 == 0:
            for owner in range(owners):
                rows = slice(owner * share, (owner + 1) * share)
                both = jnp.concatenate([left[rows], right[rows]], axis=0).astype(BF16)
                message_ref[owner, 2 * share * at : 2 * share * (at + 1), :] = both
        else:
            lines = message_ref.shape[1] // 2
            stage_ref[pl.ds(2 * at, owners, stride=2 * lines), :] = left
            stage_ref[pl.ds(2 * at + 1, owners, stride=2 * lines), :] = right
    if share % 8 and line + normed.shape[1] // LANES == mask.shape[0]:
        message_ref[...] = stage_ref[...].astype(BF16).reshape(message_ref.shape)


def start_all(pairs, sems, first=0):
    copies = [pltpu.make_async_copy(src, dst, sems.at[first + n]) for n, (src, dst) in enumerate(pairs)]
    for copy in copies:
        copy.start()
    return copies


def line_tokens(x_ref, line):
    return jnp.concatenate([x_ref[slot, line] for slot in range(x_ref.shape[0])], axis=0)


def project_kernel(share, ins, outs, stage_ref, x_ref, mask_ref, weight_ref, gate_ref, gain_in_ref, gain_out_ref, trans_gain_ref, sems):
    message_ref, gate_out, turned_out, mask_out, gains_out = outs
    x_in, mask_in, weight_in, gate_in, gain_in, gain_out, trans_gain = ins
    lines = x_ref.shape[1]
    pairs = [
        (weight_in.at[0], weight_ref),
        (x_in, x_ref),
        (gain_in, gain_in_ref),
        (mask_in, mask_ref),
        (gate_in.at[0], gate_ref),
        (gain_out, gain_out_ref),
        (trans_gain, trans_gain_ref),
    ]
    for copy in start_all(pairs, sems):
        copy.wait()
    mask = token_mask(mask_ref[...], lines)
    current = jnp.concatenate([line_tokens(x_ref, line).T for line in range(lines)], axis=1)
    normed = channel_norm(current, spread_gain(gain_in_ref[0:1, :]))
    emit_message(normed, halved(weight_ref[...]), mask, 0, message_ref, stage_ref, share)
    gate_out[...] = twice_sigmoid(dot(halved(gate_ref[...]), normed))
    turned_out[...] = current
    mask_out[...] = mask
    rows = [gain_out_ref[0:1, :], gain_in_ref[1:2, :], gain_out_ref[1:2, :], trans_gain_ref[...]]
    gains_out[...] = jnp.concatenate(rows + rows, axis=0)


def one_hot(rows, columns, wanted):
    row = lax.broadcasted_iota(jnp.int32, (rows, columns), 0)
    column = lax.broadcasted_iota(jnp.int32, (rows, columns), 1)
    return (wanted(row) == column).astype(BF16)


def swap_matrix(slots, breadth):
    size = slots * LANES
    return one_hot(
        size, size, lambda lane: lane // breadth % slots * LANES + lane // LANES * breadth + lane % breadth
    )


def combine_kernel(sources, owners, breadth, share, outgoing, ins, outs):
    near, cols, rows = len(sources), len(owners), len(owners[0])
    (both_ref,), (combined_ref,) = ins, outs
    slots = LANES // breadth
    span = both_ref.shape[1]
    lines = span // (2 * share)
    pack = max(1, slots // near)
    groups = share // pack
    size = span // pack
    swap = swap_matrix(slots, breadth)

    def source(row):
        channel = row // size * groups + row // lines % groups
        return row % lines * (2 * share) + row // (groups * lines) % 2 * share + channel

    order = one_hot(span, span, source)
    wide = []
    for row in range(rows):
        here = jnp.concatenate([both_ref[sources[col][row]] for col in range(near)], axis=1)
        here = dot(order, here).astype(BF16)
        wide.append(jnp.concatenate([here[n * size : (n + 1) * size] for n in range(pack)], axis=1))
    wide = jnp.concatenate(wide, axis=0)
    block = slots * LANES
    swapped = [dot(wide[:, first : first + block], swap) for first in range(0, wide.shape[1], block)]

    def whole(side, group):
        columns = []
        for part in swapped:
            held = []
            for row in range(rows):
                first = row * size + (side * groups + group) * lines
                held += [part[first : first + lines, slot * LANES : (slot + 1) * LANES] for slot in range(slots)]
            columns.append(jnp.concatenate(held, axis=0))
        return jnp.concatenate(columns, axis=1).astype(BF16)

    products = [None] * share
    for group in range(groups):
        left, right = whole(0, group), whole(1, group)
        for place in range(pack):
            mine = left
            if pack > 1:
                lane = lax.broadcasted_iota(jnp.int32, left.shape, 1)
                mine = jnp.where(lane // (near * breadth) == place, left, jnp.zeros_like(left))
            products[place * groups + group] = dot(mine, right, (1, 1) if outgoing else (0, 0))

    for high in range(cols // slots):
        lanes = slice(high * LANES, (high + 1) * LANES)
        held = []
        for row in range(rows):
            for product in products:
                parts = [
                    product[(row * slots + slot) * lines : (row * slots + slot + 1) * lines, lanes]
                    for slot in range(slots)
                ]
                held.append(jnp.concatenate(parts, axis=1))
        back = dot(jnp.concatenate(held, axis=0).astype(BF16), swap).astype(BF16)
        for low in range(slots):
            for row in range(rows):
                first = row * share * lines
                combined_ref[owners[high * slots + low][row]] = back[
                    first : first + share * lines, low * LANES : (low + 1) * LANES
                ]


def hold_combined(combined_ref, stage_ref, share, sources):
    span = combined_ref.shape[1]
    lines = span // share
    order = one_hot(span, span, lambda row: row % share * lines + row // share)
    order = jnp.concatenate([order] * len(sources[0]), axis=1)
    for first in range(0, len(sources), 2):
        blocks = [
            jnp.concatenate([combined_ref[source] for source in sources[owner]], axis=0)
            for owner in (first, first + 1)
        ]
        ordered = dot(order, jnp.concatenate(blocks, axis=1))
        for n in range(2):
            stage_ref[(first + n) * span : (first + n + 1) * span, :] = ordered[:, n * LANES : (n + 1) * LANES]


def read_combined(stage_ref, owners, lines, share, first, count):
    columns = []
    for line in range(first, first + count):
        if share % 8 == 0:
            held = [
                stage_ref[(owner * lines + line) * share : (owner * lines + line + 1) * share, :]
                for owner in range(owners)
            ]
            columns.append(jnp.concatenate(held, axis=0))
        else:
            columns.append(stage_ref[pl.ds(line, owners, stride=lines), :])
    return jnp.concatenate(columns, axis=1)


def middle_kernel(share, sources, next_share, chunk, ins, outs, stage_ref, message_stage_ref):
    combined_ref, x_ref, gate_ref, mask_ref, gains_ref, proj_ref, gate_weight_ref, out_ref = ins
    message_ref, gate_out, next_ref = outs
    tokens = x_ref.shape[1]
    lines = tokens // LANES
    owners = x_ref.shape[0] // share
    hold_combined(combined_ref, stage_ref, share, sources)
    mask = mask_ref[...]
    gain_out, gain = [spread_gain(gains_ref[n : n + 1, :]) for n in (0, 1)]
    out_t, proj_t, gate_t = halved(out_ref[0]), halved(proj_ref[1]), halved(gate_weight_ref[1])
    for start in range(0, tokens, chunk):
        here = slice(start, start + chunk)
        combined = read_combined(stage_ref, owners, lines, share, start // LANES, chunk // LANES)
        hidden = channel_norm(combined, gain_out)
        current = x_ref[:, here] + gate_ref[:, here] * dot(out_t, hidden)
        next_ref[:, here] = current
        normed = channel_norm(current, gain)
        emit_message(normed, proj_t, mask, start // LANES, message_ref, message_stage_ref, next_share)
        gate_out[:, here] = twice_sigmoid(dot(gate_t, normed))


def last_kernel(share, sources, chunk, ins, outs, stage_ref, result_ref, sems):
    combined_ref, x_ref, gate_ref, gains_ref, out_ref, up_ref, down_ref = ins
    (result_out,) = outs
    slots, lines, breadth, channels = result_ref.shape
    owners = x_ref.shape[0] // share
    half = down_ref.shape[0]
    count = chunk // LANES
    gain_out, gain = [spread_gain(gains_ref[n : n + 1, :]) for n in (2, 3)]
    out_t, down_t = halved(out_ref[1]), down_ref[...].T
    gate_t, up_t = halved(up_ref[:, :half]), up_ref[:, half:].T
    hold_combined(combined_ref, stage_ref, share, sources)
    combined = read_combined(stage_ref, owners, lines, share, 0, lines)
    hidden = channel_norm(combined, gain_out)
    current = x_ref[...] + gate_ref[...] * dot(out_t, hidden)
    trans_in = channel_norm(current, gain)
    block = min(256, half)
    for base in range(0, half, block):
        gate_part = dot(gate_t[base : base + block], trans_in)
        up_part = dot(up_t[base : base + block], trans_in)
        trans_hidden = (gate_part * twice_sigmoid(gate_part) * up_part).astype(BF16)
        current = current + dot(down_t[:, base : base + block], trans_hidden)
    writes = []
    for first in range(0, lines, count):
        for line in range(first, first + count):
            result = current[:, line * LANES : (line + 1) * LANES].T
            for slot in range(slots):
                result_ref[slot, line] = result[slot * breadth : (slot + 1) * breadth]
        piece = slice(first, first + count)
        writes += start_all([(result_ref.at[:, piece], result_out.at[:, piece])], sems, first // count)
    for write in writes:
        write.wait()


def call(kernel, operands, outs, scratch=(), in_hbm=False, out_hbm=False):
    in_place, held = pl.BlockSpec(memory_space=pltpu.HBM), pl.BlockSpec(memory_space=pltpu.VMEM)
    count = len(operands)

    def body(*refs):
        kernel(refs[:count], refs[count : count + len(outs)], *refs[count + len(outs) :])

    return pl.pallas_call(
        body,
        in_specs=[in_place if in_hbm else held] * count,
        out_specs=[in_place if out_hbm else held] * len(outs),
        out_shape=[jax.ShapeDtypeStruct(shape, dtype) for shape, dtype in outs],
        scratch_shapes=list(scratch),
        compiler_params=pltpu.CompilerParams(vmem_limit_bytes=VMEM_BYTES),
    )(*[pltpu.with_memory_space_constraint(array, pltpu.HBM) if in_hbm else array for array in operands])


def exchange(values, axes, order=None):
    groups = [order] if order else None
    return lax.all_to_all(values, axes, split_axis=0, concat_axis=0, axis_index_groups=groups, tiled=True)


def per_device(
    rows,
    halves,
    nears,
    pair_map,
    pair_mask,
    gain_in,
    proj_weight,
    gate_weight,
    gain_out,
    out_weight,
    trans_gain,
    trans_up,
    trans_down,
):
    height, breadth, channels = pair_map.shape
    tokens = height * breadth
    lines = tokens // LANES
    hid = gain_out.shape[1]
    cols = halves * nears
    owners = rows * cols
    share = hid // owners
    chunk = min(4 * LANES, tokens)
    split = 1
    first_share = split * share
    held = ((LANES // breadth, lines, breadth, channels), F32)
    grouped = pair_map.reshape(held[0])
    wide = ((channels, tokens), F32)
    result = pltpu.VMEM((owners * share * lines, LANES), F32)
    spare = pltpu.VMEM((8, LANES) if share % 8 == 0 else (owners * 2 * share * lines, LANES), F32)

    def message(own):
        return ((hid // own, 2 * own * lines, LANES), BF16)

    blocks = [(col + cols // 2) % cols for col in range(cols)]
    order = [col * rows + row for col in blocks for row in range(rows)]
    everyone = [[order.index(col * rows + row) for row in range(rows)] for col in range(cols)]
    beside = [[near * rows + row for row in range(rows)] for near in range(nears)] if split > 1 else everyone
    single = [[n] for n in range(owners)]
    paired = single if split == 1 else [
        [everyone[half * nears + near][row] for half in range(halves)] for near in range(nears) for row in range(rows)
    ]

    def combine(both, own, sources, outgoing):
        kernel = functools.partial(combine_kernel, sources, everyone, breadth, own, outgoing)
        answer = ((owners, own * lines, LANES), BF16)
        return exchange(call(kernel, (both,), [answer])[0], ALL_AXES, order)

    operands = (grouped, pair_mask, proj_weight, gate_weight, gain_in, gain_out, trans_gain.reshape(1, -1))
    both, gate, current, mask, gains = call(
        functools.partial(project_kernel, first_share),
        operands,
        [message(first_share), wide, wide, ((lines, LANES), F32), ((8, channels), F32)],
        (
            spare,
            *[
                pltpu.VMEM(array.shape[1:] if array.ndim == 3 else array.shape, array.dtype)
                for array in operands
            ],
            pltpu.SemaphoreType.DMA((len(operands),)),
        ),
        in_hbm=True,
    )
    both = exchange(both, NEAR_AXES) if split > 1 else exchange(both, ALL_AXES, order)
    combined = combine(both, first_share, beside, True)
    both, gate, current = call(
        functools.partial(middle_kernel, first_share, paired, share, tokens),
        (combined, current, gate, mask, gains, proj_weight, gate_weight, out_weight),
        [message(share), wide, wide],
        (result, spare),
    )
    combined = combine(exchange(both, ALL_AXES, order), share, everyone, False)
    (pair_out,) = call(
        functools.partial(last_kernel, share, single, chunk),
        (combined, current, gate, gains, out_weight, trans_up, trans_down),
        [held],
        (result, pltpu.VMEM(*held), pltpu.SemaphoreType.DMA((tokens // chunk,))),
        out_hbm=True,
    )
    return pair_out.reshape(pair_map.shape)


def solution(mesh):
    groups, rows, cols = (mesh.shape[name] for name in ("grp", "row", "col"))
    halves = 2 if cols % 2 == 0 else 1
    nears = cols // halves
    folded = Mesh(mesh.devices.reshape(groups, rows, halves, nears), ("grp", "row", "half", "near"))
    tokens = (("grp", "row"), ("half", "near"))
    in_specs = (P(*tokens, None), P(*tokens)) + (P(),) * 8

    def body(*args):
        return per_device(rows, halves, nears, *args)

    return jax.shard_map(body, mesh=folded, in_specs=in_specs, out_specs=P(*tokens, None), check_vma=False)
```

```python
import functools

import jax
import jax.numpy as jnp
from jax import lax
from jax.experimental import pallas as pl
from jax.experimental.pallas import tpu as pltpu
from jax.sharding import Mesh
from jax.sharding import PartitionSpec as P

NEAR_AXES = ("near", "row")
ALL_AXES = ("half", "near", "row")
LANES = 128
VMEM_BYTES = 24 * 1024 * 1024
F32, BF16 = jnp.float32, jnp.bfloat16


def dot(left, right, contract=(1, 0)):
    return lax.dot_general(
        left, right, (((contract[0],), (contract[1],)), ((), ())), preferred_element_type=F32
    )


def halved(weight):
    return weight.T * 0.5


def twice_sigmoid(half):
    return jnp.tanh(half) + 1.0


def channel_norm(values, gain):
    wide = jnp.concatenate([gain] * (values.shape[1] // LANES), axis=1)
    centred = values - jnp.mean(values, axis=0, keepdims=True)
    spread = jnp.mean(centred * centred, axis=0, keepdims=True)
    return (centred * lax.rsqrt(spread + 1e-05) * wide).astype(BF16)


def spread_gain(row):
    return jnp.broadcast_to(row, (LANES, row.shape[1])).T


def token_mask(mask, lines):
    height, breadth = mask.shape
    wide = jnp.concatenate([mask.astype(F32)] * (LANES // breadth), axis=1)
    row = lax.broadcasted_iota(jnp.int32, wide.shape, 0)
    lane = lax.broadcasted_iota(jnp.int32, wide.shape, 1)
    wide = jnp.where(row // lines == lane // breadth, wide, 0.0).astype(BF16)
    line = lax.broadcasted_iota(jnp.int32, (lines, height), 0)
    source = lax.broadcasted_iota(jnp.int32, (lines, height), 1)
    return dot((source % lines == line).astype(BF16), wide)


def emit_message(normed, weight_t, mask, line, message_ref, stage_ref, share):
    projected = dot(weight_t, normed)
    hid = weight_t.shape[0] // 4
    owners = hid // share
    for part in range(normed.shape[1] // LANES):
        here = projected[:, part * LANES : (part + 1) * LANES]
        at = line + part
        keep = mask[at : at + 1]
        left = twice_sigmoid(here[:hid]) * here[hid : 2 * hid] * keep
        right = twice_sigmoid(here[2 * hid : 3 * hid]) * here[3 * hid :] * keep
        if share % 8 == 0:
            for owner in range(owners):
                rows = slice(owner * share, (owner + 1) * share)
                both = jnp.concatenate([left[rows], right[rows]], axis=0).astype(BF16)
                message_ref[owner, 2 * share * at : 2 * share * (at + 1), :] = both
        else:
            lines = message_ref.shape[1] // 2
            stage_ref[pl.ds(2 * at, owners, stride=2 * lines), :] = left
            stage_ref[pl.ds(2 * at + 1, owners, stride=2 * lines), :] = right
    if share % 8 and line + normed.shape[1] // LANES == mask.shape[0]:
        message_ref[...] = stage_ref[...].astype(BF16).reshape(message_ref.shape)


def start_all(pairs, sems, first=0):
    copies = [pltpu.make_async_copy(src, dst, sems.at[first + n]) for n, (src, dst) in enumerate(pairs)]
    for copy in copies:
        copy.start()
    return copies


def line_tokens(x_ref, line):
    return jnp.concatenate([x_ref[slot, line] for slot in range(x_ref.shape[0])], axis=0)


def project_kernel(share, ins, outs, stage_ref, x_ref, mask_ref, weight_ref, gate_ref, gain_in_ref, gain_out_ref, trans_gain_ref, sems):
    message_ref, gate_out, turned_out, mask_out, gains_out = outs
    x_in, mask_in, weight_in, gate_in, gain_in, gain_out, trans_gain = ins
    lines = x_ref.shape[1]
    pairs = [
        (weight_in.at[0], weight_ref),
        (x_in, x_ref),
        (gain_in, gain_in_ref),
        (mask_in, mask_ref),
        (gate_in.at[0], gate_ref),
        (gain_out, gain_out_ref),
        (trans_gain, trans_gain_ref),
    ]
    for copy in start_all(pairs, sems):
        copy.wait()
    mask = token_mask(mask_ref[...], lines)
    current = jnp.concatenate([line_tokens(x_ref, line).T for line in range(lines)], axis=1)
    normed = channel_norm(current, spread_gain(gain_in_ref[0:1, :]))
    emit_message(normed, halved(weight_ref[...]), mask, 0, message_ref, stage_ref, share)
    gate_out[...] = twice_sigmoid(dot(halved(gate_ref[...]), normed))
    turned_out[...] = current
    mask_out[...] = mask
    rows = [gain_out_ref[0:1, :], gain_in_ref[1:2, :], gain_out_ref[1:2, :], trans_gain_ref[...]]
    gains_out[...] = jnp.concatenate(rows + rows, axis=0)


def one_hot(rows, columns, wanted):
    row = lax.broadcasted_iota(jnp.int32, (rows, columns), 0)
    column = lax.broadcasted_iota(jnp.int32, (rows, columns), 1)
    return (wanted(row) == column).astype(BF16)


def swap_matrix(slots, breadth):
    size = slots * LANES
    return one_hot(
        size, size, lambda lane: lane // breadth % slots * LANES + lane // LANES * breadth + lane % breadth
    )


def combine_kernel(sources, owners, breadth, share, outgoing, ins, outs):
    near, cols, rows = len(sources), len(owners), len(owners[0])
    (both_ref,), (combined_ref,) = ins, outs
    slots = LANES // breadth
    span = both_ref.shape[1]
    lines = span // (2 * share)
    pack = max(1, slots // near)
    groups = share // pack
    size = span // pack
    swap = swap_matrix(slots, breadth)

    def source(row):
        channel = row // size * groups + row // lines % groups
        return row % lines * (2 * share) + row // (groups * lines) % 2 * share + channel

    order = one_hot(span, span, source)
    wide = []
    for row in range(rows):
        here = jnp.concatenate([both_ref[sources[col][row]] for col in range(near)], axis=1)
        here = dot(order, here).astype(BF16)
        wide.append(jnp.concatenate([here[n * size : (n + 1) * size] for n in range(pack)], axis=1))
    wide = jnp.concatenate(wide, axis=0)
    block = slots * LANES
    swapped = [dot(wide[:, first : first + block], swap) for first in range(0, wide.shape[1], block)]

    def whole(side, group):
        columns = []
        for part in swapped:
            held = []
            for row in range(rows):
                first = row * size + (side * groups + group) * lines
                held += [part[first : first + lines, slot * LANES : (slot + 1) * LANES] for slot in range(slots)]
            columns.append(jnp.concatenate(held, axis=0))
        return jnp.concatenate(columns, axis=1).astype(BF16)

    products = [None] * share
    for group in range(groups):
        left, right = whole(0, group), whole(1, group)
        for place in range(pack):
            mine = left
            if pack > 1:
                lane = lax.broadcasted_iota(jnp.int32, left.shape, 1)
                mine = jnp.where(lane // (near * breadth) == place, left, jnp.zeros_like(left))
            products[place * groups + group] = dot(mine, right, (1, 1) if outgoing else (0, 0))

    for high in range(cols // slots):
        lanes = slice(high * LANES, (high + 1) * LANES)
        held = []
        for row in range(rows):
            for product in products:
                parts = [
                    product[(row * slots + slot) * lines : (row * slots + slot + 1) * lines, lanes]
                    for slot in range(slots)
                ]
                held.append(jnp.concatenate(parts, axis=1))
        back = dot(jnp.concatenate(held, axis=0).astype(BF16), swap).astype(BF16)
        for low in range(slots):
            for row in range(rows):
                first = row * share * lines
                combined_ref[owners[high * slots + low][row]] = back[
                    first : first + share * lines, low * LANES : (low + 1) * LANES
                ]


def hold_combined(combined_ref, stage_ref, share, sources):
    span = combined_ref.shape[1]
    lines = span // share
    order = one_hot(span, span, lambda row: row % share * lines + row // share)
    order = jnp.concatenate([order] * len(sources[0]), axis=1)
    for first in range(0, len(sources), 2):
        blocks = [
            jnp.concatenate([combined_ref[source] for source in sources[owner]], axis=0)
            for owner in (first, first + 1)
        ]
        ordered = dot(order, jnp.concatenate(blocks, axis=1))
        for n in range(2):
            stage_ref[(first + n) * span : (first + n + 1) * span, :] = ordered[:, n * LANES : (n + 1) * LANES]


def read_combined(stage_ref, owners, lines, share, first, count):
    columns = []
    for line in range(first, first + count):
        if share % 8 == 0:
            held = [
                stage_ref[(owner * lines + line) * share : (owner * lines + line + 1) * share, :]
                for owner in range(owners)
            ]
            columns.append(jnp.concatenate(held, axis=0))
        else:
            columns.append(stage_ref[pl.ds(line, owners, stride=lines), :])
    return jnp.concatenate(columns, axis=1)


def middle_kernel(share, sources, next_share, chunk, ins, outs, stage_ref, message_stage_ref):
    combined_ref, x_ref, gate_ref, mask_ref, gains_ref, proj_ref, gate_weight_ref, out_ref = ins
    message_ref, gate_out, next_ref = outs
    tokens = x_ref.shape[1]
    lines = tokens // LANES
    owners = x_ref.shape[0] // share
    hold_combined(combined_ref, stage_ref, share, sources)
    mask = mask_ref[...]
    gain_out, gain = [spread_gain(gains_ref[n : n + 1, :]) for n in (0, 1)]
    out_t, proj_t, gate_t = halved(out_ref[0]), halved(proj_ref[1]), halved(gate_weight_ref[1])
    for start in range(0, tokens, chunk):
        here = slice(start, start + chunk)
        combined = read_combined(stage_ref, owners, lines, share, start // LANES, chunk // LANES)
        hidden = channel_norm(combined, gain_out)
        current = x_ref[:, here] + gate_ref[:, here] * dot(out_t, hidden)
        next_ref[:, here] = current
        normed = channel_norm(current, gain)
        emit_message(normed, proj_t, mask, start // LANES, message_ref, message_stage_ref, next_share)
        gate_out[:, here] = twice_sigmoid(dot(gate_t, normed))


def last_kernel(share, sources, chunk, ins, outs, stage_ref, result_ref, sems):
    combined_ref, x_ref, gate_ref, gains_ref, out_ref, up_ref, down_ref = ins
    (result_out,) = outs
    slots, lines, breadth, channels = result_ref.shape
    owners = x_ref.shape[0] // share
    half = down_ref.shape[0]
    count = chunk // LANES
    gain_out, gain = [spread_gain(gains_ref[n : n + 1, :]) for n in (2, 3)]
    out_t, down_t = halved(out_ref[1]), down_ref[...].T
    gate_t, up_t = halved(up_ref[:, :half]), up_ref[:, half:].T
    hold_combined(combined_ref, stage_ref, share, sources)
    combined = read_combined(stage_ref, owners, lines, share, 0, lines)
    hidden = channel_norm(combined, gain_out)
    current = x_ref[...] + gate_ref[...] * dot(out_t, hidden)
    trans_in = channel_norm(current, gain)
    block = half
    for base in range(0, half, block):
        gate_part = dot(gate_t[base : base + block], trans_in)
        up_part = dot(up_t[base : base + block], trans_in)
        trans_hidden = (gate_part * twice_sigmoid(gate_part) * up_part).astype(BF16)
        current = current + dot(down_t[:, base : base + block], trans_hidden)
    writes = []
    for first in range(0, lines, count):
        for line in range(first, first + count):
            result = current[:, line * LANES : (line + 1) * LANES].T
            for slot in range(slots):
                result_ref[slot, line] = result[slot * breadth : (slot + 1) * breadth]
        piece = slice(first, first + count)
        writes += start_all([(result_ref.at[:, piece], result_out.at[:, piece])], sems, first // count)
    for write in writes:
        write.wait()


def call(kernel, operands, outs, scratch=(), in_hbm=False, out_hbm=False):
    in_place, held = pl.BlockSpec(memory_space=pltpu.HBM), pl.BlockSpec(memory_space=pltpu.VMEM)
    count = len(operands)

    def body(*refs):
        kernel(refs[:count], refs[count : count + len(outs)], *refs[count + len(outs) :])

    return pl.pallas_call(
        body,
        in_specs=[in_place if in_hbm else held] * count,
        out_specs=[in_place if out_hbm else held] * len(outs),
        out_shape=[jax.ShapeDtypeStruct(shape, dtype) for shape, dtype in outs],
        scratch_shapes=list(scratch),
        compiler_params=pltpu.CompilerParams(vmem_limit_bytes=VMEM_BYTES),
    )(*[pltpu.with_memory_space_constraint(array, pltpu.HBM) if in_hbm else array for array in operands])


def exchange(values, axes, order=None):
    groups = [order] if order else None
    return lax.all_to_all(values, axes, split_axis=0, concat_axis=0, axis_index_groups=groups, tiled=True)


def per_device(
    rows,
    halves,
    nears,
    pair_map,
    pair_mask,
    gain_in,
    proj_weight,
    gate_weight,
    gain_out,
    out_weight,
    trans_gain,
    trans_up,
    trans_down,
):
    height, breadth, channels = pair_map.shape
    tokens = height * breadth
    lines = tokens // LANES
    hid = gain_out.shape[1]
    cols = halves * nears
    owners = rows * cols
    share = hid // owners
    chunk = min(4 * LANES, tokens)
    split = halves if share % 8 == 0 else 1
    first_share = split * share
    held = ((LANES // breadth, lines, breadth, channels), F32)
    grouped = pair_map.reshape(held[0])
    wide = ((channels, tokens), F32)
    result = pltpu.VMEM((owners * share * lines, LANES), F32)
    spare = pltpu.VMEM((8, LANES) if share % 8 == 0 else (owners * 2 * share * lines, LANES), F32)

    def message(own):
        return ((hid // own, 2 * own * lines, LANES), BF16)

    blocks = [half * nears + near for half in range(halves) for near in reversed(range(nears))]
    order = [col * rows + row for col in blocks for row in range(rows)]
    everyone = [[order.index(col * rows + row) for row in range(rows)] for col in range(cols)]
    beside = [[near * rows + row for row in range(rows)] for near in range(nears)] if split > 1 else everyone
    single = [[n] for n in range(owners)]
    paired = single if split == 1 else [
        [everyone[half * nears + near][row] for half in range(halves)] for near in range(nears) for row in range(rows)
    ]

    def combine(both, own, sources, outgoing):
        kernel = functools.partial(combine_kernel, sources, everyone, breadth, own, outgoing)
        answer = ((owners, own * lines, LANES), BF16)
        return exchange(call(kernel, (both,), [answer])[0], ALL_AXES, order)

    operands = (grouped, pair_mask, proj_weight, gate_weight, gain_in, gain_out, trans_gain.reshape(1, -1))
    both, gate, current, mask, gains = call(
        functools.partial(project_kernel, first_share),
        operands,
        [message(first_share), wide, wide, ((lines, LANES), F32), ((8, channels), F32)],
        (
            spare,
            *[
                pltpu.VMEM(array.shape[1:] if array.ndim == 3 else array.shape, array.dtype)
                for array in operands
            ],
            pltpu.SemaphoreType.DMA((len(operands),)),
        ),
        in_hbm=True,
    )
    both = exchange(both, NEAR_AXES) if split > 1 else exchange(both, ALL_AXES, order)
    combined = combine(both, first_share, beside, True)
    both, gate, current = call(
        functools.partial(middle_kernel, first_share, paired, share, tokens),
        (combined, current, gate, mask, gains, proj_weight, gate_weight, out_weight),
        [message(share), wide, wide],
        (result, spare),
    )
    combined = combine(exchange(both, ALL_AXES, order), share, everyone, False)
    (pair_out,) = call(
        functools.partial(last_kernel, share, single, chunk),
        (combined, current, gate, gains, out_weight, trans_up, trans_down),
        [held],
        (result, pltpu.VMEM(*held), pltpu.SemaphoreType.DMA((tokens // chunk,))),
        out_hbm=True,
    )
    return pair_out.reshape(pair_map.shape)


def solution(mesh):
    groups, rows, cols = (mesh.shape[name] for name in ("grp", "row", "col"))
    halves = 2 if cols % 2 == 0 else 1
    nears = cols // halves
    folded = Mesh(mesh.devices.reshape(groups, rows, halves, nears), ("grp", "row", "half", "near"))
    tokens = (("grp", "row"), ("half", "near"))
    in_specs = (P(*tokens, None), P(*tokens)) + (P(),) * 8

    def body(*args):
        return per_device(rows, halves, nears, *args)

    return jax.shard_map(body, mesh=folded, in_specs=in_specs, out_specs=P(*tokens, None), check_vma=False)
```

```python
import functools

import jax
import jax.numpy as jnp
from jax import lax
from jax.experimental import pallas as pl
from jax.experimental.pallas import tpu as pltpu
from jax.sharding import Mesh
from jax.sharding import PartitionSpec as P

NEAR_AXES = ("near", "row")
ALL_AXES = ("half", "near", "row")
LANES = 128
VMEM_BYTES = 24 * 1024 * 1024
F32, BF16 = jnp.float32, jnp.bfloat16


def dot(left, right, contract=(1, 0)):
    return lax.dot_general(
        left, right, (((contract[0],), (contract[1],)), ((), ())), preferred_element_type=F32
    )


def halved(weight):
    return weight.T * 0.5


def twice_sigmoid(half):
    return jnp.tanh(half) + 1.0


def channel_norm(values, gain):
    wide = jnp.concatenate([gain] * (values.shape[1] // LANES), axis=1)
    centred = values - jnp.mean(values, axis=0, keepdims=True)
    spread = jnp.mean(centred * centred, axis=0, keepdims=True)
    return (centred * lax.rsqrt(spread + 1e-05) * wide).astype(BF16)


def spread_gain(row):
    return jnp.broadcast_to(row, (LANES, row.shape[1])).T


def token_mask(mask, lines):
    height, breadth = mask.shape
    wide = jnp.concatenate([mask.astype(F32)] * (LANES // breadth), axis=1)
    row = lax.broadcasted_iota(jnp.int32, wide.shape, 0)
    lane = lax.broadcasted_iota(jnp.int32, wide.shape, 1)
    wide = jnp.where(row // lines == lane // breadth, wide, 0.0).astype(BF16)
    line = lax.broadcasted_iota(jnp.int32, (lines, height), 0)
    source = lax.broadcasted_iota(jnp.int32, (lines, height), 1)
    return dot((source % lines == line).astype(BF16), wide)


def emit_message(normed, weight_t, mask, line, message_ref, stage_ref, share):
    projected = dot(weight_t, normed)
    hid = weight_t.shape[0] // 4
    owners = hid // share
    for part in range(normed.shape[1] // LANES):
        here = projected[:, part * LANES : (part + 1) * LANES]
        at = line + part
        keep = mask[at : at + 1]
        left = twice_sigmoid(here[:hid]) * here[hid : 2 * hid] * keep
        right = twice_sigmoid(here[2 * hid : 3 * hid]) * here[3 * hid :] * keep
        if share % 8 == 0:
            for owner in range(owners):
                rows = slice(owner * share, (owner + 1) * share)
                both = jnp.concatenate([left[rows], right[rows]], axis=0).astype(BF16)
                message_ref[owner, 2 * share * at : 2 * share * (at + 1), :] = both
        else:
            lines = message_ref.shape[1] // 2
            stage_ref[pl.ds(2 * at, owners, stride=2 * lines), :] = left
            stage_ref[pl.ds(2 * at + 1, owners, stride=2 * lines), :] = right
    if share % 8 and line + normed.shape[1] // LANES == mask.shape[0]:
        message_ref[...] = stage_ref[...].astype(BF16).reshape(message_ref.shape)


def start_all(pairs, sems, first=0):
    copies = [pltpu.make_async_copy(src, dst, sems.at[first + n]) for n, (src, dst) in enumerate(pairs)]
    for copy in copies:
        copy.start()
    return copies


def line_tokens(x_ref, line):
    return jnp.concatenate([x_ref[slot, line] for slot in range(x_ref.shape[0])], axis=0)


def project_kernel(share, ins, outs, stage_ref, x_ref, mask_ref, weight_ref, gate_ref, gain_in_ref, gain_out_ref, trans_gain_ref, sems):
    message_ref, gate_out, turned_out, mask_out, gains_out = outs
    x_in, mask_in, weight_in, gate_in, gain_in, gain_out, trans_gain = ins
    lines = x_ref.shape[1]
    pairs = [
        (weight_in.at[0], weight_ref),
        (x_in, x_ref),
        (gain_in, gain_in_ref),
        (mask_in, mask_ref),
        (gate_in.at[0], gate_ref),
        (gain_out, gain_out_ref),
        (trans_gain, trans_gain_ref),
    ]
    for copy in start_all(pairs, sems):
        copy.wait()
    mask = token_mask(mask_ref[...], lines)
    current = jnp.concatenate([line_tokens(x_ref, line).T for line in range(lines)], axis=1)
    normed = channel_norm(current, spread_gain(gain_in_ref[0:1, :]))
    emit_message(normed, halved(weight_ref[...]), mask, 0, message_ref, stage_ref, share)
    gate_out[...] = twice_sigmoid(dot(halved(gate_ref[...]), normed))
    turned_out[...] = current
    mask_out[...] = mask
    rows = [gain_out_ref[0:1, :], gain_in_ref[1:2, :], gain_out_ref[1:2, :], trans_gain_ref[...]]
    gains_out[...] = jnp.concatenate(rows + rows, axis=0)


def one_hot(rows, columns, wanted):
    row = lax.broadcasted_iota(jnp.int32, (rows, columns), 0)
    column = lax.broadcasted_iota(jnp.int32, (rows, columns), 1)
    return (wanted(row) == column).astype(BF16)


def swap_matrix(slots, breadth):
    size = slots * LANES
    return one_hot(
        size, size, lambda lane: lane // breadth % slots * LANES + lane // LANES * breadth + lane % breadth
    )


def combine_kernel(sources, owners, breadth, share, outgoing, ins, outs):
    near, cols, rows = len(sources), len(owners), len(owners[0])
    (both_ref,), (combined_ref,) = ins, outs
    slots = LANES // breadth
    span = both_ref.shape[1]
    lines = span // (2 * share)
    pack = max(1, slots // near)
    groups = share // pack
    size = span // pack
    swap = swap_matrix(slots, breadth)

    def source(row):
        channel = row // size * groups + row // lines % groups
        return row % lines * (2 * share) + row // (groups * lines) % 2 * share + channel

    order = one_hot(span, span, source)
    wide = []
    for row in range(rows):
        here = jnp.concatenate([both_ref[sources[col][row]] for col in range(near)], axis=1)
        here = dot(order, here).astype(BF16)
        wide.append(jnp.concatenate([here[n * size : (n + 1) * size] for n in range(pack)], axis=1))
    wide = jnp.concatenate(wide, axis=0)
    block = slots * LANES
    swapped = [dot(wide[:, first : first + block], swap) for first in range(0, wide.shape[1], block)]

    def whole(side, group):
        columns = []
        for part in swapped:
            held = []
            for row in range(rows):
                first = row * size + (side * groups + group) * lines
                held += [part[first : first + lines, slot * LANES : (slot + 1) * LANES] for slot in range(slots)]
            columns.append(jnp.concatenate(held, axis=0))
        return jnp.concatenate(columns, axis=1).astype(BF16)

    products = [None] * share
    for group in range(groups):
        left, right = whole(0, group), whole(1, group)
        for place in range(pack):
            mine = left
            if pack > 1:
                lane = lax.broadcasted_iota(jnp.int32, left.shape, 1)
                mine = jnp.where(lane // (near * breadth) == place, left, jnp.zeros_like(left))
            products[place * groups + group] = dot(mine, right, (1, 1) if outgoing else (0, 0))

    for high in range(cols // slots):
        lanes = slice(high * LANES, (high + 1) * LANES)
        held = []
        for row in range(rows):
            for product in products:
                parts = [
                    product[(row * slots + slot) * lines : (row * slots + slot + 1) * lines, lanes]
                    for slot in range(slots)
                ]
                held.append(jnp.concatenate(parts, axis=1))
        back = dot(jnp.concatenate(held, axis=0).astype(BF16), swap).astype(BF16)
        for low in range(slots):
            for row in range(rows):
                first = row * share * lines
                combined_ref[owners[high * slots + low][row]] = back[
                    first : first + share * lines, low * LANES : (low + 1) * LANES
                ]


def hold_combined(combined_ref, stage_ref, share, sources):
    span = combined_ref.shape[1]
    lines = span // share
    order = one_hot(span, span, lambda row: row % share * lines + row // share)
    order = jnp.concatenate([order] * len(sources[0]), axis=1)
    for first in range(0, len(sources), 2):
        blocks = [
            jnp.concatenate([combined_ref[source] for source in sources[owner]], axis=0)
            for owner in (first, first + 1)
        ]
        ordered = dot(order, jnp.concatenate(blocks, axis=1))
        for n in range(2):
            stage_ref[(first + n) * span : (first + n + 1) * span, :] = ordered[:, n * LANES : (n + 1) * LANES]


def read_combined(stage_ref, owners, lines, share, first, count):
    columns = []
    for line in range(first, first + count):
        if share % 8 == 0:
            held = [
                stage_ref[(owner * lines + line) * share : (owner * lines + line + 1) * share, :]
                for owner in range(owners)
            ]
            columns.append(jnp.concatenate(held, axis=0))
        else:
            columns.append(stage_ref[pl.ds(line, owners, stride=lines), :])
    return jnp.concatenate(columns, axis=1)


def middle_kernel(share, sources, next_share, chunk, ins, outs, stage_ref, message_stage_ref):
    combined_ref, x_ref, gate_ref, mask_ref, gains_ref, proj_ref, gate_weight_ref, out_ref = ins
    message_ref, gate_out, next_ref = outs
    tokens = x_ref.shape[1]
    lines = tokens // LANES
    owners = x_ref.shape[0] // share
    hold_combined(combined_ref, stage_ref, share, sources)
    mask = mask_ref[...]
    gain_out, gain = [spread_gain(gains_ref[n : n + 1, :]) for n in (0, 1)]
    out_t, proj_t, gate_t = halved(out_ref[0]), halved(proj_ref[1]), halved(gate_weight_ref[1])
    for start in range(0, tokens, chunk):
        here = slice(start, start + chunk)
        combined = read_combined(stage_ref, owners, lines, share, start // LANES, chunk // LANES)
        hidden = channel_norm(combined, gain_out)
        current = x_ref[:, here] + gate_ref[:, here] * dot(out_t, hidden)
        next_ref[:, here] = current
        normed = channel_norm(current, gain)
        emit_message(normed, proj_t, mask, start // LANES, message_ref, message_stage_ref, next_share)
        gate_out[:, here] = twice_sigmoid(dot(gate_t, normed))


def last_kernel(share, sources, chunk, ins, outs, stage_ref, result_ref, sems):
    combined_ref, x_ref, gate_ref, gains_ref, out_ref, up_ref, down_ref = ins
    (result_out,) = outs
    slots, lines, breadth, channels = result_ref.shape
    owners = x_ref.shape[0] // share
    half = down_ref.shape[0]
    count = chunk // LANES
    gain_out, gain = [spread_gain(gains_ref[n : n + 1, :]) for n in (2, 3)]
    out_t, down_t = halved(out_ref[1]), down_ref[...].T
    gate_t, up_t = halved(up_ref[:, :half]), up_ref[:, half:].T
    hold_combined(combined_ref, stage_ref, share, sources)
    combined = read_combined(stage_ref, owners, lines, share, 0, lines)
    hidden = channel_norm(combined, gain_out)
    current = x_ref[...] + gate_ref[...] * dot(out_t, hidden)
    trans_in = channel_norm(current, gain)
    gate_part, up_part = dot(gate_t, trans_in), dot(up_t, trans_in)
    trans_hidden = (gate_part * twice_sigmoid(gate_part) * up_part).astype(BF16)
    current = current + dot(down_t, trans_hidden)
    writes = []
    for first in range(0, lines, count):
        for line in range(first, first + count):
            result = current[:, line * LANES : (line + 1) * LANES].T
            for slot in range(slots):
                result_ref[slot, line] = result[slot * breadth : (slot + 1) * breadth]
        piece = slice(first, first + count)
        writes += start_all([(result_ref.at[:, piece], result_out.at[:, piece])], sems, first // count)
    for write in writes:
        write.wait()


def call(kernel, operands, outs, scratch=(), in_hbm=False, out_hbm=False):
    in_place, held = pl.BlockSpec(memory_space=pltpu.HBM), pl.BlockSpec(memory_space=pltpu.VMEM)
    count = len(operands)

    def body(*refs):
        kernel(refs[:count], refs[count : count + len(outs)], *refs[count + len(outs) :])

    return pl.pallas_call(
        body,
        in_specs=[in_place if in_hbm else held] * count,
        out_specs=[in_place if out_hbm else held] * len(outs),
        out_shape=[jax.ShapeDtypeStruct(shape, dtype) for shape, dtype in outs],
        scratch_shapes=list(scratch),
        compiler_params=pltpu.CompilerParams(vmem_limit_bytes=VMEM_BYTES),
    )(*[pltpu.with_memory_space_constraint(array, pltpu.HBM) if in_hbm else array for array in operands])


def exchange(values, axes, order=None):
    groups = [order] if order else None
    return lax.all_to_all(values, axes, split_axis=0, concat_axis=0, axis_index_groups=groups, tiled=True)


def per_device(
    rows,
    halves,
    nears,
    pair_map,
    pair_mask,
    gain_in,
    proj_weight,
    gate_weight,
    gain_out,
    out_weight,
    trans_gain,
    trans_up,
    trans_down,
):
    height, breadth, channels = pair_map.shape
    tokens = height * breadth
    lines = tokens // LANES
    hid = gain_out.shape[1]
    cols = halves * nears
    owners = rows * cols
    share = hid // owners
    chunk = min(4 * LANES, tokens)
    split = halves if share % 8 == 0 else 1
    first_share = split * share
    held = ((LANES // breadth, lines, breadth, channels), F32)
    grouped = pair_map.reshape(held[0])
    wide = ((channels, tokens), F32)
    result = pltpu.VMEM((owners * share * lines, LANES), F32)
    spare = pltpu.VMEM((8, LANES) if share % 8 == 0 else (owners * 2 * share * lines, LANES), F32)

    def message(own):
        return ((hid // own, 2 * own * lines, LANES), BF16)

    blocks = [(col + (cols - 1) // 2) % cols for col in range(cols)]
    order = [col * rows + row for col in blocks for row in range(rows)]
    everyone = [[order.index(col * rows + row) for row in range(rows)] for col in range(cols)]
    beside = [[near * rows + row for row in range(rows)] for near in range(nears)] if split > 1 else everyone
    single = [[n] for n in range(owners)]
    paired = single if split == 1 else [
        [everyone[half * nears + near][row] for half in range(halves)] for near in range(nears) for row in range(rows)
    ]

    def combine(both, own, sources, outgoing):
        kernel = functools.partial(combine_kernel, sources, everyone, breadth, own, outgoing)
        answer = ((owners, own * lines, LANES), BF16)
        return exchange(call(kernel, (both,), [answer])[0], ALL_AXES, order)

    operands = (grouped, pair_mask, proj_weight, gate_weight, gain_in, gain_out, trans_gain.reshape(1, -1))
    both, gate, current, mask, gains = call(
        functools.partial(project_kernel, first_share),
        operands,
        [message(first_share), wide, wide, ((lines, LANES), F32), ((8, channels), F32)],
        (
            spare,
            *[
                pltpu.VMEM(array.shape[1:] if array.ndim == 3 else array.shape, array.dtype)
                for array in operands
            ],
            pltpu.SemaphoreType.DMA((len(operands),)),
        ),
        in_hbm=True,
    )
    both = exchange(both, NEAR_AXES) if split > 1 else exchange(both, ALL_AXES, order)
    combined = combine(both, first_share, beside, True)
    both, gate, current = call(
        functools.partial(middle_kernel, first_share, paired, share, tokens),
        (combined, current, gate, mask, gains, proj_weight, gate_weight, out_weight),
        [message(share), wide, wide],
        (result, spare),
    )
    combined = combine(exchange(both, ALL_AXES, order), share, everyone, False)
    (pair_out,) = call(
        functools.partial(last_kernel, share, single, chunk),
        (combined, current, gate, gains, out_weight, trans_up, trans_down),
        [held],
        (result, pltpu.VMEM(*held), pltpu.SemaphoreType.DMA((tokens // chunk,))),
        out_hbm=True,
    )
    return pair_out.reshape(pair_map.shape)


def solution(mesh):
    groups, rows, cols = (mesh.shape[name] for name in ("grp", "row", "col"))
    halves = 2 if cols % 2 == 0 else 1
    nears = cols // halves
    folded = Mesh(mesh.devices.reshape(groups, rows, halves, nears), ("grp", "row", "half", "near"))
    tokens = (("grp", "row"), ("half", "near"))
    in_specs = (P(*tokens, None), P(*tokens)) + (P(),) * 8

    def body(*args):
        return per_device(rows, halves, nears, *args)

    return jax.shard_map(body, mesh=folded, in_specs=in_specs, out_specs=P(*tokens, None), check_vma=False)
```

```python
import functools

import jax
import jax.numpy as jnp
from jax import lax
from jax.experimental import pallas as pl
from jax.experimental.pallas import tpu as pltpu
from jax.sharding import Mesh
from jax.sharding import PartitionSpec as P

NEAR_AXES = ("near", "row")
ALL_AXES = ("half", "near", "row")
LANES = 128
VMEM_BYTES = 24 * 1024 * 1024
F32, BF16 = jnp.float32, jnp.bfloat16


def dot(left, right, contract=(1, 0)):
    return lax.dot_general(
        left, right, (((contract[0],), (contract[1],)), ((), ())), preferred_element_type=F32
    )


def halved(weight):
    return weight.T * 0.5


def twice_sigmoid(half):
    return jnp.tanh(half) + 1.0


def channel_norm(values, gain):
    wide = jnp.concatenate([gain] * (values.shape[1] // LANES), axis=1)
    centred = values - jnp.mean(values, axis=0, keepdims=True)
    spread = jnp.mean(centred * centred, axis=0, keepdims=True)
    return (centred * lax.rsqrt(spread + 1e-05) * wide).astype(BF16)


def spread_gain(row):
    return jnp.broadcast_to(row, (LANES, row.shape[1])).T


def token_mask(mask, lines):
    height, breadth = mask.shape
    wide = jnp.concatenate([mask.astype(F32)] * (LANES // breadth), axis=1)
    row = lax.broadcasted_iota(jnp.int32, wide.shape, 0)
    lane = lax.broadcasted_iota(jnp.int32, wide.shape, 1)
    wide = jnp.where(row // lines == lane // breadth, wide, 0.0).astype(BF16)
    line = lax.broadcasted_iota(jnp.int32, (lines, height), 0)
    source = lax.broadcasted_iota(jnp.int32, (lines, height), 1)
    return dot((source % lines == line).astype(BF16), wide)


def emit_message(normed, weight_t, mask, line, message_ref, stage_ref, share):
    projected = dot(weight_t, normed)
    hid = weight_t.shape[0] // 4
    owners = hid // share
    for part in range(normed.shape[1] // LANES):
        here = projected[:, part * LANES : (part + 1) * LANES]
        at = line + part
        keep = mask[at : at + 1]
        left = twice_sigmoid(here[:hid]) * here[hid : 2 * hid] * keep
        right = twice_sigmoid(here[2 * hid : 3 * hid]) * here[3 * hid :] * keep
        if share % 8 == 0:
            for owner in range(owners):
                rows = slice(owner * share, (owner + 1) * share)
                both = jnp.concatenate([left[rows], right[rows]], axis=0).astype(BF16)
                message_ref[owner, 2 * share * at : 2 * share * (at + 1), :] = both
        else:
            lines = message_ref.shape[1] // 2
            stage_ref[pl.ds(2 * at, owners, stride=2 * lines), :] = left
            stage_ref[pl.ds(2 * at + 1, owners, stride=2 * lines), :] = right
    if share % 8 and line + normed.shape[1] // LANES == mask.shape[0]:
        message_ref[...] = stage_ref[...].astype(BF16).reshape(message_ref.shape)


def start_all(pairs, sems, first=0):
    copies = [pltpu.make_async_copy(src, dst, sems.at[first + n]) for n, (src, dst) in enumerate(pairs)]
    for copy in copies:
        copy.start()
    return copies


def line_tokens(x_ref, line):
    return jnp.concatenate([x_ref[slot, line] for slot in range(x_ref.shape[0])], axis=0)


def project_kernel(share, ins, outs, stage_ref, x_ref, mask_ref, weight_ref, gate_ref, gain_in_ref, gain_out_ref, trans_gain_ref, sems):
    message_ref, gate_out, turned_out, mask_out, gains_out = outs
    x_in, mask_in, weight_in, gate_in, gain_in, gain_out, trans_gain = ins
    lines = x_ref.shape[1]
    pairs = [
        (weight_in.at[0], weight_ref),
        (x_in, x_ref),
        (gain_in, gain_in_ref),
        (mask_in, mask_ref),
        (gate_in.at[0], gate_ref),
        (gain_out, gain_out_ref),
        (trans_gain, trans_gain_ref),
    ]
    for copy in start_all(pairs, sems):
        copy.wait()
    mask = token_mask(mask_ref[...], lines)
    current = jnp.concatenate([line_tokens(x_ref, line).T for line in range(lines)], axis=1)
    normed = channel_norm(current, spread_gain(gain_in_ref[0:1, :]))
    emit_message(normed, halved(weight_ref[...]), mask, 0, message_ref, stage_ref, share)
    gate_out[...] = twice_sigmoid(dot(halved(gate_ref[...]), normed))
    turned_out[...] = current
    mask_out[...] = mask
    rows = [gain_out_ref[0:1, :], gain_in_ref[1:2, :], gain_out_ref[1:2, :], trans_gain_ref[...]]
    gains_out[...] = jnp.concatenate(rows + rows, axis=0)


def one_hot(rows, columns, wanted):
    row = lax.broadcasted_iota(jnp.int32, (rows, columns), 0)
    column = lax.broadcasted_iota(jnp.int32, (rows, columns), 1)
    return (wanted(row) == column).astype(BF16)


def swap_matrix(slots, breadth):
    size = slots * LANES
    return one_hot(
        size, size, lambda lane: lane // breadth % slots * LANES + lane // LANES * breadth + lane % breadth
    )


def combine_kernel(sources, owners, breadth, share, outgoing, ins, outs):
    near, cols, rows = len(sources), len(owners), len(owners[0])
    (both_ref,), (combined_ref,) = ins, outs
    slots = LANES // breadth
    span = both_ref.shape[1]
    lines = span // (2 * share)
    pack = max(1, slots // near)
    groups = share // pack
    size = span // pack
    swap = swap_matrix(slots, breadth)

    def source(row):
        channel = row // size * groups + row // lines % groups
        return row % lines * (2 * share) + row // (groups * lines) % 2 * share + channel

    order = one_hot(span, span, source)
    wide = []
    for row in range(rows):
        here = jnp.concatenate([both_ref[sources[col][row]] for col in range(near)], axis=1)
        here = dot(order, here).astype(BF16)
        wide.append(jnp.concatenate([here[n * size : (n + 1) * size] for n in range(pack)], axis=1))
    wide = jnp.concatenate(wide, axis=0)
    block = slots * LANES
    swapped = [dot(wide[:, first : first + block], swap) for first in range(0, wide.shape[1], block)]

    def whole(side, group):
        columns = []
        for part in swapped:
            held = []
            for row in range(rows):
                first = row * size + (side * groups + group) * lines
                held += [part[first : first + lines, slot * LANES : (slot + 1) * LANES] for slot in range(slots)]
            columns.append(jnp.concatenate(held, axis=0))
        return jnp.concatenate(columns, axis=1).astype(BF16)

    products = [None] * share
    for group in range(groups):
        left, right = whole(0, group), whole(1, group)
        if pack > 1:
            lane = lax.broadcasted_iota(jnp.int32, left.shape, 1) // (near * breadth)
            left = [jnp.where(lane == place, left, jnp.zeros_like(left)) for place in range(pack)]
            left = jnp.concatenate(left, axis=0)
        product = dot(left, right, (1, 1) if outgoing else (0, 0))
        tokens = product.shape[0] // pack
        for place in range(pack):
            products[place * groups + group] = product[place * tokens : (place + 1) * tokens]

    for high in range(cols // slots):
        lanes = slice(high * LANES, (high + 1) * LANES)
        held = []
        for row in range(rows):
            for product in products:
                parts = [
                    product[(row * slots + slot) * lines : (row * slots + slot + 1) * lines, lanes]
                    for slot in range(slots)
                ]
                held.append(jnp.concatenate(parts, axis=1))
        back = dot(jnp.concatenate(held, axis=0).astype(BF16), swap).astype(BF16)
        for low in range(slots):
            for row in range(rows):
                first = row * share * lines
                combined_ref[owners[high * slots + low][row]] = back[
                    first : first + share * lines, low * LANES : (low + 1) * LANES
                ]


def hold_combined(combined_ref, stage_ref, share, sources):
    span = combined_ref.shape[1]
    lines = span // share
    order = one_hot(span, span, lambda row: row % share * lines + row // share)
    order = jnp.concatenate([order] * len(sources[0]), axis=1)
    for first in range(0, len(sources), 2):
        blocks = [
            jnp.concatenate([combined_ref[source] for source in sources[owner]], axis=0)
            for owner in (first, first + 1)
        ]
        ordered = dot(order, jnp.concatenate(blocks, axis=1))
        for n in range(2):
            stage_ref[(first + n) * span : (first + n + 1) * span, :] = ordered[:, n * LANES : (n + 1) * LANES]


def read_combined(stage_ref, owners, lines, share, first, count):
    columns = []
    for line in range(first, first + count):
        if share % 8 == 0:
            held = [
                stage_ref[(owner * lines + line) * share : (owner * lines + line + 1) * share, :]
                for owner in range(owners)
            ]
            columns.append(jnp.concatenate(held, axis=0))
        else:
            columns.append(stage_ref[pl.ds(line, owners, stride=lines), :])
    return jnp.concatenate(columns, axis=1)


def middle_kernel(share, sources, next_share, chunk, ins, outs, stage_ref, message_stage_ref):
    combined_ref, x_ref, gate_ref, mask_ref, gains_ref, proj_ref, gate_weight_ref, out_ref = ins
    message_ref, gate_out, next_ref = outs
    tokens = x_ref.shape[1]
    lines = tokens // LANES
    owners = x_ref.shape[0] // share
    hold_combined(combined_ref, stage_ref, share, sources)
    mask = mask_ref[...]
    gain_out, gain = [spread_gain(gains_ref[n : n + 1, :]) for n in (0, 1)]
    out_t, proj_t, gate_t = halved(out_ref[0]), halved(proj_ref[1]), halved(gate_weight_ref[1])
    for start in range(0, tokens, chunk):
        here = slice(start, start + chunk)
        combined = read_combined(stage_ref, owners, lines, share, start // LANES, chunk // LANES)
        hidden = channel_norm(combined, gain_out)
        current = x_ref[:, here] + gate_ref[:, here] * dot(out_t, hidden)
        next_ref[:, here] = current
        normed = channel_norm(current, gain)
        emit_message(normed, proj_t, mask, start // LANES, message_ref, message_stage_ref, next_share)
        gate_out[:, here] = twice_sigmoid(dot(gate_t, normed))


def last_kernel(share, sources, chunk, ins, outs, stage_ref, result_ref, sems):
    combined_ref, x_ref, gate_ref, gains_ref, out_ref, up_ref, down_ref = ins
    (result_out,) = outs
    slots, lines, breadth, channels = result_ref.shape
    owners = x_ref.shape[0] // share
    half = down_ref.shape[0]
    count = chunk // LANES
    gain_out, gain = [spread_gain(gains_ref[n : n + 1, :]) for n in (2, 3)]
    out_t, down_t = halved(out_ref[1]), down_ref[...].T
    gate_t, up_t = halved(up_ref[:, :half]), up_ref[:, half:].T
    hold_combined(combined_ref, stage_ref, share, sources)
    combined = read_combined(stage_ref, owners, lines, share, 0, lines)
    hidden = channel_norm(combined, gain_out)
    current = x_ref[...] + gate_ref[...] * dot(out_t, hidden)
    trans_in = channel_norm(current, gain)
    gate_part, up_part = dot(gate_t, trans_in), dot(up_t, trans_in)
    trans_hidden = (gate_part * twice_sigmoid(gate_part) * up_part).astype(BF16)
    current = current + dot(down_t, trans_hidden)
    writes = []
    for first in range(0, lines, count):
        for line in range(first, first + count):
            result = current[:, line * LANES : (line + 1) * LANES].T
            for slot in range(slots):
                result_ref[slot, line] = result[slot * breadth : (slot + 1) * breadth]
        piece = slice(first, first + count)
        writes += start_all([(result_ref.at[:, piece], result_out.at[:, piece])], sems, first // count)
    for write in writes:
        write.wait()


def call(kernel, operands, outs, scratch=(), in_hbm=False, out_hbm=False):
    in_place, held = pl.BlockSpec(memory_space=pltpu.HBM), pl.BlockSpec(memory_space=pltpu.VMEM)
    count = len(operands)

    def body(*refs):
        kernel(refs[:count], refs[count : count + len(outs)], *refs[count + len(outs) :])

    return pl.pallas_call(
        body,
        in_specs=[in_place if in_hbm else held] * count,
        out_specs=[in_place if out_hbm else held] * len(outs),
        out_shape=[jax.ShapeDtypeStruct(shape, dtype) for shape, dtype in outs],
        scratch_shapes=list(scratch),
        compiler_params=pltpu.CompilerParams(vmem_limit_bytes=VMEM_BYTES),
    )(*[pltpu.with_memory_space_constraint(array, pltpu.HBM) if in_hbm else array for array in operands])


def exchange(values, axes, order=None):
    groups = [order] if order else None
    return lax.all_to_all(values, axes, split_axis=0, concat_axis=0, axis_index_groups=groups, tiled=True)


def per_device(
    rows,
    halves,
    nears,
    pair_map,
    pair_mask,
    gain_in,
    proj_weight,
    gate_weight,
    gain_out,
    out_weight,
    trans_gain,
    trans_up,
    trans_down,
):
    height, breadth, channels = pair_map.shape
    tokens = height * breadth
    lines = tokens // LANES
    hid = gain_out.shape[1]
    cols = halves * nears
    owners = rows * cols
    share = hid // owners
    chunk = min(4 * LANES, tokens)
    split = halves if share % 8 == 0 else 1
    first_share = split * share
    held = ((LANES // breadth, lines, breadth, channels), F32)
    grouped = pair_map.reshape(held[0])
    wide = ((channels, tokens), F32)
    result = pltpu.VMEM((owners * share * lines, LANES), F32)
    spare = pltpu.VMEM((8, LANES) if share % 8 == 0 else (owners * 2 * share * lines, LANES), F32)

    def message(own):
        return ((hid // own, 2 * own * lines, LANES), BF16)

    blocks = list(range(cols))
    blocks.insert(0, blocks.pop((cols - 1) // 2))
    order = [col * rows + row for col in blocks for row in range(rows)]
    everyone = [[order.index(col * rows + row) for row in range(rows)] for col in range(cols)]
    beside = [[near * rows + row for row in range(rows)] for near in range(nears)] if split > 1 else everyone
    single = [[n] for n in range(owners)]
    paired = single if split == 1 else [
        [everyone[half * nears + near][row] for half in range(halves)] for near in range(nears) for row in range(rows)
    ]

    def combine(both, own, sources, outgoing):
        kernel = functools.partial(combine_kernel, sources, everyone, breadth, own, outgoing)
        answer = ((owners, own * lines, LANES), BF16)
        return exchange(call(kernel, (both,), [answer])[0], ALL_AXES, order)

    operands = (grouped, pair_mask, proj_weight, gate_weight, gain_in, gain_out, trans_gain.reshape(1, -1))
    both, gate, current, mask, gains = call(
        functools.partial(project_kernel, first_share),
        operands,
        [message(first_share), wide, wide, ((lines, LANES), F32), ((8, channels), F32)],
        (
            spare,
            *[
                pltpu.VMEM(array.shape[1:] if array.ndim == 3 else array.shape, array.dtype)
                for array in operands
            ],
            pltpu.SemaphoreType.DMA((len(operands),)),
        ),
        in_hbm=True,
    )
    both = exchange(both, NEAR_AXES) if split > 1 else exchange(both, ALL_AXES, order)
    combined = combine(both, first_share, beside, True)
    both, gate, current = call(
        functools.partial(middle_kernel, first_share, paired, share, tokens),
        (combined, current, gate, mask, gains, proj_weight, gate_weight, out_weight),
        [message(share), wide, wide],
        (result, spare),
    )
    combined = combine(exchange(both, ALL_AXES, order), share, everyone, False)
    (pair_out,) = call(
        functools.partial(last_kernel, share, single, chunk),
        (combined, current, gate, gains, out_weight, trans_up, trans_down),
        [held],
        (result, pltpu.VMEM(*held), pltpu.SemaphoreType.DMA((tokens // chunk,))),
        out_hbm=True,
    )
    return pair_out.reshape(pair_map.shape)


def solution(mesh):
    groups, rows, cols = (mesh.shape[name] for name in ("grp", "row", "col"))
    halves = 2 if cols % 2 == 0 else 1
    nears = cols // halves
    folded = Mesh(mesh.devices.reshape(groups, rows, halves, nears), ("grp", "row", "half", "near"))
    tokens = (("grp", "row"), ("half", "near"))
    in_specs = (P(*tokens, None), P(*tokens)) + (P(),) * 8

    def body(*args):
        return per_device(rows, halves, nears, *args)

    return jax.shard_map(body, mesh=folded, in_specs=in_specs, out_specs=P(*tokens, None), check_vma=False)
```

```python
import functools

import jax
import jax.numpy as jnp
from jax import lax
from jax.experimental import pallas as pl
from jax.experimental.pallas import tpu as pltpu
from jax.sharding import Mesh
from jax.sharding import PartitionSpec as P

NEAR_AXES = ("near", "row")
ALL_AXES = ("half", "near", "row")
LANES = 128
VMEM_BYTES = 24 * 1024 * 1024
F32, BF16 = jnp.float32, jnp.bfloat16


def dot(left, right, contract=(1, 0)):
    return lax.dot_general(
        left, right, (((contract[0],), (contract[1],)), ((), ())), preferred_element_type=F32
    )


def halved(weight):
    return weight.T * 0.5


def twice_sigmoid(half):
    return jnp.tanh(half) + 1.0


def channel_norm(values, gain):
    wide = jnp.concatenate([gain] * (values.shape[1] // LANES), axis=1)
    centred = values - jnp.mean(values, axis=0, keepdims=True)
    spread = jnp.mean(centred * centred, axis=0, keepdims=True)
    return (centred * lax.rsqrt(spread + 1e-05) * wide).astype(BF16)


def spread_gain(row):
    return jnp.broadcast_to(row, (LANES, row.shape[1])).T


def token_mask(mask, lines):
    height, breadth = mask.shape
    wide = jnp.concatenate([mask.astype(F32)] * (LANES // breadth), axis=1)
    row = lax.broadcasted_iota(jnp.int32, wide.shape, 0)
    lane = lax.broadcasted_iota(jnp.int32, wide.shape, 1)
    wide = jnp.where(row // lines == lane // breadth, wide, 0.0).astype(BF16)
    line = lax.broadcasted_iota(jnp.int32, (lines, height), 0)
    source = lax.broadcasted_iota(jnp.int32, (lines, height), 1)
    return dot((source % lines == line).astype(BF16), wide)


def emit_message(normed, weight_t, mask, line, message_ref, stage_ref, share):
    projected = dot(weight_t, normed)
    hid = weight_t.shape[0] // 4
    owners = hid // share
    for part in range(normed.shape[1] // LANES):
        here = projected[:, part * LANES : (part + 1) * LANES]
        at = line + part
        keep = mask[at : at + 1]
        left = twice_sigmoid(here[:hid]) * here[hid : 2 * hid] * keep
        right = twice_sigmoid(here[2 * hid : 3 * hid]) * here[3 * hid :] * keep
        if share % 8 == 0:
            for owner in range(owners):
                rows = slice(owner * share, (owner + 1) * share)
                both = jnp.concatenate([left[rows], right[rows]], axis=0).astype(BF16)
                message_ref[owner, 2 * share * at : 2 * share * (at + 1), :] = both
        else:
            lines = message_ref.shape[1] // 2
            stage_ref[pl.ds(2 * at, owners, stride=2 * lines), :] = left
            stage_ref[pl.ds(2 * at + 1, owners, stride=2 * lines), :] = right
    if share % 8 and line + normed.shape[1] // LANES == mask.shape[0]:
        message_ref[...] = stage_ref[...].astype(BF16).reshape(message_ref.shape)


def start_all(pairs, sems, first=0):
    copies = [pltpu.make_async_copy(src, dst, sems.at[first + n]) for n, (src, dst) in enumerate(pairs)]
    for copy in copies:
        copy.start()
    return copies


def line_tokens(x_ref, line):
    return jnp.concatenate([x_ref[slot, line] for slot in range(x_ref.shape[0])], axis=0)


def project_kernel(share, ins, outs, stage_ref, x_ref, mask_ref, weight_ref, gate_ref, gain_in_ref, gain_out_ref, trans_gain_ref, sems):
    message_ref, gate_out, turned_out, mask_out, gains_out = outs
    x_in, mask_in, weight_in, gate_in, gain_in, gain_out, trans_gain = ins
    lines = x_ref.shape[1]
    pairs = [
        (weight_in.at[0], weight_ref),
        (x_in, x_ref),
        (gain_in, gain_in_ref),
        (mask_in, mask_ref),
        (gate_in.at[0], gate_ref),
        (gain_out, gain_out_ref),
        (trans_gain, trans_gain_ref),
    ]
    for copy in start_all(pairs, sems):
        copy.wait()
    mask = token_mask(mask_ref[...], lines)
    current = jnp.concatenate([line_tokens(x_ref, line).T for line in range(lines)], axis=1)
    normed = channel_norm(current, spread_gain(gain_in_ref[0:1, :]))
    emit_message(normed, halved(weight_ref[...]), mask, 0, message_ref, stage_ref, share)
    gate_out[...] = twice_sigmoid(dot(halved(gate_ref[...]), normed))
    turned_out[...] = current
    mask_out[...] = mask
    rows = [gain_out_ref[0:1, :], gain_in_ref[1:2, :], gain_out_ref[1:2, :], trans_gain_ref[...]]
    gains_out[...] = jnp.concatenate(rows + rows, axis=0)


def one_hot(rows, columns, wanted):
    row = lax.broadcasted_iota(jnp.int32, (rows, columns), 0)
    column = lax.broadcasted_iota(jnp.int32, (rows, columns), 1)
    return (wanted(row) == column).astype(BF16)


def swap_matrix(slots, breadth):
    size = slots * LANES
    return one_hot(
        size, size, lambda lane: lane // breadth % slots * LANES + lane // LANES * breadth + lane % breadth
    )


def combine_kernel(sources, owners, breadth, share, outgoing, ins, outs):
    near, cols, rows = len(sources), len(owners), len(owners[0])
    (both_ref,), (combined_ref,) = ins, outs
    slots = LANES // breadth
    span = both_ref.shape[1]
    lines = span // (2 * share)
    pack = max(1, slots // near)
    groups = share // pack
    size = span // pack
    swap = swap_matrix(slots, breadth)

    def source(row):
        channel = row // size * groups + row // lines % groups
        return row % lines * (2 * share) + row // (groups * lines) % 2 * share + channel

    order = one_hot(span, span, source)
    blocks = [both_ref[sources[col][row]] for row in range(rows) for col in range(near)]
    ordered = dot(order, jnp.concatenate(blocks, axis=1)).astype(BF16)
    wide = []
    for row in range(rows):
        here = ordered[:, row * near * LANES : (row + 1) * near * LANES]
        wide.append(jnp.concatenate([here[n * size : (n + 1) * size] for n in range(pack)], axis=1))
    wide = jnp.concatenate(wide, axis=0)
    block = slots * LANES
    swapped = [dot(wide[:, first : first + block], swap) for first in range(0, wide.shape[1], block)]

    def whole(side, group):
        columns = []
        for part in swapped:
            held = []
            for row in range(rows):
                first = row * size + (side * groups + group) * lines
                held += [part[first : first + lines, slot * LANES : (slot + 1) * LANES] for slot in range(slots)]
            columns.append(jnp.concatenate(held, axis=0))
        return jnp.concatenate(columns, axis=1).astype(BF16)

    products = [None] * share
    for group in range(groups):
        left, right = whole(0, group), whole(1, group)
        if pack > 1:
            lane = lax.broadcasted_iota(jnp.int32, left.shape, 1) // (near * breadth)
            left = [jnp.where(lane == place, left, jnp.zeros_like(left)) for place in range(pack)]
            left = jnp.concatenate(left, axis=0)
        product = dot(left, right, (1, 1) if outgoing else (0, 0))
        tokens = product.shape[0] // pack
        for place in range(pack):
            products[place * groups + group] = product[place * tokens : (place + 1) * tokens]

    for high in range(cols // slots):
        lanes = slice(high * LANES, (high + 1) * LANES)
        held = []
        for row in range(rows):
            for product in products:
                parts = [
                    product[(row * slots + slot) * lines : (row * slots + slot + 1) * lines, lanes]
                    for slot in range(slots)
                ]
                held.append(jnp.concatenate(parts, axis=1))
        back = dot(jnp.concatenate(held, axis=0).astype(BF16), swap).astype(BF16)
        for low in range(slots):
            for row in range(rows):
                first = row * share * lines
                combined_ref[owners[high * slots + low][row]] = back[
                    first : first + share * lines, low * LANES : (low + 1) * LANES
                ]


def hold_combined(combined_ref, stage_ref, share, sources):
    span = combined_ref.shape[1]
    lines = span // share
    order = one_hot(span, span, lambda row: row % share * lines + row // share)
    order = jnp.concatenate([order] * len(sources[0]), axis=1)
    blocks = [jnp.concatenate([combined_ref[source] for source in held], axis=0) for held in sources]
    ordered = dot(order, jnp.concatenate(blocks, axis=1))
    for owner in range(len(sources)):
        stage_ref[owner * span : (owner + 1) * span, :] = ordered[:, owner * LANES : (owner + 1) * LANES]


def read_combined(stage_ref, owners, lines, share, first, count):
    columns = []
    for line in range(first, first + count):
        if share % 8 == 0:
            held = [
                stage_ref[(owner * lines + line) * share : (owner * lines + line + 1) * share, :]
                for owner in range(owners)
            ]
            columns.append(jnp.concatenate(held, axis=0))
        else:
            columns.append(stage_ref[pl.ds(line, owners, stride=lines), :])
    return jnp.concatenate(columns, axis=1)


def middle_kernel(share, sources, next_share, chunk, ins, outs, stage_ref, message_stage_ref):
    combined_ref, x_ref, gate_ref, mask_ref, gains_ref, proj_ref, gate_weight_ref, out_ref = ins
    message_ref, gate_out, next_ref = outs
    tokens = x_ref.shape[1]
    lines = tokens // LANES
    owners = x_ref.shape[0] // share
    hold_combined(combined_ref, stage_ref, share, sources)
    mask = mask_ref[...]
    gain_out, gain = [spread_gain(gains_ref[n : n + 1, :]) for n in (0, 1)]
    out_t, proj_t, gate_t = halved(out_ref[0]), halved(proj_ref[1]), halved(gate_weight_ref[1])
    for start in range(0, tokens, chunk):
        here = slice(start, start + chunk)
        combined = read_combined(stage_ref, owners, lines, share, start // LANES, chunk // LANES)
        hidden = channel_norm(combined, gain_out)
        current = x_ref[:, here] + gate_ref[:, here] * dot(out_t, hidden)
        next_ref[:, here] = current
        normed = channel_norm(current, gain)
        emit_message(normed, proj_t, mask, start // LANES, message_ref, message_stage_ref, next_share)
        gate_out[:, here] = twice_sigmoid(dot(gate_t, normed))


def last_kernel(share, sources, chunk, ins, outs, stage_ref, result_ref, sems):
    combined_ref, x_ref, gate_ref, gains_ref, out_ref, up_ref, down_ref = ins
    (result_out,) = outs
    slots, lines, breadth, channels = result_ref.shape
    owners = x_ref.shape[0] // share
    half = down_ref.shape[0]
    count = chunk // LANES
    gain_out, gain = [spread_gain(gains_ref[n : n + 1, :]) for n in (2, 3)]
    out_t, down_t = halved(out_ref[1]), down_ref[...].T
    gate_t, up_t = halved(up_ref[:, :half]), up_ref[:, half:].T
    hold_combined(combined_ref, stage_ref, share, sources)
    combined = read_combined(stage_ref, owners, lines, share, 0, lines)
    hidden = channel_norm(combined, gain_out)
    current = x_ref[...] + gate_ref[...] * dot(out_t, hidden)
    trans_in = channel_norm(current, gain)
    gate_part, up_part = dot(gate_t, trans_in), dot(up_t, trans_in)
    trans_hidden = (gate_part * twice_sigmoid(gate_part) * up_part).astype(BF16)
    current = current + dot(down_t, trans_hidden)
    writes = []
    for first in range(0, lines, count):
        for line in range(first, first + count):
            result = current[:, line * LANES : (line + 1) * LANES].T
            for slot in range(slots):
                result_ref[slot, line] = result[slot * breadth : (slot + 1) * breadth]
        piece = slice(first, first + count)
        writes += start_all([(result_ref.at[:, piece], result_out.at[:, piece])], sems, first // count)
    for write in writes:
        write.wait()


def call(kernel, operands, outs, scratch=(), in_hbm=False, out_hbm=False):
    in_place, held = pl.BlockSpec(memory_space=pltpu.HBM), pl.BlockSpec(memory_space=pltpu.VMEM)
    count = len(operands)

    def body(*refs):
        kernel(refs[:count], refs[count : count + len(outs)], *refs[count + len(outs) :])

    return pl.pallas_call(
        body,
        in_specs=[in_place if in_hbm else held] * count,
        out_specs=[in_place if out_hbm else held] * len(outs),
        out_shape=[jax.ShapeDtypeStruct(shape, dtype) for shape, dtype in outs],
        scratch_shapes=list(scratch),
        compiler_params=pltpu.CompilerParams(vmem_limit_bytes=VMEM_BYTES),
    )(*[pltpu.with_memory_space_constraint(array, pltpu.HBM) if in_hbm else array for array in operands])


def exchange(values, axes, order=None):
    groups = [order] if order else None
    return lax.all_to_all(values, axes, split_axis=0, concat_axis=0, axis_index_groups=groups, tiled=True)


def per_device(
    rows,
    halves,
    nears,
    pair_map,
    pair_mask,
    gain_in,
    proj_weight,
    gate_weight,
    gain_out,
    out_weight,
    trans_gain,
    trans_up,
    trans_down,
):
    height, breadth, channels = pair_map.shape
    tokens = height * breadth
    lines = tokens // LANES
    hid = gain_out.shape[1]
    cols = halves * nears
    owners = rows * cols
    share = hid // owners
    chunk = min(4 * LANES, tokens)
    split = halves if share % 8 == 0 else 1
    first_share = split * share
    held = ((LANES // breadth, lines, breadth, channels), F32)
    grouped = pair_map.reshape(held[0])
    wide = ((channels, tokens), F32)
    result = pltpu.VMEM((owners * share * lines, LANES), F32)
    spare = pltpu.VMEM((8, LANES) if share % 8 == 0 else (owners * 2 * share * lines, LANES), F32)

    def message(own):
        return ((hid // own, 2 * own * lines, LANES), BF16)

    blocks = list(range(cols))
    blocks.insert(0, blocks.pop((cols - 1) // 2))
    order = [col * rows + row for col in blocks for row in range(rows)]
    everyone = [[order.index(col * rows + row) for row in range(rows)] for col in range(cols)]
    beside = [[near * rows + row for row in range(rows)] for near in range(nears)] if split > 1 else everyone
    single = [[n] for n in range(owners)]
    paired = single if split == 1 else [
        [everyone[half * nears + near][row] for half in range(halves)] for near in range(nears) for row in range(rows)
    ]

    def combine(both, own, sources, outgoing):
        kernel = functools.partial(combine_kernel, sources, everyone, breadth, own, outgoing)
        answer = ((owners, own * lines, LANES), BF16)
        return exchange(call(kernel, (both,), [answer])[0], ALL_AXES, order)

    operands = (grouped, pair_mask, proj_weight, gate_weight, gain_in, gain_out, trans_gain.reshape(1, -1))
    both, gate, current, mask, gains = call(
        functools.partial(project_kernel, first_share),
        operands,
        [message(first_share), wide, wide, ((lines, LANES), F32), ((8, channels), F32)],
        (
            spare,
            *[
                pltpu.VMEM(array.shape[1:] if array.ndim == 3 else array.shape, array.dtype)
                for array in operands
            ],
            pltpu.SemaphoreType.DMA((len(operands),)),
        ),
        in_hbm=True,
    )
    both = exchange(both, NEAR_AXES) if split > 1 else exchange(both, ALL_AXES, order)
    combined = combine(both, first_share, beside, True)
    both, gate, current = call(
        functools.partial(middle_kernel, first_share, paired, share, tokens),
        (combined, current, gate, mask, gains, proj_weight, gate_weight, out_weight),
        [message(share), wide, wide],
        (result, spare),
    )
    combined = combine(exchange(both, ALL_AXES, order), share, everyone, False)
    (pair_out,) = call(
        functools.partial(last_kernel, share, single, chunk),
        (combined, current, gate, gains, out_weight, trans_up, trans_down),
        [held],
        (result, pltpu.VMEM(*held), pltpu.SemaphoreType.DMA((tokens // chunk,))),
        out_hbm=True,
    )
    return pair_out.reshape(pair_map.shape)


def solution(mesh):
    groups, rows, cols = (mesh.shape[name] for name in ("grp", "row", "col"))
    halves = 2 if cols % 2 == 0 else 1
    nears = cols // halves
    folded = Mesh(mesh.devices.reshape(groups, rows, halves, nears), ("grp", "row", "half", "near"))
    tokens = (("grp", "row"), ("half", "near"))
    in_specs = (P(*tokens, None), P(*tokens)) + (P(),) * 8

    def body(*args):
        return per_device(rows, halves, nears, *args)

    return jax.shard_map(body, mesh=folded, in_specs=in_specs, out_specs=P(*tokens, None), check_vma=False)
```

```python
import functools

import jax
import jax.numpy as jnp
from jax import lax
from jax.experimental import pallas as pl
from jax.experimental.pallas import tpu as pltpu
from jax.sharding import Mesh
from jax.sharding import PartitionSpec as P

NEAR_AXES = ("near", "row")
ALL_AXES = ("half", "near", "row")
LANES = 128
VMEM_BYTES = 24 * 1024 * 1024
F32, BF16 = jnp.float32, jnp.bfloat16


def dot(left, right, contract=(1, 0)):
    return lax.dot_general(
        left, right, (((contract[0],), (contract[1],)), ((), ())), preferred_element_type=F32
    )


def halved(weight):
    return weight.T * 0.5


def twice_sigmoid(half):
    return jnp.tanh(half) + 1.0


def channel_norm(values, gain):
    wide = jnp.concatenate([gain] * (values.shape[1] // LANES), axis=1)
    centred = values - jnp.mean(values, axis=0, keepdims=True)
    spread = jnp.mean(centred * centred, axis=0, keepdims=True)
    return (centred * lax.rsqrt(spread + 1e-05) * wide).astype(BF16)


def spread_gain(row):
    return jnp.broadcast_to(row, (LANES, row.shape[1])).T


def token_mask(mask, lines):
    height, breadth = mask.shape
    wide = jnp.concatenate([mask.astype(F32)] * (LANES // breadth), axis=1)
    row = lax.broadcasted_iota(jnp.int32, wide.shape, 0)
    lane = lax.broadcasted_iota(jnp.int32, wide.shape, 1)
    wide = jnp.where(row // lines == lane // breadth, wide, 0.0).astype(BF16)
    line = lax.broadcasted_iota(jnp.int32, (lines, height), 0)
    source = lax.broadcasted_iota(jnp.int32, (lines, height), 1)
    return dot((source % lines == line).astype(BF16), wide)


def emit_message(normed, weight_t, mask, line, message_ref, stage_ref, share):
    projected = dot(weight_t, normed)
    hid = weight_t.shape[0] // 4
    owners = hid // share
    for part in range(normed.shape[1] // LANES):
        here = projected[:, part * LANES : (part + 1) * LANES]
        at = line + part
        keep = mask[at : at + 1]
        left = twice_sigmoid(here[:hid]) * here[hid : 2 * hid] * keep
        right = twice_sigmoid(here[2 * hid : 3 * hid]) * here[3 * hid :] * keep
        if share % 8 == 0:
            for owner in range(owners):
                rows = slice(owner * share, (owner + 1) * share)
                both = jnp.concatenate([left[rows], right[rows]], axis=0).astype(BF16)
                message_ref[owner, 2 * share * at : 2 * share * (at + 1), :] = both
        else:
            lines = message_ref.shape[1] // 2
            stage_ref[pl.ds(2 * at, owners, stride=2 * lines), :] = left
            stage_ref[pl.ds(2 * at + 1, owners, stride=2 * lines), :] = right
    if share % 8 and line + normed.shape[1] // LANES == mask.shape[0]:
        message_ref[...] = stage_ref[...].astype(BF16).reshape(message_ref.shape)


def start_all(pairs, sems, first=0):
    copies = [pltpu.make_async_copy(src, dst, sems.at[first + n]) for n, (src, dst) in enumerate(pairs)]
    for copy in copies:
        copy.start()
    return copies


def line_tokens(x_ref, line):
    return jnp.concatenate([x_ref[slot, line] for slot in range(x_ref.shape[0])], axis=0)


def project_kernel(share, ins, outs, stage_ref, x_ref, mask_ref, weight_ref, gate_ref, gain_in_ref, gain_out_ref, trans_gain_ref, sems):
    message_ref, gate_out, turned_out, mask_out, gains_out = outs
    x_in, mask_in, weight_in, gate_in, gain_in, gain_out, trans_gain = ins
    lines = x_ref.shape[1]
    pairs = [
        (weight_in.at[0], weight_ref),
        (x_in, x_ref),
        (gain_in, gain_in_ref),
        (mask_in, mask_ref),
        (gate_in.at[0], gate_ref),
        (gain_out, gain_out_ref),
        (trans_gain, trans_gain_ref),
    ]
    for copy in start_all(pairs, sems):
        copy.wait()
    mask = token_mask(mask_ref[...], lines)
    current = jnp.concatenate([line_tokens(x_ref, line).T for line in range(lines)], axis=1)
    normed = channel_norm(current, spread_gain(gain_in_ref[0:1, :]))
    emit_message(normed, halved(weight_ref[...]), mask, 0, message_ref, stage_ref, share)
    gate_out[...] = twice_sigmoid(dot(halved(gate_ref[...]), normed))
    turned_out[...] = current
    mask_out[...] = mask
    rows = [gain_out_ref[0:1, :], gain_in_ref[1:2, :], gain_out_ref[1:2, :], trans_gain_ref[...]]
    gains_out[...] = jnp.concatenate(rows + rows, axis=0)


def one_hot(rows, columns, wanted):
    row = lax.broadcasted_iota(jnp.int32, (rows, columns), 0)
    column = lax.broadcasted_iota(jnp.int32, (rows, columns), 1)
    return (wanted(row) == column).astype(BF16)


def swap_matrix(slots, breadth):
    size = slots * LANES
    return one_hot(
        size, size, lambda lane: lane // breadth % slots * LANES + lane // LANES * breadth + lane % breadth
    )


def combine_kernel(sources, owners, breadth, share, outgoing, ins, outs):
    near, cols, rows = len(sources), len(owners), len(owners[0])
    (both_ref,), (combined_ref,) = ins, outs
    slots = LANES // breadth
    span = both_ref.shape[1]
    lines = span // (2 * share)
    pack = max(1, slots // near)
    groups = share // pack
    size = span // pack
    swap = swap_matrix(slots, breadth)

    def source(row):
        channel = row // size * groups + row // lines % groups
        return row % lines * (2 * share) + row // (groups * lines) % 2 * share + channel

    order = one_hot(span, span, source)
    blocks = [both_ref[sources[col][row]] for row in range(rows) for col in range(near)]
    ordered = dot(order, jnp.concatenate(blocks, axis=1)).astype(BF16)
    wide = []
    for row in range(rows):
        here = ordered[:, row * near * LANES : (row + 1) * near * LANES]
        wide.append(jnp.concatenate([here[n * size : (n + 1) * size] for n in range(pack)], axis=1))
    wide = jnp.concatenate(wide, axis=0)
    block = slots * LANES
    swapped = [dot(wide[:, first : first + block], swap) for first in range(0, wide.shape[1], block)]

    def whole(side, group):
        columns = []
        for part in swapped:
            held = []
            for row in range(rows):
                first = row * size + (side * groups + group) * lines
                held += [part[first : first + lines, slot * LANES : (slot + 1) * LANES] for slot in range(slots)]
            columns.append(jnp.concatenate(held, axis=0))
        return jnp.concatenate(columns, axis=1).astype(BF16)

    products = [None] * share
    for group in range(groups):
        left, right = whole(0, group), whole(1, group)
        if pack > 1:
            lane = lax.broadcasted_iota(jnp.int32, left.shape, 1) // (near * breadth)
            left = [jnp.where(lane == place, left, jnp.zeros_like(left)) for place in range(pack)]
            left = jnp.concatenate(left, axis=0)
        product = dot(left, right, (1, 1) if outgoing else (0, 0))
        tokens = product.shape[0] // pack
        for place in range(pack):
            products[place * groups + group] = product[place * tokens : (place + 1) * tokens]

    for high in range(cols // slots):
        lanes = slice(high * LANES, (high + 1) * LANES)
        held = []
        for row in range(rows):
            for product in products:
                parts = [
                    product[(row * slots + slot) * lines : (row * slots + slot + 1) * lines, lanes]
                    for slot in range(slots)
                ]
                held.append(jnp.concatenate(parts, axis=1))
        back = dot(jnp.concatenate(held, axis=0).astype(BF16), swap).astype(BF16)
        for low in range(slots):
            for row in range(rows):
                first = row * share * lines
                combined_ref[owners[high * slots + low][row]] = back[
                    first : first + share * lines, low * LANES : (low + 1) * LANES
                ]


def hold_combined(combined_ref, stage_ref, share, sources):
    span = combined_ref.shape[1]
    lines = span // share
    order = one_hot(span, span, lambda row: row % share * lines + row // share)
    order = jnp.concatenate([order] * len(sources[0]), axis=1)
    blocks = [jnp.concatenate([combined_ref[source] for source in held], axis=0) for held in sources]
    ordered = dot(order, jnp.concatenate(blocks, axis=1))
    for owner in range(len(sources)):
        stage_ref[owner * span : (owner + 1) * span, :] = ordered[:, owner * LANES : (owner + 1) * LANES]


def read_combined(stage_ref, owners, lines, share, first, count):
    columns = []
    for line in range(first, first + count):
        if share % 8 == 0:
            held = [
                stage_ref[(owner * lines + line) * share : (owner * lines + line + 1) * share, :]
                for owner in range(owners)
            ]
            columns.append(jnp.concatenate(held, axis=0))
        else:
            columns.append(stage_ref[pl.ds(line, owners, stride=lines), :])
    return jnp.concatenate(columns, axis=1)


def middle_kernel(share, sources, next_share, chunk, ins, outs, stage_ref, message_stage_ref):
    combined_ref, x_ref, gate_ref, mask_ref, gains_ref, proj_ref, gate_weight_ref, out_ref = ins
    message_ref, gate_out, next_ref = outs
    tokens = x_ref.shape[1]
    lines = tokens // LANES
    owners = x_ref.shape[0] // share
    hold_combined(combined_ref, stage_ref, share, sources)
    mask = mask_ref[...]
    gain_out, gain = [spread_gain(gains_ref[n : n + 1, :]) for n in (0, 1)]
    out_t, proj_t, gate_t = halved(out_ref[0]), halved(proj_ref[1]), halved(gate_weight_ref[1])
    for start in range(0, tokens, chunk):
        here = slice(start, start + chunk)
        combined = read_combined(stage_ref, owners, lines, share, start // LANES, chunk // LANES)
        hidden = channel_norm(combined, gain_out)
        current = x_ref[:, here] + gate_ref[:, here] * dot(out_t, hidden)
        next_ref[:, here] = current
        normed = channel_norm(current, gain)
        emit_message(normed, proj_t, mask, start // LANES, message_ref, message_stage_ref, next_share)
        gate_out[:, here] = twice_sigmoid(dot(gate_t, normed))


def last_kernel(share, sources, chunk, ins, outs, stage_ref, result_ref, sems):
    combined_ref, x_ref, gate_ref, gains_ref, out_ref, up_ref, down_ref = ins
    (result_out,) = outs
    slots, lines, breadth, channels = result_ref.shape
    owners = x_ref.shape[0] // share
    half = down_ref.shape[0]
    count = chunk // LANES
    gain_out, gain = [spread_gain(gains_ref[n : n + 1, :]) for n in (2, 3)]
    out_t, down_t = halved(out_ref[1]), down_ref[...].T
    gate_t, up_t = halved(up_ref[:, :half]), up_ref[:, half:].T
    hold_combined(combined_ref, stage_ref, share, sources)
    combined = read_combined(stage_ref, owners, lines, share, 0, lines)
    hidden = channel_norm(combined, gain_out)
    current = x_ref[...] + gate_ref[...] * dot(out_t, hidden)
    trans_in = channel_norm(current, gain)
    gate_part, up_part = dot(gate_t, trans_in), dot(up_t, trans_in)
    trans_hidden = (gate_part * twice_sigmoid(gate_part) * up_part).astype(BF16)
    current = current + dot(down_t, trans_hidden)
    writes = []
    for first in range(0, lines, count):
        for line in range(first, first + count):
            result = current[:, line * LANES : (line + 1) * LANES].T
            for slot in range(slots):
                result_ref[slot, line] = result[slot * breadth : (slot + 1) * breadth]
        piece = slice(first, first + count)
        writes += start_all([(result_ref.at[:, piece], result_out.at[:, piece])], sems, first // count)
    for write in writes:
        write.wait()


def call(kernel, operands, outs, scratch=(), in_hbm=False, out_hbm=False):
    in_place, held = pl.BlockSpec(memory_space=pltpu.HBM), pl.BlockSpec(memory_space=pltpu.VMEM)
    count = len(operands)

    def body(*refs):
        kernel(refs[:count], refs[count : count + len(outs)], *refs[count + len(outs) :])

    return pl.pallas_call(
        body,
        in_specs=[in_place if in_hbm else held] * count,
        out_specs=[in_place if out_hbm else held] * len(outs),
        out_shape=[jax.ShapeDtypeStruct(shape, dtype) for shape, dtype in outs],
        scratch_shapes=list(scratch),
        compiler_params=pltpu.CompilerParams(vmem_limit_bytes=VMEM_BYTES),
    )(*[pltpu.with_memory_space_constraint(array, pltpu.HBM) if in_hbm else array for array in operands])


def exchange(values, axes, order):
    return lax.all_to_all(values, axes, split_axis=0, concat_axis=0, axis_index_groups=[order], tiled=True)


def per_device(
    rows,
    halves,
    nears,
    pair_map,
    pair_mask,
    gain_in,
    proj_weight,
    gate_weight,
    gain_out,
    out_weight,
    trans_gain,
    trans_up,
    trans_down,
):
    height, breadth, channels = pair_map.shape
    tokens = height * breadth
    lines = tokens // LANES
    hid = gain_out.shape[1]
    cols = halves * nears
    owners = rows * cols
    share = hid // owners
    chunk = min(4 * LANES, tokens)
    split = halves if share % 8 == 0 else 1
    first_share = split * share
    held = ((LANES // breadth, lines, breadth, channels), F32)
    grouped = pair_map.reshape(held[0])
    wide = ((channels, tokens), F32)
    result = pltpu.VMEM((owners * share * lines, LANES), F32)
    spare = pltpu.VMEM((8, LANES) if share % 8 == 0 else (owners * 2 * share * lines, LANES), F32)

    def message(own):
        return ((hid // own, 2 * own * lines, LANES), BF16)

    def listed(places):
        order = [col * rows + row for col, row in places]
        count = len(places) // rows
        return order, [[order.index(col * rows + row) for row in range(rows)] for col in range(count)]

    middle = (cols - 1) // 2
    blocks = list(range(cols))
    blocks.insert(0, blocks.pop(middle))
    order, everyone = listed([(col, row) for col in blocks for row in range(rows)])
    turned = [(col + middle) % cols for col in range(cols)]
    last_order, last_everyone = listed([(col, row) for col in turned for row in range(rows)])
    near_order, beside = order, everyone
    if split > 1:
        near_order, beside = listed([(near, row) for row in range(rows) for near in range(nears)])
    single = [[last_order.index(device)] for device in order]
    paired = [
        [everyone[half * nears + device // rows][device % rows] for half in range(split)] for device in near_order
    ]

    def combine(both, own, sources, outgoing, order, owners_at):
        kernel = functools.partial(combine_kernel, sources, owners_at, breadth, own, outgoing)
        answer = ((owners, own * lines, LANES), BF16)
        return exchange(call(kernel, (both,), [answer])[0], ALL_AXES, order)

    operands = (grouped, pair_mask, proj_weight, gate_weight, gain_in, gain_out, trans_gain.reshape(1, -1))
    both, gate, current, mask, gains = call(
        functools.partial(project_kernel, first_share),
        operands,
        [message(first_share), wide, wide, ((lines, LANES), F32), ((8, channels), F32)],
        (
            spare,
            *[
                pltpu.VMEM(array.shape[1:] if array.ndim == 3 else array.shape, array.dtype)
                for array in operands
            ],
            pltpu.SemaphoreType.DMA((len(operands),)),
        ),
        in_hbm=True,
    )
    both = exchange(both, NEAR_AXES if split > 1 else ALL_AXES, near_order)
    combined = combine(both, first_share, beside, True, order, everyone)
    both, gate, current = call(
        functools.partial(middle_kernel, first_share, paired, share, tokens),
        (combined, current, gate, mask, gains, proj_weight, gate_weight, out_weight),
        [message(share), wide, wide],
        (result, spare),
    )
    combined = combine(exchange(both, ALL_AXES, order), share, everyone, False, last_order, last_everyone)
    (pair_out,) = call(
        functools.partial(last_kernel, share, single, chunk),
        (combined, current, gate, gains, out_weight, trans_up, trans_down),
        [held],
        (result, pltpu.VMEM(*held), pltpu.SemaphoreType.DMA((tokens // chunk,))),
        out_hbm=True,
    )
    return pair_out.reshape(pair_map.shape)


def solution(mesh):
    groups, rows, cols = (mesh.shape[name] for name in ("grp", "row", "col"))
    halves = 2 if cols % 2 == 0 else 1
    nears = cols // halves
    folded = Mesh(mesh.devices.reshape(groups, rows, halves, nears), ("grp", "row", "half", "near"))
    tokens = (("grp", "row"), ("half", "near"))
    in_specs = (P(*tokens, None), P(*tokens)) + (P(),) * 8

    def body(*args):
        return per_device(rows, halves, nears, *args)

    return jax.shard_map(body, mesh=folded, in_specs=in_specs, out_specs=P(*tokens, None), check_vma=False)
```

```python
import functools

import jax
import jax.numpy as jnp
from jax import lax
from jax.experimental import pallas as pl
from jax.experimental.pallas import tpu as pltpu
from jax.sharding import Mesh
from jax.sharding import PartitionSpec as P

NEAR_AXES = ("near", "row")
ALL_AXES = ("half", "near", "row")
LANES = 128
VMEM_BYTES = 24 * 1024 * 1024
F32, BF16 = jnp.float32, jnp.bfloat16


def dot(left, right, contract=(1, 0)):
    return lax.dot_general(
        left, right, (((contract[0],), (contract[1],)), ((), ())), preferred_element_type=F32
    )


def halved(weight):
    return weight.T * 0.5


def twice_sigmoid(half):
    return jnp.tanh(half) + 1.0


def channel_norm(values, gain):
    wide = jnp.concatenate([gain] * (values.shape[1] // LANES), axis=1)
    centred = values - jnp.mean(values, axis=0, keepdims=True)
    spread = jnp.mean(centred * centred, axis=0, keepdims=True)
    return (centred * lax.rsqrt(spread + 1e-05) * wide).astype(BF16)


def spread_gain(row):
    return jnp.broadcast_to(row, (LANES, row.shape[1])).T


def token_mask(mask, lines):
    height, breadth = mask.shape
    wide = jnp.concatenate([mask.astype(F32)] * (LANES // breadth), axis=1)
    row = lax.broadcasted_iota(jnp.int32, wide.shape, 0)
    lane = lax.broadcasted_iota(jnp.int32, wide.shape, 1)
    wide = jnp.where(row // lines == lane // breadth, wide, 0.0).astype(BF16)
    line = lax.broadcasted_iota(jnp.int32, (lines, height), 0)
    source = lax.broadcasted_iota(jnp.int32, (lines, height), 1)
    return dot((source % lines == line).astype(BF16), wide)


def emit_message(normed, weight_t, mask, line, message_ref, stage_ref, share):
    projected = dot(weight_t, normed)
    hid = weight_t.shape[0] // 4
    owners = hid // share
    for part in range(normed.shape[1] // LANES):
        here = projected[:, part * LANES : (part + 1) * LANES]
        at = line + part
        keep = mask[at : at + 1]
        left = twice_sigmoid(here[:hid]) * here[hid : 2 * hid] * keep
        right = twice_sigmoid(here[2 * hid : 3 * hid]) * here[3 * hid :] * keep
        if share % 8 == 0:
            for owner in range(owners):
                rows = slice(owner * share, (owner + 1) * share)
                both = jnp.concatenate([left[rows], right[rows]], axis=0).astype(BF16)
                message_ref[owner, 2 * share * at : 2 * share * (at + 1), :] = both
        else:
            lines = message_ref.shape[1] // 2
            stage_ref[pl.ds(2 * at, owners, stride=2 * lines), :] = left
            stage_ref[pl.ds(2 * at + 1, owners, stride=2 * lines), :] = right
    if share % 8 and line + normed.shape[1] // LANES == mask.shape[0]:
        message_ref[...] = stage_ref[...].astype(BF16).reshape(message_ref.shape)


def start_all(pairs, sems, first=0):
    copies = [pltpu.make_async_copy(src, dst, sems.at[first + n]) for n, (src, dst) in enumerate(pairs)]
    for copy in copies:
        copy.start()
    return copies


def line_tokens(x_ref, line):
    return jnp.concatenate([x_ref[slot, line] for slot in range(x_ref.shape[0])], axis=0)


def project_kernel(share, ins, outs, stage_ref, x_ref, mask_ref, weight_ref, gate_ref, gain_in_ref, gain_out_ref, trans_gain_ref, sems):
    message_ref, gate_out, turned_out, mask_out, gains_out = outs
    x_in, mask_in, weight_in, gate_in, gain_in, gain_out, trans_gain = ins
    lines = x_ref.shape[1]
    pairs = [
        (weight_in.at[0], weight_ref),
        (x_in, x_ref),
        (gain_in, gain_in_ref),
        (mask_in, mask_ref),
        (gate_in.at[0], gate_ref),
        (gain_out, gain_out_ref),
        (trans_gain, trans_gain_ref),
    ]
    for copy in start_all(pairs, sems):
        copy.wait()
    mask = token_mask(mask_ref[...], lines)
    current = jnp.concatenate([line_tokens(x_ref, line).T for line in range(lines)], axis=1)
    normed = channel_norm(current, spread_gain(gain_in_ref[0:1, :]))
    emit_message(normed, halved(weight_ref[...]), mask, 0, message_ref, stage_ref, share)
    gate_out[...] = twice_sigmoid(dot(halved(gate_ref[...]), normed))
    turned_out[...] = current
    mask_out[...] = mask
    rows = [gain_out_ref[0:1, :], gain_in_ref[1:2, :], gain_out_ref[1:2, :], trans_gain_ref[...]]
    gains_out[...] = jnp.concatenate(rows + rows, axis=0)


def one_hot(rows, columns, wanted):
    row = lax.broadcasted_iota(jnp.int32, (rows, columns), 0)
    column = lax.broadcasted_iota(jnp.int32, (rows, columns), 1)
    return (wanted(row) == column).astype(BF16)


def swap_matrix(slots, breadth):
    size = slots * LANES
    return one_hot(
        size, size, lambda lane: lane // breadth % slots * LANES + lane // LANES * breadth + lane % breadth
    )


def combine_kernel(sources, owners, breadth, share, outgoing, ins, outs):
    near, cols, rows = len(sources), len(owners), len(owners[0])
    (both_ref,), (combined_ref,) = ins, outs
    slots = LANES // breadth
    span = both_ref.shape[1]
    lines = span // (2 * share)
    pack = max(1, slots // near)
    groups = share // pack
    size = span // pack
    swap = swap_matrix(slots, breadth)

    def source(row):
        channel = row // size * groups + row // lines % groups
        return row % lines * (2 * share) + row // (groups * lines) % 2 * share + channel

    order = one_hot(span, span, source)
    blocks = [both_ref[sources[col][row]] for row in range(rows) for col in range(near)]
    ordered = dot(order, jnp.concatenate(blocks, axis=1)).astype(BF16)
    wide = []
    for row in range(rows):
        here = ordered[:, row * near * LANES : (row + 1) * near * LANES]
        wide.append(jnp.concatenate([here[n * size : (n + 1) * size] for n in range(pack)], axis=1))
    wide = jnp.concatenate(wide, axis=0)
    block = slots * LANES
    swapped = [dot(wide[:, first : first + block], swap) for first in range(0, wide.shape[1], block)]

    def whole(side, group):
        columns = []
        for part in swapped:
            held = []
            for row in range(rows):
                first = row * size + (side * groups + group) * lines
                held += [part[first : first + lines, slot * LANES : (slot + 1) * LANES] for slot in range(slots)]
            columns.append(jnp.concatenate(held, axis=0))
        return jnp.concatenate(columns, axis=1).astype(BF16)

    products = [None] * share
    for group in range(groups):
        left, right = whole(0, group), whole(1, group)
        if pack > 1:
            lane = lax.broadcasted_iota(jnp.int32, left.shape, 1) // (near * breadth)
            left = [jnp.where(lane == place, left, jnp.zeros_like(left)) for place in range(pack)]
            left = jnp.concatenate(left, axis=0)
        product = dot(left, right, (1, 1) if outgoing else (0, 0))
        tokens = product.shape[0] // pack
        for place in range(pack):
            products[place * groups + group] = product[place * tokens : (place + 1) * tokens]

    for high in range(cols // slots):
        lanes = slice(high * LANES, (high + 1) * LANES)
        held = []
        for row in range(rows):
            for product in products:
                parts = [
                    product[(row * slots + slot) * lines : (row * slots + slot + 1) * lines, lanes]
                    for slot in range(slots)
                ]
                held.append(jnp.concatenate(parts, axis=1))
        back = dot(jnp.concatenate(held, axis=0).astype(BF16), swap).astype(BF16)
        for low in range(slots):
            for row in range(rows):
                first = row * share * lines
                combined_ref[owners[high * slots + low][row]] = back[
                    first : first + share * lines, low * LANES : (low + 1) * LANES
                ]


def hold_combined(combined_ref, stage_ref, share, sources):
    span = combined_ref.shape[1]
    lines = span // share
    order = one_hot(span, span, lambda row: row % share * lines + row // share)
    order = jnp.concatenate([order] * len(sources[0]), axis=1)
    blocks = [jnp.concatenate([combined_ref[source] for source in held], axis=0) for held in sources]
    ordered = dot(order, jnp.concatenate(blocks, axis=1))
    for owner in range(len(sources)):
        stage_ref[owner * span : (owner + 1) * span, :] = ordered[:, owner * LANES : (owner + 1) * LANES]


def read_combined(stage_ref, owners, lines, share, first, count):
    columns = []
    for line in range(first, first + count):
        if share % 8 == 0:
            held = [
                stage_ref[(owner * lines + line) * share : (owner * lines + line + 1) * share, :]
                for owner in range(owners)
            ]
            columns.append(jnp.concatenate(held, axis=0))
        else:
            columns.append(stage_ref[pl.ds(line, owners, stride=lines), :])
    return jnp.concatenate(columns, axis=1)


def middle_kernel(share, sources, next_share, chunk, ins, outs, stage_ref, message_stage_ref):
    combined_ref, x_ref, gate_ref, mask_ref, gains_ref, proj_ref, gate_weight_ref, out_ref = ins
    message_ref, gate_out, next_ref = outs
    tokens = x_ref.shape[1]
    lines = tokens // LANES
    owners = x_ref.shape[0] // share
    hold_combined(combined_ref, stage_ref, share, sources)
    mask = mask_ref[...]
    gain_out, gain = [spread_gain(gains_ref[n : n + 1, :]) for n in (0, 1)]
    out_t, proj_t, gate_t = halved(out_ref[0]), halved(proj_ref[1]), halved(gate_weight_ref[1])
    for start in range(0, tokens, chunk):
        here = slice(start, start + chunk)
        combined = read_combined(stage_ref, owners, lines, share, start // LANES, chunk // LANES)
        hidden = channel_norm(combined, gain_out)
        current = x_ref[:, here] + gate_ref[:, here] * dot(out_t, hidden)
        next_ref[:, here] = current
        normed = channel_norm(current, gain)
        emit_message(normed, proj_t, mask, start // LANES, message_ref, message_stage_ref, next_share)
        gate_out[:, here] = twice_sigmoid(dot(gate_t, normed))


def last_kernel(share, sources, chunk, ins, outs, stage_ref, result_ref, sems):
    combined_ref, x_ref, gate_ref, gains_ref, out_ref, up_ref, down_ref = ins
    (result_out,) = outs
    slots, lines, breadth, channels = result_ref.shape
    owners = x_ref.shape[0] // share
    half = down_ref.shape[0]
    count = chunk // LANES
    gain_out, gain = [spread_gain(gains_ref[n : n + 1, :]) for n in (2, 3)]
    out_t, down_t = halved(out_ref[1]), down_ref[...].T
    gate_t, up_t = halved(up_ref[:, :half]), up_ref[:, half:].T
    hold_combined(combined_ref, stage_ref, share, sources)
    combined = read_combined(stage_ref, owners, lines, share, 0, lines)
    hidden = channel_norm(combined, gain_out)
    current = x_ref[...] + gate_ref[...] * dot(out_t, hidden)
    trans_in = channel_norm(current, gain)
    gate_part, up_part = dot(gate_t, trans_in), dot(up_t, trans_in)
    trans_hidden = (gate_part * twice_sigmoid(gate_part) * up_part).astype(BF16)
    current = current + dot(down_t, trans_hidden)
    writes = []
    for first in range(0, lines, count):
        for line in range(first, first + count):
            result = current[:, line * LANES : (line + 1) * LANES].T
            for slot in range(slots):
                result_ref[slot, line] = result[slot * breadth : (slot + 1) * breadth]
        piece = slice(first, first + count)
        writes += start_all([(result_ref.at[:, piece], result_out.at[:, piece])], sems, first // count)
    for write in writes:
        write.wait()


def call(kernel, operands, outs, scratch=(), in_hbm=False, out_hbm=False):
    in_place, held = pl.BlockSpec(memory_space=pltpu.HBM), pl.BlockSpec(memory_space=pltpu.VMEM)
    count = len(operands)

    def body(*refs):
        kernel(refs[:count], refs[count : count + len(outs)], *refs[count + len(outs) :])

    return pl.pallas_call(
        body,
        in_specs=[in_place if in_hbm else held] * count,
        out_specs=[in_place if out_hbm else held] * len(outs),
        out_shape=[jax.ShapeDtypeStruct(shape, dtype) for shape, dtype in outs],
        scratch_shapes=list(scratch),
        compiler_params=pltpu.CompilerParams(vmem_limit_bytes=VMEM_BYTES),
    )(*[pltpu.with_memory_space_constraint(array, pltpu.HBM) if in_hbm else array for array in operands])


def exchange(values, axes, order=None):
    groups = [order] if order else None
    return lax.all_to_all(values, axes, split_axis=0, concat_axis=0, axis_index_groups=groups, tiled=True)


def per_device(
    rows,
    halves,
    nears,
    pair_map,
    pair_mask,
    gain_in,
    proj_weight,
    gate_weight,
    gain_out,
    out_weight,
    trans_gain,
    trans_up,
    trans_down,
):
    height, breadth, channels = pair_map.shape
    tokens = height * breadth
    lines = tokens // LANES
    hid = gain_out.shape[1]
    cols = halves * nears
    owners = rows * cols
    share = hid // owners
    chunk = min(4 * LANES, tokens)
    split = 1
    first_share = split * share
    held = ((LANES // breadth, lines, breadth, channels), F32)
    grouped = pair_map.reshape(held[0])
    wide = ((channels, tokens), F32)
    result = pltpu.VMEM((owners * share * lines, LANES), F32)
    spare = pltpu.VMEM((8, LANES) if share % 8 == 0 else (owners * 2 * share * lines, LANES), F32)

    def message(own):
        return ((hid // own, 2 * own * lines, LANES), BF16)

    blocks = list(range(cols))
    blocks.insert(0, blocks.pop((cols - 1) // 2))
    order = [col * rows + row for col in blocks for row in range(rows)]
    everyone = [[order.index(col * rows + row) for row in range(rows)] for col in range(cols)]
    beside = [[near * rows + row for row in range(rows)] for near in range(nears)] if split > 1 else everyone
    single = [[n] for n in range(owners)]
    paired = single if split == 1 else [
        [everyone[half * nears + near][row] for half in range(halves)] for near in range(nears) for row in range(rows)
    ]

    def combine(both, own, sources, outgoing):
        kernel = functools.partial(combine_kernel, sources, everyone, breadth, own, outgoing)
        answer = ((owners, own * lines, LANES), BF16)
        return exchange(call(kernel, (both,), [answer])[0], ALL_AXES, order)

    operands = (grouped, pair_mask, proj_weight, gate_weight, gain_in, gain_out, trans_gain.reshape(1, -1))
    both, gate, current, mask, gains = call(
        functools.partial(project_kernel, first_share),
        operands,
        [message(first_share), wide, wide, ((lines, LANES), F32), ((8, channels), F32)],
        (
            spare,
            *[
                pltpu.VMEM(array.shape[1:] if array.ndim == 3 else array.shape, array.dtype)
                for array in operands
            ],
            pltpu.SemaphoreType.DMA((len(operands),)),
        ),
        in_hbm=True,
    )
    both = exchange(both, NEAR_AXES) if split > 1 else exchange(both, ALL_AXES, order)
    combined = combine(both, first_share, beside, True)
    both, gate, current = call(
        functools.partial(middle_kernel, first_share, paired, share, tokens),
        (combined, current, gate, mask, gains, proj_weight, gate_weight, out_weight),
        [message(share), wide, wide],
        (result, spare),
    )
    combined = combine(exchange(both, ALL_AXES, order), share, everyone, False)
    (pair_out,) = call(
        functools.partial(last_kernel, share, single, chunk),
        (combined, current, gate, gains, out_weight, trans_up, trans_down),
        [held],
        (result, pltpu.VMEM(*held), pltpu.SemaphoreType.DMA((tokens // chunk,))),
        out_hbm=True,
    )
    return pair_out.reshape(pair_map.shape)


def solution(mesh):
    groups, rows, cols = (mesh.shape[name] for name in ("grp", "row", "col"))
    halves = 2 if cols % 2 == 0 else 1
    nears = cols // halves
    folded = Mesh(mesh.devices.reshape(groups, rows, halves, nears), ("grp", "row", "half", "near"))
    tokens = (("grp", "row"), ("half", "near"))
    in_specs = (P(*tokens, None), P(*tokens)) + (P(),) * 8

    def body(*args):
        return per_device(rows, halves, nears, *args)

    return jax.shard_map(body, mesh=folded, in_specs=in_specs, out_specs=P(*tokens, None), check_vma=False)
```

```python
import functools

import jax
import jax.numpy as jnp
from jax import lax
from jax.experimental import pallas as pl
from jax.experimental.pallas import tpu as pltpu
from jax.sharding import Mesh
from jax.sharding import PartitionSpec as P

NEAR_AXES = ("near", "row")
ALL_AXES = ("half", "near", "row")
LANES = 128
VMEM_BYTES = 24 * 1024 * 1024
F32, BF16 = jnp.float32, jnp.bfloat16


def dot(left, right, contract=(1, 0)):
    return lax.dot_general(
        left, right, (((contract[0],), (contract[1],)), ((), ())), preferred_element_type=F32
    )


def halved(weight):
    return weight.T * 0.5


def twice_sigmoid(half):
    return jnp.tanh(half) + 1.0


def channel_norm(values, gain):
    wide = jnp.concatenate([gain] * (values.shape[1] // LANES), axis=1)
    centred = values - jnp.mean(values, axis=0, keepdims=True)
    spread = jnp.mean(centred * centred, axis=0, keepdims=True)
    return (centred * lax.rsqrt(spread + 1e-05) * wide).astype(BF16)


def spread_gain(row):
    return jnp.broadcast_to(row, (LANES, row.shape[1])).T


def token_mask(mask, lines):
    height, breadth = mask.shape
    wide = jnp.concatenate([mask.astype(F32)] * (LANES // breadth), axis=1)
    row = lax.broadcasted_iota(jnp.int32, wide.shape, 0)
    lane = lax.broadcasted_iota(jnp.int32, wide.shape, 1)
    wide = jnp.where(row // lines == lane // breadth, wide, 0.0).astype(BF16)
    line = lax.broadcasted_iota(jnp.int32, (lines, height), 0)
    source = lax.broadcasted_iota(jnp.int32, (lines, height), 1)
    return dot((source % lines == line).astype(BF16), wide)


def emit_message(normed, weight_t, mask, message_ref, stage_ref, share):
    projected = dot(weight_t, normed)
    hid = weight_t.shape[0] // 4
    owners, lines = hid // share, mask.shape[0]
    for line in range(lines):
        here = projected[:, line * LANES : (line + 1) * LANES]
        keep = mask[line : line + 1]
        left = twice_sigmoid(here[:hid]) * here[hid : 2 * hid] * keep
        right = twice_sigmoid(here[2 * hid : 3 * hid]) * here[3 * hid :] * keep
        if share % 8 == 0:
            for owner in range(owners):
                rows = slice(owner * share, (owner + 1) * share)
                both = jnp.concatenate([left[rows], right[rows]], axis=0).astype(BF16)
                message_ref[owner, 2 * share * line : 2 * share * (line + 1), :] = both
        else:
            stage_ref[pl.ds(2 * line, owners, stride=2 * lines), :] = left
            stage_ref[pl.ds(2 * line + 1, owners, stride=2 * lines), :] = right
    if share % 8:
        message_ref[...] = stage_ref[...].astype(BF16).reshape(message_ref.shape)


def start_all(pairs, sems, first=0):
    copies = [pltpu.make_async_copy(src, dst, sems.at[first + n]) for n, (src, dst) in enumerate(pairs)]
    for copy in copies:
        copy.start()
    return copies


def line_tokens(x_ref, line):
    return jnp.concatenate([x_ref[slot, line] for slot in range(x_ref.shape[0])], axis=0)


def project_kernel(share, ins, outs, stage_ref, x_ref, mask_ref, weight_ref, gate_ref, gain_in_ref, gain_out_ref, trans_gain_ref, sems):
    message_ref, gate_out, turned_out, mask_out, gains_out = outs
    x_in, mask_in, weight_in, gate_in, gain_in, gain_out, trans_gain = ins
    lines = x_ref.shape[1]
    pairs = [
        (x_in, x_ref),
        (weight_in.at[0], weight_ref),
        (gain_in, gain_in_ref),
        (mask_in, mask_ref),
        (gate_in.at[0], gate_ref),
        (gain_out, gain_out_ref),
        (trans_gain, trans_gain_ref),
    ]
    for copy in start_all(pairs, sems):
        copy.wait()
    mask = token_mask(mask_ref[...], lines)
    current = jnp.concatenate([line_tokens(x_ref, line).T for line in range(lines)], axis=1)
    normed = channel_norm(current, spread_gain(gain_in_ref[0:1, :]))
    emit_message(normed, halved(weight_ref[...]), mask, message_ref, stage_ref, share)
    gate_out[...] = twice_sigmoid(dot(halved(gate_ref[...]), normed))
    turned_out[...] = current
    mask_out[...] = mask
    rows = [gain_out_ref[0:1, :], gain_in_ref[1:2, :], gain_out_ref[1:2, :], trans_gain_ref[...]]
    gains_out[...] = jnp.concatenate(rows + rows, axis=0)


def one_hot(rows, columns, wanted):
    row = lax.broadcasted_iota(jnp.int32, (rows, columns), 0)
    column = lax.broadcasted_iota(jnp.int32, (rows, columns), 1)
    return (wanted(row) == column).astype(BF16)


def swap_matrix(slots, breadth):
    size = slots * LANES
    return one_hot(
        size, size, lambda lane: lane // breadth % slots * LANES + lane // LANES * breadth + lane % breadth
    )


def combine_kernel(sources, owners, breadth, share, outgoing, ins, outs):
    near, cols, rows = len(sources), len(owners), len(owners[0])
    (both_ref,), (combined_ref,) = ins, outs
    slots = LANES // breadth
    span = both_ref.shape[1]
    lines = span // (2 * share)
    pack = max(1, slots // near)
    groups = share // pack
    size = span // pack
    swap = swap_matrix(slots, breadth)

    def source(row):
        channel = row // size * groups + row // lines % groups
        return row % lines * (2 * share) + row // (groups * lines) % 2 * share + channel

    order = one_hot(span, span, source)
    blocks = [both_ref[sources[col][row]] for row in range(rows) for col in range(near)]
    ordered = dot(order, jnp.concatenate(blocks, axis=1)).astype(BF16)
    wide = []
    for row in range(rows):
        here = ordered[:, row * near * LANES : (row + 1) * near * LANES]
        wide.append(jnp.concatenate([here[n * size : (n + 1) * size] for n in range(pack)], axis=1))
    wide = jnp.concatenate(wide, axis=0)
    block = slots * LANES
    swapped = [dot(wide[:, first : first + block], swap) for first in range(0, wide.shape[1], block)]

    def whole(side, group):
        columns = []
        for part in swapped:
            held = []
            for row in range(rows):
                first = row * size + (side * groups + group) * lines
                held += [part[first : first + lines, slot * LANES : (slot + 1) * LANES] for slot in range(slots)]
            columns.append(jnp.concatenate(held, axis=0))
        return jnp.concatenate(columns, axis=1).astype(BF16)

    products = [None] * share
    for group in range(groups):
        left, right = whole(0, group), whole(1, group)
        if pack > 1:
            lane = lax.broadcasted_iota(jnp.int32, left.shape, 1) // (near * breadth)
            left = [jnp.where(lane == place, left, jnp.zeros_like(left)) for place in range(pack)]
            left = jnp.concatenate(left, axis=0)
        product = dot(left, right, (1, 1) if outgoing else (0, 0))
        tokens = product.shape[0] // pack
        for place in range(pack):
            products[place * groups + group] = product[place * tokens : (place + 1) * tokens]

    for high in range(cols // slots):
        lanes = slice(high * LANES, (high + 1) * LANES)
        held = []
        for row in range(rows):
            for product in products:
                parts = [
                    product[(row * slots + slot) * lines : (row * slots + slot + 1) * lines, lanes]
                    for slot in range(slots)
                ]
                held.append(jnp.concatenate(parts, axis=1))
        back = dot(jnp.concatenate(held, axis=0).astype(BF16), swap).astype(BF16)
        for low in range(slots):
            for row in range(rows):
                first = row * share * lines
                combined_ref[owners[high * slots + low][row]] = back[
                    first : first + share * lines, low * LANES : (low + 1) * LANES
                ]


def read_combined(combined_ref, stage_ref, share, sources):
    span = combined_ref.shape[1]
    lines, owners = span // share, len(sources)
    order = one_hot(span, span, lambda row: row % share * lines + row // share)
    order = jnp.concatenate([order] * len(sources[0]), axis=1)
    blocks = [jnp.concatenate([combined_ref[source] for source in held], axis=0) for held in sources]
    ordered = dot(order, jnp.concatenate(blocks, axis=1))
    parts = [ordered[:, owner * LANES : (owner + 1) * LANES] for owner in range(owners)]
    if share % 8 == 0:
        columns = [
            jnp.concatenate([part[line * share : (line + 1) * share] for part in parts], axis=0)
            for line in range(lines)
        ]
    else:
        for owner, part in enumerate(parts):
            stage_ref[owner * span : (owner + 1) * span, :] = part
        columns = [stage_ref[pl.ds(line, owners, stride=lines), :] for line in range(lines)]
    return jnp.concatenate(columns, axis=1)


def middle_kernel(share, sources, next_share, ins, outs, stage_ref, message_stage_ref):
    combined_ref, x_ref, gate_ref, mask_ref, gains_ref, proj_ref, gate_weight_ref, out_ref = ins
    message_ref, gate_out, next_ref = outs
    gain_out, gain = [spread_gain(gains_ref[n : n + 1, :]) for n in (0, 1)]
    out_t, proj_t, gate_t = halved(out_ref[0]), halved(proj_ref[1]), halved(gate_weight_ref[1])
    hidden = channel_norm(read_combined(combined_ref, stage_ref, share, sources), gain_out)
    current = x_ref[...] + gate_ref[...] * dot(out_t, hidden)
    next_ref[...] = current
    normed = channel_norm(current, gain)
    emit_message(normed, proj_t, mask_ref[...], message_ref, message_stage_ref, next_share)
    gate_out[...] = twice_sigmoid(dot(gate_t, normed))


def last_kernel(share, sources, chunk, ins, outs, stage_ref, result_ref, sems):
    combined_ref, x_ref, gate_ref, gains_ref, out_ref, up_ref, down_ref = ins
    (result_out,) = outs
    slots, lines, breadth, channels = result_ref.shape
    half = down_ref.shape[0]
    count = chunk // LANES
    gain_out, gain = [spread_gain(gains_ref[n : n + 1, :]) for n in (2, 3)]
    out_t, down_t = halved(out_ref[1]), down_ref[...].T
    gate_t, up_t = halved(up_ref[:, :half]), up_ref[:, half:].T
    hidden = channel_norm(read_combined(combined_ref, stage_ref, share, sources), gain_out)
    current = x_ref[...] + gate_ref[...] * dot(out_t, hidden)
    trans_in = channel_norm(current, gain)
    gate_part, up_part = dot(gate_t, trans_in), dot(up_t, trans_in)
    trans_hidden = (gate_part * twice_sigmoid(gate_part) * up_part).astype(BF16)
    current = current + dot(down_t, trans_hidden)
    writes = []
    for first in range(0, lines, count):
        for line in range(first, first + count):
            result = current[:, line * LANES : (line + 1) * LANES].T
            for slot in range(slots):
                result_ref[slot, line] = result[slot * breadth : (slot + 1) * breadth]
        piece = slice(first, first + count)
        writes += start_all([(result_ref.at[:, piece], result_out.at[:, piece])], sems, first // count)
    for write in writes:
        write.wait()


def call(kernel, operands, outs, scratch=(), in_hbm=False, out_hbm=False):
    in_place, held = pl.BlockSpec(memory_space=pltpu.HBM), pl.BlockSpec(memory_space=pltpu.VMEM)
    count = len(operands)

    def body(*refs):
        kernel(refs[:count], refs[count : count + len(outs)], *refs[count + len(outs) :])

    return pl.pallas_call(
        body,
        in_specs=[in_place if in_hbm else held] * count,
        out_specs=[in_place if out_hbm else held] * len(outs),
        out_shape=[jax.ShapeDtypeStruct(shape, dtype) for shape, dtype in outs],
        scratch_shapes=list(scratch),
        compiler_params=pltpu.CompilerParams(vmem_limit_bytes=VMEM_BYTES),
    )(*[pltpu.with_memory_space_constraint(array, pltpu.HBM) if in_hbm else array for array in operands])


def exchange(values, axes, order=None):
    groups = [order] if order else None
    return lax.all_to_all(values, axes, split_axis=0, concat_axis=0, axis_index_groups=groups, tiled=True)


def per_device(
    rows,
    halves,
    nears,
    pair_map,
    pair_mask,
    gain_in,
    proj_weight,
    gate_weight,
    gain_out,
    out_weight,
    trans_gain,
    trans_up,
    trans_down,
):
    height, breadth, channels = pair_map.shape
    tokens = height * breadth
    lines = tokens // LANES
    hid = gain_out.shape[1]
    cols = halves * nears
    owners = rows * cols
    share = hid // owners
    chunk = min(4 * LANES, tokens)
    split = halves if share % 8 == 0 else 1
    first_share = split * share
    held = ((LANES // breadth, lines, breadth, channels), F32)
    grouped = pair_map.reshape(held[0])
    wide = ((channels, tokens), F32)
    result = pltpu.VMEM((owners * share * lines, LANES), F32)
    spare = pltpu.VMEM((8, LANES) if share % 8 == 0 else (owners * 2 * share * lines, LANES), F32)

    def message(own):
        return ((hid // own, 2 * own * lines, LANES), BF16)

    blocks = list(range(cols))
    blocks.insert(0, blocks.pop((cols - 1) // 2))
    order = [col * rows + row for col in blocks for row in range(rows)]
    everyone = [[order.index(col * rows + row) for row in range(rows)] for col in range(cols)]
    beside = [[near * rows + row for row in range(rows)] for near in range(nears)] if split > 1 else everyone
    single = [[n] for n in range(owners)]
    paired = single if split == 1 else [
        [everyone[half * nears + near][row] for half in range(halves)] for near in range(nears) for row in range(rows)
    ]

    def combine(both, own, sources, outgoing):
        kernel = functools.partial(combine_kernel, sources, everyone, breadth, own, outgoing)
        answer = ((owners, own * lines, LANES), BF16)
        return exchange(call(kernel, (both,), [answer])[0], ALL_AXES, order)

    operands = (grouped, pair_mask, proj_weight, gate_weight, gain_in, gain_out, trans_gain.reshape(1, -1))
    both, gate, current, mask, gains = call(
        functools.partial(project_kernel, first_share),
        operands,
        [message(first_share), wide, wide, ((lines, LANES), F32), ((8, channels), F32)],
        (
            spare,
            *[
                pltpu.VMEM(array.shape[1:] if array.ndim == 3 else array.shape, array.dtype)
                for array in operands
            ],
            pltpu.SemaphoreType.DMA((len(operands),)),
        ),
        in_hbm=True,
    )
    both = exchange(both, NEAR_AXES) if split > 1 else exchange(both, ALL_AXES, order)
    combined = combine(both, first_share, beside, True)
    both, gate, current = call(
        functools.partial(middle_kernel, first_share, paired, share),
        (combined, current, gate, mask, gains, proj_weight, gate_weight, out_weight),
        [message(share), wide, wide],
        (result, spare),
    )
    combined = combine(exchange(both, ALL_AXES, order), share, everyone, False)
    (pair_out,) = call(
        functools.partial(last_kernel, share, single, chunk),
        (combined, current, gate, gains, out_weight, trans_up, trans_down),
        [held],
        (result, pltpu.VMEM(*held), pltpu.SemaphoreType.DMA((tokens // chunk,))),
        out_hbm=True,
    )
    return pair_out.reshape(pair_map.shape)


def solution(mesh):
    groups, rows, cols = (mesh.shape[name] for name in ("grp", "row", "col"))
    halves = 2 if cols % 2 == 0 else 1
    nears = cols // halves
    folded = Mesh(mesh.devices.reshape(groups, rows, halves, nears), ("grp", "row", "half", "near"))
    tokens = (("grp", "row"), ("half", "near"))
    in_specs = (P(*tokens, None), P(*tokens)) + (P(),) * 8

    def body(*args):
        return per_device(rows, halves, nears, *args)

    return jax.shard_map(body, mesh=folded, in_specs=in_specs, out_specs=P(*tokens, None), check_vma=False)
```

```python
import functools

import jax
import jax.numpy as jnp
from jax import lax
from jax.experimental import pallas as pl
from jax.experimental.pallas import tpu as pltpu
from jax.sharding import Mesh
from jax.sharding import PartitionSpec as P

NEAR_AXES = ("near", "row")
ALL_AXES = ("half", "near", "row")
LANES = 128
VMEM_BYTES = 24 * 1024 * 1024
F32, BF16 = jnp.float32, jnp.bfloat16


def dot(left, right, contract=(1, 0)):
    return lax.dot_general(
        left, right, (((contract[0],), (contract[1],)), ((), ())), preferred_element_type=F32
    )


def halved(weight):
    return weight.T * 0.5


def twice_sigmoid(half):
    return jnp.tanh(half) + 1.0


def channel_norm(values, gain):
    wide = jnp.concatenate([gain] * (values.shape[1] // LANES), axis=1)
    centred = values - jnp.mean(values, axis=0, keepdims=True)
    spread = jnp.mean(centred * centred, axis=0, keepdims=True)
    return (centred * lax.rsqrt(spread + 1e-05) * wide).astype(BF16)


def spread_gain(row):
    return jnp.broadcast_to(row, (LANES, row.shape[1])).T


def token_mask(mask, lines):
    height, breadth = mask.shape
    wide = jnp.concatenate([mask.astype(F32)] * (LANES // breadth), axis=1)
    row = lax.broadcasted_iota(jnp.int32, wide.shape, 0)
    lane = lax.broadcasted_iota(jnp.int32, wide.shape, 1)
    wide = jnp.where(row // lines == lane // breadth, wide, 0.0).astype(BF16)
    line = lax.broadcasted_iota(jnp.int32, (lines, height), 0)
    source = lax.broadcasted_iota(jnp.int32, (lines, height), 1)
    return dot((source % lines == line).astype(BF16), wide)


def emit_message(normed, weight_t, mask, message_ref, stage_ref, share):
    projected = dot(weight_t, normed)
    hid = weight_t.shape[0] // 4
    owners, lines = hid // share, mask.shape[0]
    for line in range(lines):
        here = projected[:, line * LANES : (line + 1) * LANES]
        keep = mask[line : line + 1]
        left = twice_sigmoid(here[:hid]) * here[hid : 2 * hid] * keep
        right = twice_sigmoid(here[2 * hid : 3 * hid]) * here[3 * hid :] * keep
        if share % 8 == 0:
            for owner in range(owners):
                rows = slice(owner * share, (owner + 1) * share)
                both = jnp.concatenate([left[rows], right[rows]], axis=0).astype(BF16)
                message_ref[owner, 2 * share * line : 2 * share * (line + 1), :] = both
        else:
            stage_ref[pl.ds(2 * line, owners, stride=2 * lines), :] = left
            stage_ref[pl.ds(2 * line + 1, owners, stride=2 * lines), :] = right
    if share % 8:
        message_ref[...] = stage_ref[...].astype(BF16).reshape(message_ref.shape)


def start_all(pairs, sems, first=0):
    copies = [pltpu.make_async_copy(src, dst, sems.at[first + n]) for n, (src, dst) in enumerate(pairs)]
    for copy in copies:
        copy.start()
    return copies


def line_tokens(x_ref, line):
    return jnp.concatenate([x_ref[slot, line] for slot in range(x_ref.shape[0])], axis=0)


def project_kernel(share, ins, outs, stage_ref, x_ref, mask_ref, weight_ref, gate_ref, gain_in_ref, gain_out_ref, trans_gain_ref, sems):
    message_ref, gate_out, turned_out, mask_out, gains_out = outs
    x_in, mask_in, weight_in, gate_in, gain_in, gain_out, trans_gain = ins
    lines = x_ref.shape[1]
    pairs = [
        (x_in, x_ref),
        (weight_in.at[0], weight_ref),
        (gain_in, gain_in_ref),
        (mask_in, mask_ref),
        (gate_in.at[0], gate_ref),
        (gain_out, gain_out_ref),
        (trans_gain, trans_gain_ref),
    ]
    for copy in start_all(pairs, sems):
        copy.wait()
    mask = token_mask(mask_ref[...], lines)
    current = jnp.concatenate([line_tokens(x_ref, line).T for line in range(lines)], axis=1)
    normed = channel_norm(current, spread_gain(gain_in_ref[0:1, :]))
    emit_message(normed, halved(weight_ref[...]), mask, message_ref, stage_ref, share)
    gate_out[...] = twice_sigmoid(dot(halved(gate_ref[...]), normed))
    turned_out[...] = current
    mask_out[...] = mask
    rows = [gain_out_ref[0:1, :], gain_in_ref[1:2, :], gain_out_ref[1:2, :], trans_gain_ref[...]]
    gains_out[...] = jnp.concatenate(rows + rows, axis=0)


def one_hot(rows, columns, wanted):
    row = lax.broadcasted_iota(jnp.int32, (rows, columns), 0)
    column = lax.broadcasted_iota(jnp.int32, (rows, columns), 1)
    return (wanted(row) == column).astype(BF16)


def swap_matrix(slots, breadth):
    size = slots * LANES
    return one_hot(
        size, size, lambda lane: lane // breadth % slots * LANES + lane // LANES * breadth + lane % breadth
    )


def combine_kernel(sources, owners, breadth, share, outgoing, ins, outs):
    near, cols, rows = len(sources), len(owners), len(owners[0])
    (both_ref,), (combined_ref,) = ins, outs
    slots = LANES // breadth
    span = both_ref.shape[1]
    lines = span // (2 * share)
    pack = max(1, slots // near)
    groups = share // pack
    size = span // pack
    swap = swap_matrix(slots, breadth)

    def source(row):
        channel = row // size * groups + row // lines % groups
        return row % lines * (2 * share) + row // (groups * lines) % 2 * share + channel

    order = one_hot(span, span, source)
    blocks = [both_ref[sources[col][row]] for row in range(rows) for col in range(near)]
    ordered = dot(order, jnp.concatenate(blocks, axis=1)).astype(BF16)
    wide = []
    for row in range(rows):
        here = ordered[:, row * near * LANES : (row + 1) * near * LANES]
        wide.append(jnp.concatenate([here[n * size : (n + 1) * size] for n in range(pack)], axis=1))
    wide = jnp.concatenate(wide, axis=0)
    block = slots * LANES
    swapped = [dot(wide[:, first : first + block], swap) for first in range(0, wide.shape[1], block)]

    def whole(side, group, turned=False):
        columns = []
        for part in swapped:
            held = []
            for row in range(rows):
                first = row * size + (side * groups + group) * lines
                held += [part[first : first + lines, slot * LANES : (slot + 1) * LANES] for slot in range(slots)]
            columns.append(jnp.concatenate(held, axis=0))
        if turned:
            return jnp.concatenate([column.T for column in columns], axis=0).astype(BF16)
        return jnp.concatenate(columns, axis=1).astype(BF16)

    products = [None] * share
    for group in range(groups):
        left, right = whole(0, group, not outgoing), whole(1, group)
        if pack > 1:
            lane = lax.broadcasted_iota(jnp.int32, left.shape, 1) // (near * breadth)
            left = [jnp.where(lane == place, left, jnp.zeros_like(left)) for place in range(pack)]
            left = jnp.concatenate(left, axis=0)
        product = dot(left, right, (1, 1) if outgoing else (1, 0))
        tokens = product.shape[0] // pack
        for place in range(pack):
            products[place * groups + group] = product[place * tokens : (place + 1) * tokens]

    for high in range(cols // slots):
        lanes = slice(high * LANES, (high + 1) * LANES)
        held = []
        for row in range(rows):
            for product in products:
                parts = [
                    product[(row * slots + slot) * lines : (row * slots + slot + 1) * lines, lanes]
                    for slot in range(slots)
                ]
                held.append(jnp.concatenate(parts, axis=1))
        back = dot(jnp.concatenate(held, axis=0).astype(BF16), swap).astype(BF16)
        for low in range(slots):
            for row in range(rows):
                first = row * share * lines
                combined_ref[owners[high * slots + low][row]] = back[
                    first : first + share * lines, low * LANES : (low + 1) * LANES
                ]


def read_combined(combined_ref, stage_ref, share, sources):
    span = combined_ref.shape[1]
    lines, owners = span // share, len(sources)
    order = one_hot(span, span, lambda row: row % share * lines + row // share)
    order = jnp.concatenate([order] * len(sources[0]), axis=1)
    blocks = [jnp.concatenate([combined_ref[source] for source in held], axis=0) for held in sources]
    ordered = dot(order, jnp.concatenate(blocks, axis=1))
    parts = [ordered[:, owner * LANES : (owner + 1) * LANES] for owner in range(owners)]
    if share % 8 == 0:
        columns = [
            jnp.concatenate([part[line * share : (line + 1) * share] for part in parts], axis=0)
            for line in range(lines)
        ]
    else:
        for owner, part in enumerate(parts):
            stage_ref[owner * span : (owner + 1) * span, :] = part
        columns = [stage_ref[pl.ds(line, owners, stride=lines), :] for line in range(lines)]
    return jnp.concatenate(columns, axis=1)


def middle_kernel(share, sources, next_share, ins, outs, stage_ref, message_stage_ref):
    combined_ref, x_ref, gate_ref, mask_ref, gains_ref, proj_ref, gate_weight_ref, out_ref = ins
    message_ref, gate_out, next_ref = outs
    gain_out, gain = [spread_gain(gains_ref[n : n + 1, :]) for n in (0, 1)]
    out_t, proj_t, gate_t = halved(out_ref[0]), halved(proj_ref[1]), halved(gate_weight_ref[1])
    hidden = channel_norm(read_combined(combined_ref, stage_ref, share, sources), gain_out)
    current = x_ref[...] + gate_ref[...] * dot(out_t, hidden)
    next_ref[...] = current
    normed = channel_norm(current, gain)
    emit_message(normed, proj_t, mask_ref[...], message_ref, message_stage_ref, next_share)
    gate_out[...] = twice_sigmoid(dot(gate_t, normed))


def last_kernel(share, sources, chunk, ins, outs, stage_ref, result_ref, sems):
    combined_ref, x_ref, gate_ref, gains_ref, out_ref, up_ref, down_ref = ins
    (result_out,) = outs
    slots, lines, breadth, channels = result_ref.shape
    half = down_ref.shape[0]
    count = chunk // LANES
    gain_out, gain = [spread_gain(gains_ref[n : n + 1, :]) for n in (2, 3)]
    out_t, down_t = halved(out_ref[1]), down_ref[...].T
    gate_t, up_t = halved(up_ref[:, :half]), up_ref[:, half:].T
    hidden = channel_norm(read_combined(combined_ref, stage_ref, share, sources), gain_out)
    current = x_ref[...] + gate_ref[...] * dot(out_t, hidden)
    trans_in = channel_norm(current, gain)
    gate_part, up_part = dot(gate_t, trans_in), dot(up_t, trans_in)
    trans_hidden = (gate_part * twice_sigmoid(gate_part) * up_part).astype(BF16)
    current = current + dot(down_t, trans_hidden)
    writes = []
    for first in range(0, lines, count):
        for line in range(first, first + count):
            result = current[:, line * LANES : (line + 1) * LANES].T
            for slot in range(slots):
                result_ref[slot, line] = result[slot * breadth : (slot + 1) * breadth]
        piece = slice(first, first + count)
        writes += start_all([(result_ref.at[:, piece], result_out.at[:, piece])], sems, first // count)
    for write in writes:
        write.wait()


def call(kernel, operands, outs, scratch=(), in_hbm=False, out_hbm=False):
    in_place, held = pl.BlockSpec(memory_space=pltpu.HBM), pl.BlockSpec(memory_space=pltpu.VMEM)
    count = len(operands)

    def body(*refs):
        kernel(refs[:count], refs[count : count + len(outs)], *refs[count + len(outs) :])

    return pl.pallas_call(
        body,
        in_specs=[in_place if in_hbm else held] * count,
        out_specs=[in_place if out_hbm else held] * len(outs),
        out_shape=[jax.ShapeDtypeStruct(shape, dtype) for shape, dtype in outs],
        scratch_shapes=list(scratch),
        compiler_params=pltpu.CompilerParams(vmem_limit_bytes=VMEM_BYTES),
    )(*[pltpu.with_memory_space_constraint(array, pltpu.HBM) if in_hbm else array for array in operands])


def exchange(values, axes, order=None):
    groups = [order] if order else None
    return lax.all_to_all(values, axes, split_axis=0, concat_axis=0, axis_index_groups=groups, tiled=True)


def per_device(
    rows,
    halves,
    nears,
    pair_map,
    pair_mask,
    gain_in,
    proj_weight,
    gate_weight,
    gain_out,
    out_weight,
    trans_gain,
    trans_up,
    trans_down,
):
    height, breadth, channels = pair_map.shape
    tokens = height * breadth
    lines = tokens // LANES
    hid = gain_out.shape[1]
    cols = halves * nears
    owners = rows * cols
    share = hid // owners
    chunk = min(4 * LANES, tokens)
    split = halves if share % 8 == 0 else 1
    first_share = split * share
    held = ((LANES // breadth, lines, breadth, channels), F32)
    grouped = pair_map.reshape(held[0])
    wide = ((channels, tokens), F32)
    result = pltpu.VMEM((owners * share * lines, LANES), F32)
    spare = pltpu.VMEM((8, LANES) if share % 8 == 0 else (owners * 2 * share * lines, LANES), F32)

    def message(own):
        return ((hid // own, 2 * own * lines, LANES), BF16)

    blocks = list(range(cols))
    blocks.insert(0, blocks.pop((cols - 1) // 2))
    order = [col * rows + row for col in blocks for row in range(rows)]
    everyone = [[order.index(col * rows + row) for row in range(rows)] for col in range(cols)]
    beside = [[near * rows + row for row in range(rows)] for near in range(nears)] if split > 1 else everyone
    single = [[n] for n in range(owners)]
    paired = single if split == 1 else [
        [everyone[half * nears + near][row] for half in range(halves)] for near in range(nears) for row in range(rows)
    ]

    def combine(both, own, sources, outgoing):
        kernel = functools.partial(combine_kernel, sources, everyone, breadth, own, outgoing)
        answer = ((owners, own * lines, LANES), BF16)
        return exchange(call(kernel, (both,), [answer])[0], ALL_AXES, order)

    operands = (grouped, pair_mask, proj_weight, gate_weight, gain_in, gain_out, trans_gain.reshape(1, -1))
    both, gate, current, mask, gains = call(
        functools.partial(project_kernel, first_share),
        operands,
        [message(first_share), wide, wide, ((lines, LANES), F32), ((8, channels), F32)],
        (
            spare,
            *[
                pltpu.VMEM(array.shape[1:] if array.ndim == 3 else array.shape, array.dtype)
                for array in operands
            ],
            pltpu.SemaphoreType.DMA((len(operands),)),
        ),
        in_hbm=True,
    )
    both = exchange(both, NEAR_AXES) if split > 1 else exchange(both, ALL_AXES, order)
    combined = combine(both, first_share, beside, True)
    both, gate, current = call(
        functools.partial(middle_kernel, first_share, paired, share),
        (combined, current, gate, mask, gains, proj_weight, gate_weight, out_weight),
        [message(share), wide, wide],
        (result, spare),
    )
    combined = combine(exchange(both, ALL_AXES, order), share, everyone, False)
    (pair_out,) = call(
        functools.partial(last_kernel, share, single, chunk),
        (combined, current, gate, gains, out_weight, trans_up, trans_down),
        [held],
        (result, pltpu.VMEM(*held), pltpu.SemaphoreType.DMA((tokens // chunk,))),
        out_hbm=True,
    )
    return pair_out.reshape(pair_map.shape)


def solution(mesh):
    groups, rows, cols = (mesh.shape[name] for name in ("grp", "row", "col"))
    halves = 2 if cols % 2 == 0 else 1
    nears = cols // halves
    folded = Mesh(mesh.devices.reshape(groups, rows, halves, nears), ("grp", "row", "half", "near"))
    tokens = (("grp", "row"), ("half", "near"))
    in_specs = (P(*tokens, None), P(*tokens)) + (P(),) * 8

    def body(*args):
        return per_device(rows, halves, nears, *args)

    return jax.shard_map(body, mesh=folded, in_specs=in_specs, out_specs=P(*tokens, None), check_vma=False)
```

```python
import functools

import jax
import jax.numpy as jnp
from jax import lax
from jax.experimental import pallas as pl
from jax.experimental.pallas import tpu as pltpu
from jax.sharding import Mesh
from jax.sharding import PartitionSpec as P

NEAR_AXES = ("near", "row")
ALL_AXES = ("half", "near", "row")
LANES = 128
VMEM_BYTES = 24 * 1024 * 1024
F32, BF16 = jnp.float32, jnp.bfloat16


def dot(left, right, contract=(1, 0)):
    return lax.dot_general(
        left, right, (((contract[0],), (contract[1],)), ((), ())), preferred_element_type=F32
    )


def halved(weight):
    return weight.T * 0.5


def twice_sigmoid(half):
    return jnp.tanh(half) + 1.0


def channel_norm(values, gain):
    wide = jnp.concatenate([gain] * (values.shape[1] // LANES), axis=1)
    centred = values - jnp.mean(values, axis=0, keepdims=True)
    spread = jnp.mean(centred * centred, axis=0, keepdims=True)
    return (centred * lax.rsqrt(spread + 1e-05) * wide).astype(BF16)


def spread_gain(row):
    return jnp.broadcast_to(row, (LANES, row.shape[1])).T


def token_mask(mask, lines):
    height, breadth = mask.shape
    wide = jnp.concatenate([mask.astype(F32)] * (LANES // breadth), axis=1)
    row = lax.broadcasted_iota(jnp.int32, wide.shape, 0)
    lane = lax.broadcasted_iota(jnp.int32, wide.shape, 1)
    wide = jnp.where(row // lines == lane // breadth, wide, 0.0).astype(BF16)
    line = lax.broadcasted_iota(jnp.int32, (lines, height), 0)
    source = lax.broadcasted_iota(jnp.int32, (lines, height), 1)
    return dot((source % lines == line).astype(BF16), wide)


def emit_message(normed, weight_t, mask, message_ref, stage_ref, share):
    projected = dot(weight_t, normed)
    hid = weight_t.shape[0] // 4
    owners, lines = hid // share, mask.shape[0]
    for line in range(lines):
        here = projected[:, line * LANES : (line + 1) * LANES]
        keep = mask[line : line + 1]
        left = twice_sigmoid(here[:hid]) * here[hid : 2 * hid] * keep
        right = twice_sigmoid(here[2 * hid : 3 * hid]) * here[3 * hid :] * keep
        if share % 8 == 0:
            for owner in range(owners):
                rows = slice(owner * share, (owner + 1) * share)
                both = jnp.concatenate([left[rows], right[rows]], axis=0).astype(BF16)
                message_ref[owner, 2 * share * line : 2 * share * (line + 1), :] = both
        else:
            stage_ref[pl.ds(2 * line, owners, stride=2 * lines), :] = left
            stage_ref[pl.ds(2 * line + 1, owners, stride=2 * lines), :] = right
    if share % 8:
        message_ref[...] = stage_ref[...].astype(BF16).reshape(message_ref.shape)


def start_all(pairs, sems, first=0):
    copies = [pltpu.make_async_copy(src, dst, sems.at[first + n]) for n, (src, dst) in enumerate(pairs)]
    for copy in copies:
        copy.start()
    return copies


def line_tokens(x_ref, line):
    return jnp.concatenate([x_ref[slot, line] for slot in range(x_ref.shape[0])], axis=0)


def project_kernel(share, ins, outs, stage_ref, x_ref, mask_ref, weight_ref, gate_ref, gain_in_ref, gain_out_ref, trans_gain_ref, sems):
    message_ref, gate_out, turned_out, mask_out, gains_out = outs
    x_in, mask_in, weight_in, gate_in, gain_in, gain_out, trans_gain = ins
    lines = x_ref.shape[1]
    pairs = [
        (x_in, x_ref),
        (weight_in.at[0], weight_ref),
        (gain_in, gain_in_ref),
        (mask_in, mask_ref),
        (gate_in.at[0], gate_ref),
        (gain_out, gain_out_ref),
        (trans_gain, trans_gain_ref),
    ]
    for copy in start_all(pairs, sems):
        copy.wait()
    mask = token_mask(mask_ref[...], lines)
    current = jnp.concatenate([line_tokens(x_ref, line).T for line in range(lines)], axis=1)
    normed = channel_norm(current, spread_gain(gain_in_ref[0:1, :]))
    emit_message(normed, halved(weight_ref[...]), mask, message_ref, stage_ref, share)
    gate_out[...] = twice_sigmoid(dot(halved(gate_ref[...]), normed))
    turned_out[...] = current
    mask_out[...] = mask
    rows = [gain_out_ref[0:1, :], gain_in_ref[1:2, :], gain_out_ref[1:2, :], trans_gain_ref[...]]
    gains_out[...] = jnp.concatenate(rows + rows, axis=0)


def one_hot(rows, columns, wanted):
    row = lax.broadcasted_iota(jnp.int32, (rows, columns), 0)
    column = lax.broadcasted_iota(jnp.int32, (rows, columns), 1)
    return (wanted(row) == column).astype(BF16)


def swap_matrix(slots, breadth):
    size = slots * LANES
    return one_hot(
        size, size, lambda lane: lane // breadth % slots * LANES + lane // LANES * breadth + lane % breadth
    )


def combine_kernel(sources, owners, breadth, share, outgoing, ins, outs):
    near, cols, rows = len(sources), len(owners), len(owners[0])
    (both_ref,), (combined_ref,) = ins, outs
    slots = LANES // breadth
    span = both_ref.shape[1]
    lines = span // (2 * share)
    pack = max(1, slots // near)
    groups = share // pack
    size = span // pack
    swap = swap_matrix(slots, breadth)

    def source(row):
        channel = row // size * groups + row // lines % groups
        return row % lines * (2 * share) + row // (groups * lines) % 2 * share + channel

    order = one_hot(span, span, source)
    blocks = [both_ref[sources[col][row]] for row in range(rows) for col in range(near)]
    ordered = dot(order, jnp.concatenate(blocks, axis=1)).astype(BF16)
    wide = []
    for row in range(rows):
        here = ordered[:, row * near * LANES : (row + 1) * near * LANES]
        wide.append(jnp.concatenate([here[n * size : (n + 1) * size] for n in range(pack)], axis=1))
    wide = jnp.concatenate(wide, axis=0)
    block = slots * LANES
    swapped = [dot(wide[:, first : first + block], swap) for first in range(0, wide.shape[1], block)]

    def whole(side, group, turned=False):
        columns = []
        for part in swapped:
            held = []
            for row in range(rows):
                first = row * size + (side * groups + group) * lines
                held += [part[first : first + lines, slot * LANES : (slot + 1) * LANES] for slot in range(slots)]
            columns.append(jnp.concatenate(held, axis=0))
        if turned:
            return jnp.concatenate([column.T for column in columns], axis=0).astype(BF16)
        return jnp.concatenate(columns, axis=1).astype(BF16)

    products = [None] * share
    for group in range(groups):
        left, right = whole(0, group, not outgoing), whole(1, group)
        if pack > 1:
            lane = lax.broadcasted_iota(jnp.int32, left.shape, 1) // (near * breadth)
            left = [jnp.where(lane == place, left, jnp.zeros_like(left)) for place in range(pack)]
            left = jnp.concatenate(left, axis=0)
        product = dot(left, right, (1, 1) if outgoing else (1, 0))
        tokens = product.shape[0] // pack
        for place in range(pack):
            products[place * groups + group] = product[place * tokens : (place + 1) * tokens]

    for high in range(cols // slots):
        lanes = slice(high * LANES, (high + 1) * LANES)
        held = []
        for row in range(rows):
            for product in products:
                parts = [
                    product[(row * slots + slot) * lines : (row * slots + slot + 1) * lines, lanes]
                    for slot in range(slots)
                ]
                held.append(jnp.concatenate(parts, axis=1))
        back = dot(jnp.concatenate(held, axis=0).astype(BF16), swap).astype(BF16)
        for low in range(slots):
            for row in range(rows):
                first = row * share * lines
                combined_ref[owners[high * slots + low][row]] = back[
                    first : first + share * lines, low * LANES : (low + 1) * LANES
                ]


def read_combined(combined_ref, stage_ref, share, sources):
    span = combined_ref.shape[1]
    lines, owners = span // share, len(sources)
    order = one_hot(span, span, lambda row: row % share * lines + row // share)
    order = jnp.concatenate([order] * len(sources[0]), axis=1)
    blocks = [jnp.concatenate([combined_ref[source] for source in held], axis=0) for held in sources]
    ordered = dot(order, jnp.concatenate(blocks, axis=1))
    parts = [ordered[:, owner * LANES : (owner + 1) * LANES] for owner in range(owners)]
    if share % 8 == 0:
        columns = [
            jnp.concatenate([part[line * share : (line + 1) * share] for part in parts], axis=0)
            for line in range(lines)
        ]
    else:
        for owner, part in enumerate(parts):
            stage_ref[owner * span : (owner + 1) * span, :] = part
        columns = [stage_ref[pl.ds(line, owners, stride=lines), :] for line in range(lines)]
    return jnp.concatenate(columns, axis=1)


def middle_kernel(share, sources, next_share, ins, outs, stage_ref, message_stage_ref):
    combined_ref, x_ref, gate_ref, mask_ref, gains_ref, proj_ref, gate_weight_ref, out_ref = ins
    message_ref, gate_out, next_ref = outs
    gain_out, gain = [spread_gain(gains_ref[n : n + 1, :]) for n in (0, 1)]
    out_t, proj_t, gate_t = halved(out_ref[0]), halved(proj_ref[1]), halved(gate_weight_ref[1])
    hidden = channel_norm(read_combined(combined_ref, stage_ref, share, sources), gain_out)
    current = x_ref[...] + gate_ref[...] * dot(out_t, hidden)
    next_ref[...] = current
    normed = channel_norm(current, gain)
    emit_message(normed, proj_t, mask_ref[...], message_ref, message_stage_ref, next_share)
    gate_out[...] = twice_sigmoid(dot(gate_t, normed))


def last_kernel(share, sources, chunk, ins, outs, stage_ref, result_ref, sems):
    combined_ref, x_ref, gate_ref, gains_ref, out_ref, up_ref, down_ref = ins
    (result_out,) = outs
    slots, lines, breadth, channels = result_ref.shape
    half = down_ref.shape[0]
    count = chunk // LANES
    gain_out, gain = [spread_gain(gains_ref[n : n + 1, :]) for n in (2, 3)]
    out_t, down_t = halved(out_ref[1]), down_ref[...].T
    gate_t, up_t = halved(up_ref[:, :half]), up_ref[:, half:].T
    hidden = channel_norm(read_combined(combined_ref, stage_ref, share, sources), gain_out)
    current = x_ref[...] + gate_ref[...] * dot(out_t, hidden)
    trans_in = channel_norm(current, gain)
    gate_part, up_part = dot(gate_t, trans_in), dot(up_t, trans_in)
    trans_hidden = (gate_part * twice_sigmoid(gate_part) * up_part).astype(BF16)
    current = current + dot(down_t, trans_hidden)
    writes = []
    for first in range(0, lines, count):
        for line in range(first, first + count):
            result = current[:, line * LANES : (line + 1) * LANES].T
            for slot in range(slots):
                result_ref[slot, line] = result[slot * breadth : (slot + 1) * breadth]
        piece = slice(first, first + count)
        writes += start_all([(result_ref.at[:, piece], result_out.at[:, piece])], sems, first // count)
    for write in writes:
        write.wait()


def call(kernel, operands, outs, scratch=(), in_hbm=False, out_hbm=False):
    in_place, held = pl.BlockSpec(memory_space=pltpu.HBM), pl.BlockSpec(memory_space=pltpu.VMEM)
    count = len(operands)

    def body(*refs):
        kernel(refs[:count], refs[count : count + len(outs)], *refs[count + len(outs) :])

    return pl.pallas_call(
        body,
        in_specs=[in_place if in_hbm else held] * count,
        out_specs=[in_place if out_hbm else held] * len(outs),
        out_shape=[jax.ShapeDtypeStruct(shape, dtype) for shape, dtype in outs],
        scratch_shapes=list(scratch),
        compiler_params=pltpu.CompilerParams(vmem_limit_bytes=VMEM_BYTES),
    )(*[pltpu.with_memory_space_constraint(array, pltpu.HBM) if in_hbm else array for array in operands])


def exchange(values, axes, order=None):
    groups = [order] if order else None
    return lax.all_to_all(values, axes, split_axis=0, concat_axis=0, axis_index_groups=groups, tiled=True)


def per_device(
    rows,
    halves,
    nears,
    pair_map,
    pair_mask,
    gain_in,
    proj_weight,
    gate_weight,
    gain_out,
    out_weight,
    trans_gain,
    trans_up,
    trans_down,
):
    height, breadth, channels = pair_map.shape
    tokens = height * breadth
    lines = tokens // LANES
    hid = gain_out.shape[1]
    cols = halves * nears
    owners = rows * cols
    share = hid // owners
    chunk = tokens
    split = halves if share % 8 == 0 else 1
    first_share = split * share
    held = ((LANES // breadth, lines, breadth, channels), F32)
    grouped = pair_map.reshape(held[0])
    wide = ((channels, tokens), F32)
    result = pltpu.VMEM((owners * share * lines, LANES), F32)
    spare = pltpu.VMEM((8, LANES) if share % 8 == 0 else (owners * 2 * share * lines, LANES), F32)

    def message(own):
        return ((hid // own, 2 * own * lines, LANES), BF16)

    blocks = list(range(cols))
    blocks.insert(0, blocks.pop((cols - 1) // 2))
    order = [col * rows + row for col in blocks for row in range(rows)]
    everyone = [[order.index(col * rows + row) for row in range(rows)] for col in range(cols)]
    beside = [[near * rows + row for row in range(rows)] for near in range(nears)] if split > 1 else everyone
    single = [[n] for n in range(owners)]
    paired = single if split == 1 else [
        [everyone[half * nears + near][row] for half in range(halves)] for near in range(nears) for row in range(rows)
    ]

    def combine(both, own, sources, outgoing):
        kernel = functools.partial(combine_kernel, sources, everyone, breadth, own, outgoing)
        answer = ((owners, own * lines, LANES), BF16)
        return exchange(call(kernel, (both,), [answer])[0], ALL_AXES, order)

    operands = (grouped, pair_mask, proj_weight, gate_weight, gain_in, gain_out, trans_gain.reshape(1, -1))
    both, gate, current, mask, gains = call(
        functools.partial(project_kernel, first_share),
        operands,
        [message(first_share), wide, wide, ((lines, LANES), F32), ((8, channels), F32)],
        (
            spare,
            *[
                pltpu.VMEM(array.shape[1:] if array.ndim == 3 else array.shape, array.dtype)
                for array in operands
            ],
            pltpu.SemaphoreType.DMA((len(operands),)),
        ),
        in_hbm=True,
    )
    both = exchange(both, NEAR_AXES) if split > 1 else exchange(both, ALL_AXES, order)
    combined = combine(both, first_share, beside, True)
    both, gate, current = call(
        functools.partial(middle_kernel, first_share, paired, share),
        (combined, current, gate, mask, gains, proj_weight, gate_weight, out_weight),
        [message(share), wide, wide],
        (result, spare),
    )
    combined = combine(exchange(both, ALL_AXES, order), share, everyone, False)
    (pair_out,) = call(
        functools.partial(last_kernel, share, single, chunk),
        (combined, current, gate, gains, out_weight, trans_up, trans_down),
        [held],
        (result, pltpu.VMEM(*held), pltpu.SemaphoreType.DMA((tokens // chunk,))),
        out_hbm=True,
    )
    return pair_out.reshape(pair_map.shape)


def solution(mesh):
    groups, rows, cols = (mesh.shape[name] for name in ("grp", "row", "col"))
    halves = 2 if cols % 2 == 0 else 1
    nears = cols // halves
    folded = Mesh(mesh.devices.reshape(groups, rows, halves, nears), ("grp", "row", "half", "near"))
    tokens = (("grp", "row"), ("half", "near"))
    in_specs = (P(*tokens, None), P(*tokens)) + (P(),) * 8

    def body(*args):
        return per_device(rows, halves, nears, *args)

    return jax.shard_map(body, mesh=folded, in_specs=in_specs, out_specs=P(*tokens, None), check_vma=False)
```

```python
import functools

import jax
import jax.numpy as jnp
from jax import lax
from jax.experimental import pallas as pl
from jax.experimental.pallas import tpu as pltpu
from jax.sharding import Mesh
from jax.sharding import PartitionSpec as P

NEAR_AXES = ("near", "row")
ALL_AXES = ("half", "near", "row")
LANES = 128
VMEM_BYTES = 24 * 1024 * 1024
F32, BF16 = jnp.float32, jnp.bfloat16


def dot(left, right, contract=(1, 0)):
    return lax.dot_general(
        left, right, (((contract[0],), (contract[1],)), ((), ())), preferred_element_type=F32
    )


def halved(weight):
    return weight.T * 0.5


def twice_sigmoid(half):
    return jnp.tanh(half) + 1.0


def channel_norm(values, gain):
    wide = jnp.concatenate([gain] * (values.shape[1] // LANES), axis=1)
    centred = values - jnp.mean(values, axis=0, keepdims=True)
    spread = jnp.mean(centred * centred, axis=0, keepdims=True)
    return (centred * lax.rsqrt(spread + 1e-05) * wide).astype(BF16)


def spread_gain(row):
    return jnp.broadcast_to(row, (LANES, row.shape[1])).T


def token_mask(mask, lines):
    height, breadth = mask.shape
    wide = jnp.concatenate([mask.astype(F32)] * (LANES // breadth), axis=1)
    row = lax.broadcasted_iota(jnp.int32, wide.shape, 0)
    lane = lax.broadcasted_iota(jnp.int32, wide.shape, 1)
    wide = jnp.where(row // lines == lane // breadth, wide, 0.0).astype(BF16)
    line = lax.broadcasted_iota(jnp.int32, (lines, height), 0)
    source = lax.broadcasted_iota(jnp.int32, (lines, height), 1)
    return dot((source % lines == line).astype(BF16), wide)


def emit_message(normed, weight_t, mask, message_ref, stage_ref, share):
    projected = dot(weight_t, normed)
    hid = weight_t.shape[0] // 4
    owners, lines = hid // share, mask.shape[0]
    for line in range(lines):
        here = projected[:, line * LANES : (line + 1) * LANES]
        keep = mask[line : line + 1]
        left = twice_sigmoid(here[:hid]) * here[hid : 2 * hid] * keep
        right = twice_sigmoid(here[2 * hid : 3 * hid]) * here[3 * hid :] * keep
        if share % 8 == 0:
            for owner in range(owners):
                rows = slice(owner * share, (owner + 1) * share)
                both = jnp.concatenate([left[rows], right[rows]], axis=0).astype(BF16)
                message_ref[owner, 2 * share * line : 2 * share * (line + 1), :] = both
        else:
            stage_ref[pl.ds(2 * line, owners, stride=2 * lines), :] = left
            stage_ref[pl.ds(2 * line + 1, owners, stride=2 * lines), :] = right
    if share % 8:
        message_ref[...] = stage_ref[...].astype(BF16).reshape(message_ref.shape)


def start_all(pairs, sems, first=0):
    copies = [pltpu.make_async_copy(src, dst, sems.at[first + n]) for n, (src, dst) in enumerate(pairs)]
    for copy in copies:
        copy.start()
    return copies


def line_tokens(x_ref, line):
    return jnp.concatenate([x_ref[slot, line] for slot in range(x_ref.shape[0])], axis=0)


def project_kernel(share, ins, outs, stage_ref, x_ref, mask_ref, weight_ref, gate_ref, gain_in_ref, gain_out_ref, trans_gain_ref, sems):
    message_ref, gate_out, turned_out, mask_out, gains_out = outs
    x_in, mask_in, weight_in, gate_in, gain_in, gain_out, trans_gain = ins
    lines = x_ref.shape[1]
    pairs = [
        (x_in, x_ref),
        (weight_in.at[0], weight_ref),
        (gain_in, gain_in_ref),
        (mask_in, mask_ref),
        (gate_in.at[0], gate_ref),
        (gain_out, gain_out_ref),
        (trans_gain, trans_gain_ref),
    ]
    for copy in start_all(pairs, sems):
        copy.wait()
    mask = token_mask(mask_ref[...], lines)
    current = jnp.concatenate([line_tokens(x_ref, line).T for line in range(lines)], axis=1)
    normed = channel_norm(current, spread_gain(gain_in_ref[0:1, :]))
    emit_message(normed, halved(weight_ref[...]), mask, message_ref, stage_ref, share)
    gate_out[...] = twice_sigmoid(dot(halved(gate_ref[...]), normed))
    turned_out[...] = current
    mask_out[...] = mask
    rows = [gain_out_ref[0:1, :], gain_in_ref[1:2, :], gain_out_ref[1:2, :], trans_gain_ref[...]]
    gains_out[...] = jnp.concatenate(rows + rows, axis=0)


def one_hot(rows, columns, wanted):
    row = lax.broadcasted_iota(jnp.int32, (rows, columns), 0)
    column = lax.broadcasted_iota(jnp.int32, (rows, columns), 1)
    return (wanted(row) == column).astype(BF16)


def swap_matrix(slots, breadth):
    size = slots * LANES
    return one_hot(
        size, size, lambda lane: lane // breadth % slots * LANES + lane // LANES * breadth + lane % breadth
    )


def combine_kernel(sources, owners, breadth, share, outgoing, ins, outs):
    near, cols, rows = len(sources), len(owners), len(owners[0])
    (both_ref,), (combined_ref,) = ins, outs
    slots = LANES // breadth
    span = both_ref.shape[1]
    lines = span // (2 * share)
    pack = max(1, slots // near)
    groups = share // pack
    size = span // pack
    swap = swap_matrix(slots, breadth)

    def source(row):
        channel = row // size * groups + row // lines % groups
        return row % lines * (2 * share) + row // (groups * lines) % 2 * share + channel

    order = one_hot(span, span, source)
    blocks = [both_ref[sources[col][row]] for row in range(rows) for col in range(near)]
    ordered = dot(order, jnp.concatenate(blocks, axis=1)).astype(BF16)
    wide = []
    for row in range(rows):
        here = ordered[:, row * near * LANES : (row + 1) * near * LANES]
        wide.append(jnp.concatenate([here[n * size : (n + 1) * size] for n in range(pack)], axis=1))
    wide = jnp.concatenate(wide, axis=0)
    block = slots * LANES
    swapped = [dot(wide[:, first : first + block], swap) for first in range(0, wide.shape[1], block)]

    def whole(side, group, turned=False):
        columns = []
        for part in swapped:
            held = []
            for row in range(rows):
                first = row * size + (side * groups + group) * lines
                held += [part[first : first + lines, slot * LANES : (slot + 1) * LANES] for slot in range(slots)]
            columns.append(jnp.concatenate(held, axis=0))
        if turned:
            return jnp.concatenate([column.T for column in columns], axis=0).astype(BF16)
        return jnp.concatenate(columns, axis=1).astype(BF16)

    products = [None] * share
    for group in range(groups):
        left, right = whole(0, group, not outgoing), whole(1, group)
        if pack > 1:
            lane = lax.broadcasted_iota(jnp.int32, left.shape, 1) // (near * breadth)
            left = [jnp.where(lane == place, left, jnp.zeros_like(left)) for place in range(pack)]
            left = jnp.concatenate(left, axis=0)
        product = dot(left, right, (1, 1) if outgoing else (1, 0))
        tokens = product.shape[0] // pack
        for place in range(pack):
            products[place * groups + group] = product[place * tokens : (place + 1) * tokens]

    for high in range(cols // slots):
        lanes = slice(high * LANES, (high + 1) * LANES)
        held = []
        for row in range(rows):
            for product in products:
                parts = [
                    product[(row * slots + slot) * lines : (row * slots + slot + 1) * lines, lanes]
                    for slot in range(slots)
                ]
                held.append(jnp.concatenate(parts, axis=1))
        back = dot(jnp.concatenate(held, axis=0).astype(BF16), swap).astype(BF16)
        for low in range(slots):
            for row in range(rows):
                first = row * share * lines
                combined_ref[owners[high * slots + low][row]] = back[
                    first : first + share * lines, low * LANES : (low + 1) * LANES
                ]


def read_combined(combined_ref, stage_ref, share, sources):
    span = combined_ref.shape[1]
    lines, owners = span // share, len(sources)
    order = one_hot(span, span, lambda row: row % share * lines + row // share)
    order = jnp.concatenate([order] * len(sources[0]), axis=1)
    blocks = [jnp.concatenate([combined_ref[source] for source in held], axis=0) for held in sources]
    ordered = dot(order, jnp.concatenate(blocks, axis=1))
    parts = [ordered[:, owner * LANES : (owner + 1) * LANES] for owner in range(owners)]
    if share % 8 == 0:
        columns = [
            jnp.concatenate([part[line * share : (line + 1) * share] for part in parts], axis=0)
            for line in range(lines)
        ]
    else:
        for owner, part in enumerate(parts):
            stage_ref[owner * span : (owner + 1) * span, :] = part
        columns = [stage_ref[pl.ds(line, owners, stride=lines), :] for line in range(lines)]
    return jnp.concatenate(columns, axis=1)


def middle_kernel(share, sources, next_share, ins, outs, stage_ref, message_stage_ref):
    combined_ref, x_ref, gate_ref, mask_ref, gains_ref, proj_ref, gate_weight_ref, out_ref = ins
    message_ref, gate_out, next_ref = outs
    gain_out, gain = [spread_gain(gains_ref[n : n + 1, :]) for n in (0, 1)]
    out_t, proj_t, gate_t = halved(out_ref[0]), halved(proj_ref[1]), halved(gate_weight_ref[1])
    hidden = channel_norm(read_combined(combined_ref, stage_ref, share, sources), gain_out)
    current = x_ref[...] + gate_ref[...] * dot(out_t, hidden)
    next_ref[...] = current
    normed = channel_norm(current, gain)
    emit_message(normed, proj_t, mask_ref[...], message_ref, message_stage_ref, next_share)
    gate_out[...] = twice_sigmoid(dot(gate_t, normed))


def last_kernel(share, sources, chunk, ins, outs, stage_ref, result_ref, sems):
    combined_ref, x_ref, gate_ref, gains_ref, out_ref, up_ref, down_ref = ins
    (result_out,) = outs
    slots, lines, breadth, channels = result_ref.shape
    half = down_ref.shape[0]
    count = chunk // LANES
    gain_out, gain = [spread_gain(gains_ref[n : n + 1, :]) for n in (2, 3)]
    out_t, down_t = halved(out_ref[1]), down_ref[...].T
    gate_t, up_t = halved(up_ref[:, :half]), up_ref[:, half:].T
    hidden = channel_norm(read_combined(combined_ref, stage_ref, share, sources), gain_out)
    current = x_ref[...] + gate_ref[...] * dot(out_t, hidden)
    trans_in = channel_norm(current, gain)
    gate_part, up_part = dot(gate_t, trans_in), dot(up_t, trans_in)
    trans_hidden = (gate_part * twice_sigmoid(gate_part) * up_part).astype(BF16)
    current = current + dot(down_t, trans_hidden)
    writes = []
    for first in range(0, lines, count):
        for line in range(first, first + count):
            result = current[:, line * LANES : (line + 1) * LANES].T
            for slot in range(slots):
                result_ref[slot, line] = result[slot * breadth : (slot + 1) * breadth]
        piece = slice(first, first + count)
        writes += start_all([(result_ref.at[:, piece], result_out.at[:, piece])], sems, first // count)
    for write in writes:
        write.wait()


def call(kernel, operands, outs, scratch=(), in_hbm=False, out_hbm=False):
    in_place, held = pl.BlockSpec(memory_space=pltpu.HBM), pl.BlockSpec(memory_space=pltpu.VMEM)
    count = len(operands)

    def body(*refs):
        kernel(refs[:count], refs[count : count + len(outs)], *refs[count + len(outs) :])

    return pl.pallas_call(
        body,
        in_specs=[in_place if in_hbm else held] * count,
        out_specs=[in_place if out_hbm else held] * len(outs),
        out_shape=[jax.ShapeDtypeStruct(shape, dtype) for shape, dtype in outs],
        scratch_shapes=list(scratch),
        compiler_params=pltpu.CompilerParams(vmem_limit_bytes=VMEM_BYTES),
    )(*[pltpu.with_memory_space_constraint(array, pltpu.HBM) if in_hbm else array for array in operands])


def exchange(values, axes, order=None):
    groups = [order] if order else None
    return lax.all_to_all(values, axes, split_axis=0, concat_axis=0, axis_index_groups=groups, tiled=True)


def per_device(
    rows,
    halves,
    nears,
    pair_map,
    pair_mask,
    gain_in,
    proj_weight,
    gate_weight,
    gain_out,
    out_weight,
    trans_gain,
    trans_up,
    trans_down,
):
    height, breadth, channels = pair_map.shape
    tokens = height * breadth
    lines = tokens // LANES
    hid = gain_out.shape[1]
    cols = halves * nears
    owners = rows * cols
    share = hid // owners
    chunk = min(2 * LANES, tokens)
    split = halves if share % 8 == 0 else 1
    first_share = split * share
    held = ((LANES // breadth, lines, breadth, channels), F32)
    grouped = pair_map.reshape(held[0])
    wide = ((channels, tokens), F32)
    result = pltpu.VMEM((owners * share * lines, LANES), F32)
    spare = pltpu.VMEM((8, LANES) if share % 8 == 0 else (owners * 2 * share * lines, LANES), F32)

    def message(own):
        return ((hid // own, 2 * own * lines, LANES), BF16)

    blocks = list(range(cols))
    blocks.insert(0, blocks.pop((cols - 1) // 2))
    order = [col * rows + row for col in blocks for row in range(rows)]
    everyone = [[order.index(col * rows + row) for row in range(rows)] for col in range(cols)]
    beside = [[near * rows + row for row in range(rows)] for near in range(nears)] if split > 1 else everyone
    single = [[n] for n in range(owners)]
    paired = single if split == 1 else [
        [everyone[half * nears + near][row] for half in range(halves)] for near in range(nears) for row in range(rows)
    ]

    def combine(both, own, sources, outgoing):
        kernel = functools.partial(combine_kernel, sources, everyone, breadth, own, outgoing)
        answer = ((owners, own * lines, LANES), BF16)
        return exchange(call(kernel, (both,), [answer])[0], ALL_AXES, order)

    operands = (grouped, pair_mask, proj_weight, gate_weight, gain_in, gain_out, trans_gain.reshape(1, -1))
    both, gate, current, mask, gains = call(
        functools.partial(project_kernel, first_share),
        operands,
        [message(first_share), wide, wide, ((lines, LANES), F32), ((8, channels), F32)],
        (
            spare,
            *[
                pltpu.VMEM(array.shape[1:] if array.ndim == 3 else array.shape, array.dtype)
                for array in operands
            ],
            pltpu.SemaphoreType.DMA((len(operands),)),
        ),
        in_hbm=True,
    )
    both = exchange(both, NEAR_AXES) if split > 1 else exchange(both, ALL_AXES, order)
    combined = combine(both, first_share, beside, True)
    both, gate, current = call(
        functools.partial(middle_kernel, first_share, paired, share),
        (combined, current, gate, mask, gains, proj_weight, gate_weight, out_weight),
        [message(share), wide, wide],
        (result, spare),
    )
    combined = combine(exchange(both, ALL_AXES, order), share, everyone, False)
    (pair_out,) = call(
        functools.partial(last_kernel, share, single, chunk),
        (combined, current, gate, gains, out_weight, trans_up, trans_down),
        [held],
        (result, pltpu.VMEM(*held), pltpu.SemaphoreType.DMA((tokens // chunk,))),
        out_hbm=True,
    )
    return pair_out.reshape(pair_map.shape)


def solution(mesh):
    groups, rows, cols = (mesh.shape[name] for name in ("grp", "row", "col"))
    halves = 2 if cols % 2 == 0 else 1
    nears = cols // halves
    folded = Mesh(mesh.devices.reshape(groups, rows, halves, nears), ("grp", "row", "half", "near"))
    tokens = (("grp", "row"), ("half", "near"))
    in_specs = (P(*tokens, None), P(*tokens)) + (P(),) * 8

    def body(*args):
        return per_device(rows, halves, nears, *args)

    return jax.shard_map(body, mesh=folded, in_specs=in_specs, out_specs=P(*tokens, None), check_vma=False)
```
